32 devices in a mesh: groups: 2 (over y), tok: 8 (over z, core), head: 2 (over x), tile: 1.
Axes of the slice: x: 2, y: 2, z: 4, core: 2. Of those that a mesh axis runs over, the one named last changes fastest.
Arguments:
- queries: bfloat16 [3072, 1, 16, 320], P(('groups', 'tok'), 'tile', 'head'), parts along dimension 0, may hold values from -6 to 6
- keys: bfloat16 [3072, 1, 16, 320], P(('groups', 'tok'), 'tile', 'head'), parts along dimension 0, may hold values from -6 to 6
- values: bfloat16 [3072, 1, 16, 320], P(('groups', 'tok'), 'tile', 'head'), parts along dimension 0, may hold values from -6 to 6
- rates: float32 [1, 16, 3072], P('tile', 'head', ('groups', 'tok')), parts along dimension 2, may hold values from 0.0003 to 0.003
- fast_weights: bfloat16 [1, 16, 3, 320, 320], P('tile', 'head'), may hold values from -0.3125 to 0.3125
- norm_gain: float32 [1, 16, 320], P('tile', 'head'), may hold values from 0.5 to 1.5
- frame_order: int32 [16], P('groups'), parts along dimension 0, may hold values from 0 to 7, each once
- gate_input: bfloat16 [24, 16, 8, 5120], P(None, ('groups', 'head'), 'tok', 'tile'), parts along dimension 1, may hold values from -6 to 6
- conv_weights: float32 [3, 3, 5120], P(None, None, 'tile'), may hold values from -2.5 to 2.5
Outputs:
- output: bfloat16 [24, 16, 8, 5120], P(None, ('groups', 'head'), 'tok', 'tile'), parts along dimension 1
The draws below stay inside these ranges and needn't reach their ends.
There are 2 independent parts, one for each index of `groups`. The reference program is written for one: setup_inputs(seed, part) draws one part's arguments, and reference() takes and returns one part's arrays. A program takes and returns all parts, laid end to end along the dimension named above; an argument that names none is the same for every part. Nothing has to cross between parts.
Inputs may be any that keep to these rules, and one draw needn't show every extreme that they name: frame_order names each of the 8 frames once.
All inputs are finite; a program needn't handle non-finite values.
Results may differ from the reference program's by a relative error of at most 0.011.
Values may be sent and summed in bfloat16 or wider, within the bound.
No kernel may reach another device: no remote copies, remote signals or barrier semaphores. Data moves between devices by JAX's collectives and lax.ppermute only.
A program may use at most 64 MiB of HBM per device.

```python
import math
import jax
import jax.numpy as jnp
from jax import lax

HEADS = 16
DH = 320
FH = 320
HT = 24
D = 5120
HEAD_BLOCKS = 1
TILE_HEADS = 16
WT = 8
F = 8
TOKENS = 1536


def level_of(stream_key, extent, cuts, low, top_value):
    def one(dim, blocks):
        heights = jax.random.uniform(jax.random.fold_in(jax.random.fold_in(stream_key, 6), dim), (blocks,), jnp.float32, low / len(cuts), top_value / len(cuts))
        return jnp.repeat(jnp.exp(heights), extent[dim] // blocks).reshape((-1,) + (1,) * (len(extent) - dim - 1))

    level = one(*cuts[0])
    for cut in cuts[1:]:
        level = level * one(*cut)
    return level


def centred(stream_key, dims, scale, reach, pieces=(), kind=jnp.bfloat16):
    entries = scale * jax.random.normal(stream_key, dims, jnp.float32)
    if pieces:
        entries = entries * level_of(stream_key, dims, pieces, -0.22, 0.18)
    return jnp.clip(entries, -reach, reach).astype(kind)


def setup_inputs(seed: int = 0, part: int = 0) -> dict:
    streams_of = jax.random.split(jax.random.key(seed), 10)
    part_keys = jax.random.split(jax.random.fold_in(streams_of[9], part), 10)
    queries = centred(part_keys[0], (TOKENS, HEAD_BLOCKS, TILE_HEADS, DH), 1.0, 6.0, ((0, 8), (2, 2)))
    keys = centred(part_keys[1], (TOKENS, HEAD_BLOCKS, TILE_HEADS, DH), 1.0, 6.0, ((0, 8), (2, 2)))
    values = centred(part_keys[2], (TOKENS, HEAD_BLOCKS, TILE_HEADS, DH), 1.0, 6.0, ((0, 8), (2, 2)))
    rates = jnp.clip(jnp.exp(math.log(0.003) - 2.3025851 * jax.random.uniform(part_keys[3], (HEAD_BLOCKS, TILE_HEADS, TOKENS), jnp.float32) ** level_of(part_keys[3], (HEAD_BLOCKS, TILE_HEADS, TOKENS), ((1, 2), (2, 8)), -0.2, 0.2)), 0.0003, 0.003)
    fast_weights = centred(streams_of[4], (HEAD_BLOCKS, TILE_HEADS, 3, FH, DH), DH ** -0.5, 0.3125, ((1, 2),))
    norm_gain = jnp.clip(1.0 + 0.1 * jax.random.normal(streams_of[5], (HEAD_BLOCKS, TILE_HEADS, DH), jnp.float32), 0.5, 1.5)
    frame_order = jax.random.permutation(part_keys[6], F).astype(jnp.int32)
    gate_input = centred(part_keys[7], (HT, F, WT, D), 1.0, 6.0, ((1, 2), (2, 8)))
    conv_weights = centred(streams_of[8], (3, 3, D), 0.35, 2.5, (), jnp.float32)
    return {"queries": queries, "keys": keys, "values": values, "rates": rates, "fast_weights": fast_weights, "norm_gain": norm_gain, "frame_order": frame_order, "gate_input": gate_input, "conv_weights": conv_weights}


epsilon = 1e-06

def renormed(previous, gradient):
    before = previous.astype(jnp.float32)
    updated = before - gradient
    scale_old = jnp.sqrt(lax.optimization_barrier(jnp.mean(before * before, axis=-1, keepdims=True)) + epsilon)
    scale_new = jnp.sqrt(lax.optimization_barrier(jnp.mean(updated * updated, axis=-1, keepdims=True)) + epsilon)
    return (updated * (scale_old / scale_new)).astype(jnp.bfloat16)

def one_head(items):
    key_head, value_head, query_head, rate_head, weight_head, gain_head = items
    first_pre = jnp.dot(key_head, weight_head[0].T, preferred_element_type=jnp.float32)
    third_pre = jnp.dot(key_head, weight_head[1].T, preferred_element_type=jnp.float32)
    sigmoid_first = jax.nn.sigmoid(first_pre)
    activated = first_pre * sigmoid_first
    hidden = (activated * third_pre).astype(jnp.bfloat16)
    target = (-rate_head[:, None] * value_head.astype(jnp.float32)).astype(jnp.bfloat16)
    grad_down = jnp.dot(target.T, hidden, preferred_element_type=jnp.float32)
    hidden_grad = jnp.dot(target, weight_head[2], preferred_element_type=jnp.float32)
    grad_first_in = (hidden_grad * third_pre * sigmoid_first * (1.0 + first_pre * (1.0 - sigmoid_first))).astype(jnp.bfloat16)
    grad_third_in = (hidden_grad * activated).astype(jnp.bfloat16)
    grad_first = jnp.dot(grad_first_in.T, key_head, preferred_element_type=jnp.float32)
    grad_third = jnp.dot(grad_third_in.T, key_head, preferred_element_type=jnp.float32)
    gradients = jnp.stack([grad_first, grad_third, grad_down], axis=0)
    updated = renormed(weight_head, gradients)
    proj_first = jnp.dot(query_head, updated[0].T, preferred_element_type=jnp.float32)
    proj_third = jnp.dot(query_head, updated[1].T, preferred_element_type=jnp.float32)
    mixed_hidden = (jax.nn.silu(proj_first) * proj_third).astype(jnp.bfloat16)
    outputs = jnp.dot(mixed_hidden, updated[2].T, preferred_element_type=jnp.float32)
    normed = outputs * lax.rsqrt(lax.optimization_barrier(jnp.mean(outputs * outputs, axis=-1, keepdims=True)) + epsilon) * gain_head[None, :]
    return normed.astype(jnp.bfloat16)

def reference(queries, keys, values, rates, fast_weights, norm_gain, frame_order, gate_input, conv_weights):
    query_rows = jnp.moveaxis(queries.reshape(TOKENS, HEADS, DH), 1, 0)
    key_rows = jnp.moveaxis(keys.reshape(TOKENS, HEADS, DH), 1, 0)
    value_rows = jnp.moveaxis(values.reshape(TOKENS, HEADS, DH), 1, 0)
    token_rates = rates.reshape(HEADS, TOKENS)
    weights = fast_weights.reshape(HEADS, 3, DH, DH)
    head_gains = norm_gain.reshape(HEADS, DH)
    normed_all = lax.map(one_head, (key_rows, value_rows, query_rows, token_rates, weights, head_gains))
    flat = jnp.moveaxis(normed_all, 0, 1).reshape(F, HT, WT, D)
    numbers = jnp.arange(F, dtype=jnp.int32)
    inverse = lax.optimization_barrier(jnp.sum(jnp.where(frame_order[None, :] == numbers[:, None], numbers[None, :], 0), axis=1)).astype(jnp.int32)
    frames = jnp.take(flat, inverse, axis=0)
    frame_grid = jnp.transpose(frames, (1, 0, 2, 3))
    padded = jnp.pad(frame_grid, ((1, 1), (0, 0), (1, 1), (0, 0)))
    result = jnp.zeros((HT, F, WT, D), jnp.float32)
    for row_tap in range(3):
        for col_tap in range(3):
            result = result + conv_weights[row_tap, col_tap] * padded[row_tap:row_tap + HT, :, col_tap:col_tap + WT].astype(jnp.float32)
    rounded = lax.optimization_barrier(result.astype(jnp.bfloat16))
    return (rounded.astype(jnp.float32) * jax.nn.silu(gate_input.astype(jnp.float32))).astype(jnp.bfloat16)
```

```python
import functools

import jax
import jax.numpy as jnp
from jax import lax
from jax.experimental import pallas as pl
from jax.experimental.pallas import tpu as pltpu
from jax.sharding import PartitionSpec as P

epsilon = 1e-06
LANES = 128
VMEM_BYTES = 56 * 1024 * 1024


def split_lanes(source, scratch, rows, head_size):
    full = head_size // LANES
    tail = head_size - full * LANES
    wide = source.reshape(rows, head_size).astype(jnp.float32)
    for tile in range(full):
        scratch[tile] = wide[:, tile * LANES : (tile + 1) * LANES]
    scratch[full, :, 0:tail] = wide[:, full * LANES :]


def join_halves(first, second, tail):
    lane = lax.broadcasted_iota(jnp.int32, first[-1].shape, 1)
    middle = jnp.where(lane < tail, first[-1], pltpu.roll(second[-1], tail, 1))
    return first[:-1] + [middle] + second[:-1]


def part_halves(packed, head_size):
    full = head_size // LANES
    tail = head_size - full * LANES
    first = packed[:, :head_size]
    middle = packed[:, head_size : (full + 1) * LANES]
    second = jnp.concatenate([packed[:, (full + 1) * LANES :], middle], axis=1)
    return first, second


def pack_pairs_kernel(key_ref, value_ref, rate_ref, out_ref, key_tiles, value_tiles):
    tok_rows, heads, head_size = key_ref.shape
    half = tok_rows // 2
    full = head_size // LANES
    tail = head_size - full * LANES
    split_lanes(key_ref[...], key_tiles, tok_rows * heads, head_size)
    split_lanes(value_ref[...], value_tiles, tok_rows * heads, head_size)
    columns = rate_ref[...]
    for head in range(heads):
        for row, tiles in ((0, key_tiles), (half, value_tiles)):
            sides = []
            for side in range(2):
                parts = [
                    tiles[tile, pl.ds(side * half * heads + head, half, stride=heads), :]
                    for tile in range(full + 1)
                ]
                if tiles is value_tiles:
                    rate = -columns[side * half : (side + 1) * half, head : head + 1]
                    parts = [rate * part for part in parts]
                sides.append(parts)
            for tile, part in enumerate(join_halves(sides[0], sides[1], tail)):
                out_ref[head, row : row + half, tile * LANES : (tile + 1) * LANES] = part.astype(
                    jnp.bfloat16
                )


def pack_queries_kernel(height, query_ref, out_ref, query_tiles):
    tok_rows, heads, head_size = query_ref.shape
    half = tok_rows // 2
    width = tok_rows // height
    full = head_size // LANES
    tail = head_size - full * LANES
    split_lanes(query_ref[...], query_tiles, tok_rows * heads, head_size)
    for head in range(heads):
        sides = []
        for side in range(2):
            sides.append(
                [
                    jnp.concatenate(
                        [
                            query_tiles[
                                tile, pl.ds(column * heads + head, height, stride=width * heads), :
                            ]
                            for column in range(side * width // 2, (side + 1) * width // 2)
                        ],
                        axis=0,
                    )
                    for tile in range(full + 1)
                ]
            )
        for tile, part in enumerate(join_halves(sides[0], sides[1], tail)):
            out_ref[head, :, tile * LANES : (tile + 1) * LANES] = part.astype(jnp.bfloat16)


def contract(first, second, dims):
    return lax.dot_general(first, second, (dims, ((), ())), preferred_element_type=jnp.float32)


NN = ((1,), (0,))
NT = ((1,), (1,))


def update_kernel(step, pair_ref, weight_ref, out_ref, grad_ref):
    shards, rows, _ = pair_ref.shape
    half = rows // 2
    head_size = weight_ref.shape[-1]
    first_weight = weight_ref[0]
    third_weight = weight_ref[1]
    down_turned = weight_ref[2].astype(jnp.float32).T.astype(jnp.bfloat16)
    for start in range(0, shards, step):
        key_parts, target_parts = [], []
        for shard in range(start, start + step):
            key_parts.extend(part_halves(pair_ref[shard, 0:half, :], head_size))
            target_parts.extend(part_halves(pair_ref[shard, half:rows, :], head_size))
        key_rows = jnp.concatenate(key_parts, axis=0)
        target = jnp.concatenate(target_parts, axis=0)
        first_pre = contract(first_weight, key_rows, NT)
        third_pre = contract(third_weight, key_rows, NT)
        hidden_grad = contract(down_turned, target, NT)
        sigmoid_first = jax.nn.sigmoid(first_pre)
        activated = first_pre * sigmoid_first
        hidden = (activated * third_pre).astype(jnp.bfloat16)
        grad_first_in = (
            hidden_grad * third_pre * sigmoid_first * (1.0 + first_pre * (1.0 - sigmoid_first))
        ).astype(jnp.bfloat16)
        grad_third_in = (hidden_grad * activated).astype(jnp.bfloat16)
        grads = (
            contract(grad_first_in, key_rows, NN),
            contract(grad_third_in, key_rows, NN),
            contract(hidden, target, NN),
        )
        for index, grad in enumerate(grads):
            if start == 0:
                grad_ref[index] = grad
            else:
                grad_ref[index] += grad
    for index in range(3):
        before = weight_ref[index].astype(jnp.float32)
        axis = 1
        if index == 2:
            before = before.T
            axis = 0
        updated = before - grad_ref[index]
        scale_old = jnp.sqrt(jnp.mean(before * before, axis=axis, keepdims=True) + epsilon)
        scale_new = jnp.sqrt(jnp.mean(updated * updated, axis=axis, keepdims=True) + epsilon)
        out_ref[index] = (updated * (scale_old / scale_new)).astype(jnp.bfloat16)


def apply_kernel(
    height, frames_here, order_ref, query_ref, weight_ref, gain_ref, tap_ref, out_ref, grid_ref, turned_ref
):
    shards, half, _ = query_ref.shape
    width = 2 * half // height
    head_size = weight_ref.shape[-1]
    full = head_size // LANES
    tail = head_size - full * LANES
    padded = (full + 1) * LANES
    top = 8
    for shard in range(shards):
        zeros = jnp.zeros(grid_ref.shape[2:], jnp.float32)
        grid_ref[shard, 0] = zeros
        grid_ref[shard, width + 1] = zeros
        for column in range(1, width + 1):
            grid_ref[shard, column, 0:top] = zeros[0:top]
            grid_ref[shard, column, top + height :] = zeros[top + height :]
    gain = gain_ref[...]
    for shard in range(shards):
        rows = jnp.concatenate(part_halves(query_ref[shard], head_size), axis=0)
        proj_first = contract(rows, weight_ref[0], NT)
        proj_third = contract(rows, weight_ref[1], NT)
        mixed = (proj_first * jax.nn.sigmoid(proj_first) * proj_third).astype(jnp.bfloat16)
        outputs = contract(mixed, weight_ref[2], NN)
        scale = lax.rsqrt(jnp.mean(outputs * outputs, axis=-1, keepdims=True) + epsilon)
        normed = (outputs * scale * gain).astype(jnp.bfloat16).astype(jnp.float32)
        for column in range(width):
            grid_ref[shard, column + 1, top : top + height, 0:head_size] = normed[
                column * height : (column + 1) * height
            ]
        frame = order_ref[shard]
        block = frame // frames_here
        slot = frame % frames_here
        for tile in range(full + 1):
            lanes = slice(tile * LANES, (tile + 1) * LANES)
            for column in range(width):
                total = jnp.zeros((height, LANES), jnp.float32)
                for row_tap in range(3):
                    for col_tap in range(3):
                        tap = tap_ref[row_tap * 3 + col_tap : row_tap * 3 + col_tap + 1, lanes]
                        first = top + row_tap - 1
                        total = total + tap * grid_ref[
                            shard, column + col_tap, first : first + height, lanes
                        ]
                turned_ref[
                    block, column, tile, pl.ds(slot, height, stride=frames_here), :
                ] = total
    blocks = turned_ref.shape[0]
    side_rows = out_ref.shape[1]
    for block in range(blocks):
        for column in range(width):
            sides = [
                [
                    turned_ref[block, column, tile, side * side_rows : (side + 1) * side_rows, :]
                    for tile in range(full + 1)
                ]
                for side in range(2)
            ]
            for tile, part in enumerate(join_halves(sides[0], sides[1], tail)):
                out_ref[column * blocks + block, :, tile * LANES : (tile + 1) * LANES] = part.astype(
                    jnp.bfloat16
                )


def gate_kernel(blocks, conv_ref, gate_ref, out_ref):
    chunks, side_rows, _ = conv_ref.shape
    height, frames_here, channels = gate_ref.shape
    head_size = channels // chunks
    shards = chunks // blocks
    rows_here = height // 2
    for pair in range(chunks // 2):
        lanes = slice(pair * 2 * head_size, (pair + 1) * 2 * head_size)
        halves = []
        for head in (2 * pair, 2 * pair + 1):
            chunk = (head % shards) * blocks + head // shards
            halves.append(part_halves(conv_ref[chunk].astype(jnp.float32), head_size))
        for side in range(2):
            conv = jnp.concatenate([halves[0][side], halves[1][side]], axis=1)
            gate = gate_ref[side * rows_here : (side + 1) * rows_here, :, lanes].astype(jnp.float32)
            conv = conv.reshape(rows_here, frames_here, 2 * head_size)
            out_ref[side * rows_here : (side + 1) * rows_here, :, lanes] = (
                conv * (gate * jax.nn.sigmoid(gate))
            ).astype(jnp.bfloat16)


def in_vmem(count):
    return [pl.BlockSpec(memory_space=pltpu.VMEM)] * count


def call(kernel, out, operands, scratch=(), flops=0, specs=None):
    moved = sum(item.size * item.dtype.itemsize for item in operands) + out.size * 2
    return pl.pallas_call(
        kernel,
        out_shape=out,
        in_specs=specs or in_vmem(len(operands)),
        out_specs=pl.BlockSpec(memory_space=pltpu.VMEM),
        scratch_shapes=scratch,
        compiler_params=pltpu.CompilerParams(vmem_limit_bytes=VMEM_BYTES),
        cost_estimate=pl.CostEstimate(flops=flops, bytes_accessed=moved, transcendentals=0),
    )(*operands)


def by_heads(
    queries, keys, values, rates, fast_weights, norm_gain, frame_order, gate_input, conv_weights
):
    tok_rows = queries.shape[0]
    head_count = queries.shape[1] * queries.shape[2]
    head_size = queries.shape[3]
    height, frames_here = gate_input.shape[:2]
    shards = lax.axis_size("tok")
    blocks = lax.axis_size("head")
    half = tok_rows // 2
    wide = 2 * head_size
    tiles = head_size // LANES + 1
    own = lax.axis_index("tok")
    own_channel = lax.axis_index("head") * head_count + own

    def rows_of(array):
        return array.reshape(tok_rows, head_count, head_size)

    tile_scratch = pltpu.VMEM((tiles, tok_rows * head_count, LANES), jnp.float32)
    pairs = call(
        pack_pairs_kernel,
        jax.ShapeDtypeStruct((head_count, tok_rows, wide), jnp.bfloat16),
        (rows_of(keys), rows_of(values), rates.reshape(head_count, tok_rows).T),
        (tile_scratch, tile_scratch),
    )
    pairs = lax.all_to_all(pairs, "tok", split_axis=0, concat_axis=0, tiled=True)
    asked = call(
        functools.partial(pack_queries_kernel, height),
        jax.ShapeDtypeStruct((head_count, half, wide), jnp.bfloat16),
        (rows_of(queries),),
        (tile_scratch,),
    )
    asked = lax.all_to_all(asked, "tok", split_axis=0, concat_axis=0, tiled=True)
    weights = fast_weights.reshape(head_count, 3, head_size, head_size)
    own_weights = lax.dynamic_index_in_dim(weights, own, 0, keepdims=False)
    own_gain = lax.dynamic_index_in_dim(
        norm_gain.reshape(head_count, head_size), own, 0, keepdims=True
    )
    taps = conv_weights.reshape(9, blocks * head_count, head_size)
    own_taps = lax.dynamic_index_in_dim(taps, own_channel, 1, keepdims=False)
    own_taps = jnp.pad(own_taps, ((0, 0), (0, tiles * LANES - head_size)))
    product = 2 * shards * tok_rows * head_size * head_size
    updated = call(
        functools.partial(update_kernel, 2 if shards % 2 == 0 else 1),
        jax.ShapeDtypeStruct((3, head_size, head_size), jnp.bfloat16),
        (pairs, own_weights),
        (pltpu.VMEM((3, head_size, head_size), jnp.float32),),
        flops=6 * product,
    )
    side_rows = frames_here * height // 2
    outgoing = call(
        functools.partial(apply_kernel, height, frames_here),
        jax.ShapeDtypeStruct((shards * blocks, side_rows, wide), jnp.bfloat16),
        (frame_order, asked, updated, own_gain, own_taps),
        (
            pltpu.VMEM((shards, shards + 2, height + 16, tiles * LANES), jnp.float32),
            pltpu.VMEM((blocks, shards, tiles, 2 * side_rows, LANES), jnp.float32),
        ),
        flops=3 * product,
        specs=[pl.BlockSpec(memory_space=pltpu.SMEM)] + in_vmem(4),
    )
    arrived = lax.all_to_all(outgoing, ("tok", "head"), split_axis=0, concat_axis=0, tiled=True)
    gate = gate_input.reshape(height, frames_here, gate_input.shape[3])
    gated = call(
        functools.partial(gate_kernel, blocks),
        jax.ShapeDtypeStruct(gate.shape, jnp.bfloat16),
        (arrived, gate),
    )
    return gated.reshape(gate_input.shape)


def fits_by_heads(queries, gate_input, frame_order):
    tok_rows, head_size = queries.shape[0], queries.shape[3]
    head_count = queries.shape[1] * queries.shape[2]
    height, frames_here, col_width = gate_input.shape[:3]
    shards = lax.axis_size("tok")
    return (
        head_count == shards
        and frame_order.shape[0] == shards
        and lax.axis_size("tile") == 1
        and col_width == 1
        and shards % 2 == 0
        and head_size % LANES == LANES // 2
        and height % 8 == 0
        and tok_rows == height * shards
        and tok_rows % 32 == 0
        and frames_here * height % 32 == 0
        and frames_here * lax.axis_size("head") == shards
    )


def renormed(previous, gradient):
    before = previous.astype(jnp.float32)
    updated = before - gradient
    scale_old = jnp.sqrt(jnp.mean(before * before, axis=-1, keepdims=True) + epsilon)
    scale_new = jnp.sqrt(jnp.mean(updated * updated, axis=-1, keepdims=True) + epsilon)
    return (updated * (scale_old / scale_new)).astype(jnp.bfloat16)


def by_tokens(
    queries, keys, values, rates, fast_weights, norm_gain, frame_order, gate_input, conv_weights
):
    tok_rows = queries.shape[0]
    head_count = queries.shape[1] * queries.shape[2]
    head_size = queries.shape[3]
    query_rows = queries.reshape(tok_rows, head_count, head_size)
    key_rows = keys.reshape(tok_rows, head_count, head_size)
    value_rows = values.reshape(tok_rows, head_count, head_size)
    token_rates = rates.reshape(head_count, tok_rows)
    weights = fast_weights.reshape(head_count, 3, head_size, head_size)
    head_gains = norm_gain.reshape(head_count, head_size)
    first_pre = jnp.einsum(
        "thd,hfd->htf", key_rows, weights[:, 0], preferred_element_type=jnp.float32
    )
    third_pre = jnp.einsum(
        "thd,hfd->htf", key_rows, weights[:, 1], preferred_element_type=jnp.float32
    )
    sigmoid_first = jax.nn.sigmoid(first_pre)
    activated = first_pre * sigmoid_first
    hidden = (activated * third_pre).astype(jnp.bfloat16)
    target = (-token_rates.T[:, :, None] * value_rows.astype(jnp.float32)).astype(jnp.bfloat16)
    grad_down = jnp.einsum("thd,htf->hdf", target, hidden, preferred_element_type=jnp.float32)
    hidden_grad = jnp.einsum(
        "thd,hdf->htf", target, weights[:, 2], preferred_element_type=jnp.float32
    )
    grad_first_in = (
        hidden_grad * third_pre * sigmoid_first * (1.0 + first_pre * (1.0 - sigmoid_first))
    ).astype(jnp.bfloat16)
    grad_third_in = (hidden_grad * activated).astype(jnp.bfloat16)
    grad_first = jnp.einsum(
        "htf,thd->hfd", grad_first_in, key_rows, preferred_element_type=jnp.float32
    )
    grad_third = jnp.einsum(
        "htf,thd->hfd", grad_third_in, key_rows, preferred_element_type=jnp.float32
    )
    gradients = jnp.stack([grad_first, grad_third, grad_down], axis=1)
    row_share = lax.psum_scatter(gradients, "tok", scatter_dimension=2, tiled=True)
    row_count = row_share.shape[2]
    own_rows = lax.dynamic_slice_in_dim(weights, lax.axis_index("tok") * row_count, row_count, 2)
    updated = lax.all_gather(renormed(own_rows, row_share), "tok", axis=2, tiled=True)
    proj_first = jnp.einsum(
        "thd,hfd->thf", query_rows, updated[:, 0], preferred_element_type=jnp.float32
    )
    proj_third = jnp.einsum(
        "thd,hfd->thf", query_rows, updated[:, 1], preferred_element_type=jnp.float32
    )
    mixed_hidden = (jax.nn.silu(proj_first) * proj_third).astype(jnp.bfloat16)
    outputs = jnp.einsum(
        "thf,hdf->thd", mixed_hidden, updated[:, 2], preferred_element_type=jnp.float32
    )
    normed = (
        outputs
        * lax.rsqrt(jnp.mean(outputs * outputs, axis=-1, keepdims=True) + epsilon)
        * head_gains[None]
    )
    normed = normed.astype(jnp.bfloat16)
    height = gate_input.shape[0]
    col_width = gate_input.shape[2]
    shards = lax.axis_size("tok")
    full_width = col_width * shards
    channels_here = head_count * head_size
    frame_grid = normed.reshape(height, full_width, channels_here)
    own_taps = lax.dynamic_slice_in_dim(
        conv_weights, lax.axis_index("head") * channels_here, channels_here, 2
    )
    padded = jnp.pad(frame_grid, ((1, 1), (1, 1), (0, 0)))
    local_sum = jnp.zeros((height, full_width, channels_here), jnp.float32)
    for row_tap in range(3):
        for col_tap in range(3):
            local_sum = local_sum + own_taps[row_tap, col_tap] * padded[
                row_tap : row_tap + height, col_tap : col_tap + full_width
            ].astype(jnp.float32)
    outgoing = local_sum.astype(jnp.bfloat16).reshape(height, shards, col_width, channels_here)
    arrived = lax.all_to_all(outgoing, "tok", split_axis=1, concat_axis=1, tiled=True)
    frame_count = frame_order.shape[0]
    numbers = jnp.arange(frame_count, dtype=jnp.int32)
    inverse = jnp.sum(
        jnp.where(frame_order[None, :] == numbers[:, None], numbers[None, :], 0), axis=1
    )
    ordered = jnp.take(arrived, inverse, axis=1)
    tile_block = lax.all_to_all(ordered, "head", split_axis=1, concat_axis=3, tiled=True)
    return (tile_block.astype(jnp.float32) * jax.nn.silu(gate_input.astype(jnp.float32))).astype(
        jnp.bfloat16
    )


def local(queries, keys, values, rates, fast_weights, norm_gain, frame_order, gate_input, conv_weights):
    args = (
        queries, keys, values, rates, fast_weights, norm_gain, frame_order, gate_input, conv_weights
    )
    if fits_by_heads(queries, gate_input, frame_order):
        return by_heads(*args)
    return by_tokens(*args)


def solution(mesh):
    in_specs = (
        P(("groups", "tok"), "tile", "head", None),
        P(("groups", "tok"), "tile", "head", None),
        P(("groups", "tok"), "tile", "head", None),
        P("tile", "head", ("groups", "tok")),
        P("tile", "head", None, None, None),
        P("tile", "head", None),
        P("groups"),
        P(None, ("groups", "head"), "tok", "tile"),
        P(None, None, "tile"),
    )
    out_specs = P(None, ("groups", "head"), "tok", "tile")
    return jax.shard_map(local, mesh=mesh, in_specs=in_specs, out_specs=out_specs, check_vma=False)
```

```python
import functools

import jax
import jax.numpy as jnp
from jax import lax
from jax.experimental import pallas as pl
from jax.experimental.pallas import tpu as pltpu
from jax.sharding import PartitionSpec as P

epsilon = 1e-06
LANES = 128
VMEM_BYTES = 56 * 1024 * 1024


def split_lanes(source, scratch, rows, head_size):
    full = head_size // LANES
    tail = head_size - full * LANES
    wide = source.reshape(rows, head_size).astype(jnp.float32)
    for tile in range(full):
        scratch[tile] = wide[:, tile * LANES : (tile + 1) * LANES]
    scratch[full, :, 0:tail] = wide[:, full * LANES :]


def join_halves(first, second, tail):
    lane = lax.broadcasted_iota(jnp.int32, first[-1].shape, 1)
    middle = jnp.where(lane < tail, first[-1], pltpu.roll(second[-1], tail, 1))
    return first[:-1] + [middle] + second[:-1]


def part_halves(packed, head_size):
    full = head_size // LANES
    tail = head_size - full * LANES
    first = packed[:, :head_size]
    middle = packed[:, head_size : (full + 1) * LANES]
    second = jnp.concatenate([packed[:, (full + 1) * LANES :], middle], axis=1)
    return first, second


def partner_head(partner):
    return lax.axis_index("tok") ^ partner


def pack_pairs_kernel(key_ref, value_ref, rate_ref, *rest):
    outs, key_tiles, value_tiles = rest[:-2], rest[-2], rest[-1]
    tok_rows, heads, head_size = key_ref.shape
    half = tok_rows // 2
    full = head_size // LANES
    tail = head_size - full * LANES
    split_lanes(key_ref[...], key_tiles, tok_rows * heads, head_size)
    split_lanes(value_ref[...], value_tiles, tok_rows * heads, head_size)
    for partner in range(heads):
        head = partner_head(partner)
        rate_row = -rate_ref[pl.ds(head, 1), :]
        rates = jnp.broadcast_to(rate_row, (LANES, tok_rows)).T
        for row, tiles in ((0, key_tiles), (half, value_tiles)):
            sides = []
            for side in range(2):
                parts = [
                    tiles[tile, pl.ds(side * half * heads + head, half, stride=heads), :]
                    for tile in range(full + 1)
                ]
                if tiles is value_tiles:
                    rate = rates[side * half : (side + 1) * half]
                    parts = [rate * part for part in parts]
                sides.append(parts)
            for tile, part in enumerate(join_halves(sides[0], sides[1], tail)):
                outs[partner][row : row + half, tile * LANES : (tile + 1) * LANES] = part.astype(
                    jnp.bfloat16
                )


def pack_queries_kernel(height, query_ref, *rest):
    outs, query_tiles = rest[:-1], rest[-1]
    tok_rows, heads, head_size = query_ref.shape
    width = tok_rows // height
    full = head_size // LANES
    tail = head_size - full * LANES
    split_lanes(query_ref[...], query_tiles, tok_rows * heads, head_size)
    for partner in range(heads):
        head = partner_head(partner)
        sides = []
        for side in range(2):
            sides.append(
                [
                    jnp.concatenate(
                        [
                            query_tiles[
                                tile, pl.ds(column * heads + head, height, stride=width * heads), :
                            ]
                            for column in range(side * width // 2, (side + 1) * width // 2)
                        ],
                        axis=0,
                    )
                    for tile in range(full + 1)
                ]
            )
        for tile, part in enumerate(join_halves(sides[0], sides[1], tail)):
            outs[partner][:, tile * LANES : (tile + 1) * LANES] = part.astype(jnp.bfloat16)


def exchange(parts):
    count = len(parts)
    arrived = list(parts)
    for partner in range(count - 1, 0, -1):
        pairs = [(place, place ^ partner) for place in range(count)]
        arrived[partner] = lax.ppermute(parts[partner], "tok", pairs)
    return arrived


def contract(first, second, dims):
    return lax.dot_general(first, second, (dims, ((), ())), preferred_element_type=jnp.float32)


NN = ((1,), (0,))
NT = ((1,), (1,))


def update_kernel(step, *refs):
    pair_refs, (weight_ref, out_ref, grad_ref) = refs[:-3], refs[-3:]
    shards = len(pair_refs)
    rows = pair_refs[0].shape[0]
    half = rows // 2
    head_size = weight_ref.shape[-1]
    first_weight = weight_ref[0]
    third_weight = weight_ref[1]
    down_turned = weight_ref[2].astype(jnp.float32).T.astype(jnp.bfloat16)
    for start in range(0, shards, step):
        key_parts, target_parts = [], []
        for shard in range(start, start + step):
            key_parts.extend(part_halves(pair_refs[shard][0:half, :], head_size))
            target_parts.extend(part_halves(pair_refs[shard][half:rows, :], head_size))
        key_rows = jnp.concatenate(key_parts, axis=0)
        target = jnp.concatenate(target_parts, axis=0)
        first_pre = contract(first_weight, key_rows, NT)
        third_pre = contract(third_weight, key_rows, NT)
        hidden_grad = contract(down_turned, target, NT)
        sigmoid_first = jax.nn.sigmoid(first_pre)
        activated = first_pre * sigmoid_first
        hidden = (activated * third_pre).astype(jnp.bfloat16)
        grad_first_in = (
            hidden_grad * third_pre * sigmoid_first * (1.0 + first_pre * (1.0 - sigmoid_first))
        ).astype(jnp.bfloat16)
        grad_third_in = (hidden_grad * activated).astype(jnp.bfloat16)
        grads = (
            contract(grad_first_in, key_rows, NN),
            contract(grad_third_in, key_rows, NN),
            contract(hidden, target, NN),
        )
        for index, grad in enumerate(grads):
            if start == 0:
                grad_ref[index] = grad
            else:
                grad_ref[index] += grad
    for index in range(3):
        before = weight_ref[index].astype(jnp.float32)
        axis = 1
        if index == 2:
            before = before.T
            axis = 0
        updated = before - grad_ref[index]
        scale_old = jnp.sqrt(jnp.mean(before * before, axis=axis, keepdims=True) + epsilon)
        scale_new = jnp.sqrt(jnp.mean(updated * updated, axis=axis, keepdims=True) + epsilon)
        out_ref[index] = (updated * (scale_old / scale_new)).astype(jnp.bfloat16)


def apply_kernel(height, frames_here, order_ref, *refs):
    query_refs = refs[:-6]
    weight_ref, gain_ref, tap_ref, out_ref, grid_ref, turned_ref = refs[-6:]
    shards = len(query_refs)
    half = query_refs[0].shape[0]
    width = 2 * half // height
    head_size = weight_ref.shape[-1]
    full = head_size // LANES
    tail = head_size - full * LANES
    padded = (full + 1) * LANES
    top = 8
    for shard in range(shards):
        zeros = jnp.zeros(grid_ref.shape[2:], jnp.float32)
        grid_ref[shard, 0] = zeros
        grid_ref[shard, width + 1] = zeros
        for column in range(1, width + 1):
            grid_ref[shard, column, 0:top] = zeros[0:top]
            grid_ref[shard, column, top + height :] = zeros[top + height :]
    gain = gain_ref[...]
    for shard in range(shards):
        rows = jnp.concatenate(part_halves(query_refs[shard][...], head_size), axis=0)
        proj_first = contract(rows, weight_ref[0], NT)
        proj_third = contract(rows, weight_ref[1], NT)
        mixed = (proj_first * jax.nn.sigmoid(proj_first) * proj_third).astype(jnp.bfloat16)
        outputs = contract(mixed, weight_ref[2], NN)
        scale = lax.rsqrt(jnp.mean(outputs * outputs, axis=-1, keepdims=True) + epsilon)
        normed = (outputs * scale * gain).astype(jnp.bfloat16).astype(jnp.float32)
        for column in range(width):
            grid_ref[shard, column + 1, top : top + height, 0:head_size] = normed[
                column * height : (column + 1) * height
            ]
        frame = order_ref[shard]
        block = frame // frames_here
        slot = frame % frames_here
        for tile in range(full + 1):
            lanes = slice(tile * LANES, (tile + 1) * LANES)
            for column in range(width):
                total = jnp.zeros((height, LANES), jnp.float32)
                for row_tap in range(3):
                    for col_tap in range(3):
                        tap = tap_ref[row_tap * 3 + col_tap : row_tap * 3 + col_tap + 1, lanes]
                        first = top + row_tap - 1
                        total = total + tap * grid_ref[
                            shard, column + col_tap, first : first + height, lanes
                        ]
                turned_ref[
                    block, column, tile, pl.ds(slot, height, stride=frames_here), :
                ] = total
    blocks = turned_ref.shape[0]
    side_rows = out_ref.shape[1]
    for block in range(blocks):
        for column in range(width):
            sides = [
                [
                    turned_ref[block, column, tile, side * side_rows : (side + 1) * side_rows, :]
                    for tile in range(full + 1)
                ]
                for side in range(2)
            ]
            for tile, part in enumerate(join_halves(sides[0], sides[1], tail)):
                out_ref[column * blocks + block, :, tile * LANES : (tile + 1) * LANES] = part.astype(
                    jnp.bfloat16
                )


def gate_kernel(blocks, conv_ref, gate_ref, out_ref):
    chunks, side_rows, _ = conv_ref.shape
    height, frames_here, channels = gate_ref.shape
    head_size = channels // chunks
    shards = chunks // blocks
    rows_here = height // 2
    for pair in range(chunks // 2):
        lanes = slice(pair * 2 * head_size, (pair + 1) * 2 * head_size)
        halves = []
        for head in (2 * pair, 2 * pair + 1):
            chunk = (head % shards) * blocks + head // shards
            halves.append(part_halves(conv_ref[chunk].astype(jnp.float32), head_size))
        for side in range(2):
            conv = jnp.concatenate([halves[0][side], halves[1][side]], axis=1)
            gate = gate_ref[side * rows_here : (side + 1) * rows_here, :, lanes].astype(jnp.float32)
            conv = conv.reshape(rows_here, frames_here, 2 * head_size)
            out_ref[side * rows_here : (side + 1) * rows_here, :, lanes] = (
                conv * (gate * jax.nn.sigmoid(gate))
            ).astype(jnp.bfloat16)


def in_vmem(count):
    return [pl.BlockSpec(memory_space=pltpu.VMEM)] * count


def call(kernel, out, operands, scratch=(), flops=0, specs=None):
    moved = sum(item.size * item.dtype.itemsize for item in operands)
    moved += sum(item.size * item.dtype.itemsize for item in jax.tree.leaves(out))
    return pl.pallas_call(
        kernel,
        out_shape=out,
        in_specs=specs or in_vmem(len(operands)),
        out_specs=jax.tree.map(lambda _: pl.BlockSpec(memory_space=pltpu.VMEM), out),
        scratch_shapes=scratch,
        compiler_params=pltpu.CompilerParams(vmem_limit_bytes=VMEM_BYTES),
        cost_estimate=pl.CostEstimate(flops=flops, bytes_accessed=moved, transcendentals=0),
    )(*operands)


def by_heads(
    queries, keys, values, rates, fast_weights, norm_gain, frame_order, gate_input, conv_weights
):
    tok_rows = queries.shape[0]
    head_count = queries.shape[1] * queries.shape[2]
    head_size = queries.shape[3]
    height, frames_here = gate_input.shape[:2]
    shards = lax.axis_size("tok")
    blocks = lax.axis_size("head")
    half = tok_rows // 2
    wide = 2 * head_size
    tiles = head_size // LANES + 1
    own = lax.axis_index("tok")
    own_channel = lax.axis_index("head") * head_count + own

    def rows_of(array):
        return array.reshape(tok_rows, head_count, head_size)

    tile_scratch = pltpu.VMEM((tiles, tok_rows * head_count, LANES), jnp.float32)
    pairs = call(
        pack_pairs_kernel,
        [jax.ShapeDtypeStruct((tok_rows, wide), jnp.bfloat16)] * shards,
        (rows_of(keys), rows_of(values), rates.reshape(head_count, tok_rows)),
        (tile_scratch, tile_scratch),
    )
    pairs = exchange(pairs)
    asked = call(
        functools.partial(pack_queries_kernel, height),
        [jax.ShapeDtypeStruct((half, wide), jnp.bfloat16)] * shards,
        (rows_of(queries),),
        (tile_scratch,),
    )
    asked = exchange(asked)
    weights = fast_weights.reshape(head_count, 3, head_size, head_size)
    own_weights = lax.dynamic_index_in_dim(weights, own, 0, keepdims=False)
    own_gain = lax.dynamic_index_in_dim(
        norm_gain.reshape(head_count, head_size), own, 0, keepdims=True
    )
    taps = conv_weights.reshape(9, blocks * head_count, head_size)
    own_taps = lax.dynamic_index_in_dim(taps, own_channel, 1, keepdims=False)
    own_taps = jnp.pad(own_taps, ((0, 0), (0, tiles * LANES - head_size)))
    frames = frame_order[own ^ jnp.arange(shards, dtype=jnp.int32)]
    product = 2 * shards * tok_rows * head_size * head_size
    updated = call(
        functools.partial(update_kernel, 2 if shards % 2 == 0 else 1),
        jax.ShapeDtypeStruct((3, head_size, head_size), jnp.bfloat16),
        (*pairs, own_weights),
        (pltpu.VMEM((3, head_size, head_size), jnp.float32),),
        flops=6 * product,
    )
    side_rows = frames_here * height // 2
    outgoing = call(
        functools.partial(apply_kernel, height, frames_here),
        jax.ShapeDtypeStruct((shards * blocks, side_rows, wide), jnp.bfloat16),
        (frames, *asked, updated, own_gain, own_taps),
        (
            pltpu.VMEM((shards, shards + 2, height + 16, tiles * LANES), jnp.float32),
            pltpu.VMEM((blocks, shards, tiles, 2 * side_rows, LANES), jnp.float32),
        ),
        flops=3 * product,
        specs=[pl.BlockSpec(memory_space=pltpu.SMEM)] + in_vmem(shards + 3),
    )
    arrived = lax.all_to_all(outgoing, ("tok", "head"), split_axis=0, concat_axis=0, tiled=True)
    gate = gate_input.reshape(height, frames_here, gate_input.shape[3])
    gated = call(
        functools.partial(gate_kernel, blocks),
        jax.ShapeDtypeStruct(gate.shape, jnp.bfloat16),
        (arrived, gate),
    )
    return gated.reshape(gate_input.shape)


def fits_by_heads(queries, gate_input, frame_order):
    tok_rows, head_size = queries.shape[0], queries.shape[3]
    head_count = queries.shape[1] * queries.shape[2]
    height, frames_here, col_width = gate_input.shape[:3]
    shards = lax.axis_size("tok")
    return (
        head_count == shards
        and frame_order.shape[0] == shards
        and lax.axis_size("tile") == 1
        and col_width == 1
        and shards % 2 == 0
        and shards & (shards - 1) == 0
        and head_size % LANES == LANES // 2
        and height % 8 == 0
        and tok_rows == height * shards
        and tok_rows % 32 == 0
        and frames_here * height % 32 == 0
        and frames_here * lax.axis_size("head") == shards
    )


def renormed(previous, gradient):
    before = previous.astype(jnp.float32)
    updated = before - gradient
    scale_old = jnp.sqrt(jnp.mean(before * before, axis=-1, keepdims=True) + epsilon)
    scale_new = jnp.sqrt(jnp.mean(updated * updated, axis=-1, keepdims=True) + epsilon)
    return (updated * (scale_old / scale_new)).astype(jnp.bfloat16)


def by_tokens(
    queries, keys, values, rates, fast_weights, norm_gain, frame_order, gate_input, conv_weights
):
    tok_rows = queries.shape[0]
    head_count = queries.shape[1] * queries.shape[2]
    head_size = queries.shape[3]
    query_rows = queries.reshape(tok_rows, head_count, head_size)
    key_rows = keys.reshape(tok_rows, head_count, head_size)
    value_rows = values.reshape(tok_rows, head_count, head_size)
    token_rates = rates.reshape(head_count, tok_rows)
    weights = fast_weights.reshape(head_count, 3, head_size, head_size)
    head_gains = norm_gain.reshape(head_count, head_size)
    first_pre = jnp.einsum(
        "thd,hfd->htf", key_rows, weights[:, 0], preferred_element_type=jnp.float32
    )
    third_pre = jnp.einsum(
        "thd,hfd->htf", key_rows, weights[:, 1], preferred_element_type=jnp.float32
    )
    sigmoid_first = jax.nn.sigmoid(first_pre)
    activated = first_pre * sigmoid_first
    hidden = (activated * third_pre).astype(jnp.bfloat16)
    target = (-token_rates.T[:, :, None] * value_rows.astype(jnp.float32)).astype(jnp.bfloat16)
    grad_down = jnp.einsum("thd,htf->hdf", target, hidden, preferred_element_type=jnp.float32)
    hidden_grad = jnp.einsum(
        "thd,hdf->htf", target, weights[:, 2], preferred_element_type=jnp.float32
    )
    grad_first_in = (
        hidden_grad * third_pre * sigmoid_first * (1.0 + first_pre * (1.0 - sigmoid_first))
    ).astype(jnp.bfloat16)
    grad_third_in = (hidden_grad * activated).astype(jnp.bfloat16)
    grad_first = jnp.einsum(
        "htf,thd->hfd", grad_first_in, key_rows, preferred_element_type=jnp.float32
    )
    grad_third = jnp.einsum(
        "htf,thd->hfd", grad_third_in, key_rows, preferred_element_type=jnp.float32
    )
    gradients = jnp.stack([grad_first, grad_third, grad_down], axis=1)
    row_share = lax.psum_scatter(gradients, "tok", scatter_dimension=2, tiled=True)
    row_count = row_share.shape[2]
    own_rows = lax.dynamic_slice_in_dim(weights, lax.axis_index("tok") * row_count, row_count, 2)
    updated = lax.all_gather(renormed(own_rows, row_share), "tok", axis=2, tiled=True)
    proj_first = jnp.einsum(
        "thd,hfd->thf", query_rows, updated[:, 0], preferred_element_type=jnp.float32
    )
    proj_third = jnp.einsum(
        "thd,hfd->thf", query_rows, updated[:, 1], preferred_element_type=jnp.float32
    )
    mixed_hidden = (jax.nn.silu(proj_first) * proj_third).astype(jnp.bfloat16)
    outputs = jnp.einsum(
        "thf,hdf->thd", mixed_hidden, updated[:, 2], preferred_element_type=jnp.float32
    )
    normed = (
        outputs
        * lax.rsqrt(jnp.mean(outputs * outputs, axis=-1, keepdims=True) + epsilon)
        * head_gains[None]
    )
    normed = normed.astype(jnp.bfloat16)
    height = gate_input.shape[0]
    col_width = gate_input.shape[2]
    shards = lax.axis_size("tok")
    full_width = col_width * shards
    channels_here = head_count * head_size
    frame_grid = normed.reshape(height, full_width, channels_here)
    own_taps = lax.dynamic_slice_in_dim(
        conv_weights, lax.axis_index("head") * channels_here, channels_here, 2
    )
    padded = jnp.pad(frame_grid, ((1, 1), (1, 1), (0, 0)))
    local_sum = jnp.zeros((height, full_width, channels_here), jnp.float32)
    for row_tap in range(3):
        for col_tap in range(3):
            local_sum = local_sum + own_taps[row_tap, col_tap] * padded[
                row_tap : row_tap + height, col_tap : col_tap + full_width
            ].astype(jnp.float32)
    outgoing = local_sum.astype(jnp.bfloat16).reshape(height, shards, col_width, channels_here)
    arrived = lax.all_to_all(outgoing, "tok", split_axis=1, concat_axis=1, tiled=True)
    frame_count = frame_order.shape[0]
    numbers = jnp.arange(frame_count, dtype=jnp.int32)
    inverse = jnp.sum(
        jnp.where(frame_order[None, :] == numbers[:, None], numbers[None, :], 0), axis=1
    )
    ordered = jnp.take(arrived, inverse, axis=1)
    tile_block = lax.all_to_all(ordered, "head", split_axis=1, concat_axis=3, tiled=True)
    return (tile_block.astype(jnp.float32) * jax.nn.silu(gate_input.astype(jnp.float32))).astype(
        jnp.bfloat16
    )


def local(queries, keys, values, rates, fast_weights, norm_gain, frame_order, gate_input, conv_weights):
    args = (
        queries, keys, values, rates, fast_weights, norm_gain, frame_order, gate_input, conv_weights
    )
    if fits_by_heads(queries, gate_input, frame_order):
        return by_heads(*args)
    return by_tokens(*args)


def solution(mesh):
    in_specs = (
        P(("groups", "tok"), "tile", "head", None),
        P(("groups", "tok"), "tile", "head", None),
        P(("groups", "tok"), "tile", "head", None),
        P("tile", "head", ("groups", "tok")),
        P("tile", "head", None, None, None),
        P("tile", "head", None),
        P("groups"),
        P(None, ("groups", "head"), "tok", "tile"),
        P(None, None, "tile"),
    )
    out_specs = P(None, ("groups", "head"), "tok", "tile")
    return jax.shard_map(local, mesh=mesh, in_specs=in_specs, out_specs=out_specs, check_vma=False)
```

```python
import functools

import jax
import jax.numpy as jnp
from jax import lax
from jax.experimental import pallas as pl
from jax.experimental.pallas import tpu as pltpu
from jax.sharding import PartitionSpec as P

epsilon = 1e-06
LANES = 128
VMEM_BYTES = 56 * 1024 * 1024


def split_lanes(source, scratch, rows, head_size):
    full = head_size // LANES
    tail = head_size - full * LANES
    wide = source.reshape(rows, head_size).astype(jnp.float32)
    for tile in range(full):
        scratch[tile] = wide[:, tile * LANES : (tile + 1) * LANES]
    scratch[full, :, 0:tail] = wide[:, full * LANES :]


def join_halves(first, second, tail):
    lane = lax.broadcasted_iota(jnp.int32, first[-1].shape, 1)
    middle = jnp.where(lane < tail, first[-1], pltpu.roll(second[-1], tail, 1))
    return first[:-1] + [middle] + second[:-1]


def part_halves(packed, head_size):
    full = head_size // LANES
    tail = head_size - full * LANES
    first = packed[:, :head_size]
    middle = packed[:, head_size : (full + 1) * LANES]
    second = jnp.concatenate([packed[:, (full + 1) * LANES :], middle], axis=1)
    return first, second


def partner_head(partner):
    return lax.axis_index("tok") ^ partner


def pack_pairs_kernel(key_ref, value_ref, rate_ref, *rest):
    outs, key_tiles, value_tiles = rest[:-2], rest[-2], rest[-1]
    tok_rows, heads, head_size = key_ref.shape
    half = tok_rows // 2
    full = head_size // LANES
    tail = head_size - full * LANES
    split_lanes(key_ref[...], key_tiles, tok_rows * heads, head_size)
    split_lanes(value_ref[...], value_tiles, tok_rows * heads, head_size)
    for partner in range(heads):
        head = partner_head(partner)
        rate_row = -rate_ref[pl.ds(head, 1), :]
        rates = jnp.broadcast_to(rate_row, (LANES, tok_rows)).T
        for row, tiles in ((0, key_tiles), (half, value_tiles)):
            sides = []
            for side in range(2):
                parts = [
                    tiles[tile, pl.ds(side * half * heads + head, half, stride=heads), :]
                    for tile in range(full + 1)
                ]
                if tiles is value_tiles:
                    rate = rates[side * half : (side + 1) * half]
                    parts = [rate * part for part in parts]
                sides.append(parts)
            for tile, part in enumerate(join_halves(sides[0], sides[1], tail)):
                outs[partner][row : row + half, tile * LANES : (tile + 1) * LANES] = part.astype(
                    jnp.bfloat16
                )


def pack_queries_kernel(height, query_ref, *rest):
    outs, query_tiles = rest[:-1], rest[-1]
    tok_rows, heads, head_size = query_ref.shape
    width = tok_rows // height
    full = head_size // LANES
    tail = head_size - full * LANES
    split_lanes(query_ref[...], query_tiles, tok_rows * heads, head_size)
    for partner in range(heads):
        head = partner_head(partner)
        sides = []
        for side in range(2):
            sides.append(
                [
                    jnp.concatenate(
                        [
                            query_tiles[
                                tile, pl.ds(column * heads + head, height, stride=width * heads), :
                            ]
                            for column in range(side * width // 2, (side + 1) * width // 2)
                        ],
                        axis=0,
                    )
                    for tile in range(full + 1)
                ]
            )
        for tile, part in enumerate(join_halves(sides[0], sides[1], tail)):
            outs[partner][:, tile * LANES : (tile + 1) * LANES] = part.astype(jnp.bfloat16)


def exchange(parts):
    count = len(parts)
    arrived = list(parts)
    for partner in range(count - 1, 0, -1):
        pairs = [(place, place ^ partner) for place in range(count)]
        arrived[partner] = lax.ppermute(parts[partner], "tok", pairs)
    return arrived


def exchange_all(parts):
    count = len(parts)
    arrived = list(parts)
    for partner in range(count - 1, 0, -1):
        pairs = [(place, place ^ partner) for place in range(count)]
        arrived[partner] = lax.ppermute(parts[partner], ("tok", "head"), pairs)
    return arrived


def contract(first, second, dims):
    return lax.dot_general(first, second, (dims, ((), ())), preferred_element_type=jnp.float32)


NN = ((1,), (0,))
NT = ((1,), (1,))


def update_kernel(step, *refs):
    pair_refs, (weight_ref, out_ref, grad_ref) = refs[:-3], refs[-3:]
    shards = len(pair_refs)
    rows = pair_refs[0].shape[0]
    half = rows // 2
    head_size = weight_ref.shape[-1]
    first_weight = weight_ref[0]
    third_weight = weight_ref[1]
    down_turned = weight_ref[2].astype(jnp.float32).T.astype(jnp.bfloat16)
    for start in range(0, shards, step):
        key_parts, target_parts = [], []
        for shard in range(start, start + step):
            key_parts.extend(part_halves(pair_refs[shard][0:half, :], head_size))
            target_parts.extend(part_halves(pair_refs[shard][half:rows, :], head_size))
        key_rows = jnp.concatenate(key_parts, axis=0)
        target = jnp.concatenate(target_parts, axis=0)
        first_pre = contract(first_weight, key_rows, NT)
        third_pre = contract(third_weight, key_rows, NT)
        hidden_grad = contract(down_turned, target, NT)
        sigmoid_first = jax.nn.sigmoid(first_pre)
        activated = first_pre * sigmoid_first
        hidden = (activated * third_pre).astype(jnp.bfloat16)
        grad_first_in = (
            hidden_grad * third_pre * sigmoid_first * (1.0 + first_pre * (1.0 - sigmoid_first))
        ).astype(jnp.bfloat16)
        grad_third_in = (hidden_grad * activated).astype(jnp.bfloat16)
        grads = (
            contract(grad_first_in, key_rows, NN),
            contract(grad_third_in, key_rows, NN),
            contract(hidden, target, NN),
        )
        for index, grad in enumerate(grads):
            if start == 0:
                grad_ref[index] = grad
            else:
                grad_ref[index] += grad
    for index in range(3):
        before = weight_ref[index].astype(jnp.float32)
        axis = 1
        if index == 2:
            before = before.T
            axis = 0
        updated = before - grad_ref[index]
        scale_old = jnp.sqrt(jnp.mean(before * before, axis=axis, keepdims=True) + epsilon)
        scale_new = jnp.sqrt(jnp.mean(updated * updated, axis=axis, keepdims=True) + epsilon)
        out_ref[index] = (updated * (scale_old / scale_new)).astype(jnp.bfloat16)


def apply_kernel(height, frames_here, blocks, order_ref, *refs):
    shards = (len(refs) - 5) // (blocks + 1)
    query_refs = refs[:shards]
    weight_ref, gain_ref, tap_ref = refs[shards : shards + 3]
    out_refs = refs[shards + 3 : -2]
    grid_ref, turned_ref = refs[-2:]
    half = query_refs[0].shape[0]
    width = 2 * half // height
    head_size = weight_ref.shape[-1]
    full = head_size // LANES
    tail = head_size - full * LANES
    top = 8
    edge = jnp.zeros((top, LANES), jnp.float32)
    whole = jnp.zeros(grid_ref.shape[3:], jnp.float32)
    for shard in range(shards):
        for tile in range(full + 1):
            grid_ref[shard, tile, 0] = whole
            grid_ref[shard, tile, width + 1] = whole
            for column in range(1, width + 1):
                grid_ref[shard, tile, column, 0:top] = edge
                grid_ref[shard, tile, column, top + height :] = edge
    gain = gain_ref[...]
    for shard in range(shards):
        rows = jnp.concatenate(part_halves(query_refs[shard][...], head_size), axis=0)
        proj_first = contract(rows, weight_ref[0], NT)
        proj_third = contract(rows, weight_ref[1], NT)
        mixed = (proj_first * jax.nn.sigmoid(proj_first) * proj_third).astype(jnp.bfloat16)
        outputs = contract(mixed, weight_ref[2], NN)
        scale = lax.rsqrt(jnp.mean(outputs * outputs, axis=-1, keepdims=True) + epsilon)
        normed = (outputs * scale * gain).astype(jnp.bfloat16).astype(jnp.float32)
        frame = order_ref[shard]
        block = frame // frames_here
        slot = frame % frames_here
        for tile in range(full + 1):
            lanes = slice(tile * LANES, min((tile + 1) * LANES, head_size))
            for column in range(width):
                grid_ref[shard, tile, column + 1, top : top + height, 0 : lanes.stop - lanes.start] = (
                    normed[column * height : (column + 1) * height, lanes]
                )
            taps = [
                tap_ref[index : index + 1, tile * LANES : (tile + 1) * LANES] for index in range(9)
            ]
            for column in range(width):
                total = None
                for row_tap in range(3):
                    first = top + row_tap - 1
                    for col_tap in range(3):
                        term = taps[row_tap * 3 + col_tap] * grid_ref[
                            shard, tile, column + col_tap, first : first + height, :
                        ]
                        total = term if total is None else total + term
                turned_ref[
                    block, column, tile, pl.ds(slot, height, stride=frames_here), :
                ] = total
    side_rows = out_refs[0].shape[0]
    for partner in range(shards):
        column = partner_head(partner)
        for other in range(blocks):
            block = lax.axis_index("head") ^ other
            sides = [
                [
                    turned_ref[block, column, tile, side * side_rows : (side + 1) * side_rows, :]
                    for tile in range(full + 1)
                ]
                for side in range(2)
            ]
            for tile, part in enumerate(join_halves(sides[0], sides[1], tail)):
                out_refs[partner * blocks + other][:, tile * LANES : (tile + 1) * LANES] = (
                    part.astype(jnp.bfloat16)
                )


def silu_kernel(gate_ref, out_ref):
    height, frames_here, channels = gate_ref.shape
    gate = gate_ref[...].astype(jnp.float32)
    out_ref[...] = (gate * jax.nn.sigmoid(gate)).reshape(height * frames_here, channels)


def gate_kernel(blocks, *refs):
    conv_refs, (gate_ref, out_ref) = refs[:-2], refs[-2:]
    height, frames_here, channels = out_ref.shape
    shards = len(conv_refs) // blocks
    head_size = channels // len(conv_refs)
    side_rows = conv_refs[0].shape[0]
    rows_here = height // 2
    own = lax.axis_index("tok")
    odd = own % 2
    for partner in range(0, shards, 2):
        for other in range(blocks):
            one = conv_refs[partner * blocks + other][...].astype(jnp.float32)
            two = conv_refs[(partner + 1) * blocks + other][...].astype(jnp.float32)
            low = part_halves(jnp.where(odd == 1, two, one), head_size)
            high = part_halves(jnp.where(odd == 1, one, two), head_size)
            head = (lax.axis_index("head") ^ other) * shards + ((own - odd) ^ partner)
            lanes = pl.ds(pl.multiple_of(head * head_size, 2 * head_size), 2 * head_size)
            for side in range(2):
                conv = jnp.concatenate([low[side], high[side]], axis=1)
                conv = conv * gate_ref[side * side_rows : (side + 1) * side_rows, lanes]
                out_ref[side * rows_here : (side + 1) * rows_here, :, lanes] = conv.reshape(
                    rows_here, frames_here, 2 * head_size
                ).astype(jnp.bfloat16)


def in_vmem(count):
    return [pl.BlockSpec(memory_space=pltpu.VMEM)] * count


def call(kernel, out, operands, scratch=(), flops=0, specs=None):
    moved = sum(item.size * item.dtype.itemsize for item in operands)
    moved += sum(item.size * item.dtype.itemsize for item in jax.tree.leaves(out))
    return pl.pallas_call(
        kernel,
        out_shape=out,
        in_specs=specs or in_vmem(len(operands)),
        out_specs=jax.tree.map(lambda _: pl.BlockSpec(memory_space=pltpu.VMEM), out),
        scratch_shapes=scratch,
        compiler_params=pltpu.CompilerParams(vmem_limit_bytes=VMEM_BYTES),
        cost_estimate=pl.CostEstimate(flops=flops, bytes_accessed=moved, transcendentals=0),
    )(*operands)


def by_heads(
    queries, keys, values, rates, fast_weights, norm_gain, frame_order, gate_input, conv_weights
):
    tok_rows = queries.shape[0]
    head_count = queries.shape[1] * queries.shape[2]
    head_size = queries.shape[3]
    height, frames_here = gate_input.shape[:2]
    shards = lax.axis_size("tok")
    blocks = lax.axis_size("head")
    half = tok_rows // 2
    wide = 2 * head_size
    tiles = head_size // LANES + 1
    own = lax.axis_index("tok")
    own_channel = lax.axis_index("head") * head_count + own

    def rows_of(array):
        return array.reshape(tok_rows, head_count, head_size)

    tile_scratch = pltpu.VMEM((tiles, tok_rows * head_count, LANES), jnp.float32)
    pairs = call(
        pack_pairs_kernel,
        [jax.ShapeDtypeStruct((tok_rows, wide), jnp.bfloat16)] * shards,
        (rows_of(keys), rows_of(values), rates.reshape(head_count, tok_rows)),
        (tile_scratch, tile_scratch),
    )
    pairs = exchange(pairs)
    asked = call(
        functools.partial(pack_queries_kernel, height),
        [jax.ShapeDtypeStruct((half, wide), jnp.bfloat16)] * shards,
        (rows_of(queries),),
        (tile_scratch,),
    )
    asked = exchange(asked)
    weights = fast_weights.reshape(head_count, 3, head_size, head_size)
    own_weights = lax.dynamic_index_in_dim(weights, own, 0, keepdims=False)
    own_gain = lax.dynamic_index_in_dim(
        norm_gain.reshape(head_count, head_size), own, 0, keepdims=True
    )
    taps = conv_weights.reshape(9, blocks * head_count, head_size)
    own_taps = lax.dynamic_index_in_dim(taps, own_channel, 1, keepdims=False)
    own_taps = jnp.pad(own_taps, ((0, 0), (0, tiles * LANES - head_size)))
    frames = frame_order[own ^ jnp.arange(shards, dtype=jnp.int32)]
    product = 2 * shards * tok_rows * head_size * head_size
    updated = call(
        functools.partial(update_kernel, 2 if shards % 2 == 0 else 1),
        jax.ShapeDtypeStruct((3, head_size, head_size), jnp.bfloat16),
        (*pairs, own_weights),
        (pltpu.VMEM((3, head_size, head_size), jnp.float32),),
        flops=6 * product,
    )
    side_rows = frames_here * height // 2
    outgoing = call(
        functools.partial(apply_kernel, height, frames_here, blocks),
        [jax.ShapeDtypeStruct((side_rows, wide), jnp.bfloat16)] * (shards * blocks),
        (frames, *asked, updated, own_gain, own_taps),
        (
            pltpu.VMEM((shards, tiles, shards + 2, height + 16, LANES), jnp.float32),
            pltpu.VMEM((blocks, shards, tiles, 2 * side_rows, LANES), jnp.float32),
        ),
        flops=3 * product,
        specs=[pl.BlockSpec(memory_space=pltpu.SMEM)] + in_vmem(shards + 3),
    )
    arrived = exchange_all(outgoing)
    gate = gate_input.reshape(height, frames_here, gate_input.shape[3])
    opened = call(
        silu_kernel,
        jax.ShapeDtypeStruct((height * frames_here, gate_input.shape[3]), jnp.float32),
        (gate,),
    )
    gated = call(
        functools.partial(gate_kernel, blocks),
        jax.ShapeDtypeStruct(gate.shape, jnp.bfloat16),
        (*arrived, opened),
    )
    return gated.reshape(gate_input.shape)


def fits_by_heads(queries, gate_input, frame_order):
    tok_rows, head_size = queries.shape[0], queries.shape[3]
    head_count = queries.shape[1] * queries.shape[2]
    height, frames_here, col_width = gate_input.shape[:3]
    shards = lax.axis_size("tok")
    return (
        head_count == shards
        and frame_order.shape[0] == shards
        and lax.axis_size("tile") == 1
        and col_width == 1
        and shards % 2 == 0
        and shards & (shards - 1) == 0
        and head_size % LANES == LANES // 2
        and height % 8 == 0
        and tok_rows == height * shards
        and tok_rows % 32 == 0
        and frames_here * height % 32 == 0
        and frames_here * lax.axis_size("head") == shards
        and lax.axis_size("head") & (lax.axis_size("head") - 1) == 0
    )


def renormed(previous, gradient):
    before = previous.astype(jnp.float32)
    updated = before - gradient
    scale_old = jnp.sqrt(jnp.mean(before * before, axis=-1, keepdims=True) + epsilon)
    scale_new = jnp.sqrt(jnp.mean(updated * updated, axis=-1, keepdims=True) + epsilon)
    return (updated * (scale_old / scale_new)).astype(jnp.bfloat16)


def by_tokens(
    queries, keys, values, rates, fast_weights, norm_gain, frame_order, gate_input, conv_weights
):
    tok_rows = queries.shape[0]
    head_count = queries.shape[1] * queries.shape[2]
    head_size = queries.shape[3]
    query_rows = queries.reshape(tok_rows, head_count, head_size)
    key_rows = keys.reshape(tok_rows, head_count, head_size)
    value_rows = values.reshape(tok_rows, head_count, head_size)
    token_rates = rates.reshape(head_count, tok_rows)
    weights = fast_weights.reshape(head_count, 3, head_size, head_size)
    head_gains = norm_gain.reshape(head_count, head_size)
    first_pre = jnp.einsum(
        "thd,hfd->htf", key_rows, weights[:, 0], preferred_element_type=jnp.float32
    )
    third_pre = jnp.einsum(
        "thd,hfd->htf", key_rows, weights[:, 1], preferred_element_type=jnp.float32
    )
    sigmoid_first = jax.nn.sigmoid(first_pre)
    activated = first_pre * sigmoid_first
    hidden = (activated * third_pre).astype(jnp.bfloat16)
    target = (-token_rates.T[:, :, None] * value_rows.astype(jnp.float32)).astype(jnp.bfloat16)
    grad_down = jnp.einsum("thd,htf->hdf", target, hidden, preferred_element_type=jnp.float32)
    hidden_grad = jnp.einsum(
        "thd,hdf->htf", target, weights[:, 2], preferred_element_type=jnp.float32
    )
    grad_first_in = (
        hidden_grad * third_pre * sigmoid_first * (1.0 + first_pre * (1.0 - sigmoid_first))
    ).astype(jnp.bfloat16)
    grad_third_in = (hidden_grad * activated).astype(jnp.bfloat16)
    grad_first = jnp.einsum(
        "htf,thd->hfd", grad_first_in, key_rows, preferred_element_type=jnp.float32
    )
    grad_third = jnp.einsum(
        "htf,thd->hfd", grad_third_in, key_rows, preferred_element_type=jnp.float32
    )
    gradients = jnp.stack([grad_first, grad_third, grad_down], axis=1)
    row_share = lax.psum_scatter(gradients, "tok", scatter_dimension=2, tiled=True)
    row_count = row_share.shape[2]
    own_rows = lax.dynamic_slice_in_dim(weights, lax.axis_index("tok") * row_count, row_count, 2)
    updated = lax.all_gather(renormed(own_rows, row_share), "tok", axis=2, tiled=True)
    proj_first = jnp.einsum(
        "thd,hfd->thf", query_rows, updated[:, 0], preferred_element_type=jnp.float32
    )
    proj_third = jnp.einsum(
        "thd,hfd->thf", query_rows, updated[:, 1], preferred_element_type=jnp.float32
    )
    mixed_hidden = (jax.nn.silu(proj_first) * proj_third).astype(jnp.bfloat16)
    outputs = jnp.einsum(
        "thf,hdf->thd", mixed_hidden, updated[:, 2], preferred_element_type=jnp.float32
    )
    normed = (
        outputs
        * lax.rsqrt(jnp.mean(outputs * outputs, axis=-1, keepdims=True) + epsilon)
        * head_gains[None]
    )
    normed = normed.astype(jnp.bfloat16)
    height = gate_input.shape[0]
    col_width = gate_input.shape[2]
    shards = lax.axis_size("tok")
    full_width = col_width * shards
    channels_here = head_count * head_size
    frame_grid = normed.reshape(height, full_width, channels_here)
    own_taps = lax.dynamic_slice_in_dim(
        conv_weights, lax.axis_index("head") * channels_here, channels_here, 2
    )
    padded = jnp.pad(frame_grid, ((1, 1), (1, 1), (0, 0)))
    local_sum = jnp.zeros((height, full_width, channels_here), jnp.float32)
    for row_tap in range(3):
        for col_tap in range(3):
            local_sum = local_sum + own_taps[row_tap, col_tap] * padded[
                row_tap : row_tap + height, col_tap : col_tap + full_width
            ].astype(jnp.float32)
    outgoing = local_sum.astype(jnp.bfloat16).reshape(height, shards, col_width, channels_here)
    arrived = lax.all_to_all(outgoing, "tok", split_axis=1, concat_axis=1, tiled=True)
    frame_count = frame_order.shape[0]
    numbers = jnp.arange(frame_count, dtype=jnp.int32)
    inverse = jnp.sum(
        jnp.where(frame_order[None, :] == numbers[:, None], numbers[None, :], 0), axis=1
    )
    ordered = jnp.take(arrived, inverse, axis=1)
    tile_block = lax.all_to_all(ordered, "head", split_axis=1, concat_axis=3, tiled=True)
    return (tile_block.astype(jnp.float32) * jax.nn.silu(gate_input.astype(jnp.float32))).astype(
        jnp.bfloat16
    )


def local(queries, keys, values, rates, fast_weights, norm_gain, frame_order, gate_input, conv_weights):
    args = (
        queries, keys, values, rates, fast_weights, norm_gain, frame_order, gate_input, conv_weights
    )
    if fits_by_heads(queries, gate_input, frame_order):
        return by_heads(*args)
    return by_tokens(*args)


def solution(mesh):
    in_specs = (
        P(("groups", "tok"), "tile", "head", None),
        P(("groups", "tok"), "tile", "head", None),
        P(("groups", "tok"), "tile", "head", None),
        P("tile", "head", ("groups", "tok")),
        P("tile", "head", None, None, None),
        P("tile", "head", None),
        P("groups"),
        P(None, ("groups", "head"), "tok", "tile"),
        P(None, None, "tile"),
    )
    out_specs = P(None, ("groups", "head"), "tok", "tile")
    return jax.shard_map(local, mesh=mesh, in_specs=in_specs, out_specs=out_specs, check_vma=False)
```

```python
import functools

import jax
import jax.numpy as jnp
from jax import lax
from jax.experimental import pallas as pl
from jax.experimental.pallas import tpu as pltpu
from jax.sharding import PartitionSpec as P

epsilon = 1e-06
LANES = 128
VMEM_BYTES = 56 * 1024 * 1024


def split_lanes(source, scratch, rows, head_size):
    full = head_size // LANES
    tail = head_size - full * LANES
    wide = source.reshape(rows, head_size).astype(jnp.float32)
    for tile in range(full):
        scratch[tile] = wide[:, tile * LANES : (tile + 1) * LANES]
    scratch[full, :, 0:tail] = wide[:, full * LANES :]


def join_halves(first, second, tail):
    lane = lax.broadcasted_iota(jnp.int32, first[-1].shape, 1)
    middle = jnp.where(lane < tail, first[-1], pltpu.roll(second[-1], tail, 1))
    return first[:-1] + [middle] + second[:-1]


def part_halves(packed, head_size):
    full = head_size // LANES
    tail = head_size - full * LANES
    first = packed[:, :head_size]
    middle = packed[:, head_size : (full + 1) * LANES]
    second = jnp.concatenate([packed[:, (full + 1) * LANES :], middle], axis=1)
    return first, second


def partner_head(partner):
    return lax.axis_index("tok") ^ partner


def pack_pairs(head, rate_ref, key_tiles, value_tiles, out_ref, start, head_size):
    heads, tok_rows = rate_ref.shape
    half = tok_rows // 2
    full = head_size // LANES
    tail = head_size - full * LANES
    rate_row = -rate_ref[pl.ds(head, 1), :]
    rates = jnp.broadcast_to(rate_row, (LANES, tok_rows)).T
    for row, tiles in ((start, key_tiles), (start + half, value_tiles)):
        sides = []
        for side in range(2):
            parts = [
                tiles[tile, pl.ds(side * half * heads + head, half, stride=heads), :]
                for tile in range(full + 1)
            ]
            if tiles is value_tiles:
                rate = rates[side * half : (side + 1) * half]
                parts = [rate * part for part in parts]
            sides.append(parts)
        for tile, part in enumerate(join_halves(sides[0], sides[1], tail)):
            out_ref[row : row + half, tile * LANES : (tile + 1) * LANES] = part.astype(jnp.bfloat16)


def pack_query(head, heads, height, query_tiles, out_ref, start, head_size):
    tok_rows = query_tiles.shape[1] // heads
    half = tok_rows // 2
    width = tok_rows // height
    full = head_size // LANES
    tail = head_size - full * LANES
    sides = []
    for side in range(2):
        sides.append(
            [
                jnp.concatenate(
                    [
                        query_tiles[
                            tile, pl.ds(column * heads + head, height, stride=width * heads), :
                        ]
                        for column in range(side * width // 2, (side + 1) * width // 2)
                    ],
                    axis=0,
                )
                for tile in range(full + 1)
            ]
        )
    for tile, part in enumerate(join_halves(sides[0], sides[1], tail)):
        out_ref[start : start + half, tile * LANES : (tile + 1) * LANES] = part.astype(jnp.bfloat16)


def pack_mirror_kernel(key_ref, value_ref, rate_ref, *rest):
    outs, key_tiles, value_tiles = rest[:-2], rest[-2], rest[-1]
    tok_rows, heads, head_size = key_ref.shape
    split_lanes(key_ref[...], key_tiles, tok_rows * heads, head_size)
    split_lanes(value_ref[...], value_tiles, tok_rows * heads, head_size)
    for partner, out_ref in enumerate(outs):
        head = partner_head(partner ^ (heads // 2))
        pack_pairs(head, rate_ref, key_tiles, value_tiles, out_ref, 0, head_size)


def pack_across_kernel(height, query_ref, *rest):
    outs, query_tiles = rest[:-1], rest[-1]
    tok_rows, heads, head_size = query_ref.shape
    split_lanes(query_ref[...], query_tiles, tok_rows * heads, head_size)
    for partner, out_ref in enumerate(outs):
        head = partner_head(partner ^ (heads // 2))
        pack_query(head, heads, height, query_tiles, out_ref, 0, head_size)


def pack_near_kernel(height, key_ref, value_ref, rate_ref, query_ref, *rest):
    outs, (key_tiles, value_tiles, query_tiles) = rest[:-3], rest[-3:]
    tok_rows, heads, head_size = key_ref.shape
    split_lanes(key_ref[...], key_tiles, tok_rows * heads, head_size)
    split_lanes(value_ref[...], value_tiles, tok_rows * heads, head_size)
    split_lanes(query_ref[...], query_tiles, tok_rows * heads, head_size)
    for partner, out_ref in enumerate(outs):
        head = partner_head(partner)
        pack_pairs(head, rate_ref, key_tiles, value_tiles, out_ref, 0, head_size)
        pack_query(head, heads, height, query_tiles, out_ref, tok_rows, head_size)


def send(part, partner):
    pairs = [(place, place ^ partner) for place in range(lax.axis_size("tok"))]
    return lax.ppermute(part, "tok", pairs)


def contract(first, second, dims):
    return lax.dot_general(first, second, (dims, ((), ())), preferred_element_type=jnp.float32)


NN = ((1,), (0,))
NT = ((1,), (1,))


def add_gradients(pair_refs, tok_rows, weight_ref, grad_ref):
    half = tok_rows // 2
    head_size = weight_ref.shape[-1]
    first_weight = weight_ref[0]
    third_weight = weight_ref[1]
    down_turned = weight_ref[2].astype(jnp.float32).T.astype(jnp.bfloat16)
    step = 2 if len(pair_refs) % 2 == 0 else 1
    for start in range(0, len(pair_refs), step):
        key_parts, target_parts = [], []
        for pair_ref in pair_refs[start : start + step]:
            key_parts.extend(part_halves(pair_ref[0:half, :], head_size))
            target_parts.extend(part_halves(pair_ref[half:tok_rows, :], head_size))
        key_rows = jnp.concatenate(key_parts, axis=0)
        target = jnp.concatenate(target_parts, axis=0)
        first_pre = contract(first_weight, key_rows, NT)
        third_pre = contract(third_weight, key_rows, NT)
        hidden_grad = contract(down_turned, target, NT)
        sigmoid_first = jax.nn.sigmoid(first_pre)
        activated = first_pre * sigmoid_first
        hidden = (activated * third_pre).astype(jnp.bfloat16)
        grad_first_in = (
            hidden_grad * third_pre * sigmoid_first * (1.0 + first_pre * (1.0 - sigmoid_first))
        ).astype(jnp.bfloat16)
        grad_third_in = (hidden_grad * activated).astype(jnp.bfloat16)
        grads = (
            contract(grad_first_in, key_rows, NN),
            contract(grad_third_in, key_rows, NN),
            contract(hidden, target, NN),
        )
        for index, grad in enumerate(grads):
            if start == 0:
                grad_ref[index, :, 0:head_size] = grad
            else:
                grad_ref[index, :, 0:head_size] += grad


def mirror_kernel(count, *refs):
    pair_refs, (weight_ref, out_ref, grad_ref) = refs[:count], refs[-3:]
    head_size = weight_ref.shape[-1]
    full = head_size // LANES
    tail = head_size - full * LANES
    half = head_size // 2
    add_gradients(pair_refs, pair_refs[0].shape[0], weight_ref, grad_ref)

    def tiles_of(index, rows):
        return [
            grad_ref[index, rows, tile * LANES : (tile + 1) * LANES] for tile in range(full + 1)
        ]

    both = join_halves(tiles_of(0, slice(0, head_size)), tiles_of(1, slice(0, head_size)), tail)
    down = join_halves(tiles_of(2, slice(0, half)), tiles_of(2, slice(half, head_size)), tail)
    for tile, (above, below) in enumerate(zip(both, down)):
        lanes = slice(tile * LANES, (tile + 1) * LANES)
        out_ref[0:head_size, lanes] = above.astype(jnp.bfloat16)
        out_ref[head_size : head_size + half, lanes] = below.astype(jnp.bfloat16)


def own_kernel(tok_rows, *refs):
    pair_refs, (weight_ref, out_ref) = refs[:-2], refs[-2:]
    add_gradients(pair_refs, tok_rows, weight_ref, out_ref)


def renorm(weight_ref, grad_ref, mirror_ref, out_ref):
    head_size = weight_ref.shape[-1]
    first, third = part_halves(mirror_ref[0:head_size, :], head_size)
    down = jnp.concatenate(part_halves(mirror_ref[head_size:, :], head_size), axis=0)
    for index, other in enumerate((first, third, down)):
        before = weight_ref[index].astype(jnp.float32)
        axis = 1
        if index == 2:
            before = before.T
            axis = 0
        grad = grad_ref[index, :, 0:head_size] + other.astype(jnp.float32)
        updated = before - grad
        scale_old = jnp.sqrt(jnp.mean(before * before, axis=axis, keepdims=True) + epsilon)
        scale_new = jnp.sqrt(jnp.mean(updated * updated, axis=axis, keepdims=True) + epsilon)
        out_ref[index] = (updated * (scale_old / scale_new)).astype(jnp.bfloat16)


def apply_kernel(height, frames_here, shards, order_ref, *refs):
    near_refs, far_refs = refs[: shards // 2], refs[shards // 2 : shards]
    before_ref, grad_ref, mirror_ref, gain_ref, tap_ref, out_ref = refs[shards:-3]
    weight_ref, grid_ref, turned_ref = refs[-3:]
    half = far_refs[0].shape[0]
    query_parts = [ref[ref.shape[0] - half :, :] for ref in (*near_refs, *far_refs)]
    renorm(before_ref, grad_ref, mirror_ref, weight_ref)
    width = 2 * half // height
    head_size = weight_ref.shape[-1]
    full = head_size // LANES
    tail = head_size - full * LANES
    top = 8
    edge = jnp.zeros((top, LANES), jnp.float32)
    whole = jnp.zeros(grid_ref.shape[3:], jnp.float32)
    for shard in range(shards):
        for tile in range(full + 1):
            grid_ref[shard, tile, 0] = whole
            grid_ref[shard, tile, width + 1] = whole
            for column in range(1, width + 1):
                grid_ref[shard, tile, column, 0:top] = edge
                grid_ref[shard, tile, column, top + height :] = edge
    gain = gain_ref[...]
    for shard in range(shards):
        rows = jnp.concatenate(part_halves(query_parts[shard], head_size), axis=0)
        proj_first = contract(rows, weight_ref[0], NT)
        proj_third = contract(rows, weight_ref[1], NT)
        mixed = (proj_first * jax.nn.sigmoid(proj_first) * proj_third).astype(jnp.bfloat16)
        outputs = contract(mixed, weight_ref[2], NN)
        scale = lax.rsqrt(jnp.mean(outputs * outputs, axis=-1, keepdims=True) + epsilon)
        normed = (outputs * scale * gain).astype(jnp.bfloat16).astype(jnp.float32)
        frame = order_ref[shard]
        block = frame // frames_here
        slot = frame % frames_here
        for tile in range(full + 1):
            lanes = slice(tile * LANES, min((tile + 1) * LANES, head_size))
            for column in range(width):
                grid_ref[shard, tile, column + 1, top : top + height, 0 : lanes.stop - lanes.start] = (
                    normed[column * height : (column + 1) * height, lanes]
                )
            taps = [
                tap_ref[index : index + 1, tile * LANES : (tile + 1) * LANES] for index in range(9)
            ]
            for column in range(width):
                total = None
                for row_tap in range(3):
                    first = top + row_tap - 1
                    for col_tap in range(3):
                        term = taps[row_tap * 3 + col_tap] * grid_ref[
                            shard, tile, column + col_tap, first : first + height, :
                        ]
                        total = term if total is None else total + term
                turned_ref[
                    block, column, tile, pl.ds(slot, height, stride=frames_here), :
                ] = total
    blocks = turned_ref.shape[0]
    side_rows = out_ref.shape[1]
    for block in range(blocks):
        for column in range(width):
            sides = [
                [
                    turned_ref[block, column, tile, side * side_rows : (side + 1) * side_rows, :]
                    for tile in range(full + 1)
                ]
                for side in range(2)
            ]
            for tile, part in enumerate(join_halves(sides[0], sides[1], tail)):
                out_ref[column * blocks + block, :, tile * LANES : (tile + 1) * LANES] = part.astype(
                    jnp.bfloat16
                )


def gate_kernel(blocks, conv_ref, gate_ref, out_ref):
    chunks, side_rows, _ = conv_ref.shape
    height, frames_here, channels = gate_ref.shape
    head_size = channels // chunks
    shards = chunks // blocks
    rows_here = height // 2
    for pair in range(chunks // 2):
        lanes = slice(pair * 2 * head_size, (pair + 1) * 2 * head_size)
        halves = []
        for head in (2 * pair, 2 * pair + 1):
            chunk = (head % shards) * blocks + head // shards
            halves.append(part_halves(conv_ref[chunk].astype(jnp.float32), head_size))
        for side in range(2):
            conv = jnp.concatenate([halves[0][side], halves[1][side]], axis=1)
            gate = gate_ref[side * rows_here : (side + 1) * rows_here, :, lanes].astype(jnp.float32)
            conv = conv.reshape(rows_here, frames_here, 2 * head_size)
            out_ref[side * rows_here : (side + 1) * rows_here, :, lanes] = (
                conv * (gate * jax.nn.sigmoid(gate))
            ).astype(jnp.bfloat16)


def in_vmem(count):
    return [pl.BlockSpec(memory_space=pltpu.VMEM)] * count


def call(kernel, out, operands, scratch=(), flops=0, specs=None):
    moved = sum(item.size * item.dtype.itemsize for item in operands)
    moved += sum(item.size * item.dtype.itemsize for item in jax.tree.leaves(out))
    return pl.pallas_call(
        kernel,
        out_shape=out,
        in_specs=specs or in_vmem(len(operands)),
        out_specs=jax.tree.map(lambda _: pl.BlockSpec(memory_space=pltpu.VMEM), out),
        scratch_shapes=scratch,
        compiler_params=pltpu.CompilerParams(vmem_limit_bytes=VMEM_BYTES),
        cost_estimate=pl.CostEstimate(flops=flops, bytes_accessed=moved, transcendentals=0),
    )(*operands)


def by_heads(
    queries, keys, values, rates, fast_weights, norm_gain, frame_order, gate_input, conv_weights
):
    tok_rows = queries.shape[0]
    head_count = queries.shape[1] * queries.shape[2]
    head_size = queries.shape[3]
    height, frames_here = gate_input.shape[:2]
    shards = lax.axis_size("tok")
    blocks = lax.axis_size("head")
    half = tok_rows // 2
    wide = 2 * head_size
    tiles = head_size // LANES + 1
    own = lax.axis_index("tok")
    own_channel = lax.axis_index("head") * head_count + own

    def rows_of(array):
        return array.reshape(tok_rows, head_count, head_size)

    def own_of(array, place):
        return lax.dynamic_index_in_dim(array, place, 0, keepdims=False)

    line = shards // 2
    tile_scratch = pltpu.VMEM((tiles, tok_rows * head_count, LANES), jnp.float32)
    token_rates = rates.reshape(head_count, tok_rows)
    mirrored = call(
        pack_mirror_kernel,
        [jax.ShapeDtypeStruct((tok_rows, wide), jnp.bfloat16)] * line,
        (rows_of(keys), rows_of(values), token_rates),
        (tile_scratch, tile_scratch),
    )
    mirrored = [mirrored[0]] + [send(mirrored[k], k) for k in range(1, line)]
    across = call(
        functools.partial(pack_across_kernel, height),
        [jax.ShapeDtypeStruct((half, wide), jnp.bfloat16)] * line,
        (rows_of(queries),),
        (tile_scratch,),
    )
    across = [send(across[k], k ^ line) for k in range(line)]
    packed = call(
        functools.partial(pack_near_kernel, height),
        [jax.ShapeDtypeStruct((tok_rows + half, wide), jnp.bfloat16)] * line,
        (rows_of(keys), rows_of(values), token_rates, rows_of(queries)),
        (tile_scratch, tile_scratch, tile_scratch),
    )
    near = [packed[0]] + [send(packed[k], k) for k in range(1, line)]
    weights = fast_weights.reshape(head_count, 3, head_size, head_size)
    own_weights = own_of(weights, own)
    own_gain = own_of(norm_gain.reshape(head_count, 1, head_size), own)
    taps = conv_weights.reshape(9, blocks * head_count, head_size)
    own_taps = lax.dynamic_index_in_dim(taps, own_channel, 1, keepdims=False)
    own_taps = jnp.pad(own_taps, ((0, 0), (0, tiles * LANES - head_size)))
    frames = frame_order[own ^ jnp.arange(shards, dtype=jnp.int32)]
    product = shards * tok_rows * head_size * head_size
    grad_shape = (3, head_size, tiles * LANES)
    ahead = (*across[: line // 2], packed[0])
    crossing = call(
        functools.partial(mirror_kernel, line),
        jax.ShapeDtypeStruct((head_size + head_size // 2, wide), jnp.bfloat16),
        (*mirrored, *ahead, own_of(weights, own ^ line)),
        (pltpu.VMEM(grad_shape, jnp.float32),),
        flops=6 * product,
        specs=in_vmem(line) + [pl.BlockSpec(memory_space=pl.ANY)] * len(ahead) + in_vmem(1),
    )
    crossed = send(crossing, line)
    gradients = call(
        functools.partial(own_kernel, tok_rows),
        jax.ShapeDtypeStruct(grad_shape, jnp.float32),
        (*near, own_weights),
        flops=6 * product,
    )
    side_rows = frames_here * height // 2
    outgoing = call(
        functools.partial(apply_kernel, height, frames_here, shards),
        jax.ShapeDtypeStruct((shards * blocks, side_rows, wide), jnp.bfloat16),
        (frames, *near, *across, own_weights, gradients, crossed, own_gain, own_taps),
        (
            pltpu.VMEM((3, head_size, head_size), jnp.bfloat16),
            pltpu.VMEM((shards, tiles, shards + 2, height + 16, LANES), jnp.float32),
            pltpu.VMEM((blocks, shards, tiles, 2 * side_rows, LANES), jnp.float32),
        ),
        flops=6 * product,
        specs=[pl.BlockSpec(memory_space=pltpu.SMEM)] + in_vmem(shards + 5),
    )
    arrived = lax.all_to_all(outgoing, ("tok", "head"), split_axis=0, concat_axis=0, tiled=True)
    gate = gate_input.reshape(height, frames_here, gate_input.shape[3])
    gated = call(
        functools.partial(gate_kernel, blocks),
        jax.ShapeDtypeStruct(gate.shape, jnp.bfloat16),
        (arrived, gate),
    )
    return gated.reshape(gate_input.shape)


def fits_by_heads(queries, gate_input, frame_order):
    tok_rows, head_size = queries.shape[0], queries.shape[3]
    head_count = queries.shape[1] * queries.shape[2]
    height, frames_here, col_width = gate_input.shape[:3]
    shards = lax.axis_size("tok")
    return (
        head_count == shards
        and frame_order.shape[0] == shards
        and lax.axis_size("tile") == 1
        and col_width == 1
        and shards % 2 == 0
        and shards & (shards - 1) == 0
        and head_size % LANES == LANES // 2
        and height % 8 == 0
        and tok_rows == height * shards
        and tok_rows % 32 == 0
        and head_size % 32 == 0
        and frames_here * height % 32 == 0
        and frames_here * lax.axis_size("head") == shards
        and lax.axis_size("head") & (lax.axis_size("head") - 1) == 0
    )


def renormed(previous, gradient):
    before = previous.astype(jnp.float32)
    updated = before - gradient
    scale_old = jnp.sqrt(jnp.mean(before * before, axis=-1, keepdims=True) + epsilon)
    scale_new = jnp.sqrt(jnp.mean(updated * updated, axis=-1, keepdims=True) + epsilon)
    return (updated * (scale_old / scale_new)).astype(jnp.bfloat16)


def by_tokens(
    queries, keys, values, rates, fast_weights, norm_gain, frame_order, gate_input, conv_weights
):
    tok_rows = queries.shape[0]
    head_count = queries.shape[1] * queries.shape[2]
    head_size = queries.shape[3]
    query_rows = queries.reshape(tok_rows, head_count, head_size)
    key_rows = keys.reshape(tok_rows, head_count, head_size)
    value_rows = values.reshape(tok_rows, head_count, head_size)
    token_rates = rates.reshape(head_count, tok_rows)
    weights = fast_weights.reshape(head_count, 3, head_size, head_size)
    head_gains = norm_gain.reshape(head_count, head_size)
    first_pre = jnp.einsum(
        "thd,hfd->htf", key_rows, weights[:, 0], preferred_element_type=jnp.float32
    )
    third_pre = jnp.einsum(
        "thd,hfd->htf", key_rows, weights[:, 1], preferred_element_type=jnp.float32
    )
    sigmoid_first = jax.nn.sigmoid(first_pre)
    activated = first_pre * sigmoid_first
    hidden = (activated * third_pre).astype(jnp.bfloat16)
    target = (-token_rates.T[:, :, None] * value_rows.astype(jnp.float32)).astype(jnp.bfloat16)
    grad_down = jnp.einsum("thd,htf->hdf", target, hidden, preferred_element_type=jnp.float32)
    hidden_grad = jnp.einsum(
        "thd,hdf->htf", target, weights[:, 2], preferred_element_type=jnp.float32
    )
    grad_first_in = (
        hidden_grad * third_pre * sigmoid_first * (1.0 + first_pre * (1.0 - sigmoid_first))
    ).astype(jnp.bfloat16)
    grad_third_in = (hidden_grad * activated).astype(jnp.bfloat16)
    grad_first = jnp.einsum(
        "htf,thd->hfd", grad_first_in, key_rows, preferred_element_type=jnp.float32
    )
    grad_third = jnp.einsum(
        "htf,thd->hfd", grad_third_in, key_rows, preferred_element_type=jnp.float32
    )
    gradients = jnp.stack([grad_first, grad_third, grad_down], axis=1)
    row_share = lax.psum_scatter(gradients, "tok", scatter_dimension=2, tiled=True)
    row_count = row_share.shape[2]
    own_rows = lax.dynamic_slice_in_dim(weights, lax.axis_index("tok") * row_count, row_count, 2)
    updated = lax.all_gather(renormed(own_rows, row_share), "tok", axis=2, tiled=True)
    proj_first = jnp.einsum(
        "thd,hfd->thf", query_rows, updated[:, 0], preferred_element_type=jnp.float32
    )
    proj_third = jnp.einsum(
        "thd,hfd->thf", query_rows, updated[:, 1], preferred_element_type=jnp.float32
    )
    mixed_hidden = (jax.nn.silu(proj_first) * proj_third).astype(jnp.bfloat16)
    outputs = jnp.einsum(
        "thf,hdf->thd", mixed_hidden, updated[:, 2], preferred_element_type=jnp.float32
    )
    normed = (
        outputs
        * lax.rsqrt(jnp.mean(outputs * outputs, axis=-1, keepdims=True) + epsilon)
        * head_gains[None]
    )
    normed = normed.astype(jnp.bfloat16)
    height = gate_input.shape[0]
    col_width = gate_input.shape[2]
    shards = lax.axis_size("tok")
    full_width = col_width * shards
    channels_here = head_count * head_size
    frame_grid = normed.reshape(height, full_width, channels_here)
    own_taps = lax.dynamic_slice_in_dim(
        conv_weights, lax.axis_index("head") * channels_here, channels_here, 2
    )
    padded = jnp.pad(frame_grid, ((1, 1), (1, 1), (0, 0)))
    local_sum = jnp.zeros((height, full_width, channels_here), jnp.float32)
    for row_tap in range(3):
        for col_tap in range(3):
            local_sum = local_sum + own_taps[row_tap, col_tap] * padded[
                row_tap : row_tap + height, col_tap : col_tap + full_width
            ].astype(jnp.float32)
    outgoing = local_sum.astype(jnp.bfloat16).reshape(height, shards, col_width, channels_here)
    arrived = lax.all_to_all(outgoing, "tok", split_axis=1, concat_axis=1, tiled=True)
    frame_count = frame_order.shape[0]
    numbers = jnp.arange(frame_count, dtype=jnp.int32)
    inverse = jnp.sum(
        jnp.where(frame_order[None, :] == numbers[:, None], numbers[None, :], 0), axis=1
    )
    ordered = jnp.take(arrived, inverse, axis=1)
    tile_block = lax.all_to_all(ordered, "head", split_axis=1, concat_axis=3, tiled=True)
    return (tile_block.astype(jnp.float32) * jax.nn.silu(gate_input.astype(jnp.float32))).astype(
        jnp.bfloat16
    )


def local(queries, keys, values, rates, fast_weights, norm_gain, frame_order, gate_input, conv_weights):
    args = (
        queries, keys, values, rates, fast_weights, norm_gain, frame_order, gate_input, conv_weights
    )
    if fits_by_heads(queries, gate_input, frame_order):
        return by_heads(*args)
    return by_tokens(*args)


def solution(mesh):
    in_specs = (
        P(("groups", "tok"), "tile", "head", None),
        P(("groups", "tok"), "tile", "head", None),
        P(("groups", "tok"), "tile", "head", None),
        P("tile", "head", ("groups", "tok")),
        P("tile", "head", None, None, None),
        P("tile", "head", None),
        P("groups"),
        P(None, ("groups", "head"), "tok", "tile"),
        P(None, None, "tile"),
    )
    out_specs = P(None, ("groups", "head"), "tok", "tile")
    return jax.shard_map(local, mesh=mesh, in_specs=in_specs, out_specs=out_specs, check_vma=False)
```

```python
import functools

import jax
import jax.numpy as jnp
from jax import lax
from jax.experimental import pallas as pl
from jax.experimental.pallas import tpu as pltpu
from jax.sharding import PartitionSpec as P

epsilon = 1e-06
LANES = 128
VMEM_BYTES = 56 * 1024 * 1024


def split_lanes(source, scratch, rows, head_size):
    full = head_size // LANES
    tail = head_size - full * LANES
    wide = source.reshape(rows, head_size).astype(jnp.float32)
    for tile in range(full):
        scratch[tile] = wide[:, tile * LANES : (tile + 1) * LANES]
    scratch[full, :, 0:tail] = wide[:, full * LANES :]


def join_halves(first, second, tail):
    lane = lax.broadcasted_iota(jnp.int32, first[-1].shape, 1)
    middle = jnp.where(lane < tail, first[-1], pltpu.roll(second[-1], tail, 1))
    return first[:-1] + [middle] + second[:-1]


def part_halves(packed, head_size):
    full = head_size // LANES
    tail = head_size - full * LANES
    first = packed[:, :head_size]
    middle = packed[:, head_size : (full + 1) * LANES]
    second = jnp.concatenate([packed[:, (full + 1) * LANES :], middle], axis=1)
    return first, second


def partner_head(partner):
    return lax.axis_index("tok") ^ partner


def pack_pairs(head, rate_ref, key_tiles, value_tiles, out_ref, start, head_size):
    heads, tok_rows = rate_ref.shape
    half = tok_rows // 2
    full = head_size // LANES
    tail = head_size - full * LANES
    rate_row = -rate_ref[pl.ds(head, 1), :]
    rates = jnp.broadcast_to(rate_row, (LANES, tok_rows)).T
    for row, tiles in ((start, key_tiles), (start + half, value_tiles)):
        sides = []
        for side in range(2):
            parts = [
                tiles[tile, pl.ds(side * half * heads + head, half, stride=heads), :]
                for tile in range(full + 1)
            ]
            if tiles is value_tiles:
                rate = rates[side * half : (side + 1) * half]
                parts = [rate * part for part in parts]
            sides.append(parts)
        for tile, part in enumerate(join_halves(sides[0], sides[1], tail)):
            out_ref[row : row + half, tile * LANES : (tile + 1) * LANES] = part.astype(jnp.bfloat16)


def pack_query(head, heads, height, query_tiles, out_ref, start, head_size):
    tok_rows = query_tiles.shape[1] // heads
    half = tok_rows // 2
    width = tok_rows // height
    full = head_size // LANES
    tail = head_size - full * LANES
    sides = []
    for side in range(2):
        sides.append(
            [
                jnp.concatenate(
                    [
                        query_tiles[
                            tile, pl.ds(column * heads + head, height, stride=width * heads), :
                        ]
                        for column in range(side * width // 2, (side + 1) * width // 2)
                    ],
                    axis=0,
                )
                for tile in range(full + 1)
            ]
        )
    for tile, part in enumerate(join_halves(sides[0], sides[1], tail)):
        out_ref[start : start + half, tile * LANES : (tile + 1) * LANES] = part.astype(jnp.bfloat16)


def pack_mirror_kernel(key_ref, value_ref, rate_ref, *rest):
    outs, (key_tiles, value_tiles) = rest[:-2], rest[-2:]
    tok_rows, heads, head_size = key_ref.shape
    split_lanes(key_ref[...], key_tiles, tok_rows * heads, head_size)
    split_lanes(value_ref[...], value_tiles, tok_rows * heads, head_size)
    for partner, out_ref in enumerate(outs):
        head = partner_head(partner ^ (heads // 2))
        pack_pairs(head, rate_ref, key_tiles, value_tiles, out_ref, 0, head_size)


def pack_across_kernel(height, query_ref, *rest):
    outs, query_tiles = rest[:-1], rest[-1]
    tok_rows, heads, head_size = query_ref.shape
    half = tok_rows // 2
    split_lanes(query_ref[...], query_tiles, tok_rows * heads, head_size)
    for partner in range(heads // 2):
        head = partner_head(partner ^ (heads // 2))
        start = partner % 2 * half
        pack_query(head, heads, height, query_tiles, outs[partner // 2], start, head_size)


def pack_near_kernel(height, key_ref, value_ref, rate_ref, query_ref, *rest):
    outs, (key_tiles, value_tiles, query_tiles) = rest[-3 - key_ref.shape[1] // 2 : -3], rest[-3:]
    tok_rows, heads, head_size = key_ref.shape
    split_lanes(key_ref[...], key_tiles, tok_rows * heads, head_size)
    split_lanes(value_ref[...], value_tiles, tok_rows * heads, head_size)
    split_lanes(query_ref[...], query_tiles, tok_rows * heads, head_size)
    for partner, out_ref in enumerate(outs):
        head = partner_head(partner)
        pack_pairs(head, rate_ref, key_tiles, value_tiles, out_ref, 0, head_size)
        pack_query(head, heads, height, query_tiles, out_ref, tok_rows, head_size)


def relay(landed):
    return [part for one in landed for part in (one, send(one, 1))]


def send(part, partner):
    pairs = [(place, place ^ partner) for place in range(lax.axis_size("tok"))]
    return lax.ppermute(part, "tok", pairs)


def contract(first, second, dims):
    return lax.dot_general(first, second, (dims, ((), ())), preferred_element_type=jnp.float32)


NN = ((1,), (0,))
NT = ((1,), (1,))


def add_gradients(pair_refs, tok_rows, weight_ref, grad_ref):
    half = tok_rows // 2
    head_size = weight_ref.shape[-1]
    first_weight = weight_ref[0]
    third_weight = weight_ref[1]
    down_turned = weight_ref[2].astype(jnp.float32).T.astype(jnp.bfloat16)
    step = 2 if len(pair_refs) % 2 == 0 else 1
    for start in range(0, len(pair_refs), step):
        key_parts, target_parts = [], []
        for pair_ref in pair_refs[start : start + step]:
            key_parts.extend(part_halves(pair_ref[0:half, :], head_size))
            target_parts.extend(part_halves(pair_ref[half:tok_rows, :], head_size))
        key_rows = jnp.concatenate(key_parts, axis=0)
        target = jnp.concatenate(target_parts, axis=0)
        first_pre = contract(first_weight, key_rows, NT)
        third_pre = contract(third_weight, key_rows, NT)
        hidden_grad = contract(down_turned, target, NT)
        sigmoid_first = jax.nn.sigmoid(first_pre)
        activated = first_pre * sigmoid_first
        hidden = (activated * third_pre).astype(jnp.bfloat16)
        grad_first_in = (
            hidden_grad * third_pre * sigmoid_first * (1.0 + first_pre * (1.0 - sigmoid_first))
        ).astype(jnp.bfloat16)
        grad_third_in = (hidden_grad * activated).astype(jnp.bfloat16)
        grads = (
            contract(grad_first_in, key_rows, NN),
            contract(grad_third_in, key_rows, NN),
            contract(hidden, target, NN),
        )
        for index, grad in enumerate(grads):
            if start == 0:
                grad_ref[index, :, 0:head_size] = grad
            else:
                grad_ref[index, :, 0:head_size] += grad


def mirror_kernel(count, tok_rows, *refs):
    pair_refs, (weight_ref, out_ref, grad_ref) = refs[:count], refs[-3:]
    head_size = weight_ref.shape[-1]
    full = head_size // LANES
    tail = head_size - full * LANES
    half = head_size // 2
    add_gradients(pair_refs, tok_rows, weight_ref, grad_ref)

    def tiles_of(index, rows):
        return [
            grad_ref[index, rows, tile * LANES : (tile + 1) * LANES] for tile in range(full + 1)
        ]

    both = join_halves(tiles_of(0, slice(0, head_size)), tiles_of(1, slice(0, head_size)), tail)
    down = join_halves(tiles_of(2, slice(0, half)), tiles_of(2, slice(half, head_size)), tail)
    for tile, (above, below) in enumerate(zip(both, down)):
        lanes = slice(tile * LANES, (tile + 1) * LANES)
        out_ref[0:head_size, lanes] = above.astype(jnp.bfloat16)
        out_ref[head_size : head_size + half, lanes] = below.astype(jnp.bfloat16)


def own_kernel(tok_rows, *refs):
    pair_refs, (weight_ref, out_ref) = refs[:-2], refs[-2:]
    add_gradients(pair_refs, tok_rows, weight_ref, out_ref)


def renorm(weight_ref, grad_ref, mirror_ref, out_ref):
    head_size = weight_ref.shape[-1]
    first, third = part_halves(mirror_ref[0:head_size, :], head_size)
    down = jnp.concatenate(part_halves(mirror_ref[head_size:, :], head_size), axis=0)
    for index, other in enumerate((first, third, down)):
        before = weight_ref[index].astype(jnp.float32)
        axis = 1
        if index == 2:
            before = before.T
            axis = 0
        grad = grad_ref[index, :, 0:head_size] + other.astype(jnp.float32)
        updated = before - grad
        scale_old = jnp.sqrt(jnp.mean(before * before, axis=axis, keepdims=True) + epsilon)
        scale_new = jnp.sqrt(jnp.mean(updated * updated, axis=axis, keepdims=True) + epsilon)
        out_ref[index] = (updated * (scale_old / scale_new)).astype(jnp.bfloat16)


def apply_kernel(height, frames_here, shards, order_ref, *refs):
    near_refs, far_refs = refs[: shards // 2], refs[shards // 2 : shards]
    before_ref, grad_ref, mirror_ref, gain_ref, tap_ref, out_ref = refs[shards:-3]
    weight_ref, grid_ref, turned_ref = refs[-3:]
    half = far_refs[0].shape[0] // 2
    query_parts = [ref[ref.shape[0] - half :, :] for ref in near_refs]
    for index, ref in enumerate(far_refs):
        query_parts.append(ref[index % 2 * half : (index % 2 + 1) * half, :])
    renorm(before_ref, grad_ref, mirror_ref, weight_ref)
    width = 2 * half // height
    head_size = weight_ref.shape[-1]
    full = head_size // LANES
    tail = head_size - full * LANES
    top = 8
    edge = jnp.zeros((top, LANES), jnp.float32)
    whole = jnp.zeros(grid_ref.shape[3:], jnp.float32)
    for shard in range(shards):
        for tile in range(full + 1):
            grid_ref[shard, tile, 0] = whole
            grid_ref[shard, tile, width + 1] = whole
            for column in range(1, width + 1):
                grid_ref[shard, tile, column, 0:top] = edge
                grid_ref[shard, tile, column, top + height :] = edge
    gain = gain_ref[...]
    for shard in range(shards):
        rows = jnp.concatenate(part_halves(query_parts[shard], head_size), axis=0)
        proj_first = contract(rows, weight_ref[0], NT)
        proj_third = contract(rows, weight_ref[1], NT)
        mixed = (proj_first * jax.nn.sigmoid(proj_first) * proj_third).astype(jnp.bfloat16)
        outputs = contract(mixed, weight_ref[2], NN)
        scale = lax.rsqrt(jnp.mean(outputs * outputs, axis=-1, keepdims=True) + epsilon)
        normed = (outputs * scale * gain).astype(jnp.bfloat16).astype(jnp.float32)
        frame = order_ref[shard]
        block = frame // frames_here
        slot = frame % frames_here
        for tile in range(full + 1):
            lanes = slice(tile * LANES, min((tile + 1) * LANES, head_size))
            for column in range(width):
                grid_ref[shard, tile, column + 1, top : top + height, 0 : lanes.stop - lanes.start] = (
                    normed[column * height : (column + 1) * height, lanes]
                )
            taps = [
                tap_ref[index : index + 1, tile * LANES : (tile + 1) * LANES] for index in range(9)
            ]
            for column in range(width):
                total = None
                for row_tap in range(3):
                    first = top + row_tap - 1
                    for col_tap in range(3):
                        term = taps[row_tap * 3 + col_tap] * grid_ref[
                            shard, tile, column + col_tap, first : first + height, :
                        ]
                        total = term if total is None else total + term
                turned_ref[
                    block, column, tile, pl.ds(slot, height, stride=frames_here), :
                ] = total
    blocks = turned_ref.shape[0]
    side_rows = out_ref.shape[1]
    for block in range(blocks):
        for column in range(width):
            sides = [
                [
                    turned_ref[block, column, tile, side * side_rows : (side + 1) * side_rows, :]
                    for tile in range(full + 1)
                ]
                for side in range(2)
            ]
            for tile, part in enumerate(join_halves(sides[0], sides[1], tail)):
                out_ref[column * blocks + block, :, tile * LANES : (tile + 1) * LANES] = part.astype(
                    jnp.bfloat16
                )


def gate_kernel(blocks, conv_ref, gate_ref, out_ref):
    chunks, side_rows, _ = conv_ref.shape
    height, frames_here, channels = gate_ref.shape
    head_size = channels // chunks
    shards = chunks // blocks
    rows_here = height // 2
    for pair in range(chunks // 2):
        lanes = slice(pair * 2 * head_size, (pair + 1) * 2 * head_size)
        halves = []
        for head in (2 * pair, 2 * pair + 1):
            chunk = (head % shards) * blocks + head // shards
            halves.append(part_halves(conv_ref[chunk].astype(jnp.float32), head_size))
        for side in range(2):
            conv = jnp.concatenate([halves[0][side], halves[1][side]], axis=1)
            gate = gate_ref[side * rows_here : (side + 1) * rows_here, :, lanes].astype(jnp.float32)
            conv = conv.reshape(rows_here, frames_here, 2 * head_size)
            out_ref[side * rows_here : (side + 1) * rows_here, :, lanes] = (
                conv * (gate * jax.nn.sigmoid(gate))
            ).astype(jnp.bfloat16)


def in_vmem(count):
    return [pl.BlockSpec(memory_space=pltpu.VMEM)] * count


def call(kernel, out, operands, scratch=(), flops=0, specs=None):
    return pl.pallas_call(
        kernel,
        out_shape=out,
        in_specs=specs or in_vmem(len(operands)),
        out_specs=jax.tree.map(lambda _: pl.BlockSpec(memory_space=pltpu.VMEM), out),
        scratch_shapes=scratch,
        compiler_params=pltpu.CompilerParams(vmem_limit_bytes=VMEM_BYTES),
        cost_estimate=pl.CostEstimate(flops=flops, bytes_accessed=0, transcendentals=0),
    )(*operands)


def after(part, earlier):
    anywhere = pl.BlockSpec(memory_space=pl.ANY)
    return pl.pallas_call(
        lambda part_ref, earlier_ref, out_ref: None,
        out_shape=jax.ShapeDtypeStruct(part.shape, part.dtype),
        in_specs=[anywhere, anywhere],
        out_specs=anywhere,
        input_output_aliases={0: 0},
        cost_estimate=pl.CostEstimate(flops=0, bytes_accessed=0, transcendentals=0),
    )(part, earlier)


def by_heads(
    queries, keys, values, rates, fast_weights, norm_gain, frame_order, gate_input, conv_weights
):
    tok_rows = queries.shape[0]
    head_count = queries.shape[1] * queries.shape[2]
    head_size = queries.shape[3]
    height, frames_here = gate_input.shape[:2]
    shards = lax.axis_size("tok")
    blocks = lax.axis_size("head")
    half = tok_rows // 2
    wide = 2 * head_size
    tiles = head_size // LANES + 1
    own = lax.axis_index("tok")
    own_channel = lax.axis_index("head") * head_count + own

    def rows_of(array):
        return array.reshape(tok_rows, head_count, head_size)

    def own_of(array, place):
        return lax.dynamic_index_in_dim(array, place, 0, keepdims=False)

    line = shards // 2
    tile_scratch = pltpu.VMEM((tiles, tok_rows * head_count, LANES), jnp.float32)
    token_rates = rates.reshape(head_count, tok_rows)
    chips = line // 2

    one = jax.ShapeDtypeStruct((tok_rows, wide), jnp.bfloat16)
    mirrored = call(
        pack_mirror_kernel,
        [one] * line,
        (rows_of(keys), rows_of(values), token_rates),
        (tile_scratch, tile_scratch),
    )
    mirrored = [mirrored[0]] + [send(mirrored[k], k) for k in range(1, line)]
    across = call(
        functools.partial(pack_across_kernel, height),
        [one] * chips,
        (rows_of(queries),),
        (tile_scratch,),
    )
    across_landed = [send(part, line + 2 * index) for index, part in enumerate(across)]
    packed = call(
        functools.partial(pack_near_kernel, height),
        [jax.ShapeDtypeStruct((tok_rows + half, wide), jnp.bfloat16)] * line,
        (rows_of(keys), rows_of(values), token_rates, rows_of(queries), across[0]),
        (tile_scratch, tile_scratch, tile_scratch),
        specs=in_vmem(4) + [pl.BlockSpec(memory_space=pl.ANY)],
    )
    near = [packed[0]] + [send(packed[k], k) for k in range(1, line)]
    weights = fast_weights.reshape(head_count, 3, head_size, head_size)
    own_weights = own_of(weights, own)
    own_gain = own_of(norm_gain.reshape(head_count, 1, head_size), own)
    taps = conv_weights.reshape(9, blocks * head_count, head_size)
    own_taps = lax.dynamic_index_in_dim(taps, own_channel, 1, keepdims=False)
    own_taps = jnp.pad(own_taps, ((0, 0), (0, tiles * LANES - head_size)))
    frames = frame_order[own ^ jnp.arange(shards, dtype=jnp.int32)]
    product = shards * tok_rows * head_size * head_size
    grad_shape = (3, head_size, tiles * LANES)
    ahead = (*across_landed, packed[0])
    crossing = call(
        functools.partial(mirror_kernel, line, tok_rows),
        jax.ShapeDtypeStruct((head_size + head_size // 2, wide), jnp.bfloat16),
        (*mirrored, *ahead, own_of(weights, own ^ line)),
        (pltpu.VMEM(grad_shape, jnp.float32),),
        flops=0,
        specs=in_vmem(line) + [pl.BlockSpec(memory_space=pl.ANY)] * len(ahead) + in_vmem(1),
    )
    crossed = send(crossing, line)
    across = relay([after(part, crossing) for part in across_landed])
    gradients = call(
        functools.partial(own_kernel, tok_rows),
        jax.ShapeDtypeStruct(grad_shape, jnp.float32),
        (*near, own_weights),
        flops=0,
    )
    side_rows = frames_here * height // 2
    outgoing = call(
        functools.partial(apply_kernel, height, frames_here, shards),
        jax.ShapeDtypeStruct((shards * blocks, side_rows, wide), jnp.bfloat16),
        (frames, *near, *across, own_weights, gradients, crossed, own_gain, own_taps),
        (
            pltpu.VMEM((3, head_size, head_size), jnp.bfloat16),
            pltpu.VMEM((shards, tiles, shards + 2, height + 16, LANES), jnp.float32),
            pltpu.VMEM((blocks, shards, tiles, 2 * side_rows, LANES), jnp.float32),
        ),
        flops=0,
        specs=[pl.BlockSpec(memory_space=pltpu.SMEM)] + in_vmem(shards + 5),
    )
    arrived = lax.all_to_all(outgoing, ("tok", "head"), split_axis=0, concat_axis=0, tiled=True)
    gate = gate_input.reshape(height, frames_here, gate_input.shape[3])
    gated = call(
        functools.partial(gate_kernel, blocks),
        jax.ShapeDtypeStruct(gate.shape, jnp.bfloat16),
        (arrived, gate),
    )
    return gated.reshape(gate_input.shape)


def fits_by_heads(queries, gate_input, frame_order):
    tok_rows, head_size = queries.shape[0], queries.shape[3]
    head_count = queries.shape[1] * queries.shape[2]
    height, frames_here, col_width = gate_input.shape[:3]
    shards = lax.axis_size("tok")
    return (
        head_count == shards
        and frame_order.shape[0] == shards
        and lax.axis_size("tile") == 1
        and col_width == 1
        and shards % 2 == 0
        and shards & (shards - 1) == 0
        and head_size % LANES == LANES // 2
        and height % 8 == 0
        and tok_rows == height * shards
        and tok_rows % 32 == 0
        and head_size % 32 == 0
        and frames_here * height % 32 == 0
        and frames_here * lax.axis_size("head") == shards
        and lax.axis_size("head") & (lax.axis_size("head") - 1) == 0
    )


def renormed(previous, gradient):
    before = previous.astype(jnp.float32)
    updated = before - gradient
    scale_old = jnp.sqrt(jnp.mean(before * before, axis=-1, keepdims=True) + epsilon)
    scale_new = jnp.sqrt(jnp.mean(updated * updated, axis=-1, keepdims=True) + epsilon)
    return (updated * (scale_old / scale_new)).astype(jnp.bfloat16)


def by_tokens(
    queries, keys, values, rates, fast_weights, norm_gain, frame_order, gate_input, conv_weights
):
    tok_rows = queries.shape[0]
    head_count = queries.shape[1] * queries.shape[2]
    head_size = queries.shape[3]
    query_rows = queries.reshape(tok_rows, head_count, head_size)
    key_rows = keys.reshape(tok_rows, head_count, head_size)
    value_rows = values.reshape(tok_rows, head_count, head_size)
    token_rates = rates.reshape(head_count, tok_rows)
    weights = fast_weights.reshape(head_count, 3, head_size, head_size)
    head_gains = norm_gain.reshape(head_count, head_size)
    first_pre = jnp.einsum(
        "thd,hfd->htf", key_rows, weights[:, 0], preferred_element_type=jnp.float32
    )
    third_pre = jnp.einsum(
        "thd,hfd->htf", key_rows, weights[:, 1], preferred_element_type=jnp.float32
    )
    sigmoid_first = jax.nn.sigmoid(first_pre)
    activated = first_pre * sigmoid_first
    hidden = (activated * third_pre).astype(jnp.bfloat16)
    target = (-token_rates.T[:, :, None] * value_rows.astype(jnp.float32)).astype(jnp.bfloat16)
    grad_down = jnp.einsum("thd,htf->hdf", target, hidden, preferred_element_type=jnp.float32)
    hidden_grad = jnp.einsum(
        "thd,hdf->htf", target, weights[:, 2], preferred_element_type=jnp.float32
    )
    grad_first_in = (
        hidden_grad * third_pre * sigmoid_first * (1.0 + first_pre * (1.0 - sigmoid_first))
    ).astype(jnp.bfloat16)
    grad_third_in = (hidden_grad * activated).astype(jnp.bfloat16)
    grad_first = jnp.einsum(
        "htf,thd->hfd", grad_first_in, key_rows, preferred_element_type=jnp.float32
    )
    grad_third = jnp.einsum(
        "htf,thd->hfd", grad_third_in, key_rows, preferred_element_type=jnp.float32
    )
    gradients = jnp.stack([grad_first, grad_third, grad_down], axis=1)
    row_share = lax.psum_scatter(gradients, "tok", scatter_dimension=2, tiled=True)
    row_count = row_share.shape[2]
    own_rows = lax.dynamic_slice_in_dim(weights, lax.axis_index("tok") * row_count, row_count, 2)
    updated = lax.all_gather(renormed(own_rows, row_share), "tok", axis=2, tiled=True)
    proj_first = jnp.einsum(
        "thd,hfd->thf", query_rows, updated[:, 0], preferred_element_type=jnp.float32
    )
    proj_third = jnp.einsum(
        "thd,hfd->thf", query_rows, updated[:, 1], preferred_element_type=jnp.float32
    )
    mixed_hidden = (jax.nn.silu(proj_first) * proj_third).astype(jnp.bfloat16)
    outputs = jnp.einsum(
        "thf,hdf->thd", mixed_hidden, updated[:, 2], preferred_element_type=jnp.float32
    )
    normed = (
        outputs
        * lax.rsqrt(jnp.mean(outputs * outputs, axis=-1, keepdims=True) + epsilon)
        * head_gains[None]
    )
    normed = normed.astype(jnp.bfloat16)
    height = gate_input.shape[0]
    col_width = gate_input.shape[2]
    shards = lax.axis_size("tok")
    full_width = col_width * shards
    channels_here = head_count * head_size
    frame_grid = normed.reshape(height, full_width, channels_here)
    own_taps = lax.dynamic_slice_in_dim(
        conv_weights, lax.axis_index("head") * channels_here, channels_here, 2
    )
    padded = jnp.pad(frame_grid, ((1, 1), (1, 1), (0, 0)))
    local_sum = jnp.zeros((height, full_width, channels_here), jnp.float32)
    for row_tap in range(3):
        for col_tap in range(3):
            local_sum = local_sum + own_taps[row_tap, col_tap] * padded[
                row_tap : row_tap + height, col_tap : col_tap + full_width
            ].astype(jnp.float32)
    outgoing = local_sum.astype(jnp.bfloat16).reshape(height, shards, col_width, channels_here)
    arrived = lax.all_to_all(outgoing, "tok", split_axis=1, concat_axis=1, tiled=True)
    frame_count = frame_order.shape[0]
    numbers = jnp.arange(frame_count, dtype=jnp.int32)
    inverse = jnp.sum(
        jnp.where(frame_order[None, :] == numbers[:, None], numbers[None, :], 0), axis=1
    )
    ordered = jnp.take(arrived, inverse, axis=1)
    tile_block = lax.all_to_all(ordered, "head", split_axis=1, concat_axis=3, tiled=True)
    return (tile_block.astype(jnp.float32) * jax.nn.silu(gate_input.astype(jnp.float32))).astype(
        jnp.bfloat16
    )


def local(queries, keys, values, rates, fast_weights, norm_gain, frame_order, gate_input, conv_weights):
    args = (
        queries, keys, values, rates, fast_weights, norm_gain, frame_order, gate_input, conv_weights
    )
    if fits_by_heads(queries, gate_input, frame_order):
        return by_heads(*args)
    return by_tokens(*args)


def solution(mesh):
    in_specs = (
        P(("groups", "tok"), "tile", "head", None),
        P(("groups", "tok"), "tile", "head", None),
        P(("groups", "tok"), "tile", "head", None),
        P("tile", "head", ("groups", "tok")),
        P("tile", "head", None, None, None),
        P("tile", "head", None),
        P("groups"),
        P(None, ("groups", "head"), "tok", "tile"),
        P(None, None, "tile"),
    )
    out_specs = P(None, ("groups", "head"), "tok", "tile")
    return jax.shard_map(local, mesh=mesh, in_specs=in_specs, out_specs=out_specs, check_vma=False)
```

```python
import functools

import jax
import jax.numpy as jnp
from jax import lax
from jax.experimental import pallas as pl
from jax.experimental.pallas import tpu as pltpu
from jax.sharding import PartitionSpec as P

epsilon = 1e-06
LANES = 128
VMEM_BYTES = 56 * 1024 * 1024


def split_lanes(source, scratch, rows, head_size):
    full = head_size // LANES
    tail = head_size - full * LANES
    wide = source.reshape(rows, head_size).astype(jnp.float32)
    for tile in range(full):
        scratch[tile] = wide[:, tile * LANES : (tile + 1) * LANES]
    scratch[full, :, 0:tail] = wide[:, full * LANES :]


def join_halves(first, second, tail):
    lane = lax.broadcasted_iota(jnp.int32, first[-1].shape, 1)
    middle = jnp.where(lane < tail, first[-1], pltpu.roll(second[-1], tail, 1))
    return first[:-1] + [middle] + second[:-1]


def part_halves(packed, head_size):
    full = head_size // LANES
    tail = head_size - full * LANES
    first = packed[:, :head_size]
    middle = packed[:, head_size : (full + 1) * LANES]
    second = jnp.concatenate([packed[:, (full + 1) * LANES :], middle], axis=1)
    return first, second


def partner_head(partner):
    return lax.axis_index("tok") ^ partner


def pack_pairs(head, rate_ref, key_tiles, value_tiles, out_ref, start, head_size):
    heads, tok_rows = rate_ref.shape
    half = tok_rows // 2
    full = head_size // LANES
    tail = head_size - full * LANES
    rate_row = -rate_ref[pl.ds(head, 1), :]
    rates = jnp.broadcast_to(rate_row, (LANES, tok_rows)).T
    for row, tiles in ((start, key_tiles), (start + half, value_tiles)):
        sides = []
        for side in range(2):
            parts = [
                tiles[tile, pl.ds(side * half * heads + head, half, stride=heads), :]
                for tile in range(full + 1)
            ]
            if tiles is value_tiles:
                rate = rates[side * half : (side + 1) * half]
                parts = [rate * part for part in parts]
            sides.append(parts)
        for tile, part in enumerate(join_halves(sides[0], sides[1], tail)):
            out_ref[row : row + half, tile * LANES : (tile + 1) * LANES] = part.astype(jnp.bfloat16)


def pack_query(head, heads, height, query_tiles, out_ref, start, head_size):
    tok_rows = query_tiles.shape[1] // heads
    half = tok_rows // 2
    width = tok_rows // height
    full = head_size // LANES
    tail = head_size - full * LANES
    sides = []
    for side in range(2):
        sides.append(
            [
                jnp.concatenate(
                    [
                        query_tiles[
                            tile, pl.ds(column * heads + head, height, stride=width * heads), :
                        ]
                        for column in range(side * width // 2, (side + 1) * width // 2)
                    ],
                    axis=0,
                )
                for tile in range(full + 1)
            ]
        )
    for tile, part in enumerate(join_halves(sides[0], sides[1], tail)):
        out_ref[start : start + half, tile * LANES : (tile + 1) * LANES] = part.astype(jnp.bfloat16)


def pack_mirror_kernel(key_ref, value_ref, rate_ref, *rest):
    outs, (key_tiles, value_tiles) = rest[:-2], rest[-2:]
    tok_rows, heads, head_size = key_ref.shape
    split_lanes(key_ref[...], key_tiles, tok_rows * heads, head_size)
    split_lanes(value_ref[...], value_tiles, tok_rows * heads, head_size)
    for partner, out_ref in enumerate(outs):
        head = partner_head(partner ^ (heads // 2))
        pack_pairs(head, rate_ref, key_tiles, value_tiles, out_ref, 0, head_size)


def pack_across_kernel(height, query_ref, *rest):
    outs, query_tiles = rest[:-1], rest[-1]
    tok_rows, heads, head_size = query_ref.shape
    half = tok_rows // 2
    split_lanes(query_ref[...], query_tiles, tok_rows * heads, head_size)
    for partner in range(heads // 2):
        head = partner_head(partner ^ (heads // 2))
        start = partner % 2 * half
        pack_query(head, heads, height, query_tiles, outs[partner // 2], start, head_size)


def pack_near_kernel(height, key_ref, value_ref, rate_ref, query_ref, ahead_ref, *rest):
    outs, (key_tiles, value_tiles, query_tiles) = rest[:-3], rest[-3:]
    tok_rows, heads, head_size = key_ref.shape
    split_lanes(key_ref[...], key_tiles, tok_rows * heads, head_size)
    split_lanes(value_ref[...], value_tiles, tok_rows * heads, head_size)
    split_lanes(query_ref[...], query_tiles, tok_rows * heads, head_size)
    for partner, out_ref in enumerate(outs):
        head = partner_head(partner)
        pack_pairs(head, rate_ref, key_tiles, value_tiles, out_ref, 0, head_size)
        pack_query(head, heads, height, query_tiles, out_ref, tok_rows, head_size)


def relay(landed):
    return [part for one in landed for part in (one, send(one, 1))]


def send(part, partner):
    pairs = [(place, place ^ partner) for place in range(lax.axis_size("tok"))]
    return lax.ppermute(part, "tok", pairs)


def contract(first, second, dims):
    return lax.dot_general(first, second, (dims, ((), ())), preferred_element_type=jnp.float32)


NN = ((1,), (0,))
NT = ((1,), (1,))


def add_gradients(pair_refs, tok_rows, weight_ref, hidden, grad_ref):
    half = tok_rows // 2
    head_size = weight_ref.shape[-1]
    first_weight = weight_ref[0, hidden]
    third_weight = weight_ref[1, hidden]
    down_turned = weight_ref[2].astype(jnp.float32).T[hidden].astype(jnp.bfloat16)
    step = 2 if len(pair_refs) % 2 == 0 else 1
    for start in range(0, len(pair_refs), step):
        key_parts, target_parts = [], []
        for pair_ref in pair_refs[start : start + step]:
            key_parts.extend(part_halves(pair_ref[0:half, :], head_size))
            target_parts.extend(part_halves(pair_ref[half:tok_rows, :], head_size))
        key_rows = jnp.concatenate(key_parts, axis=0)
        target = jnp.concatenate(target_parts, axis=0)
        first_pre = contract(first_weight, key_rows, NT)
        third_pre = contract(third_weight, key_rows, NT)
        hidden_grad = contract(down_turned, target, NT)
        sigmoid_first = jax.nn.sigmoid(first_pre)
        activated = first_pre * sigmoid_first
        mixed = (activated * third_pre).astype(jnp.bfloat16)
        grad_first_in = (
            hidden_grad * third_pre * sigmoid_first * (1.0 + first_pre * (1.0 - sigmoid_first))
        ).astype(jnp.bfloat16)
        grad_third_in = (hidden_grad * activated).astype(jnp.bfloat16)
        grads = (
            contract(grad_first_in, key_rows, NN),
            contract(grad_third_in, key_rows, NN),
            contract(mixed, target, NN),
        )
        for index, grad in enumerate(grads):
            if start == 0:
                grad_ref[index, :, 0:head_size] = grad
            else:
                grad_ref[index, :, 0:head_size] += grad


def mirror_kernel(count, tok_rows, first, *refs):
    pair_refs, (weight_ref, out_ref, grad_ref) = refs[:count], refs[-3:]
    head_size = weight_ref.shape[-1]
    full = head_size // LANES
    tail = head_size - full * LANES
    units = grad_ref.shape[1]
    half = units // 2
    add_gradients(pair_refs, tok_rows, weight_ref, slice(first, first + units), grad_ref)

    def tiles_of(index, rows):
        return [
            grad_ref[index, rows, tile * LANES : (tile + 1) * LANES] for tile in range(full + 1)
        ]

    both = join_halves(tiles_of(0, slice(0, units)), tiles_of(1, slice(0, units)), tail)
    down = join_halves(tiles_of(2, slice(0, half)), tiles_of(2, slice(half, units)), tail)
    for tile, (above, below) in enumerate(zip(both, down)):
        lanes = slice(tile * LANES, (tile + 1) * LANES)
        out_ref[0:units, lanes] = above.astype(jnp.bfloat16)
        out_ref[units : units + half, lanes] = below.astype(jnp.bfloat16)


def own_kernel(tok_rows, *refs):
    pair_refs, (weight_ref, out_ref) = refs[:-2], refs[-2:]
    add_gradients(pair_refs, tok_rows, weight_ref, slice(0, weight_ref.shape[-1]), out_ref)


def renorm(weight_ref, grad_ref, mirror_refs, out_ref):
    head_size = weight_ref.shape[-1]
    units = head_size // len(mirror_refs)
    firsts, thirds, downs = [], [], []
    for mirror_ref in mirror_refs:
        first, third = part_halves(mirror_ref[0:units, :], head_size)
        firsts.append(first)
        thirds.append(third)
        downs.extend(part_halves(mirror_ref[units:, :], head_size))
    first, third, down = (jnp.concatenate(parts, axis=0) for parts in (firsts, thirds, downs))
    for index, other in enumerate((first, third, down)):
        before = weight_ref[index].astype(jnp.float32)
        axis = 1
        if index == 2:
            before = before.T
            axis = 0
        grad = grad_ref[index, :, 0:head_size] + other.astype(jnp.float32)
        updated = before - grad
        scale_old = jnp.sqrt(jnp.mean(before * before, axis=axis, keepdims=True) + epsilon)
        scale_new = jnp.sqrt(jnp.mean(updated * updated, axis=axis, keepdims=True) + epsilon)
        out_ref[index] = (updated * (scale_old / scale_new)).astype(jnp.bfloat16)


def apply_kernel(height, frames_here, shards, order_ref, *refs):
    near_refs, far_refs = refs[: shards // 2], refs[shards // 2 : shards]
    before_ref, grad_ref, *mirror_refs = refs[shards:-6]
    gain_ref, tap_ref, out_ref = refs[-6:-3]
    weight_ref, grid_ref, turned_ref = refs[-3:]
    half = far_refs[0].shape[0] // 2
    query_parts = [ref[ref.shape[0] - half :, :] for ref in near_refs]
    for index, ref in enumerate(far_refs):
        query_parts.append(ref[index % 2 * half : (index % 2 + 1) * half, :])
    renorm(before_ref, grad_ref, mirror_refs, weight_ref)
    width = 2 * half // height
    head_size = weight_ref.shape[-1]
    full = head_size // LANES
    tail = head_size - full * LANES
    top = 8
    edge = jnp.zeros((top, LANES), jnp.float32)
    whole = jnp.zeros(grid_ref.shape[3:], jnp.float32)
    for shard in range(shards):
        for tile in range(full + 1):
            grid_ref[shard, tile, 0] = whole
            grid_ref[shard, tile, width + 1] = whole
            for column in range(1, width + 1):
                grid_ref[shard, tile, column, 0:top] = edge
                grid_ref[shard, tile, column, top + height :] = edge
    gain = gain_ref[...]
    for shard in range(shards):
        rows = jnp.concatenate(part_halves(query_parts[shard], head_size), axis=0)
        proj_first = contract(rows, weight_ref[0], NT)
        proj_third = contract(rows, weight_ref[1], NT)
        mixed = (proj_first * jax.nn.sigmoid(proj_first) * proj_third).astype(jnp.bfloat16)
        outputs = contract(mixed, weight_ref[2], NN)
        scale = lax.rsqrt(jnp.mean(outputs * outputs, axis=-1, keepdims=True) + epsilon)
        normed = (outputs * scale * gain).astype(jnp.bfloat16).astype(jnp.float32)
        frame = order_ref[shard]
        block = frame // frames_here
        slot = frame % frames_here
        for tile in range(full + 1):
            lanes = slice(tile * LANES, min((tile + 1) * LANES, head_size))
            for column in range(width):
                grid_ref[shard, tile, column + 1, top : top + height, 0 : lanes.stop - lanes.start] = (
                    normed[column * height : (column + 1) * height, lanes]
                )
            taps = [
                tap_ref[index : index + 1, tile * LANES : (tile + 1) * LANES] for index in range(9)
            ]
            for column in range(width):
                total = None
                for row_tap in range(3):
                    first = top + row_tap - 1
                    for col_tap in range(3):
                        term = taps[row_tap * 3 + col_tap] * grid_ref[
                            shard, tile, column + col_tap, first : first + height, :
                        ]
                        total = term if total is None else total + term
                turned_ref[
                    block, column, tile, pl.ds(slot, height, stride=frames_here), :
                ] = total
    blocks = turned_ref.shape[0]
    side_rows = out_ref.shape[1]
    for block in range(blocks):
        for column in range(width):
            sides = [
                [
                    turned_ref[block, column, tile, side * side_rows : (side + 1) * side_rows, :]
                    for tile in range(full + 1)
                ]
                for side in range(2)
            ]
            for tile, part in enumerate(join_halves(sides[0], sides[1], tail)):
                out_ref[column * blocks + block, :, tile * LANES : (tile + 1) * LANES] = part.astype(
                    jnp.bfloat16
                )


def gate_kernel(blocks, conv_ref, gate_ref, out_ref):
    chunks, side_rows, _ = conv_ref.shape
    height, frames_here, channels = gate_ref.shape
    head_size = channels // chunks
    shards = chunks // blocks
    rows_here = height // 2
    for pair in range(chunks // 2):
        lanes = slice(pair * 2 * head_size, (pair + 1) * 2 * head_size)
        halves = []
        for head in (2 * pair, 2 * pair + 1):
            chunk = (head % shards) * blocks + head // shards
            halves.append(part_halves(conv_ref[chunk].astype(jnp.float32), head_size))
        for side in range(2):
            conv = jnp.concatenate([halves[0][side], halves[1][side]], axis=1)
            gate = gate_ref[side * rows_here : (side + 1) * rows_here, :, lanes].astype(jnp.float32)
            conv = conv.reshape(rows_here, frames_here, 2 * head_size)
            out_ref[side * rows_here : (side + 1) * rows_here, :, lanes] = (
                conv * (gate * jax.nn.sigmoid(gate))
            ).astype(jnp.bfloat16)


def in_vmem(count):
    return [pl.BlockSpec(memory_space=pltpu.VMEM)] * count


def call(kernel, out, operands, scratch=(), specs=None):
    return pl.pallas_call(
        kernel,
        out_shape=out,
        in_specs=specs or in_vmem(len(operands)),
        out_specs=jax.tree.map(lambda _: pl.BlockSpec(memory_space=pltpu.VMEM), out),
        scratch_shapes=scratch,
        compiler_params=pltpu.CompilerParams(vmem_limit_bytes=VMEM_BYTES),
        cost_estimate=pl.CostEstimate(flops=0, bytes_accessed=0, transcendentals=0),
    )(*operands)


def after(part, *earlier):
    anywhere = pl.BlockSpec(memory_space=pl.ANY)
    return pl.pallas_call(
        lambda *refs: None,
        out_shape=jax.ShapeDtypeStruct(part.shape, part.dtype),
        in_specs=[anywhere] * (1 + len(earlier)),
        out_specs=anywhere,
        input_output_aliases={0: 0},
        cost_estimate=pl.CostEstimate(flops=0, bytes_accessed=0, transcendentals=0),
    )(part, *earlier)


def by_heads(
    queries, keys, values, rates, fast_weights, norm_gain, frame_order, gate_input, conv_weights
):
    tok_rows = queries.shape[0]
    head_count = queries.shape[1] * queries.shape[2]
    head_size = queries.shape[3]
    height, frames_here = gate_input.shape[:2]
    shards = lax.axis_size("tok")
    blocks = lax.axis_size("head")
    half = tok_rows // 2
    wide = 2 * head_size
    tiles = head_size // LANES + 1
    own = lax.axis_index("tok")
    own_channel = lax.axis_index("head") * head_count + own

    def rows_of(array):
        return array.reshape(tok_rows, head_count, head_size)

    def own_of(array, place):
        return lax.dynamic_index_in_dim(array, place, 0, keepdims=False)

    line = shards // 2
    tile_scratch = pltpu.VMEM((tiles, tok_rows * head_count, LANES), jnp.float32)
    token_rates = rates.reshape(head_count, tok_rows)
    chips = line // 2

    one = jax.ShapeDtypeStruct((tok_rows, wide), jnp.bfloat16)
    mirrored = call(
        pack_mirror_kernel,
        [one] * line,
        (rows_of(keys), rows_of(values), token_rates),
        (tile_scratch, tile_scratch),
    )
    mirrored = [mirrored[0]] + [send(mirrored[k], k) for k in range(1, line)]
    across = call(
        functools.partial(pack_across_kernel, height),
        [one] * chips,
        (rows_of(queries),),
        (tile_scratch,),
    )
    across_landed = [send(part, line + 2 * index) for index, part in enumerate(across)]
    packed = call(
        functools.partial(pack_near_kernel, height),
        [jax.ShapeDtypeStruct((tok_rows + half, wide), jnp.bfloat16)] * line,
        (rows_of(keys), rows_of(values), token_rates, rows_of(queries), across[0]),
        (tile_scratch, tile_scratch, tile_scratch),
        specs=in_vmem(4) + [pl.BlockSpec(memory_space=pl.ANY)],
    )
    held = [after(part, *mirrored[1:], *across_landed) for part in packed[1:]]
    near = [packed[0]] + [send(held[k - 1], k) for k in range(1, line)]
    weights = fast_weights.reshape(head_count, 3, head_size, head_size)
    own_weights = own_of(weights, own)
    own_gain = own_of(norm_gain.reshape(head_count, 1, head_size), own)
    taps = conv_weights.reshape(9, blocks * head_count, head_size)
    own_taps = lax.dynamic_index_in_dim(taps, own_channel, 1, keepdims=False)
    own_taps = jnp.pad(own_taps, ((0, 0), (0, tiles * LANES - head_size)))
    frames = frame_order[own ^ jnp.arange(shards, dtype=jnp.int32)]
    grad_shape = (3, head_size, tiles * LANES)
    ahead = (*across_landed, *held)
    mirror_weights = own_of(weights, own ^ line)
    units = head_size // 2
    crossed = []
    for first in range(0, head_size, units):
        part = call(
            functools.partial(mirror_kernel, line, tok_rows, first),
            jax.ShapeDtypeStruct((units + units // 2, wide), jnp.bfloat16),
            (*mirrored, *ahead, mirror_weights),
            (pltpu.VMEM((3, units, tiles * LANES), jnp.float32),),
            specs=in_vmem(line) + [pl.BlockSpec(memory_space=pl.ANY)] * len(ahead) + in_vmem(1),
        )
        crossed.append(send(part, line))
    gradients = call(
        functools.partial(own_kernel, tok_rows),
        jax.ShapeDtypeStruct(grad_shape, jnp.float32),
        (*near, own_weights),
    )
    across = relay([after(part, gradients) for part in across_landed])
    side_rows = frames_here * height // 2
    outgoing = call(
        functools.partial(apply_kernel, height, frames_here, shards),
        jax.ShapeDtypeStruct((shards * blocks, side_rows, wide), jnp.bfloat16),
        (frames, *near, *across, own_weights, gradients, *crossed, own_gain, own_taps),
        (
            pltpu.VMEM((3, head_size, head_size), jnp.bfloat16),
            pltpu.VMEM((shards, tiles, shards + 2, height + 16, LANES), jnp.float32),
            pltpu.VMEM((blocks, shards, tiles, 2 * side_rows, LANES), jnp.float32),
        ),
        specs=[pl.BlockSpec(memory_space=pltpu.SMEM)] + in_vmem(shards + 6),
    )
    arrived = lax.all_to_all(outgoing, ("tok", "head"), split_axis=0, concat_axis=0, tiled=True)
    gate = gate_input.reshape(height, frames_here, gate_input.shape[3])
    gated = call(
        functools.partial(gate_kernel, blocks),
        jax.ShapeDtypeStruct(gate.shape, jnp.bfloat16),
        (arrived, gate),
    )
    return gated.reshape(gate_input.shape)


def fits_by_heads(queries, gate_input, frame_order):
    tok_rows, head_size = queries.shape[0], queries.shape[3]
    head_count = queries.shape[1] * queries.shape[2]
    height, frames_here, col_width = gate_input.shape[:3]
    shards = lax.axis_size("tok")
    return (
        head_count == shards
        and frame_order.shape[0] == shards
        and lax.axis_size("tile") == 1
        and col_width == 1
        and shards % 2 == 0
        and shards & (shards - 1) == 0
        and head_size % LANES == LANES // 2
        and height % 8 == 0
        and tok_rows == height * shards
        and tok_rows % 32 == 0
        and head_size % 64 == 0
        and frames_here * height % 32 == 0
        and frames_here * lax.axis_size("head") == shards
        and lax.axis_size("head") & (lax.axis_size("head") - 1) == 0
    )


def renormed(previous, gradient):
    before = previous.astype(jnp.float32)
    updated = before - gradient
    scale_old = jnp.sqrt(jnp.mean(before * before, axis=-1, keepdims=True) + epsilon)
    scale_new = jnp.sqrt(jnp.mean(updated * updated, axis=-1, keepdims=True) + epsilon)
    return (updated * (scale_old / scale_new)).astype(jnp.bfloat16)


def by_tokens(
    queries, keys, values, rates, fast_weights, norm_gain, frame_order, gate_input, conv_weights
):
    tok_rows = queries.shape[0]
    head_count = queries.shape[1] * queries.shape[2]
    head_size = queries.shape[3]
    query_rows = queries.reshape(tok_rows, head_count, head_size)
    key_rows = keys.reshape(tok_rows, head_count, head_size)
    value_rows = values.reshape(tok_rows, head_count, head_size)
    token_rates = rates.reshape(head_count, tok_rows)
    weights = fast_weights.reshape(head_count, 3, head_size, head_size)
    head_gains = norm_gain.reshape(head_count, head_size)
    first_pre = jnp.einsum(
        "thd,hfd->htf", key_rows, weights[:, 0], preferred_element_type=jnp.float32
    )
    third_pre = jnp.einsum(
        "thd,hfd->htf", key_rows, weights[:, 1], preferred_element_type=jnp.float32
    )
    sigmoid_first = jax.nn.sigmoid(first_pre)
    activated = first_pre * sigmoid_first
    hidden = (activated * third_pre).astype(jnp.bfloat16)
    target = (-token_rates.T[:, :, None] * value_rows.astype(jnp.float32)).astype(jnp.bfloat16)
    grad_down = jnp.einsum("thd,htf->hdf", target, hidden, preferred_element_type=jnp.float32)
    hidden_grad = jnp.einsum(
        "thd,hdf->htf", target, weights[:, 2], preferred_element_type=jnp.float32
    )
    grad_first_in = (
        hidden_grad * third_pre * sigmoid_first * (1.0 + first_pre * (1.0 - sigmoid_first))
    ).astype(jnp.bfloat16)
    grad_third_in = (hidden_grad * activated).astype(jnp.bfloat16)
    grad_first = jnp.einsum(
        "htf,thd->hfd", grad_first_in, key_rows, preferred_element_type=jnp.float32
    )
    grad_third = jnp.einsum(
        "htf,thd->hfd", grad_third_in, key_rows, preferred_element_type=jnp.float32
    )
    gradients = jnp.stack([grad_first, grad_third, grad_down], axis=1)
    row_share = lax.psum_scatter(gradients, "tok", scatter_dimension=2, tiled=True)
    row_count = row_share.shape[2]
    own_rows = lax.dynamic_slice_in_dim(weights, lax.axis_index("tok") * row_count, row_count, 2)
    updated = lax.all_gather(renormed(own_rows, row_share), "tok", axis=2, tiled=True)
    proj_first = jnp.einsum(
        "thd,hfd->thf", query_rows, updated[:, 0], preferred_element_type=jnp.float32
    )
    proj_third = jnp.einsum(
        "thd,hfd->thf", query_rows, updated[:, 1], preferred_element_type=jnp.float32
    )
    mixed_hidden = (jax.nn.silu(proj_first) * proj_third).astype(jnp.bfloat16)
    outputs = jnp.einsum(
        "thf,hdf->thd", mixed_hidden, updated[:, 2], preferred_element_type=jnp.float32
    )
    normed = (
        outputs
        * lax.rsqrt(jnp.mean(outputs * outputs, axis=-1, keepdims=True) + epsilon)
        * head_gains[None]
    )
    normed = normed.astype(jnp.bfloat16)
    height = gate_input.shape[0]
    col_width = gate_input.shape[2]
    shards = lax.axis_size("tok")
    full_width = col_width * shards
    channels_here = head_count * head_size
    frame_grid = normed.reshape(height, full_width, channels_here)
    own_taps = lax.dynamic_slice_in_dim(
        conv_weights, lax.axis_index("head") * channels_here, channels_here, 2
    )
    padded = jnp.pad(frame_grid, ((1, 1), (1, 1), (0, 0)))
    local_sum = jnp.zeros((height, full_width, channels_here), jnp.float32)
    for row_tap in range(3):
        for col_tap in range(3):
            local_sum = local_sum + own_taps[row_tap, col_tap] * padded[
                row_tap : row_tap + height, col_tap : col_tap + full_width
            ].astype(jnp.float32)
    outgoing = local_sum.astype(jnp.bfloat16).reshape(height, shards, col_width, channels_here)
    arrived = lax.all_to_all(outgoing, "tok", split_axis=1, concat_axis=1, tiled=True)
    frame_count = frame_order.shape[0]
    numbers = jnp.arange(frame_count, dtype=jnp.int32)
    inverse = jnp.sum(
        jnp.where(frame_order[None, :] == numbers[:, None], numbers[None, :], 0), axis=1
    )
    ordered = jnp.take(arrived, inverse, axis=1)
    tile_block = lax.all_to_all(ordered, "head", split_axis=1, concat_axis=3, tiled=True)
    return (tile_block.astype(jnp.float32) * jax.nn.silu(gate_input.astype(jnp.float32))).astype(
        jnp.bfloat16
    )


def local(queries, keys, values, rates, fast_weights, norm_gain, frame_order, gate_input, conv_weights):
    args = (
        queries, keys, values, rates, fast_weights, norm_gain, frame_order, gate_input, conv_weights
    )
    if fits_by_heads(queries, gate_input, frame_order):
        return by_heads(*args)
    return by_tokens(*args)


def solution(mesh):
    in_specs = (
        P(("groups", "tok"), "tile", "head", None),
        P(("groups", "tok"), "tile", "head", None),
        P(("groups", "tok"), "tile", "head", None),
        P("tile", "head", ("groups", "tok")),
        P("tile", "head", None, None, None),
        P("tile", "head", None),
        P("groups"),
        P(None, ("groups", "head"), "tok", "tile"),
        P(None, None, "tile"),
    )
    out_specs = P(None, ("groups", "head"), "tok", "tile")
    return jax.shard_map(local, mesh=mesh, in_specs=in_specs, out_specs=out_specs, check_vma=False)
```

```python
import functools

import jax
import jax.numpy as jnp
from jax import lax
from jax.experimental import pallas as pl
from jax.experimental.pallas import tpu as pltpu
from jax.sharding import PartitionSpec as P

epsilon = 1e-06
LANES = 128
VMEM_BYTES = 56 * 1024 * 1024


def split_lanes(source, scratch, rows, head_size):
    full = head_size // LANES
    tail = head_size - full * LANES
    wide = source.reshape(rows, head_size).astype(jnp.float32)
    for tile in range(full):
        scratch[tile] = wide[:, tile * LANES : (tile + 1) * LANES]
    scratch[full, :, 0:tail] = wide[:, full * LANES :]


def join_halves(first, second, tail):
    lane = lax.broadcasted_iota(jnp.int32, first[-1].shape, 1)
    middle = jnp.where(lane < tail, first[-1], pltpu.roll(second[-1], tail, 1))
    return first[:-1] + [middle] + second[:-1]


def part_halves(packed, head_size):
    full = head_size // LANES
    tail = head_size - full * LANES
    first = packed[:, :head_size]
    middle = packed[:, head_size : (full + 1) * LANES]
    second = jnp.concatenate([packed[:, (full + 1) * LANES :], middle], axis=1)
    return first, second


def partner_head(partner):
    return lax.axis_index("tok") ^ partner


def pack_pairs(head, rate_ref, key_tiles, value_tiles, out_ref, start, head_size):
    heads, tok_rows = rate_ref.shape
    half = tok_rows // 2
    full = head_size // LANES
    tail = head_size - full * LANES
    rate_row = -rate_ref[pl.ds(head, 1), :]
    rates = jnp.broadcast_to(rate_row, (LANES, tok_rows)).T
    for row, tiles in ((start, key_tiles), (start + half, value_tiles)):
        sides = []
        for side in range(2):
            parts = [
                tiles[tile, pl.ds(side * half * heads + head, half, stride=heads), :]
                for tile in range(full + 1)
            ]
            if tiles is value_tiles:
                rate = rates[side * half : (side + 1) * half]
                parts = [rate * part for part in parts]
            sides.append(parts)
        for tile, part in enumerate(join_halves(sides[0], sides[1], tail)):
            out_ref[row : row + half, tile * LANES : (tile + 1) * LANES] = part.astype(jnp.bfloat16)


def pack_query(head, heads, height, query_tiles, out_ref, start, head_size):
    tok_rows = query_tiles.shape[1] // heads
    half = tok_rows // 2
    width = tok_rows // height
    full = head_size // LANES
    tail = head_size - full * LANES
    sides = []
    for side in range(2):
        sides.append(
            [
                jnp.concatenate(
                    [
                        query_tiles[
                            tile, pl.ds(column * heads + head, height, stride=width * heads), :
                        ]
                        for column in range(side * width // 2, (side + 1) * width // 2)
                    ],
                    axis=0,
                )
                for tile in range(full + 1)
            ]
        )
    for tile, part in enumerate(join_halves(sides[0], sides[1], tail)):
        out_ref[start : start + half, tile * LANES : (tile + 1) * LANES] = part.astype(jnp.bfloat16)


def pack_mirror_kernel(key_ref, value_ref, rate_ref, *rest):
    outs, (key_tiles, value_tiles) = rest[:-2], rest[-2:]
    tok_rows, heads, head_size = key_ref.shape
    split_lanes(key_ref[...], key_tiles, tok_rows * heads, head_size)
    split_lanes(value_ref[...], value_tiles, tok_rows * heads, head_size)
    for partner, out_ref in enumerate(outs):
        head = partner_head(partner ^ (heads // 2))
        pack_pairs(head, rate_ref, key_tiles, value_tiles, out_ref, 0, head_size)


def pack_across_kernel(height, query_ref, *rest):
    outs, query_tiles = rest[:-1], rest[-1]
    tok_rows, heads, head_size = query_ref.shape
    half = tok_rows // 2
    split_lanes(query_ref[...], query_tiles, tok_rows * heads, head_size)
    for partner in range(heads // 2):
        head = partner_head(partner ^ (heads // 2))
        start = partner % 2 * half
        pack_query(head, heads, height, query_tiles, outs[partner // 2], start, head_size)


def pack_near_kernel(height, key_ref, value_ref, rate_ref, query_ref, *rest):
    outs, (key_tiles, value_tiles, query_tiles) = rest[2:-3], rest[-3:]
    tok_rows, heads, head_size = key_ref.shape
    split_lanes(key_ref[...], key_tiles, tok_rows * heads, head_size)
    split_lanes(value_ref[...], value_tiles, tok_rows * heads, head_size)
    split_lanes(query_ref[...], query_tiles, tok_rows * heads, head_size)
    for partner, out_ref in enumerate(outs):
        head = partner_head(partner)
        pack_pairs(head, rate_ref, key_tiles, value_tiles, out_ref, 0, head_size)
        pack_query(head, heads, height, query_tiles, out_ref, tok_rows, head_size)


def relay(landed):
    return [part for one in landed for part in (one, send(one, 1))]


def send(part, partner):
    pairs = [(place, place ^ partner) for place in range(lax.axis_size("tok"))]
    return lax.ppermute(part, "tok", pairs)


def sigmoid(value):
    return 0.5 + 0.5 * jnp.tanh(0.5 * value)


def contract(first, second, dims):
    return lax.dot_general(first, second, (dims, ((), ())), preferred_element_type=jnp.float32)


NN = ((1,), (0,))
NT = ((1,), (1,))


def add_gradients(pair_refs, tok_rows, weight_ref, hidden, grad_ref):
    half = tok_rows // 2
    head_size = weight_ref.shape[-1]
    first_weight = weight_ref[0, hidden]
    third_weight = weight_ref[1, hidden]
    down_turned = weight_ref[2].astype(jnp.float32).T[hidden].astype(jnp.bfloat16)
    step = 2 if len(pair_refs) % 2 == 0 else 1
    for start in range(0, len(pair_refs), step):
        key_parts, target_parts = [], []
        for pair_ref in pair_refs[start : start + step]:
            key_parts.extend(part_halves(pair_ref[0:half, :], head_size))
            target_parts.extend(part_halves(pair_ref[half:tok_rows, :], head_size))
        key_rows = jnp.concatenate(key_parts, axis=0)
        target = jnp.concatenate(target_parts, axis=0)
        first_pre = contract(first_weight, key_rows, NT)
        third_pre = contract(third_weight, key_rows, NT)
        hidden_grad = contract(down_turned, target, NT)
        sigmoid_first = sigmoid(first_pre)
        activated = first_pre * sigmoid_first
        mixed = (activated * third_pre).astype(jnp.bfloat16)
        grad_first_in = (
            hidden_grad * third_pre * sigmoid_first * (1.0 + first_pre * (1.0 - sigmoid_first))
        ).astype(jnp.bfloat16)
        grad_third_in = (hidden_grad * activated).astype(jnp.bfloat16)
        grads = (
            contract(grad_first_in, key_rows, NN),
            contract(grad_third_in, key_rows, NN),
            contract(mixed, target, NN),
        )
        for index, grad in enumerate(grads):
            if start == 0:
                grad_ref[index, :, 0:head_size] = grad
            else:
                grad_ref[index, :, 0:head_size] += grad


def mirror_kernel(count, tok_rows, first, *refs):
    pair_refs, (weight_ref, out_ref, grad_ref) = refs[:count], refs[-3:]
    head_size = weight_ref.shape[-1]
    full = head_size // LANES
    tail = head_size - full * LANES
    units = grad_ref.shape[1]
    half = units // 2
    add_gradients(pair_refs, tok_rows, weight_ref, slice(first, first + units), grad_ref)

    def tiles_of(index, rows):
        return [
            grad_ref[index, rows, tile * LANES : (tile + 1) * LANES] for tile in range(full + 1)
        ]

    both = join_halves(tiles_of(0, slice(0, units)), tiles_of(1, slice(0, units)), tail)
    down = join_halves(tiles_of(2, slice(0, half)), tiles_of(2, slice(half, units)), tail)
    for tile, (above, below) in enumerate(zip(both, down)):
        lanes = slice(tile * LANES, (tile + 1) * LANES)
        out_ref[0:units, lanes] = above.astype(jnp.bfloat16)
        out_ref[units : units + half, lanes] = below.astype(jnp.bfloat16)


def own_kernel(tok_rows, *refs):
    pair_refs, (weight_ref, out_ref) = refs[:-2], refs[-2:]
    add_gradients(pair_refs, tok_rows, weight_ref, slice(0, weight_ref.shape[-1]), out_ref)


def renorm(weight_ref, grad_ref, mirror_ref, out_ref):
    head_size = weight_ref.shape[-1]
    units = head_size // mirror_ref.shape[0]
    firsts, thirds, downs = [], [], []
    for part in range(mirror_ref.shape[0]):
        first, third = part_halves(mirror_ref[part, 0:units, :], head_size)
        firsts.append(first)
        thirds.append(third)
        downs.extend(part_halves(mirror_ref[part, units:, :], head_size))
    first, third, down = (jnp.concatenate(parts, axis=0) for parts in (firsts, thirds, downs))
    whole = head_size // LANES * LANES
    out_ref[2, :, whole:] = jnp.zeros((head_size, out_ref.shape[2] - whole), jnp.bfloat16)
    for index, other in enumerate((first, third, down)):
        before = weight_ref[index].astype(jnp.float32)
        axis = 1
        if index == 2:
            before = before.T
            axis = 0
        grad = grad_ref[index, :, 0:head_size] + other.astype(jnp.float32)
        updated = before - grad
        scale_old = jnp.sqrt(jnp.mean(before * before, axis=axis, keepdims=True) + epsilon)
        scale_new = jnp.sqrt(jnp.mean(updated * updated, axis=axis, keepdims=True) + epsilon)
        out_ref[index, :, 0:head_size] = (updated * (scale_old / scale_new)).astype(jnp.bfloat16)


def apply_kernel(height, frames_here, shards, order_ref, *refs):
    near_refs, far_refs = refs[: shards // 2], refs[shards // 2 : shards]
    before_any, grad_any, *mirror_any = refs[shards:-10]
    gain_ref, tap_ref, out_ref = refs[-10:-7]
    query_ref, before_ref, grad_ref, mirror_ref, weight_ref, turned_ref, sems = refs[-7:]
    half = query_ref.shape[1]
    width = 2 * half // height
    head_size = before_ref.shape[-1]
    full = head_size // LANES
    tail = head_size - full * LANES

    sources = [(before_any, before_ref), (grad_any, grad_ref)]
    sources += [(ref, mirror_ref.at[index]) for index, ref in enumerate(mirror_any)]
    ahead = len(sources)
    for shard, ref in enumerate((*near_refs, *far_refs)):
        start = ref.shape[0] - half if shard < shards // 2 else shard % 2 * half
        sources.append((ref.at[pl.ds(start, half), :], query_ref.at[shard]))
    copies = [
        pltpu.make_async_copy(source, target, sems.at[index])
        for index, (source, target) in enumerate(sources)
    ]
    for copy in copies:
        copy.start()
    for copy in copies[:ahead]:
        copy.wait()
    renorm(before_ref, grad_ref, mirror_ref, weight_ref)

    gain = gain_ref[...]
    row = lax.broadcasted_iota(jnp.int32, (height, LANES), 0)
    batch = 2
    for first in range(0, shards, batch):
        parts = []
        for shard in range(first, first + batch):
            copies[ahead + shard].wait()
            parts.extend(part_halves(query_ref[shard], head_size))
        rows = jnp.concatenate(parts, axis=0)
        proj_first = contract(rows, weight_ref[0, :, 0:head_size], NT)
        proj_third = contract(rows, weight_ref[1, :, 0:head_size], NT)
        mixed = (proj_first * sigmoid(proj_first) * proj_third).astype(jnp.bfloat16)
        outputs = contract(mixed, weight_ref[2], NN)
        mean = jnp.sum(outputs * outputs, axis=-1, keepdims=True) * (1.0 / head_size)
        normed = outputs * lax.rsqrt(mean + epsilon) * gain
        normed = normed.astype(jnp.bfloat16).astype(jnp.float32)
        for shard in range(first, first + batch):
            base = (shard - first) * width * height
            frame = order_ref[shard]
            block = frame // frames_here
            slot = frame % frames_here
            for tile in range(full + 1):
                lanes = slice(tile * LANES, (tile + 1) * LANES)
                taps = [tap_ref[index : index + 1, lanes] for index in range(9)]
                columns = [
                    normed[base + column * height : base + (column + 1) * height, lanes]
                    for column in range(width)
                ]
                for column in range(width):
                    sums = []
                    for row_tap in range(3):
                        total = None
                        for col_tap in range(3):
                            if 0 <= column + col_tap - 1 < width:
                                term = taps[row_tap * 3 + col_tap] * columns[column + col_tap - 1]
                                total = term if total is None else total + term
                        sums.append(total)
                    above = jnp.where(row == 0, 0.0, pltpu.roll(sums[0], 1, 0))
                    below = jnp.where(row == height - 1, 0.0, pltpu.roll(sums[2], height - 1, 0))
                    turned_ref[
                        block, column, tile, pl.ds(slot, height, stride=frames_here), :
                    ] = sums[1] + above + below
    blocks = turned_ref.shape[0]
    side_rows = out_ref.shape[1]
    for block in range(blocks):
        for column in range(width):
            sides = [
                [
                    turned_ref[block, column, tile, side * side_rows : (side + 1) * side_rows, :]
                    for tile in range(full + 1)
                ]
                for side in range(2)
            ]
            for tile, part in enumerate(join_halves(sides[0], sides[1], tail)):
                out_ref[column * blocks + block, :, tile * LANES : (tile + 1) * LANES] = part.astype(
                    jnp.bfloat16
                )


def gate_kernel(blocks, conv_ref, gate_ref, out_ref):
    chunks, side_rows, _ = conv_ref.shape
    height, frames_here, channels = gate_ref.shape
    head_size = channels // chunks
    shards = chunks // blocks
    rows_here = height // 2
    for pair in range(chunks // 2):
        lanes = slice(pair * 2 * head_size, (pair + 1) * 2 * head_size)
        halves = []
        for head in (2 * pair, 2 * pair + 1):
            chunk = (head % shards) * blocks + head // shards
            halves.append(part_halves(conv_ref[chunk].astype(jnp.float32), head_size))
        for side in range(2):
            conv = jnp.concatenate([halves[0][side], halves[1][side]], axis=1)
            gate = gate_ref[side * rows_here : (side + 1) * rows_here, :, lanes].astype(jnp.float32)
            conv = conv.reshape(rows_here, frames_here, 2 * head_size)
            out_ref[side * rows_here : (side + 1) * rows_here, :, lanes] = (
                conv * (gate * sigmoid(gate))
            ).astype(jnp.bfloat16)


def in_vmem(count):
    return [pl.BlockSpec(memory_space=pltpu.VMEM)] * count


def call(kernel, out, operands, scratch=(), specs=None):
    return pl.pallas_call(
        kernel,
        out_shape=out,
        in_specs=specs or in_vmem(len(operands)),
        out_specs=jax.tree.map(lambda _: pl.BlockSpec(memory_space=pltpu.VMEM), out),
        scratch_shapes=scratch,
        compiler_params=pltpu.CompilerParams(vmem_limit_bytes=VMEM_BYTES),
        cost_estimate=pl.CostEstimate(flops=0, bytes_accessed=0, transcendentals=0),
    )(*operands)


def after(part, *earlier):
    anywhere = pl.BlockSpec(memory_space=pl.ANY)
    return pl.pallas_call(
        lambda *refs: None,
        out_shape=jax.ShapeDtypeStruct(part.shape, part.dtype),
        in_specs=[anywhere] * (1 + len(earlier)),
        out_specs=anywhere,
        input_output_aliases={0: 0},
        cost_estimate=pl.CostEstimate(flops=0, bytes_accessed=0, transcendentals=0),
    )(part, *earlier)


def by_heads(
    queries, keys, values, rates, fast_weights, norm_gain, frame_order, gate_input, conv_weights
):
    tok_rows = queries.shape[0]
    head_count = queries.shape[1] * queries.shape[2]
    head_size = queries.shape[3]
    height, frames_here = gate_input.shape[:2]
    shards = lax.axis_size("tok")
    blocks = lax.axis_size("head")
    half = tok_rows // 2
    wide = 2 * head_size
    tiles = head_size // LANES + 1
    own = lax.axis_index("tok")
    own_channel = lax.axis_index("head") * head_count + own

    def rows_of(array):
        return array.reshape(tok_rows, head_count, head_size)

    def own_of(array, place):
        return lax.dynamic_index_in_dim(array, place, 0, keepdims=False)

    line = shards // 2
    tile_scratch = pltpu.VMEM((tiles, tok_rows * head_count, LANES), jnp.float32)
    token_rates = rates.reshape(head_count, tok_rows)
    chips = line // 2

    one = jax.ShapeDtypeStruct((tok_rows, wide), jnp.bfloat16)
    mirrored = call(
        pack_mirror_kernel,
        [one] * line,
        (rows_of(keys), rows_of(values), token_rates),
        (tile_scratch, tile_scratch),
    )
    mirrored = [mirrored[0]] + [send(mirrored[k], k) for k in range(1, line)]
    across = call(
        functools.partial(pack_across_kernel, height),
        [one] * chips,
        (rows_of(queries),),
        (tile_scratch,),
    )
    across_landed = [send(part, line + 2 * index) for index, part in enumerate(across)]
    weights = fast_weights.reshape(head_count, 3, head_size, head_size)
    mirror_weights = own_of(weights, own ^ line)
    packed = call(
        functools.partial(pack_near_kernel, height),
        [jax.ShapeDtypeStruct((tok_rows + half, wide), jnp.bfloat16)] * line,
        (rows_of(keys), rows_of(values), token_rates, rows_of(queries), across[0], mirror_weights),
        (tile_scratch, tile_scratch, tile_scratch),
        specs=in_vmem(4) + [pl.BlockSpec(memory_space=pl.ANY)] * 2,
    )
    held = [after(part, *mirrored[1:], *across_landed) for part in packed[1:]]
    near = [packed[0]] + [send(held[k - 1], k) for k in range(1, line)]
    own_weights = own_of(weights, own)
    own_gain = own_of(norm_gain.reshape(head_count, 1, head_size), own)
    taps = conv_weights.reshape(9, blocks * head_count, head_size)
    own_taps = lax.dynamic_index_in_dim(taps, own_channel, 1, keepdims=False)
    own_taps = jnp.pad(own_taps, ((0, 0), (0, tiles * LANES - head_size)))
    own_gain = jnp.pad(own_gain, ((0, 0), (0, tiles * LANES - head_size)))
    frames = frame_order[own ^ jnp.arange(shards, dtype=jnp.int32)]
    grad_shape = (3, head_size, tiles * LANES)
    ahead = (*across_landed, *held)
    units = head_size // 2
    crossed = []
    for first in range(0, head_size, units):
        part = call(
            functools.partial(mirror_kernel, line, tok_rows, first),
            jax.ShapeDtypeStruct((units + units // 2, wide), jnp.bfloat16),
            (*mirrored, *ahead, mirror_weights),
            (pltpu.VMEM((3, units, tiles * LANES), jnp.float32),),
            specs=in_vmem(line) + [pl.BlockSpec(memory_space=pl.ANY)] * len(ahead) + in_vmem(1),
        )
        crossed.append(send(part, line))
    gradients = call(
        functools.partial(own_kernel, tok_rows),
        jax.ShapeDtypeStruct(grad_shape, jnp.float32),
        (*near, own_weights),
    )
    across = relay([after(part, gradients) for part in across_landed])
    side_rows = frames_here * height // 2
    anywhere = pl.BlockSpec(memory_space=pl.ANY)
    outgoing = call(
        functools.partial(apply_kernel, height, frames_here, shards),
        jax.ShapeDtypeStruct((shards * blocks, side_rows, wide), jnp.bfloat16),
        (frames, *near, *across, own_weights, gradients, *crossed, own_gain, own_taps),
        (
            pltpu.VMEM((shards, half, wide), jnp.bfloat16),
            pltpu.VMEM((3, head_size, head_size), jnp.bfloat16),
            pltpu.VMEM(grad_shape, jnp.float32),
            pltpu.VMEM((len(crossed), *crossed[0].shape), jnp.bfloat16),
            pltpu.VMEM(grad_shape, jnp.bfloat16),
            pltpu.VMEM((blocks, shards, tiles, 2 * side_rows, LANES), jnp.float32),
            pltpu.SemaphoreType.DMA((shards + 2 + len(crossed),)),
        ),
        specs=[pl.BlockSpec(memory_space=pltpu.SMEM)]
        + [anywhere] * (shards + 2 + len(crossed))
        + in_vmem(2),
    )
    arrived = lax.all_to_all(outgoing, ("tok", "head"), split_axis=0, concat_axis=0, tiled=True)
    gate = gate_input.reshape(height, frames_here, gate_input.shape[3])
    gated = call(
        functools.partial(gate_kernel, blocks),
        jax.ShapeDtypeStruct(gate.shape, jnp.bfloat16),
        (arrived, gate),
    )
    return gated.reshape(gate_input.shape)


def fits_by_heads(queries, gate_input, frame_order):
    tok_rows, head_size = queries.shape[0], queries.shape[3]
    head_count = queries.shape[1] * queries.shape[2]
    height, frames_here, col_width = gate_input.shape[:3]
    shards = lax.axis_size("tok")
    return (
        head_count == shards
        and frame_order.shape[0] == shards
        and lax.axis_size("tile") == 1
        and col_width == 1
        and shards % 2 == 0
        and shards & (shards - 1) == 0
        and head_size % LANES == LANES // 2
        and height % 8 == 0
        and tok_rows == height * shards
        and tok_rows % 32 == 0
        and head_size % 64 == 0
        and frames_here * height % 32 == 0
        and frames_here * lax.axis_size("head") == shards
        and lax.axis_size("head") & (lax.axis_size("head") - 1) == 0
    )


def renormed(previous, gradient):
    before = previous.astype(jnp.float32)
    updated = before - gradient
    scale_old = jnp.sqrt(jnp.mean(before * before, axis=-1, keepdims=True) + epsilon)
    scale_new = jnp.sqrt(jnp.mean(updated * updated, axis=-1, keepdims=True) + epsilon)
    return (updated * (scale_old / scale_new)).astype(jnp.bfloat16)


def by_tokens(
    queries, keys, values, rates, fast_weights, norm_gain, frame_order, gate_input, conv_weights
):
    tok_rows = queries.shape[0]
    head_count = queries.shape[1] * queries.shape[2]
    head_size = queries.shape[3]
    query_rows = queries.reshape(tok_rows, head_count, head_size)
    key_rows = keys.reshape(tok_rows, head_count, head_size)
    value_rows = values.reshape(tok_rows, head_count, head_size)
    token_rates = rates.reshape(head_count, tok_rows)
    weights = fast_weights.reshape(head_count, 3, head_size, head_size)
    head_gains = norm_gain.reshape(head_count, head_size)
    first_pre = jnp.einsum(
        "thd,hfd->htf", key_rows, weights[:, 0], preferred_element_type=jnp.float32
    )
    third_pre = jnp.einsum(
        "thd,hfd->htf", key_rows, weights[:, 1], preferred_element_type=jnp.float32
    )
    sigmoid_first = jax.nn.sigmoid(first_pre)
    activated = first_pre * sigmoid_first
    hidden = (activated * third_pre).astype(jnp.bfloat16)
    target = (-token_rates.T[:, :, None] * value_rows.astype(jnp.float32)).astype(jnp.bfloat16)
    grad_down = jnp.einsum("thd,htf->hdf", target, hidden, preferred_element_type=jnp.float32)
    hidden_grad = jnp.einsum(
        "thd,hdf->htf", target, weights[:, 2], preferred_element_type=jnp.float32
    )
    grad_first_in = (
        hidden_grad * third_pre * sigmoid_first * (1.0 + first_pre * (1.0 - sigmoid_first))
    ).astype(jnp.bfloat16)
    grad_third_in = (hidden_grad * activated).astype(jnp.bfloat16)
    grad_first = jnp.einsum(
        "htf,thd->hfd", grad_first_in, key_rows, preferred_element_type=jnp.float32
    )
    grad_third = jnp.einsum(
        "htf,thd->hfd", grad_third_in, key_rows, preferred_element_type=jnp.float32
    )
    gradients = jnp.stack([grad_first, grad_third, grad_down], axis=1)
    row_share = lax.psum_scatter(gradients, "tok", scatter_dimension=2, tiled=True)
    row_count = row_share.shape[2]
    own_rows = lax.dynamic_slice_in_dim(weights, lax.axis_index("tok") * row_count, row_count, 2)
    updated = lax.all_gather(renormed(own_rows, row_share), "tok", axis=2, tiled=True)
    proj_first = jnp.einsum(
        "thd,hfd->thf", query_rows, updated[:, 0], preferred_element_type=jnp.float32
    )
    proj_third = jnp.einsum(
        "thd,hfd->thf", query_rows, updated[:, 1], preferred_element_type=jnp.float32
    )
    mixed_hidden = (jax.nn.silu(proj_first) * proj_third).astype(jnp.bfloat16)
    outputs = jnp.einsum(
        "thf,hdf->thd", mixed_hidden, updated[:, 2], preferred_element_type=jnp.float32
    )
    normed = (
        outputs
        * lax.rsqrt(jnp.mean(outputs * outputs, axis=-1, keepdims=True) + epsilon)
        * head_gains[None]
    )
    normed = normed.astype(jnp.bfloat16)
    height = gate_input.shape[0]
    col_width = gate_input.shape[2]
    shards = lax.axis_size("tok")
    full_width = col_width * shards
    channels_here = head_count * head_size
    frame_grid = normed.reshape(height, full_width, channels_here)
    own_taps = lax.dynamic_slice_in_dim(
        conv_weights, lax.axis_index("head") * channels_here, channels_here, 2
    )
    padded = jnp.pad(frame_grid, ((1, 1), (1, 1), (0, 0)))
    local_sum = jnp.zeros((height, full_width, channels_here), jnp.float32)
    for row_tap in range(3):
        for col_tap in range(3):
            local_sum = local_sum + own_taps[row_tap, col_tap] * padded[
                row_tap : row_tap + height, col_tap : col_tap + full_width
            ].astype(jnp.float32)
    outgoing = local_sum.astype(jnp.bfloat16).reshape(height, shards, col_width, channels_here)
    arrived = lax.all_to_all(outgoing, "tok", split_axis=1, concat_axis=1, tiled=True)
    frame_count = frame_order.shape[0]
    numbers = jnp.arange(frame_count, dtype=jnp.int32)
    inverse = jnp.sum(
        jnp.where(frame_order[None, :] == numbers[:, None], numbers[None, :], 0), axis=1
    )
    ordered = jnp.take(arrived, inverse, axis=1)
    tile_block = lax.all_to_all(ordered, "head", split_axis=1, concat_axis=3, tiled=True)
    return (tile_block.astype(jnp.float32) * jax.nn.silu(gate_input.astype(jnp.float32))).astype(
        jnp.bfloat16
    )


def local(queries, keys, values, rates, fast_weights, norm_gain, frame_order, gate_input, conv_weights):
    args = (
        queries, keys, values, rates, fast_weights, norm_gain, frame_order, gate_input, conv_weights
    )
    if fits_by_heads(queries, gate_input, frame_order):
        return by_heads(*args)
    return by_tokens(*args)


def solution(mesh):
    in_specs = (
        P(("groups", "tok"), "tile", "head", None),
        P(("groups", "tok"), "tile", "head", None),
        P(("groups", "tok"), "tile", "head", None),
        P("tile", "head", ("groups", "tok")),
        P("tile", "head", None, None, None),
        P("tile", "head", None),
        P("groups"),
        P(None, ("groups", "head"), "tok", "tile"),
        P(None, None, "tile"),
    )
    out_specs = P(None, ("groups", "head"), "tok", "tile")
    return jax.shard_map(local, mesh=mesh, in_specs=in_specs, out_specs=out_specs, check_vma=False)
```

```python
import functools

import jax
import jax.numpy as jnp
from jax import lax
from jax.experimental import pallas as pl
from jax.experimental.pallas import tpu as pltpu
from jax.sharding import PartitionSpec as P

epsilon = 1e-06
LANES = 128
VMEM_BYTES = 24 * 1024 * 1024


def split_lanes(source, scratch, rows, head_size):
    full = head_size // LANES
    tail = head_size - full * LANES
    wide = source.reshape(rows, head_size).astype(jnp.float32)
    for tile in range(full):
        scratch[tile] = wide[:, tile * LANES : (tile + 1) * LANES]
    scratch[full, :, 0:tail] = wide[:, full * LANES :]


def join_halves(first, second, tail):
    lane = lax.broadcasted_iota(jnp.int32, first[-1].shape, 1)
    middle = jnp.where(lane < tail, first[-1], pltpu.roll(second[-1], tail, 1))
    return first[:-1] + [middle] + second[:-1]


def part_halves(packed, head_size):
    full = head_size // LANES
    tail = head_size - full * LANES
    first = packed[:, :head_size]
    middle = packed[:, head_size : (full + 1) * LANES]
    second = jnp.concatenate([packed[:, (full + 1) * LANES :], middle], axis=1)
    return first, second


def partner_head(partner):
    return lax.axis_index("tok") ^ partner


def pack_pairs(head, rate_ref, key_tiles, value_tiles, out_ref, start, head_size):
    heads, tok_rows = rate_ref.shape
    half = tok_rows // 2
    full = head_size // LANES
    tail = head_size - full * LANES
    rate_row = -rate_ref[pl.ds(head, 1), :]
    rates = jnp.broadcast_to(rate_row, (LANES, tok_rows)).T
    for row, tiles in ((start, key_tiles), (start + half, value_tiles)):
        sides = []
        for side in range(2):
            parts = [
                tiles[tile, pl.ds(side * half * heads + head, half, stride=heads), :]
                for tile in range(full + 1)
            ]
            if tiles is value_tiles:
                rate = rates[side * half : (side + 1) * half]
                parts = [rate * part for part in parts]
            sides.append(parts)
        for tile, part in enumerate(join_halves(sides[0], sides[1], tail)):
            out_ref[row : row + half, tile * LANES : (tile + 1) * LANES] = part.astype(jnp.bfloat16)


def pack_query(head, heads, height, query_tiles, out_ref, start, head_size):
    tok_rows = query_tiles.shape[1] // heads
    half = tok_rows // 2
    width = tok_rows // height
    full = head_size // LANES
    tail = head_size - full * LANES
    sides = []
    for side in range(2):
        sides.append(
            [
                jnp.concatenate(
                    [
                        query_tiles[
                            tile, pl.ds(column * heads + head, height, stride=width * heads), :
                        ]
                        for column in range(side * width // 2, (side + 1) * width // 2)
                    ],
                    axis=0,
                )
                for tile in range(full + 1)
            ]
        )
    for tile, part in enumerate(join_halves(sides[0], sides[1], tail)):
        out_ref[start : start + half, tile * LANES : (tile + 1) * LANES] = part.astype(jnp.bfloat16)


def pack_mirror_kernel(key_ref, value_ref, rate_ref, *rest):
    outs, (key_tiles, value_tiles) = rest[:-2], rest[-2:]
    tok_rows, heads, head_size = key_ref.shape
    split_lanes(key_ref[...], key_tiles, tok_rows * heads, head_size)
    split_lanes(value_ref[...], value_tiles, tok_rows * heads, head_size)
    for partner, out_ref in enumerate(outs):
        head = partner_head(partner ^ (heads // 2))
        pack_pairs(head, rate_ref, key_tiles, value_tiles, out_ref, 0, head_size)


def pack_across_kernel(height, query_ref, *rest):
    outs, query_tiles = rest[:-1], rest[-1]
    tok_rows, heads, head_size = query_ref.shape
    half = tok_rows // 2
    split_lanes(query_ref[...], query_tiles, tok_rows * heads, head_size)
    for partner in range(heads // 2):
        head = partner_head(partner ^ (heads // 2))
        start = partner % 2 * half
        pack_query(head, heads, height, query_tiles, outs[partner // 2], start, head_size)


def pack_near_kernel(height, key_ref, value_ref, rate_ref, query_ref, *rest):
    outs, (key_tiles, value_tiles, query_tiles) = rest[2:-3], rest[-3:]
    tok_rows, heads, head_size = key_ref.shape
    split_lanes(key_ref[...], key_tiles, tok_rows * heads, head_size)
    split_lanes(value_ref[...], value_tiles, tok_rows * heads, head_size)
    split_lanes(query_ref[...], query_tiles, tok_rows * heads, head_size)
    for partner, out_ref in enumerate(outs):
        head = partner_head(partner)
        pack_pairs(head, rate_ref, key_tiles, value_tiles, out_ref, 0, head_size)
        pack_query(head, heads, height, query_tiles, out_ref, tok_rows, head_size)


def relay(landed):
    return [part for one in landed for part in (one, send(one, 1))]


def send(part, partner):
    pairs = [(place, place ^ partner) for place in range(lax.axis_size("tok"))]
    return lax.ppermute(part, "tok", pairs)


def sigmoid(value):
    return 0.5 + 0.5 * jnp.tanh(0.5 * value)


def contract(first, second, dims):
    return lax.dot_general(first, second, (dims, ((), ())), preferred_element_type=jnp.float32)


NN = ((1,), (0,))
NT = ((1,), (1,))


def add_gradients(pair_refs, tok_rows, weight_ref, hidden, grad_ref):
    half = tok_rows // 2
    head_size = weight_ref.shape[-1]
    first_weight = weight_ref[0, hidden]
    third_weight = weight_ref[1, hidden]
    down_turned = weight_ref[2].astype(jnp.float32).T[hidden].astype(jnp.bfloat16)
    step = 2 if len(pair_refs) % 2 == 0 else 1
    for start in range(0, len(pair_refs), step):
        key_parts, target_parts = [], []
        for pair_ref in pair_refs[start : start + step]:
            key_parts.extend(part_halves(pair_ref[0:half, :], head_size))
            target_parts.extend(part_halves(pair_ref[half:tok_rows, :], head_size))
        key_rows = jnp.concatenate(key_parts, axis=0)
        target = jnp.concatenate(target_parts, axis=0)
        first_pre = contract(first_weight, key_rows, NT)
        third_pre = contract(third_weight, key_rows, NT)
        hidden_grad = contract(down_turned, target, NT)
        sigmoid_first = sigmoid(first_pre)
        activated = first_pre * sigmoid_first
        mixed = (activated * third_pre).astype(jnp.bfloat16)
        grad_first_in = (
            hidden_grad * third_pre * sigmoid_first * (1.0 + first_pre * (1.0 - sigmoid_first))
        ).astype(jnp.bfloat16)
        grad_third_in = (hidden_grad * activated).astype(jnp.bfloat16)
        grads = (
            contract(grad_first_in, key_rows, NN),
            contract(grad_third_in, key_rows, NN),
            contract(mixed, target, NN),
        )
        for index, grad in enumerate(grads):
            if start == 0:
                grad_ref[index, :, 0:head_size] = grad
            else:
                grad_ref[index, :, 0:head_size] += grad


def mirror_kernel(count, tok_rows, first, *refs):
    pair_refs, (weight_ref, out_ref, grad_ref) = refs[:count], refs[-3:]
    head_size = weight_ref.shape[-1]
    full = head_size // LANES
    tail = head_size - full * LANES
    units = grad_ref.shape[1]
    half = units // 2
    add_gradients(pair_refs, tok_rows, weight_ref, slice(first, first + units), grad_ref)

    def tiles_of(index, rows):
        return [
            grad_ref[index, rows, tile * LANES : (tile + 1) * LANES] for tile in range(full + 1)
        ]

    both = join_halves(tiles_of(0, slice(0, units)), tiles_of(1, slice(0, units)), tail)
    down = join_halves(tiles_of(2, slice(0, half)), tiles_of(2, slice(half, units)), tail)
    for tile, (above, below) in enumerate(zip(both, down)):
        lanes = slice(tile * LANES, (tile + 1) * LANES)
        out_ref[0:units, lanes] = above.astype(jnp.bfloat16)
        out_ref[units : units + half, lanes] = below.astype(jnp.bfloat16)


def own_kernel(tok_rows, *refs):
    pair_refs, (weight_ref, out_ref) = refs[:-2], refs[-2:]
    add_gradients(pair_refs, tok_rows, weight_ref, slice(0, weight_ref.shape[-1]), out_ref)


def renorm(weight_ref, grad_ref, mirror_refs, out_ref):
    head_size = weight_ref.shape[-1]
    units = head_size // len(mirror_refs)
    firsts, thirds, downs = [], [], []
    for mirror_ref in mirror_refs:
        first, third = part_halves(mirror_ref[0:units, :], head_size)
        firsts.append(first)
        thirds.append(third)
        downs.extend(part_halves(mirror_ref[units:, :], head_size))
    first, third, down = (jnp.concatenate(parts, axis=0) for parts in (firsts, thirds, downs))
    for index, other in enumerate((first, third, down)):
        before = weight_ref[index].astype(jnp.float32)
        axis = 1
        if index == 2:
            before = before.T
            axis = 0
        grad = grad_ref[index, :, 0:head_size] + other.astype(jnp.float32)
        updated = before - grad
        scale_old = jnp.sqrt(jnp.mean(before * before, axis=axis, keepdims=True) + epsilon)
        scale_new = jnp.sqrt(jnp.mean(updated * updated, axis=axis, keepdims=True) + epsilon)
        out_ref[index] = (updated * (scale_old / scale_new)).astype(jnp.bfloat16)


def apply_kernel(height, frames_here, shards, order_ref, *refs):
    near_refs, far_refs = refs[: shards // 2], refs[shards // 2 : shards]
    before_ref, grad_ref, *mirror_refs = refs[shards:-6]
    gain_ref, tap_ref, out_ref = refs[-6:-3]
    weight_ref, grid_ref, turned_ref = refs[-3:]
    half = far_refs[0].shape[0] // 2
    query_parts = [ref[ref.shape[0] - half :, :] for ref in near_refs]
    for index, ref in enumerate(far_refs):
        query_parts.append(ref[index % 2 * half : (index % 2 + 1) * half, :])
    renorm(before_ref, grad_ref, mirror_refs, weight_ref)
    width = 2 * half // height
    head_size = weight_ref.shape[-1]
    full = head_size // LANES
    tail = head_size - full * LANES
    top = 8
    edge = jnp.zeros((top, LANES), jnp.float32)
    whole = jnp.zeros(grid_ref.shape[3:], jnp.float32)
    for shard in range(shards):
        for tile in range(full + 1):
            grid_ref[shard, tile, 0] = whole
            grid_ref[shard, tile, width + 1] = whole
            for column in range(1, width + 1):
                grid_ref[shard, tile, column, 0:top] = edge
                grid_ref[shard, tile, column, top + height :] = edge
    gain = gain_ref[...]
    for shard in range(shards):
        rows = jnp.concatenate(part_halves(query_parts[shard], head_size), axis=0)
        proj_first = contract(rows, weight_ref[0], NT)
        proj_third = contract(rows, weight_ref[1], NT)
        mixed = (proj_first * jax.nn.sigmoid(proj_first) * proj_third).astype(jnp.bfloat16)
        outputs = contract(mixed, weight_ref[2], NN)
        scale = lax.rsqrt(jnp.mean(outputs * outputs, axis=-1, keepdims=True) + epsilon)
        normed = (outputs * scale * gain).astype(jnp.bfloat16).astype(jnp.float32)
        frame = order_ref[shard]
        block = frame // frames_here
        slot = frame % frames_here
        for tile in range(full + 1):
            lanes = slice(tile * LANES, min((tile + 1) * LANES, head_size))
            for column in range(width):
                grid_ref[shard, tile, column + 1, top : top + height, 0 : lanes.stop - lanes.start] = (
                    normed[column * height : (column + 1) * height, lanes]
                )
            taps = [
                tap_ref[index : index + 1, tile * LANES : (tile + 1) * LANES] for index in range(9)
            ]
            for column in range(width):
                total = None
                for row_tap in range(3):
                    first = top + row_tap - 1
                    for col_tap in range(3):
                        term = taps[row_tap * 3 + col_tap] * grid_ref[
                            shard, tile, column + col_tap, first : first + height, :
                        ]
                        total = term if total is None else total + term
                turned_ref[
                    block, column, tile, pl.ds(slot, height, stride=frames_here), :
                ] = total
    blocks = turned_ref.shape[0]
    side_rows = out_ref.shape[1]
    for block in range(blocks):
        for column in range(width):
            sides = [
                [
                    turned_ref[block, column, tile, side * side_rows : (side + 1) * side_rows, :]
                    for tile in range(full + 1)
                ]
                for side in range(2)
            ]
            for tile, part in enumerate(join_halves(sides[0], sides[1], tail)):
                out_ref[column * blocks + block, :, tile * LANES : (tile + 1) * LANES] = part.astype(
                    jnp.bfloat16
                )


def gate_kernel(blocks, conv_ref, gate_ref, out_ref):
    chunks, side_rows, _ = conv_ref.shape
    height, frames_here, channels = gate_ref.shape
    head_size = channels // chunks
    shards = chunks // blocks
    rows_here = height // 2
    for pair in range(chunks // 2):
        lanes = slice(pair * 2 * head_size, (pair + 1) * 2 * head_size)
        halves = []
        for head in (2 * pair, 2 * pair + 1):
            chunk = (head % shards) * blocks + head // shards
            halves.append(part_halves(conv_ref[chunk].astype(jnp.float32), head_size))
        for side in range(2):
            conv = jnp.concatenate([halves[0][side], halves[1][side]], axis=1)
            gate = gate_ref[side * rows_here : (side + 1) * rows_here, :, lanes].astype(jnp.float32)
            conv = conv.reshape(rows_here, frames_here, 2 * head_size)
            out_ref[side * rows_here : (side + 1) * rows_here, :, lanes] = (
                conv * (gate * sigmoid(gate))
            ).astype(jnp.bfloat16)


def in_vmem(count):
    return [pl.BlockSpec(memory_space=pltpu.VMEM)] * count


def call(kernel, out, operands, scratch=(), specs=None, leave=True):
    specs = specs or in_vmem(len(operands))
    operands = [
        pltpu.with_memory_space_constraint(item, pltpu.VMEM)
        if spec.memory_space == pltpu.VMEM
        else item
        for item, spec in zip(operands, specs)
    ]
    if leave:
        out = jax.tree.map(lambda item: pltpu.VMEM(item.shape, item.dtype), out)
    return pl.pallas_call(
        kernel,
        out_shape=out,
        in_specs=specs,
        out_specs=jax.tree.map(lambda _: pl.BlockSpec(memory_space=pltpu.VMEM), out),
        scratch_shapes=scratch,
        compiler_params=pltpu.CompilerParams(vmem_limit_bytes=VMEM_BYTES),
        cost_estimate=pl.CostEstimate(flops=0, bytes_accessed=0, transcendentals=0),
    )(*operands)


def after(part, *earlier):
    anywhere = pl.BlockSpec(memory_space=pl.ANY)
    return pl.pallas_call(
        lambda *refs: None,
        out_shape=jax.ShapeDtypeStruct(part.shape, part.dtype),
        in_specs=[anywhere] * (1 + len(earlier)),
        out_specs=anywhere,
        input_output_aliases={0: 0},
        cost_estimate=pl.CostEstimate(flops=0, bytes_accessed=0, transcendentals=0),
    )(part, *earlier)


def by_heads(
    queries, keys, values, rates, fast_weights, norm_gain, frame_order, gate_input, conv_weights
):
    tok_rows = queries.shape[0]
    head_count = queries.shape[1] * queries.shape[2]
    head_size = queries.shape[3]
    height, frames_here = gate_input.shape[:2]
    shards = lax.axis_size("tok")
    blocks = lax.axis_size("head")
    half = tok_rows // 2
    wide = 2 * head_size
    tiles = head_size // LANES + 1
    own = lax.axis_index("tok")
    own_channel = lax.axis_index("head") * head_count + own

    def rows_of(array):
        return array.reshape(tok_rows, head_count, head_size)

    def own_of(array, place):
        return lax.dynamic_index_in_dim(array, place, 0, keepdims=False)

    line = shards // 2
    tile_scratch = pltpu.VMEM((tiles, tok_rows * head_count, LANES), jnp.float32)
    token_rates = rates.reshape(head_count, tok_rows)
    chips = line // 2

    one = jax.ShapeDtypeStruct((tok_rows, wide), jnp.bfloat16)
    mirrored = call(
        pack_mirror_kernel,
        [one] * line,
        (rows_of(keys), rows_of(values), token_rates),
        (tile_scratch, tile_scratch),
    )
    mirrored = [mirrored[0]] + [send(mirrored[k], k) for k in range(1, line)]
    across = call(
        functools.partial(pack_across_kernel, height),
        [one] * chips,
        (rows_of(queries),),
        (tile_scratch,),
    )
    across_landed = [send(part, line + 2 * index) for index, part in enumerate(across)]
    weights = fast_weights.reshape(head_count, 3, head_size, head_size)
    mirror_weights = own_of(weights, own ^ line)
    packed = call(
        functools.partial(pack_near_kernel, height),
        [jax.ShapeDtypeStruct((tok_rows + half, wide), jnp.bfloat16)] * line,
        (rows_of(keys), rows_of(values), token_rates, rows_of(queries), across[0], mirror_weights),
        (tile_scratch, tile_scratch, tile_scratch),
        specs=in_vmem(4) + [pl.BlockSpec(memory_space=pl.ANY)] * 2,
    )
    held = [after(part, *mirrored[1:], *across_landed) for part in packed[1:]]
    near = [packed[0]] + [send(held[k - 1], k) for k in range(1, line)]
    own_weights = own_of(weights, own)
    own_gain = own_of(norm_gain.reshape(head_count, 1, head_size), own)
    taps = conv_weights.reshape(9, blocks * head_count, head_size)
    own_taps = lax.dynamic_index_in_dim(taps, own_channel, 1, keepdims=False)
    own_taps = jnp.pad(own_taps, ((0, 0), (0, tiles * LANES - head_size)))
    frames = frame_order[own ^ jnp.arange(shards, dtype=jnp.int32)]
    grad_shape = (3, head_size, tiles * LANES)
    ahead = (*across_landed, *held)
    units = head_size // 2
    crossed = []
    for first in range(0, head_size, units):
        part = call(
            functools.partial(mirror_kernel, line, tok_rows, first),
            jax.ShapeDtypeStruct((units + units // 2, wide), jnp.bfloat16),
            (*mirrored, *ahead, mirror_weights),
            (pltpu.VMEM((3, units, tiles * LANES), jnp.float32),),
            specs=in_vmem(line) + [pl.BlockSpec(memory_space=pl.ANY)] * len(ahead) + in_vmem(1),
        )
        crossed.append(send(part, line))
    gradients = call(
        functools.partial(own_kernel, tok_rows),
        jax.ShapeDtypeStruct(grad_shape, jnp.float32),
        (*near, own_weights),
    )
    across = relay([after(part, gradients) for part in across_landed])
    side_rows = frames_here * height // 2
    outgoing = call(
        functools.partial(apply_kernel, height, frames_here, shards),
        jax.ShapeDtypeStruct((shards * blocks, side_rows, wide), jnp.bfloat16),
        (frames, *near, *across, own_weights, gradients, *crossed, own_gain, own_taps),
        (
            pltpu.VMEM((3, head_size, head_size), jnp.bfloat16),
            pltpu.VMEM((shards, tiles, shards + 2, height + 16, LANES), jnp.float32),
            pltpu.VMEM((blocks, shards, tiles, 2 * side_rows, LANES), jnp.float32),
        ),
        specs=[pl.BlockSpec(memory_space=pltpu.SMEM)] + in_vmem(shards + 6),
    )
    arrived = lax.all_to_all(outgoing, ("tok", "head"), split_axis=0, concat_axis=0, tiled=True)
    gate = gate_input.reshape(height, frames_here, gate_input.shape[3])
    gated = call(
        functools.partial(gate_kernel, blocks),
        jax.ShapeDtypeStruct(gate.shape, jnp.bfloat16),
        (arrived, gate),
        leave=False,
    )
    return gated.reshape(gate_input.shape)


def fits_by_heads(queries, gate_input, frame_order):
    tok_rows, head_size = queries.shape[0], queries.shape[3]
    head_count = queries.shape[1] * queries.shape[2]
    height, frames_here, col_width = gate_input.shape[:3]
    shards = lax.axis_size("tok")
    return (
        head_count == shards
        and frame_order.shape[0] == shards
        and lax.axis_size("tile") == 1
        and col_width == 1
        and shards % 2 == 0
        and shards & (shards - 1) == 0
        and head_size % LANES == LANES // 2
        and height % 8 == 0
        and tok_rows == height * shards
        and tok_rows % 32 == 0
        and head_size % 64 == 0
        and frames_here * height % 32 == 0
        and frames_here * lax.axis_size("head") == shards
        and lax.axis_size("head") & (lax.axis_size("head") - 1) == 0
    )


def renormed(previous, gradient):
    before = previous.astype(jnp.float32)
    updated = before - gradient
    scale_old = jnp.sqrt(jnp.mean(before * before, axis=-1, keepdims=True) + epsilon)
    scale_new = jnp.sqrt(jnp.mean(updated * updated, axis=-1, keepdims=True) + epsilon)
    return (updated * (scale_old / scale_new)).astype(jnp.bfloat16)


def by_tokens(
    queries, keys, values, rates, fast_weights, norm_gain, frame_order, gate_input, conv_weights
):
    tok_rows = queries.shape[0]
    head_count = queries.shape[1] * queries.shape[2]
    head_size = queries.shape[3]
    query_rows = queries.reshape(tok_rows, head_count, head_size)
    key_rows = keys.reshape(tok_rows, head_count, head_size)
    value_rows = values.reshape(tok_rows, head_count, head_size)
    token_rates = rates.reshape(head_count, tok_rows)
    weights = fast_weights.reshape(head_count, 3, head_size, head_size)
    head_gains = norm_gain.reshape(head_count, head_size)
    first_pre = jnp.einsum(
        "thd,hfd->htf", key_rows, weights[:, 0], preferred_element_type=jnp.float32
    )
    third_pre = jnp.einsum(
        "thd,hfd->htf", key_rows, weights[:, 1], preferred_element_type=jnp.float32
    )
    sigmoid_first = jax.nn.sigmoid(first_pre)
    activated = first_pre * sigmoid_first
    hidden = (activated * third_pre).astype(jnp.bfloat16)
    target = (-token_rates.T[:, :, None] * value_rows.astype(jnp.float32)).astype(jnp.bfloat16)
    grad_down = jnp.einsum("thd,htf->hdf", target, hidden, preferred_element_type=jnp.float32)
    hidden_grad = jnp.einsum(
        "thd,hdf->htf", target, weights[:, 2], preferred_element_type=jnp.float32
    )
    grad_first_in = (
        hidden_grad * third_pre * sigmoid_first * (1.0 + first_pre * (1.0 - sigmoid_first))
    ).astype(jnp.bfloat16)
    grad_third_in = (hidden_grad * activated).astype(jnp.bfloat16)
    grad_first = jnp.einsum(
        "htf,thd->hfd", grad_first_in, key_rows, preferred_element_type=jnp.float32
    )
    grad_third = jnp.einsum(
        "htf,thd->hfd", grad_third_in, key_rows, preferred_element_type=jnp.float32
    )
    gradients = jnp.stack([grad_first, grad_third, grad_down], axis=1)
    row_share = lax.psum_scatter(gradients, "tok", scatter_dimension=2, tiled=True)
    row_count = row_share.shape[2]
    own_rows = lax.dynamic_slice_in_dim(weights, lax.axis_index("tok") * row_count, row_count, 2)
    updated = lax.all_gather(renormed(own_rows, row_share), "tok", axis=2, tiled=True)
    proj_first = jnp.einsum(
        "thd,hfd->thf", query_rows, updated[:, 0], preferred_element_type=jnp.float32
    )
    proj_third = jnp.einsum(
        "thd,hfd->thf", query_rows, updated[:, 1], preferred_element_type=jnp.float32
    )
    mixed_hidden = (jax.nn.silu(proj_first) * proj_third).astype(jnp.bfloat16)
    outputs = jnp.einsum(
        "thf,hdf->thd", mixed_hidden, updated[:, 2], preferred_element_type=jnp.float32
    )
    normed = (
        outputs
        * lax.rsqrt(jnp.mean(outputs * outputs, axis=-1, keepdims=True) + epsilon)
        * head_gains[None]
    )
    normed = normed.astype(jnp.bfloat16)
    height = gate_input.shape[0]
    col_width = gate_input.shape[2]
    shards = lax.axis_size("tok")
    full_width = col_width * shards
    channels_here = head_count * head_size
    frame_grid = normed.reshape(height, full_width, channels_here)
    own_taps = lax.dynamic_slice_in_dim(
        conv_weights, lax.axis_index("head") * channels_here, channels_here, 2
    )
    padded = jnp.pad(frame_grid, ((1, 1), (1, 1), (0, 0)))
    local_sum = jnp.zeros((height, full_width, channels_here), jnp.float32)
    for row_tap in range(3):
        for col_tap in range(3):
            local_sum = local_sum + own_taps[row_tap, col_tap] * padded[
                row_tap : row_tap + height, col_tap : col_tap + full_width
            ].astype(jnp.float32)
    outgoing = local_sum.astype(jnp.bfloat16).reshape(height, shards, col_width, channels_here)
    arrived = lax.all_to_all(outgoing, "tok", split_axis=1, concat_axis=1, tiled=True)
    frame_count = frame_order.shape[0]
    numbers = jnp.arange(frame_count, dtype=jnp.int32)
    inverse = jnp.sum(
        jnp.where(frame_order[None, :] == numbers[:, None], numbers[None, :], 0), axis=1
    )
    ordered = jnp.take(arrived, inverse, axis=1)
    tile_block = lax.all_to_all(ordered, "head", split_axis=1, concat_axis=3, tiled=True)
    return (tile_block.astype(jnp.float32) * jax.nn.silu(gate_input.astype(jnp.float32))).astype(
        jnp.bfloat16
    )


def local(queries, keys, values, rates, fast_weights, norm_gain, frame_order, gate_input, conv_weights):
    args = (
        queries, keys, values, rates, fast_weights, norm_gain, frame_order, gate_input, conv_weights
    )
    if fits_by_heads(queries, gate_input, frame_order):
        return by_heads(*args)
    return by_tokens(*args)


def solution(mesh):
    in_specs = (
        P(("groups", "tok"), "tile", "head", None),
        P(("groups", "tok"), "tile", "head", None),
        P(("groups", "tok"), "tile", "head", None),
        P("tile", "head", ("groups", "tok")),
        P("tile", "head", None, None, None),
        P("tile", "head", None),
        P("groups"),
        P(None, ("groups", "head"), "tok", "tile"),
        P(None, None, "tile"),
    )
    out_specs = P(None, ("groups", "head"), "tok", "tile")
    return jax.shard_map(local, mesh=mesh, in_specs=in_specs, out_specs=out_specs, check_vma=False)
```

```python
import functools

import jax
import jax.numpy as jnp
from jax import lax
from jax.experimental import pallas as pl
from jax.experimental.pallas import tpu as pltpu
from jax.sharding import PartitionSpec as P

epsilon = 1e-06
LANES = 128
VMEM_BYTES = 24 * 1024 * 1024


def split_lanes(source, scratch, rows, head_size):
    full = head_size // LANES
    tail = head_size - full * LANES
    wide = source.reshape(rows, head_size).astype(jnp.float32)
    for tile in range(full):
        scratch[tile] = wide[:, tile * LANES : (tile + 1) * LANES]
    scratch[full, :, 0:tail] = wide[:, full * LANES :]


def join_halves(first, second, tail):
    lane = lax.broadcasted_iota(jnp.int32, first[-1].shape, 1)
    middle = jnp.where(lane < tail, first[-1], pltpu.roll(second[-1], tail, 1))
    return first[:-1] + [middle] + second[:-1]


def part_halves(packed, head_size):
    full = head_size // LANES
    tail = head_size - full * LANES
    first = packed[:, :head_size]
    middle = packed[:, head_size : (full + 1) * LANES]
    second = jnp.concatenate([packed[:, (full + 1) * LANES :], middle], axis=1)
    return first, second


def partner_head(partner):
    return lax.axis_index("tok") ^ partner


def pack_pairs(head, rate_ref, key_tiles, value_tiles, out_ref, start, head_size):
    heads, tok_rows = rate_ref.shape
    half = tok_rows // 2
    full = head_size // LANES
    tail = head_size - full * LANES
    rate_row = -rate_ref[pl.ds(head, 1), :]
    rates = jnp.broadcast_to(rate_row, (LANES, tok_rows)).T
    for row, tiles in ((start, key_tiles), (start + half, value_tiles)):
        sides = []
        for side in range(2):
            parts = [
                tiles[tile, pl.ds(side * half * heads + head, half, stride=heads), :]
                for tile in range(full + 1)
            ]
            if tiles is value_tiles:
                rate = rates[side * half : (side + 1) * half]
                parts = [rate * part for part in parts]
            sides.append(parts)
        for tile, part in enumerate(join_halves(sides[0], sides[1], tail)):
            out_ref[row : row + half, tile * LANES : (tile + 1) * LANES] = part.astype(jnp.bfloat16)


def pack_query(head, heads, height, query_tiles, out_ref, start, head_size):
    tok_rows = query_tiles.shape[1] // heads
    half = tok_rows // 2
    width = tok_rows // height
    full = head_size // LANES
    tail = head_size - full * LANES
    sides = []
    for side in range(2):
        sides.append(
            [
                jnp.concatenate(
                    [
                        query_tiles[
                            tile, pl.ds(column * heads + head, height, stride=width * heads), :
                        ]
                        for column in range(side * width // 2, (side + 1) * width // 2)
                    ],
                    axis=0,
                )
                for tile in range(full + 1)
            ]
        )
    for tile, part in enumerate(join_halves(sides[0], sides[1], tail)):
        out_ref[start : start + half, tile * LANES : (tile + 1) * LANES] = part.astype(jnp.bfloat16)


def pack_mirror_kernel(key_ref, value_ref, rate_ref, *rest):
    outs, (key_tiles, value_tiles) = rest[:-2], rest[-2:]
    tok_rows, heads, head_size = key_ref.shape
    split_lanes(key_ref[...], key_tiles, tok_rows * heads, head_size)
    split_lanes(value_ref[...], value_tiles, tok_rows * heads, head_size)
    for partner, out_ref in enumerate(outs):
        head = partner_head(partner ^ (heads // 2))
        pack_pairs(head, rate_ref, key_tiles, value_tiles, out_ref, 0, head_size)


def pack_across_kernel(height, query_ref, *rest):
    outs, query_tiles = rest[:-1], rest[-1]
    tok_rows, heads, head_size = query_ref.shape
    half = tok_rows // 2
    split_lanes(query_ref[...], query_tiles, tok_rows * heads, head_size)
    for partner in range(heads // 2):
        head = partner_head(partner ^ (heads // 2))
        start = partner % 2 * half
        pack_query(head, heads, height, query_tiles, outs[partner // 2], start, head_size)


def pack_near_kernel(height, unread, key_ref, value_ref, rate_ref, query_ref, *rest):
    outs, (key_tiles, value_tiles, query_tiles) = rest[unread:-3], rest[-3:]
    tok_rows, heads, head_size = key_ref.shape
    split_lanes(key_ref[...], key_tiles, tok_rows * heads, head_size)
    split_lanes(value_ref[...], value_tiles, tok_rows * heads, head_size)
    split_lanes(query_ref[...], query_tiles, tok_rows * heads, head_size)
    for partner, out_ref in enumerate(outs):
        head = partner_head(partner)
        pack_pairs(head, rate_ref, key_tiles, value_tiles, out_ref, 0, head_size)
        pack_query(head, heads, height, query_tiles, out_ref, tok_rows, head_size)


def relay(landed):
    return [part for one in landed for part in (one, send(one, 1))]


def send(part, partner):
    pairs = [(place, place ^ partner) for place in range(lax.axis_size("tok"))]
    return lax.ppermute(part, "tok", pairs)


def sigmoid(value):
    return 0.5 + 0.5 * jnp.tanh(0.5 * value)


def contract(first, second, dims):
    return lax.dot_general(first, second, (dims, ((), ())), preferred_element_type=jnp.float32)


NN = ((1,), (0,))
NT = ((1,), (1,))


def add_gradients(pair_refs, tok_rows, weight_ref, hidden, grad_ref):
    half = tok_rows // 2
    head_size = weight_ref.shape[-1]
    first_weight = weight_ref[0, hidden]
    third_weight = weight_ref[1, hidden]
    down_turned = weight_ref[2].astype(jnp.float32).T[hidden].astype(jnp.bfloat16)
    step = 2 if len(pair_refs) % 2 == 0 else 1
    for start in range(0, len(pair_refs), step):
        key_parts, target_parts = [], []
        for pair_ref in pair_refs[start : start + step]:
            key_parts.extend(part_halves(pair_ref[0:half, :], head_size))
            target_parts.extend(part_halves(pair_ref[half:tok_rows, :], head_size))
        key_rows = jnp.concatenate(key_parts, axis=0)
        target = jnp.concatenate(target_parts, axis=0)
        first_pre = contract(first_weight, key_rows, NT)
        third_pre = contract(third_weight, key_rows, NT)
        hidden_grad = contract(down_turned, target, NT)
        sigmoid_first = sigmoid(first_pre)
        activated = first_pre * sigmoid_first
        mixed = (activated * third_pre).astype(jnp.bfloat16)
        grad_first_in = (
            hidden_grad * third_pre * sigmoid_first * (1.0 + first_pre * (1.0 - sigmoid_first))
        ).astype(jnp.bfloat16)
        grad_third_in = (hidden_grad * activated).astype(jnp.bfloat16)
        grads = (
            contract(grad_first_in, key_rows, NN),
            contract(grad_third_in, key_rows, NN),
            contract(mixed, target, NN),
        )
        for index, grad in enumerate(grads):
            if start == 0:
                grad_ref[index, :, 0:head_size] = grad
            else:
                grad_ref[index, :, 0:head_size] += grad


def mirror_kernel(count, tok_rows, first, *refs):
    pair_refs, (weight_ref, out_ref, grad_ref) = refs[:count], refs[-3:]
    head_size = weight_ref.shape[-1]
    full = head_size // LANES
    tail = head_size - full * LANES
    units = grad_ref.shape[1]
    half = units // 2
    add_gradients(pair_refs, tok_rows, weight_ref, slice(first, first + units), grad_ref)

    def tiles_of(index, rows):
        return [
            grad_ref[index, rows, tile * LANES : (tile + 1) * LANES] for tile in range(full + 1)
        ]

    both = join_halves(tiles_of(0, slice(0, units)), tiles_of(1, slice(0, units)), tail)
    down = join_halves(tiles_of(2, slice(0, half)), tiles_of(2, slice(half, units)), tail)
    for tile, (above, below) in enumerate(zip(both, down)):
        lanes = slice(tile * LANES, (tile + 1) * LANES)
        out_ref[0:units, lanes] = above.astype(jnp.bfloat16)
        out_ref[units : units + half, lanes] = below.astype(jnp.bfloat16)


def own_kernel(tok_rows, *refs):
    pair_refs, (weight_ref, out_ref) = refs[:-2], refs[-2:]
    add_gradients(pair_refs, tok_rows, weight_ref, slice(0, weight_ref.shape[-1]), out_ref)


def renorm(weight_ref, grad_ref, mirror_refs, out_ref):
    head_size = weight_ref.shape[-1]
    units = head_size // len(mirror_refs)
    firsts, thirds, downs = [], [], []
    for mirror_ref in mirror_refs:
        first, third = part_halves(mirror_ref[0:units, :], head_size)
        firsts.append(first)
        thirds.append(third)
        downs.extend(part_halves(mirror_ref[units:, :], head_size))
    first, third, down = (jnp.concatenate(parts, axis=0) for parts in (firsts, thirds, downs))
    for index, other in enumerate((first, third, down)):
        before = weight_ref[index].astype(jnp.float32)
        axis = 1
        if index == 2:
            before = before.T
            axis = 0
        grad = grad_ref[index, :, 0:head_size] + other.astype(jnp.float32)
        updated = before - grad
        scale_old = jnp.sqrt(jnp.mean(before * before, axis=axis, keepdims=True) + epsilon)
        scale_new = jnp.sqrt(jnp.mean(updated * updated, axis=axis, keepdims=True) + epsilon)
        out_ref[index] = (updated * (scale_old / scale_new)).astype(jnp.bfloat16)


def apply_kernel(height, frames_here, shards, order_ref, *refs):
    near_refs, far_refs = refs[: shards // 2], refs[shards // 2 : shards]
    before_ref, grad_ref, *mirror_refs = refs[shards:-6]
    gain_ref, tap_ref, out_ref = refs[-6:-3]
    weight_ref, grid_ref, turned_ref = refs[-3:]
    half = far_refs[0].shape[0] // 2
    query_parts = [ref[ref.shape[0] - half :, :] for ref in near_refs]
    for index, ref in enumerate(far_refs):
        query_parts.append(ref[index % 2 * half : (index % 2 + 1) * half, :])
    renorm(before_ref, grad_ref, mirror_refs, weight_ref)
    width = 2 * half // height
    head_size = weight_ref.shape[-1]
    full = head_size // LANES
    tail = head_size - full * LANES
    top = 8
    edge = jnp.zeros((top, LANES), jnp.float32)
    whole = jnp.zeros(grid_ref.shape[3:], jnp.float32)
    for shard in range(shards):
        for tile in range(full + 1):
            grid_ref[shard, tile, 0] = whole
            grid_ref[shard, tile, width + 1] = whole
            for column in range(1, width + 1):
                grid_ref[shard, tile, column, 0:top] = edge
                grid_ref[shard, tile, column, top + height :] = edge
    gain = gain_ref[...]
    for shard in range(shards):
        rows = jnp.concatenate(part_halves(query_parts[shard], head_size), axis=0)
        proj_first = contract(rows, weight_ref[0], NT)
        proj_third = contract(rows, weight_ref[1], NT)
        mixed = (proj_first * jax.nn.sigmoid(proj_first) * proj_third).astype(jnp.bfloat16)
        outputs = contract(mixed, weight_ref[2], NN)
        scale = lax.rsqrt(jnp.mean(outputs * outputs, axis=-1, keepdims=True) + epsilon)
        normed = (outputs * scale * gain).astype(jnp.bfloat16).astype(jnp.float32)
        frame = order_ref[shard]
        block = frame // frames_here
        slot = frame % frames_here
        for tile in range(full + 1):
            lanes = slice(tile * LANES, min((tile + 1) * LANES, head_size))
            for column in range(width):
                grid_ref[shard, tile, column + 1, top : top + height, 0 : lanes.stop - lanes.start] = (
                    normed[column * height : (column + 1) * height, lanes]
                )
            taps = [
                tap_ref[index : index + 1, tile * LANES : (tile + 1) * LANES] for index in range(9)
            ]
            for column in range(width):
                total = None
                for row_tap in range(3):
                    first = top + row_tap - 1
                    for col_tap in range(3):
                        term = taps[row_tap * 3 + col_tap] * grid_ref[
                            shard, tile, column + col_tap, first : first + height, :
                        ]
                        total = term if total is None else total + term
                turned_ref[
                    block, column, tile, pl.ds(slot, height, stride=frames_here), :
                ] = total
    blocks = turned_ref.shape[0]
    side_rows = out_ref.shape[1]
    for block in range(blocks):
        for column in range(width):
            sides = [
                [
                    turned_ref[block, column, tile, side * side_rows : (side + 1) * side_rows, :]
                    for tile in range(full + 1)
                ]
                for side in range(2)
            ]
            for tile, part in enumerate(join_halves(sides[0], sides[1], tail)):
                out_ref[column * blocks + block, :, tile * LANES : (tile + 1) * LANES] = part.astype(
                    jnp.bfloat16
                )


def gate_kernel(blocks, conv_ref, gate_ref, out_ref):
    chunks, side_rows, _ = conv_ref.shape
    height, frames_here, channels = gate_ref.shape
    head_size = channels // chunks
    shards = chunks // blocks
    rows_here = height // 2
    for pair in range(chunks // 2):
        lanes = slice(pair * 2 * head_size, (pair + 1) * 2 * head_size)
        halves = []
        for head in (2 * pair, 2 * pair + 1):
            chunk = (head % shards) * blocks + head // shards
            halves.append(part_halves(conv_ref[chunk].astype(jnp.float32), head_size))
        for side in range(2):
            conv = jnp.concatenate([halves[0][side], halves[1][side]], axis=1)
            gate = gate_ref[side * rows_here : (side + 1) * rows_here, :, lanes].astype(jnp.float32)
            conv = conv.reshape(rows_here, frames_here, 2 * head_size)
            out_ref[side * rows_here : (side + 1) * rows_here, :, lanes] = (
                conv * (gate * sigmoid(gate))
            ).astype(jnp.bfloat16)


def in_vmem(count):
    return [pl.BlockSpec(memory_space=pltpu.VMEM)] * count


def call(kernel, out, operands, scratch=(), specs=None, leave=True):
    specs = specs or in_vmem(len(operands))
    operands = [
        pltpu.with_memory_space_constraint(item, pltpu.VMEM)
        if spec.memory_space == pltpu.VMEM
        else item
        for item, spec in zip(operands, specs)
    ]
    if leave:
        out = jax.tree.map(lambda item: pltpu.VMEM(item.shape, item.dtype), out)
    return pl.pallas_call(
        kernel,
        out_shape=out,
        in_specs=specs,
        out_specs=jax.tree.map(lambda _: pl.BlockSpec(memory_space=pltpu.VMEM), out),
        scratch_shapes=scratch,
        compiler_params=pltpu.CompilerParams(vmem_limit_bytes=VMEM_BYTES),
        cost_estimate=pl.CostEstimate(flops=0, bytes_accessed=0, transcendentals=0),
    )(*operands)


def after(part, *earlier):
    anywhere = pl.BlockSpec(memory_space=pl.ANY)
    return pl.pallas_call(
        lambda *refs: None,
        out_shape=jax.ShapeDtypeStruct(part.shape, part.dtype),
        in_specs=[anywhere] * (1 + len(earlier)),
        out_specs=anywhere,
        input_output_aliases={0: 0},
        compiler_params=pltpu.CompilerParams(vmem_limit_bytes=1024 * 1024),
        cost_estimate=pl.CostEstimate(flops=0, bytes_accessed=0, transcendentals=0),
    )(part, *earlier)


def by_heads(
    queries, keys, values, rates, fast_weights, norm_gain, frame_order, gate_input, conv_weights
):
    tok_rows = queries.shape[0]
    head_count = queries.shape[1] * queries.shape[2]
    head_size = queries.shape[3]
    height, frames_here = gate_input.shape[:2]
    shards = lax.axis_size("tok")
    blocks = lax.axis_size("head")
    half = tok_rows // 2
    wide = 2 * head_size
    tiles = head_size // LANES + 1
    own = lax.axis_index("tok")
    own_channel = lax.axis_index("head") * head_count + own

    def rows_of(array):
        return array.reshape(tok_rows, head_count, head_size)

    def own_of(array, place):
        return lax.dynamic_index_in_dim(array, place, 0, keepdims=False)

    line = shards // 2
    tile_scratch = pltpu.VMEM((tiles, tok_rows * head_count, LANES), jnp.float32)
    token_rates = rates.reshape(head_count, tok_rows)
    chips = line // 2

    one = jax.ShapeDtypeStruct((tok_rows, wide), jnp.bfloat16)
    mirrored = call(
        pack_mirror_kernel,
        [one] * line,
        (rows_of(keys), rows_of(values), token_rates),
        (tile_scratch, tile_scratch),
    )
    mirrored = [mirrored[0]] + [send(mirrored[k], k) for k in range(1, line)]
    across = call(
        functools.partial(pack_across_kernel, height),
        [one] * chips,
        (rows_of(queries),),
        (tile_scratch,),
    )
    across_landed = [send(part, line + 2 * index) for index, part in enumerate(across)]
    weights = fast_weights.reshape(head_count, 3, head_size, head_size)
    own_weights = own_of(weights, own)
    mirror_weights = own_of(weights, own ^ line)
    own_gain = own_of(norm_gain.reshape(head_count, 1, head_size), own)
    taps = conv_weights.reshape(9, blocks * head_count, head_size)
    own_taps = lax.dynamic_index_in_dim(taps, own_channel, 1, keepdims=False)
    own_taps = jnp.pad(own_taps, ((0, 0), (0, tiles * LANES - head_size)))
    early = (across[0], own_weights, mirror_weights, own_gain, own_taps)
    packed = call(
        functools.partial(pack_near_kernel, height, len(early)),
        [jax.ShapeDtypeStruct((tok_rows + half, wide), jnp.bfloat16)] * line,
        (rows_of(keys), rows_of(values), token_rates, rows_of(queries), *early),
        (tile_scratch, tile_scratch, tile_scratch),
        specs=in_vmem(4) + [pl.BlockSpec(memory_space=pl.ANY)] * len(early),
    )
    held = [after(part, *mirrored[1:], *across_landed) for part in packed[1:]]
    near = [packed[0]] + [send(held[k - 1], k) for k in range(1, line)]
    frames = frame_order[own ^ jnp.arange(shards, dtype=jnp.int32)]
    grad_shape = (3, head_size, tiles * LANES)
    ahead = (*across_landed, *held)
    units = head_size // 2
    crossed = []
    for first in range(0, head_size, units):
        part = call(
            functools.partial(mirror_kernel, line, tok_rows, first),
            jax.ShapeDtypeStruct((units + units // 2, wide), jnp.bfloat16),
            (*mirrored, *ahead, mirror_weights),
            (pltpu.VMEM((3, units, tiles * LANES), jnp.float32),),
            specs=in_vmem(line) + [pl.BlockSpec(memory_space=pl.ANY)] * len(ahead) + in_vmem(1),
        )
        crossed.append(send(part, line))
    gradients = call(
        functools.partial(own_kernel, tok_rows),
        jax.ShapeDtypeStruct(grad_shape, jnp.float32),
        (*near, own_weights),
    )
    across = relay([after(part, gradients) for part in across_landed])
    side_rows = frames_here * height // 2
    outgoing = call(
        functools.partial(apply_kernel, height, frames_here, shards),
        jax.ShapeDtypeStruct((shards * blocks, side_rows, wide), jnp.bfloat16),
        (frames, *near, *across, own_weights, gradients, *crossed, own_gain, own_taps),
        (
            pltpu.VMEM((3, head_size, head_size), jnp.bfloat16),
            pltpu.VMEM((shards, tiles, shards + 2, height + 16, LANES), jnp.float32),
            pltpu.VMEM((blocks, shards, tiles, 2 * side_rows, LANES), jnp.float32),
        ),
        specs=[pl.BlockSpec(memory_space=pltpu.SMEM)] + in_vmem(shards + 6),
    )
    arrived = lax.all_to_all(outgoing, ("tok", "head"), split_axis=0, concat_axis=0, tiled=True)
    gate = gate_input.reshape(height, frames_here, gate_input.shape[3])
    gated = call(
        functools.partial(gate_kernel, blocks),
        jax.ShapeDtypeStruct(gate.shape, jnp.bfloat16),
        (arrived, gate),
        leave=False,
    )
    return gated.reshape(gate_input.shape)


def fits_by_heads(queries, gate_input, frame_order):
    tok_rows, head_size = queries.shape[0], queries.shape[3]
    head_count = queries.shape[1] * queries.shape[2]
    height, frames_here, col_width = gate_input.shape[:3]
    shards = lax.axis_size("tok")
    return (
        head_count == shards
        and frame_order.shape[0] == shards
        and lax.axis_size("tile") == 1
        and col_width == 1
        and shards % 2 == 0
        and shards & (shards - 1) == 0
        and head_size % LANES == LANES // 2
        and height % 8 == 0
        and tok_rows == height * shards
        and tok_rows % 32 == 0
        and head_size % 64 == 0
        and frames_here * height % 32 == 0
        and frames_here * lax.axis_size("head") == shards
        and lax.axis_size("head") & (lax.axis_size("head") - 1) == 0
    )


def renormed(previous, gradient):
    before = previous.astype(jnp.float32)
    updated = before - gradient
    scale_old = jnp.sqrt(jnp.mean(before * before, axis=-1, keepdims=True) + epsilon)
    scale_new = jnp.sqrt(jnp.mean(updated * updated, axis=-1, keepdims=True) + epsilon)
    return (updated * (scale_old / scale_new)).astype(jnp.bfloat16)


def by_tokens(
    queries, keys, values, rates, fast_weights, norm_gain, frame_order, gate_input, conv_weights
):
    tok_rows = queries.shape[0]
    head_count = queries.shape[1] * queries.shape[2]
    head_size = queries.shape[3]
    query_rows = queries.reshape(tok_rows, head_count, head_size)
    key_rows = keys.reshape(tok_rows, head_count, head_size)
    value_rows = values.reshape(tok_rows, head_count, head_size)
    token_rates = rates.reshape(head_count, tok_rows)
    weights = fast_weights.reshape(head_count, 3, head_size, head_size)
    head_gains = norm_gain.reshape(head_count, head_size)
    first_pre = jnp.einsum(
        "thd,hfd->htf", key_rows, weights[:, 0], preferred_element_type=jnp.float32
    )
    third_pre = jnp.einsum(
        "thd,hfd->htf", key_rows, weights[:, 1], preferred_element_type=jnp.float32
    )
    sigmoid_first = jax.nn.sigmoid(first_pre)
    activated = first_pre * sigmoid_first
    hidden = (activated * third_pre).astype(jnp.bfloat16)
    target = (-token_rates.T[:, :, None] * value_rows.astype(jnp.float32)).astype(jnp.bfloat16)
    grad_down = jnp.einsum("thd,htf->hdf", target, hidden, preferred_element_type=jnp.float32)
    hidden_grad = jnp.einsum(
        "thd,hdf->htf", target, weights[:, 2], preferred_element_type=jnp.float32
    )
    grad_first_in = (
        hidden_grad * third_pre * sigmoid_first * (1.0 + first_pre * (1.0 - sigmoid_first))
    ).astype(jnp.bfloat16)
    grad_third_in = (hidden_grad * activated).astype(jnp.bfloat16)
    grad_first = jnp.einsum(
        "htf,thd->hfd", grad_first_in, key_rows, preferred_element_type=jnp.float32
    )
    grad_third = jnp.einsum(
        "htf,thd->hfd", grad_third_in, key_rows, preferred_element_type=jnp.float32
    )
    gradients = jnp.stack([grad_first, grad_third, grad_down], axis=1)
    row_share = lax.psum_scatter(gradients, "tok", scatter_dimension=2, tiled=True)
    row_count = row_share.shape[2]
    own_rows = lax.dynamic_slice_in_dim(weights, lax.axis_index("tok") * row_count, row_count, 2)
    updated = lax.all_gather(renormed(own_rows, row_share), "tok", axis=2, tiled=True)
    proj_first = jnp.einsum(
        "thd,hfd->thf", query_rows, updated[:, 0], preferred_element_type=jnp.float32
    )
    proj_third = jnp.einsum(
        "thd,hfd->thf", query_rows, updated[:, 1], preferred_element_type=jnp.float32
    )
    mixed_hidden = (jax.nn.silu(proj_first) * proj_third).astype(jnp.bfloat16)
    outputs = jnp.einsum(
        "thf,hdf->thd", mixed_hidden, updated[:, 2], preferred_element_type=jnp.float32
    )
    normed = (
        outputs
        * lax.rsqrt(jnp.mean(outputs * outputs, axis=-1, keepdims=True) + epsilon)
        * head_gains[None]
    )
    normed = normed.astype(jnp.bfloat16)
    height = gate_input.shape[0]
    col_width = gate_input.shape[2]
    shards = lax.axis_size("tok")
    full_width = col_width * shards
    channels_here = head_count * head_size
    frame_grid = normed.reshape(height, full_width, channels_here)
    own_taps = lax.dynamic_slice_in_dim(
        conv_weights, lax.axis_index("head") * channels_here, channels_here, 2
    )
    padded = jnp.pad(frame_grid, ((1, 1), (1, 1), (0, 0)))
    local_sum = jnp.zeros((height, full_width, channels_here), jnp.float32)
    for row_tap in range(3):
        for col_tap in range(3):
            local_sum = local_sum + own_taps[row_tap, col_tap] * padded[
                row_tap : row_tap + height, col_tap : col_tap + full_width
            ].astype(jnp.float32)
    outgoing = local_sum.astype(jnp.bfloat16).reshape(height, shards, col_width, channels_here)
    arrived = lax.all_to_all(outgoing, "tok", split_axis=1, concat_axis=1, tiled=True)
    frame_count = frame_order.shape[0]
    numbers = jnp.arange(frame_count, dtype=jnp.int32)
    inverse = jnp.sum(
        jnp.where(frame_order[None, :] == numbers[:, None], numbers[None, :], 0), axis=1
    )
    ordered = jnp.take(arrived, inverse, axis=1)
    tile_block = lax.all_to_all(ordered, "head", split_axis=1, concat_axis=3, tiled=True)
    return (tile_block.astype(jnp.float32) * jax.nn.silu(gate_input.astype(jnp.float32))).astype(
        jnp.bfloat16
    )


def local(queries, keys, values, rates, fast_weights, norm_gain, frame_order, gate_input, conv_weights):
    args = (
        queries, keys, values, rates, fast_weights, norm_gain, frame_order, gate_input, conv_weights
    )
    if fits_by_heads(queries, gate_input, frame_order):
        return by_heads(*args)
    return by_tokens(*args)


def solution(mesh):
    in_specs = (
        P(("groups", "tok"), "tile", "head", None),
        P(("groups", "tok"), "tile", "head", None),
        P(("groups", "tok"), "tile", "head", None),
        P("tile", "head", ("groups", "tok")),
        P("tile", "head", None, None, None),
        P("tile", "head", None),
        P("groups"),
        P(None, ("groups", "head"), "tok", "tile"),
        P(None, None, "tile"),
    )
    out_specs = P(None, ("groups", "head"), "tok", "tile")
    return jax.shard_map(local, mesh=mesh, in_specs=in_specs, out_specs=out_specs, check_vma=False)
```

```python
import functools

import jax
import jax.numpy as jnp
from jax import lax
from jax.experimental import pallas as pl
from jax.experimental.pallas import tpu as pltpu
from jax.sharding import PartitionSpec as P

epsilon = 1e-06
LANES = 128
VMEM_BYTES = 16 * 1024 * 1024


def split_lanes(source, scratch, rows, head_size):
    full = head_size // LANES
    tail = head_size - full * LANES
    wide = source.reshape(rows, head_size).astype(jnp.float32)
    for tile in range(full):
        scratch[tile] = wide[:, tile * LANES : (tile + 1) * LANES]
    scratch[full, :, 0:tail] = wide[:, full * LANES :]


def join_halves(first, second, tail):
    lane = lax.broadcasted_iota(jnp.int32, first[-1].shape, 1)
    middle = jnp.where(lane < tail, first[-1], pltpu.roll(second[-1], tail, 1))
    return first[:-1] + [middle] + second[:-1]


def part_halves(packed, head_size):
    full = head_size // LANES
    tail = head_size - full * LANES
    first = packed[:, :head_size]
    middle = packed[:, head_size : (full + 1) * LANES]
    second = jnp.concatenate([packed[:, (full + 1) * LANES :], middle], axis=1)
    return first, second


def partner_head(partner):
    return lax.axis_index("tok") ^ partner


def pack_pairs(head, rate_ref, key_tiles, value_tiles, out_ref, start, head_size):
    heads, tok_rows = rate_ref.shape
    half = tok_rows // 2
    full = head_size // LANES
    tail = head_size - full * LANES
    rate_row = -rate_ref[pl.ds(head, 1), :]
    rates = jnp.broadcast_to(rate_row, (LANES, tok_rows)).T
    for row, tiles in ((start, key_tiles), (start + half, value_tiles)):
        sides = []
        for side in range(2):
            parts = [
                tiles[tile, pl.ds(side * half * heads + head, half, stride=heads), :]
                for tile in range(full + 1)
            ]
            if tiles is value_tiles:
                rate = rates[side * half : (side + 1) * half]
                parts = [rate * part for part in parts]
            sides.append(parts)
        for tile, part in enumerate(join_halves(sides[0], sides[1], tail)):
            out_ref[row : row + half, tile * LANES : (tile + 1) * LANES] = part.astype(jnp.bfloat16)


def pack_query(head, heads, height, query_tiles, out_ref, start, head_size):
    tok_rows = query_tiles.shape[1] // heads
    half = tok_rows // 2
    width = tok_rows // height
    full = head_size // LANES
    tail = head_size - full * LANES
    sides = []
    for side in range(2):
        sides.append(
            [
                jnp.concatenate(
                    [
                        query_tiles[
                            tile, pl.ds(column * heads + head, height, stride=width * heads), :
                        ]
                        for column in range(side * width // 2, (side + 1) * width // 2)
                    ],
                    axis=0,
                )
                for tile in range(full + 1)
            ]
        )
    for tile, part in enumerate(join_halves(sides[0], sides[1], tail)):
        out_ref[start : start + half, tile * LANES : (tile + 1) * LANES] = part.astype(jnp.bfloat16)


def pack_mirror_kernel(key_ref, value_ref, rate_ref, *rest):
    outs, (key_tiles, value_tiles) = rest[:-2], rest[-2:]
    tok_rows, heads, head_size = key_ref.shape
    split_lanes(key_ref[...], key_tiles, tok_rows * heads, head_size)
    split_lanes(value_ref[...], value_tiles, tok_rows * heads, head_size)
    for partner, out_ref in enumerate(outs):
        head = partner_head(partner ^ (heads // 2))
        pack_pairs(head, rate_ref, key_tiles, value_tiles, out_ref, 0, head_size)


def pack_across_kernel(height, query_ref, *rest):
    outs, query_tiles = rest[:-1], rest[-1]
    tok_rows, heads, head_size = query_ref.shape
    half = tok_rows // 2
    line = heads // 2
    split_lanes(query_ref[...], query_tiles, tok_rows * heads, head_size)
    for partner in range(line):
        head = partner_head(partner ^ line)
        if partner < line - 2:
            out_ref, start = outs[partner // 2], partner % 2 * half
        else:
            out_ref, start = outs[partner - line], 0
        pack_query(head, heads, height, query_tiles, out_ref, start, head_size)


def pack_near_kernel(height, unread, key_ref, value_ref, rate_ref, query_ref, *rest):
    outs, (key_tiles, value_tiles, query_tiles) = rest[unread:-3], rest[-3:]
    tok_rows, heads, head_size = key_ref.shape
    split_lanes(key_ref[...], key_tiles, tok_rows * heads, head_size)
    split_lanes(value_ref[...], value_tiles, tok_rows * heads, head_size)
    split_lanes(query_ref[...], query_tiles, tok_rows * heads, head_size)
    for partner, out_ref in enumerate(outs):
        head = partner_head(partner)
        pack_pairs(head, rate_ref, key_tiles, value_tiles, out_ref, 0, head_size)
        pack_query(head, heads, height, query_tiles, out_ref, tok_rows, head_size)


def relay(landed):
    return [part for one in landed for part in (one, send(one, 1))]


def send(part, partner):
    pairs = [(place, place ^ partner) for place in range(lax.axis_size("tok"))]
    return lax.ppermute(part, "tok", pairs)


def sigmoid(value):
    return 0.5 + 0.5 * jnp.tanh(0.5 * value)


def contract(first, second, dims):
    return lax.dot_general(first, second, (dims, ((), ())), preferred_element_type=jnp.float32)


NN = ((1,), (0,))
NT = ((1,), (1,))


def add_gradients(pair_refs, tok_rows, weight_ref, hidden, grad_ref):
    half = tok_rows // 2
    head_size = weight_ref.shape[-1]
    first_weight = weight_ref[0, hidden]
    third_weight = weight_ref[1, hidden]
    down_turned = weight_ref[2].astype(jnp.float32).T[hidden].astype(jnp.bfloat16)
    step = 2 if len(pair_refs) % 2 == 0 else 1
    for start in range(0, len(pair_refs), step):
        key_parts, target_parts = [], []
        for pair_ref in pair_refs[start : start + step]:
            key_parts.extend(part_halves(pair_ref[0:half, :], head_size))
            target_parts.extend(part_halves(pair_ref[half:tok_rows, :], head_size))
        key_rows = jnp.concatenate(key_parts, axis=0)
        target = jnp.concatenate(target_parts, axis=0)
        first_pre = contract(first_weight, key_rows, NT)
        third_pre = contract(third_weight, key_rows, NT)
        hidden_grad = contract(down_turned, target, NT)
        sigmoid_first = sigmoid(first_pre)
        activated = first_pre * sigmoid_first
        mixed = (activated * third_pre).astype(jnp.bfloat16)
        grad_first_in = (
            hidden_grad * third_pre * sigmoid_first * (1.0 + first_pre * (1.0 - sigmoid_first))
        ).astype(jnp.bfloat16)
        grad_third_in = (hidden_grad * activated).astype(jnp.bfloat16)
        grads = (
            contract(grad_first_in, key_rows, NN),
            contract(grad_third_in, key_rows, NN),
            contract(mixed, target, NN),
        )
        for index, grad in enumerate(grads):
            if start == 0:
                grad_ref[index, :, 0:head_size] = grad
            else:
                grad_ref[index, :, 0:head_size] += grad


def mirror_kernel(count, tok_rows, first, *refs):
    pair_refs, (weight_ref, out_ref, grad_ref) = refs[:count], refs[-3:]
    head_size = weight_ref.shape[-1]
    full = head_size // LANES
    tail = head_size - full * LANES
    units = grad_ref.shape[1]
    half = units // 2
    add_gradients(pair_refs, tok_rows, weight_ref, slice(first, first + units), grad_ref)

    def tiles_of(index, rows):
        return [
            grad_ref[index, rows, tile * LANES : (tile + 1) * LANES] for tile in range(full + 1)
        ]

    both = join_halves(tiles_of(0, slice(0, units)), tiles_of(1, slice(0, units)), tail)
    down = join_halves(tiles_of(2, slice(0, half)), tiles_of(2, slice(half, units)), tail)
    for tile, (above, below) in enumerate(zip(both, down)):
        lanes = slice(tile * LANES, (tile + 1) * LANES)
        out_ref[0:units, lanes] = above.astype(jnp.bfloat16)
        out_ref[units : units + half, lanes] = below.astype(jnp.bfloat16)


def own_kernel(tok_rows, unread, *refs):
    pair_refs, (weight_ref, out_ref) = refs[unread:-2], refs[-2:]
    add_gradients(pair_refs, tok_rows, weight_ref, slice(0, weight_ref.shape[-1]), out_ref)


def renorm(weight_ref, grad_ref, mirror_refs, out_ref):
    head_size = weight_ref.shape[-1]
    units = head_size // len(mirror_refs)
    firsts, thirds, downs = [], [], []
    for mirror_ref in mirror_refs:
        first, third = part_halves(mirror_ref[0:units, :], head_size)
        firsts.append(first)
        thirds.append(third)
        downs.extend(part_halves(mirror_ref[units:, :], head_size))
    first, third, down = (jnp.concatenate(parts, axis=0) for parts in (firsts, thirds, downs))
    for index, other in enumerate((first, third, down)):
        before = weight_ref[index].astype(jnp.float32)
        axis = 1
        if index == 2:
            before = before.T
            axis = 0
        grad = grad_ref[index, :, 0:head_size] + other.astype(jnp.float32)
        updated = before - grad
        scale_old = jnp.sqrt(jnp.mean(before * before, axis=axis, keepdims=True) + epsilon)
        scale_new = jnp.sqrt(jnp.mean(updated * updated, axis=axis, keepdims=True) + epsilon)
        out_ref[index] = (updated * (scale_old / scale_new)).astype(jnp.bfloat16)


def apply_kernel(height, frames_here, shards, order_ref, *refs):
    near_refs, far_refs = refs[: shards // 2], refs[shards // 2 : shards]
    before_ref, grad_ref, *mirror_refs = refs[shards:-6]
    gain_ref, tap_ref, out_ref = refs[-6:-3]
    weight_ref, grid_ref, turned_ref = refs[-3:]
    half = far_refs[-1].shape[0]
    query_parts = [ref[ref.shape[0] - half :, :] for ref in near_refs]
    for index, ref in enumerate(far_refs):
        start = index % 2 * half if ref.shape[0] > half else 0
        query_parts.append(ref[start : start + half, :])
    renorm(before_ref, grad_ref, mirror_refs, weight_ref)
    width = 2 * half // height
    head_size = weight_ref.shape[-1]
    full = head_size // LANES
    tail = head_size - full * LANES
    top = 8
    edge = jnp.zeros((top, LANES), jnp.float32)
    whole = jnp.zeros(grid_ref.shape[3:], jnp.float32)
    for shard in range(shards):
        for tile in range(full + 1):
            grid_ref[shard, tile, 0] = whole
            grid_ref[shard, tile, width + 1] = whole
            for column in range(1, width + 1):
                grid_ref[shard, tile, column, 0:top] = edge
                grid_ref[shard, tile, column, top + height :] = edge
    gain = gain_ref[...]
    for shard in range(shards):
        rows = jnp.concatenate(part_halves(query_parts[shard], head_size), axis=0)
        proj_first = contract(rows, weight_ref[0], NT)
        proj_third = contract(rows, weight_ref[1], NT)
        mixed = (proj_first * jax.nn.sigmoid(proj_first) * proj_third).astype(jnp.bfloat16)
        outputs = contract(mixed, weight_ref[2], NN)
        scale = lax.rsqrt(jnp.mean(outputs * outputs, axis=-1, keepdims=True) + epsilon)
        normed = (outputs * scale * gain).astype(jnp.bfloat16).astype(jnp.float32)
        frame = order_ref[shard]
        block = frame // frames_here
        slot = frame % frames_here
        for tile in range(full + 1):
            lanes = slice(tile * LANES, min((tile + 1) * LANES, head_size))
            for column in range(width):
                grid_ref[shard, tile, column + 1, top : top + height, 0 : lanes.stop - lanes.start] = (
                    normed[column * height : (column + 1) * height, lanes]
                )
            taps = [
                tap_ref[index : index + 1, tile * LANES : (tile + 1) * LANES] for index in range(9)
            ]
            for column in range(width):
                total = None
                for row_tap in range(3):
                    first = top + row_tap - 1
                    for col_tap in range(3):
                        term = taps[row_tap * 3 + col_tap] * grid_ref[
                            shard, tile, column + col_tap, first : first + height, :
                        ]
                        total = term if total is None else total + term
                turned_ref[
                    block, column, tile, pl.ds(slot, height, stride=frames_here), :
                ] = total
    blocks = turned_ref.shape[0]
    side_rows = out_ref.shape[1]
    for block in range(blocks):
        for column in range(width):
            sides = [
                [
                    turned_ref[block, column, tile, side * side_rows : (side + 1) * side_rows, :]
                    for tile in range(full + 1)
                ]
                for side in range(2)
            ]
            for tile, part in enumerate(join_halves(sides[0], sides[1], tail)):
                out_ref[column * blocks + block, :, tile * LANES : (tile + 1) * LANES] = part.astype(
                    jnp.bfloat16
                )


def gate_kernel(blocks, conv_ref, gate_ref, out_ref):
    chunks, side_rows, _ = conv_ref.shape
    height, frames_here, channels = gate_ref.shape
    head_size = channels // chunks
    shards = chunks // blocks
    rows_here = height // 2
    for pair in range(chunks // 2):
        lanes = slice(pair * 2 * head_size, (pair + 1) * 2 * head_size)
        halves = []
        for head in (2 * pair, 2 * pair + 1):
            chunk = (head % shards) * blocks + head // shards
            halves.append(part_halves(conv_ref[chunk].astype(jnp.float32), head_size))
        for side in range(2):
            conv = jnp.concatenate([halves[0][side], halves[1][side]], axis=1)
            gate = gate_ref[side * rows_here : (side + 1) * rows_here, :, lanes].astype(jnp.float32)
            conv = conv.reshape(rows_here, frames_here, 2 * head_size)
            out_ref[side * rows_here : (side + 1) * rows_here, :, lanes] = (
                conv * (gate * sigmoid(gate))
            ).astype(jnp.bfloat16)


def in_vmem(count):
    return [pl.BlockSpec(memory_space=pltpu.VMEM)] * count


def call(kernel, out, operands, scratch=(), specs=None, leave=True):
    specs = specs or in_vmem(len(operands))
    operands = [
        pltpu.with_memory_space_constraint(item, pltpu.VMEM)
        if spec.memory_space == pltpu.VMEM
        else item
        for item, spec in zip(operands, specs)
    ]
    if leave:
        out = jax.tree.map(lambda item: pltpu.VMEM(item.shape, item.dtype), out)
    return pl.pallas_call(
        kernel,
        out_shape=out,
        in_specs=specs,
        out_specs=jax.tree.map(lambda _: pl.BlockSpec(memory_space=pltpu.VMEM), out),
        scratch_shapes=scratch,
        compiler_params=pltpu.CompilerParams(vmem_limit_bytes=VMEM_BYTES),
        cost_estimate=pl.CostEstimate(flops=0, bytes_accessed=0, transcendentals=0),
    )(*operands)


def after(part, *earlier):
    anywhere = pl.BlockSpec(memory_space=pl.ANY)
    return pl.pallas_call(
        lambda *refs: None,
        out_shape=jax.ShapeDtypeStruct(part.shape, part.dtype),
        in_specs=[anywhere] * (1 + len(earlier)),
        out_specs=anywhere,
        input_output_aliases={0: 0},
        compiler_params=pltpu.CompilerParams(vmem_limit_bytes=1024 * 1024),
        cost_estimate=pl.CostEstimate(flops=0, bytes_accessed=0, transcendentals=0),
    )(part, *earlier)


def by_heads(
    queries, keys, values, rates, fast_weights, norm_gain, frame_order, gate_input, conv_weights
):
    tok_rows = queries.shape[0]
    head_count = queries.shape[1] * queries.shape[2]
    head_size = queries.shape[3]
    height, frames_here = gate_input.shape[:2]
    shards = lax.axis_size("tok")
    blocks = lax.axis_size("head")
    half = tok_rows // 2
    wide = 2 * head_size
    tiles = head_size // LANES + 1
    own = lax.axis_index("tok")
    own_channel = lax.axis_index("head") * head_count + own

    def rows_of(array):
        return array.reshape(tok_rows, head_count, head_size)

    def own_of(array, place):
        return lax.dynamic_index_in_dim(array, place, 0, keepdims=False)

    line = shards // 2
    tile_scratch = pltpu.VMEM((tiles, tok_rows * head_count, LANES), jnp.float32)
    token_rates = rates.reshape(head_count, tok_rows)
    chips = line // 2

    one = jax.ShapeDtypeStruct((tok_rows, wide), jnp.bfloat16)
    mirrored = call(
        pack_mirror_kernel,
        [one] * line,
        (rows_of(keys), rows_of(values), token_rates),
        (tile_scratch, tile_scratch),
    )
    mirrored = [mirrored[0]] + [send(mirrored[k], k) for k in range(1, line)]
    across = call(
        functools.partial(pack_across_kernel, height),
        [one] * (chips - 1) + [jax.ShapeDtypeStruct((half, wide), jnp.bfloat16)] * 2,
        (rows_of(queries),),
        (tile_scratch,),
    )
    across_landed = [send(part, line + 2 * index) for index, part in enumerate(across[:-1])]
    weights = fast_weights.reshape(head_count, 3, head_size, head_size)
    own_weights = own_of(weights, own)
    mirror_weights = own_of(weights, own ^ line)
    own_gain = own_of(norm_gain.reshape(head_count, 1, head_size), own)
    taps = conv_weights.reshape(9, blocks * head_count, head_size)
    own_taps = lax.dynamic_index_in_dim(taps, own_channel, 1, keepdims=False)
    own_taps = jnp.pad(own_taps, ((0, 0), (0, tiles * LANES - head_size)))
    early = (across[0], own_weights, mirror_weights, own_gain, own_taps)
    packed = call(
        functools.partial(pack_near_kernel, height, len(early)),
        [jax.ShapeDtypeStruct((tok_rows + half, wide), jnp.bfloat16)] * line,
        (rows_of(keys), rows_of(values), token_rates, rows_of(queries), *early),
        (tile_scratch, tile_scratch, tile_scratch),
        specs=in_vmem(4) + [pl.BlockSpec(memory_space=pl.ANY)] * len(early),
    )
    held = [after(part, *mirrored[1:], *across_landed) for part in packed[1:]]
    near = [packed[0]] + [send(held[k - 1], k) for k in range(1, line)]
    last_held = after(across[-1], *mirrored[1:], *across_landed)
    last_landed = send(last_held, shards - 1)
    frames = frame_order[own ^ jnp.arange(shards, dtype=jnp.int32)]
    grad_shape = (3, head_size, tiles * LANES)
    ahead = (last_held, *held)
    units = head_size // 2
    crossed = []
    for first in range(0, head_size, units):
        part = call(
            functools.partial(mirror_kernel, line, tok_rows, first),
            jax.ShapeDtypeStruct((units + units // 2, wide), jnp.bfloat16),
            (*mirrored, *ahead, mirror_weights),
            (pltpu.VMEM((3, units, tiles * LANES), jnp.float32),),
            specs=in_vmem(line) + [pl.BlockSpec(memory_space=pl.ANY)] * len(ahead) + in_vmem(1),
        )
        crossed.append(send(part, line))
        ahead = (last_landed,)
    gradients = call(
        functools.partial(own_kernel, tok_rows, 1),
        jax.ShapeDtypeStruct(grad_shape, jnp.float32),
        (last_landed, *near, own_weights),
        specs=[pl.BlockSpec(memory_space=pl.ANY)] + in_vmem(line + 1),
    )
    across = relay([after(part, gradients) for part in across_landed[:-1]])
    across += [across_landed[-1], last_landed]
    side_rows = frames_here * height // 2
    outgoing = call(
        functools.partial(apply_kernel, height, frames_here, shards),
        jax.ShapeDtypeStruct((shards * blocks, side_rows, wide), jnp.bfloat16),
        (frames, *near, *across, own_weights, gradients, *crossed, own_gain, own_taps),
        (
            pltpu.VMEM((3, head_size, head_size), jnp.bfloat16),
            pltpu.VMEM((shards, tiles, shards + 2, height + 16, LANES), jnp.float32),
            pltpu.VMEM((blocks, shards, tiles, 2 * side_rows, LANES), jnp.float32),
        ),
        specs=[pl.BlockSpec(memory_space=pltpu.SMEM)] + in_vmem(shards + 4 + len(crossed)),
    )
    arrived = lax.all_to_all(outgoing, ("tok", "head"), split_axis=0, concat_axis=0, tiled=True)
    gate = gate_input.reshape(height, frames_here, gate_input.shape[3])
    gated = call(
        functools.partial(gate_kernel, blocks),
        jax.ShapeDtypeStruct(gate.shape, jnp.bfloat16),
        (arrived, gate),
        leave=False,
    )
    return gated.reshape(gate_input.shape)


def fits_by_heads(queries, gate_input, frame_order):
    tok_rows, head_size = queries.shape[0], queries.shape[3]
    head_count = queries.shape[1] * queries.shape[2]
    height, frames_here, col_width = gate_input.shape[:3]
    shards = lax.axis_size("tok")
    return (
        head_count == shards
        and frame_order.shape[0] == shards
        and lax.axis_size("tile") == 1
        and col_width == 1
        and shards % 2 == 0
        and shards & (shards - 1) == 0
        and head_size % LANES == LANES // 2
        and height % 8 == 0
        and tok_rows == height * shards
        and tok_rows % 32 == 0
        and head_size % 64 == 0
        and frames_here * height % 32 == 0
        and frames_here * lax.axis_size("head") == shards
        and lax.axis_size("head") & (lax.axis_size("head") - 1) == 0
    )


def renormed(previous, gradient):
    before = previous.astype(jnp.float32)
    updated = before - gradient
    scale_old = jnp.sqrt(jnp.mean(before * before, axis=-1, keepdims=True) + epsilon)
    scale_new = jnp.sqrt(jnp.mean(updated * updated, axis=-1, keepdims=True) + epsilon)
    return (updated * (scale_old / scale_new)).astype(jnp.bfloat16)


def by_tokens(
    queries, keys, values, rates, fast_weights, norm_gain, frame_order, gate_input, conv_weights
):
    tok_rows = queries.shape[0]
    head_count = queries.shape[1] * queries.shape[2]
    head_size = queries.shape[3]
    query_rows = queries.reshape(tok_rows, head_count, head_size)
    key_rows = keys.reshape(tok_rows, head_count, head_size)
    value_rows = values.reshape(tok_rows, head_count, head_size)
    token_rates = rates.reshape(head_count, tok_rows)
    weights = fast_weights.reshape(head_count, 3, head_size, head_size)
    head_gains = norm_gain.reshape(head_count, head_size)
    first_pre = jnp.einsum(
        "thd,hfd->htf", key_rows, weights[:, 0], preferred_element_type=jnp.float32
    )
    third_pre = jnp.einsum(
        "thd,hfd->htf", key_rows, weights[:, 1], preferred_element_type=jnp.float32
    )
    sigmoid_first = jax.nn.sigmoid(first_pre)
    activated = first_pre * sigmoid_first
    hidden = (activated * third_pre).astype(jnp.bfloat16)
    target = (-token_rates.T[:, :, None] * value_rows.astype(jnp.float32)).astype(jnp.bfloat16)
    grad_down = jnp.einsum("thd,htf->hdf", target, hidden, preferred_element_type=jnp.float32)
    hidden_grad = jnp.einsum(
        "thd,hdf->htf", target, weights[:, 2], preferred_element_type=jnp.float32
    )
    grad_first_in = (
        hidden_grad * third_pre * sigmoid_first * (1.0 + first_pre * (1.0 - sigmoid_first))
    ).astype(jnp.bfloat16)
    grad_third_in = (hidden_grad * activated).astype(jnp.bfloat16)
    grad_first = jnp.einsum(
        "htf,thd->hfd", grad_first_in, key_rows, preferred_element_type=jnp.float32
    )
    grad_third = jnp.einsum(
        "htf,thd->hfd", grad_third_in, key_rows, preferred_element_type=jnp.float32
    )
    gradients = jnp.stack([grad_first, grad_third, grad_down], axis=1)
    row_share = lax.psum_scatter(gradients, "tok", scatter_dimension=2, tiled=True)
    row_count = row_share.shape[2]
    own_rows = lax.dynamic_slice_in_dim(weights, lax.axis_index("tok") * row_count, row_count, 2)
    updated = lax.all_gather(renormed(own_rows, row_share), "tok", axis=2, tiled=True)
    proj_first = jnp.einsum(
        "thd,hfd->thf", query_rows, updated[:, 0], preferred_element_type=jnp.float32
    )
    proj_third = jnp.einsum(
        "thd,hfd->thf", query_rows, updated[:, 1], preferred_element_type=jnp.float32
    )
    mixed_hidden = (jax.nn.silu(proj_first) * proj_third).astype(jnp.bfloat16)
    outputs = jnp.einsum(
        "thf,hdf->thd", mixed_hidden, updated[:, 2], preferred_element_type=jnp.float32
    )
    normed = (
        outputs
        * lax.rsqrt(jnp.mean(outputs * outputs, axis=-1, keepdims=True) + epsilon)
        * head_gains[None]
    )
    normed = normed.astype(jnp.bfloat16)
    height = gate_input.shape[0]
    col_width = gate_input.shape[2]
    shards = lax.axis_size("tok")
    full_width = col_width * shards
    channels_here = head_count * head_size
    frame_grid = normed.reshape(height, full_width, channels_here)
    own_taps = lax.dynamic_slice_in_dim(
        conv_weights, lax.axis_index("head") * channels_here, channels_here, 2
    )
    padded = jnp.pad(frame_grid, ((1, 1), (1, 1), (0, 0)))
    local_sum = jnp.zeros((height, full_width, channels_here), jnp.float32)
    for row_tap in range(3):
        for col_tap in range(3):
            local_sum = local_sum + own_taps[row_tap, col_tap] * padded[
                row_tap : row_tap + height, col_tap : col_tap + full_width
            ].astype(jnp.float32)
    outgoing = local_sum.astype(jnp.bfloat16).reshape(height, shards, col_width, channels_here)
    arrived = lax.all_to_all(outgoing, "tok", split_axis=1, concat_axis=1, tiled=True)
    frame_count = frame_order.shape[0]
    numbers = jnp.arange(frame_count, dtype=jnp.int32)
    inverse = jnp.sum(
        jnp.where(frame_order[None, :] == numbers[:, None], numbers[None, :], 0), axis=1
    )
    ordered = jnp.take(arrived, inverse, axis=1)
    tile_block = lax.all_to_all(ordered, "head", split_axis=1, concat_axis=3, tiled=True)
    return (tile_block.astype(jnp.float32) * jax.nn.silu(gate_input.astype(jnp.float32))).astype(
        jnp.bfloat16
    )


def local(queries, keys, values, rates, fast_weights, norm_gain, frame_order, gate_input, conv_weights):
    args = (
        queries, keys, values, rates, fast_weights, norm_gain, frame_order, gate_input, conv_weights
    )
    if fits_by_heads(queries, gate_input, frame_order):
        return by_heads(*args)
    return by_tokens(*args)


def solution(mesh):
    in_specs = (
        P(("groups", "tok"), "tile", "head", None),
        P(("groups", "tok"), "tile", "head", None),
        P(("groups", "tok"), "tile", "head", None),
        P("tile", "head", ("groups", "tok")),
        P("tile", "head", None, None, None),
        P("tile", "head", None),
        P("groups"),
        P(None, ("groups", "head"), "tok", "tile"),
        P(None, None, "tile"),
    )
    out_specs = P(None, ("groups", "head"), "tok", "tile")
    return jax.shard_map(local, mesh=mesh, in_specs=in_specs, out_specs=out_specs, check_vma=False)
```

```python
import functools

import jax
import jax.numpy as jnp
from jax import lax
from jax.experimental import pallas as pl
from jax.experimental.pallas import tpu as pltpu
from jax.sharding import PartitionSpec as P

epsilon = 1e-06
LANES = 128
VMEM_BYTES = 24 * 1024 * 1024


def split_lanes(source, scratch, rows, head_size):
    full = head_size // LANES
    tail = head_size - full * LANES
    wide = source.reshape(rows, head_size).astype(jnp.float32)
    for tile in range(full):
        scratch[tile] = wide[:, tile * LANES : (tile + 1) * LANES]
    scratch[full, :, 0:tail] = wide[:, full * LANES :]


def join_halves(first, second, tail):
    lane = lax.broadcasted_iota(jnp.int32, first[-1].shape, 1)
    middle = jnp.where(lane < tail, first[-1], pltpu.roll(second[-1], tail, 1))
    return first[:-1] + [middle] + second[:-1]


def part_halves(packed, head_size):
    full = head_size // LANES
    tail = head_size - full * LANES
    first = packed[:, :head_size]
    middle = packed[:, head_size : (full + 1) * LANES]
    second = jnp.concatenate([packed[:, (full + 1) * LANES :], middle], axis=1)
    return first, second


def partner_head(partner):
    return lax.axis_index("tok") ^ partner


def pack_pairs(head, rate_ref, key_tiles, value_tiles, out_ref, start, head_size):
    heads, tok_rows = rate_ref.shape
    half = tok_rows // 2
    full = head_size // LANES
    tail = head_size - full * LANES
    rate_row = -rate_ref[pl.ds(head, 1), :]
    rates = jnp.broadcast_to(rate_row, (LANES, tok_rows)).T
    for row, tiles in ((start, key_tiles), (start + half, value_tiles)):
        sides = []
        for side in range(2):
            parts = [
                tiles[tile, pl.ds(side * half * heads + head, half, stride=heads), :]
                for tile in range(full + 1)
            ]
            if tiles is value_tiles:
                rate = rates[side * half : (side + 1) * half]
                parts = [rate * part for part in parts]
            sides.append(parts)
        for tile, part in enumerate(join_halves(sides[0], sides[1], tail)):
            out_ref[row : row + half, tile * LANES : (tile + 1) * LANES] = part.astype(jnp.bfloat16)


def pack_query(head, heads, height, query_tiles, out_ref, start, head_size):
    tok_rows = query_tiles.shape[1] // heads
    half = tok_rows // 2
    width = tok_rows // height
    full = head_size // LANES
    tail = head_size - full * LANES
    sides = []
    for side in range(2):
        sides.append(
            [
                jnp.concatenate(
                    [
                        query_tiles[
                            tile, pl.ds(column * heads + head, height, stride=width * heads), :
                        ]
                        for column in range(side * width // 2, (side + 1) * width // 2)
                    ],
                    axis=0,
                )
                for tile in range(full + 1)
            ]
        )
    for tile, part in enumerate(join_halves(sides[0], sides[1], tail)):
        out_ref[start : start + half, tile * LANES : (tile + 1) * LANES] = part.astype(jnp.bfloat16)


def pack_mirror_kernel(key_ref, value_ref, rate_ref, *rest):
    outs, (key_tiles, value_tiles) = rest[:-2], rest[-2:]
    tok_rows, heads, head_size = key_ref.shape
    split_lanes(key_ref[...], key_tiles, tok_rows * heads, head_size)
    split_lanes(value_ref[...], value_tiles, tok_rows * heads, head_size)
    for partner, out_ref in enumerate(outs):
        head = partner_head(partner ^ (heads // 2))
        pack_pairs(head, rate_ref, key_tiles, value_tiles, out_ref, 0, head_size)


def pack_across_kernel(height, query_ref, *rest):
    outs, query_tiles = rest[:-1], rest[-1]
    tok_rows, heads, head_size = query_ref.shape
    half = tok_rows // 2
    split_lanes(query_ref[...], query_tiles, tok_rows * heads, head_size)
    for partner in range(heads // 2):
        head = partner_head(partner ^ (heads // 2))
        start = partner % 2 * half
        pack_query(head, heads, height, query_tiles, outs[partner // 2], start, head_size)


def pack_near_kernel(height, unread, key_ref, value_ref, rate_ref, query_ref, *rest):
    outs, (key_tiles, value_tiles, query_tiles) = rest[unread:-3], rest[-3:]
    tok_rows, heads, head_size = key_ref.shape
    split_lanes(key_ref[...], key_tiles, tok_rows * heads, head_size)
    split_lanes(value_ref[...], value_tiles, tok_rows * heads, head_size)
    split_lanes(query_ref[...], query_tiles, tok_rows * heads, head_size)
    for partner, out_ref in enumerate(outs):
        head = partner_head(partner)
        pack_pairs(head, rate_ref, key_tiles, value_tiles, out_ref, 0, head_size)
        pack_query(head, heads, height, query_tiles, out_ref, tok_rows, head_size)


def relay(landed):
    return [part for one in landed for part in (one, send(one, 1))]


def send(part, partner):
    pairs = [(place, place ^ partner) for place in range(lax.axis_size("tok"))]
    return lax.ppermute(part, "tok", pairs)


def sigmoid(value):
    return 0.5 + 0.5 * jnp.tanh(0.5 * value)


def contract(first, second, dims):
    return lax.dot_general(first, second, (dims, ((), ())), preferred_element_type=jnp.float32)


NN = ((1,), (0,))
NT = ((1,), (1,))


def add_gradients(pair_refs, tok_rows, weight_ref, prior_ref, grad_ref):
    half = tok_rows // 2
    head_size = weight_ref.shape[-1]
    first_weight = weight_ref[0]
    third_weight = weight_ref[1]
    down_turned = weight_ref[2].astype(jnp.float32).T.astype(jnp.bfloat16)
    step = 2 if len(pair_refs) % 2 == 0 else 1
    for start in range(0, len(pair_refs), step):
        key_parts, target_parts = [], []
        for pair_ref in pair_refs[start : start + step]:
            key_parts.extend(part_halves(pair_ref[0:half, :], head_size))
            target_parts.extend(part_halves(pair_ref[half:tok_rows, :], head_size))
        key_rows = jnp.concatenate(key_parts, axis=0)
        target = jnp.concatenate(target_parts, axis=0)
        first_pre = contract(first_weight, key_rows, NT)
        third_pre = contract(third_weight, key_rows, NT)
        hidden_grad = contract(down_turned, target, NT)
        sigmoid_first = sigmoid(first_pre)
        activated = first_pre * sigmoid_first
        mixed = (activated * third_pre).astype(jnp.bfloat16)
        grad_first_in = (
            hidden_grad * third_pre * sigmoid_first * (1.0 + first_pre * (1.0 - sigmoid_first))
        ).astype(jnp.bfloat16)
        grad_third_in = (hidden_grad * activated).astype(jnp.bfloat16)
        grads = (
            contract(grad_first_in, key_rows, NN),
            contract(grad_third_in, key_rows, NN),
            contract(mixed, target, NN),
        )
        for index, grad in enumerate(grads):
            if start == 0 and prior_ref is None:
                grad_ref[index, :, 0:head_size] = grad
            elif start == 0:
                grad_ref[index, :, 0:head_size] = prior_ref[index, :, 0:head_size] + grad
            else:
                grad_ref[index, :, 0:head_size] += grad


def sum_kernel(count, tok_rows, prior, *refs):
    pair_refs, weight_ref, out_ref = refs[:count], refs[count], refs[-1]
    prior_ref = refs[count + 1] if prior else None
    add_gradients(pair_refs, tok_rows, weight_ref, prior_ref, out_ref)


def mirror_kernel(count, tok_rows, *refs):
    pair_refs, weight_ref, prior_ref = refs[:count], refs[count], refs[count + 1]
    out_ref, grad_ref = refs[-2:]
    head_size = weight_ref.shape[-1]
    full = head_size // LANES
    tail = head_size - full * LANES
    half = head_size // 2
    add_gradients(pair_refs, tok_rows, weight_ref, prior_ref, grad_ref)

    def tiles_of(index, rows):
        return [
            grad_ref[index, rows, tile * LANES : (tile + 1) * LANES] for tile in range(full + 1)
        ]

    both = join_halves(tiles_of(0, slice(0, head_size)), tiles_of(1, slice(0, head_size)), tail)
    down = join_halves(tiles_of(2, slice(0, half)), tiles_of(2, slice(half, head_size)), tail)
    for tile, (above, below) in enumerate(zip(both, down)):
        lanes = slice(tile * LANES, (tile + 1) * LANES)
        out_ref[0:head_size, lanes] = above.astype(jnp.bfloat16)
        out_ref[head_size : head_size + half, lanes] = below.astype(jnp.bfloat16)


def renorm(weight_ref, grad_ref, mirror_refs, out_ref):
    head_size = weight_ref.shape[-1]
    units = head_size // len(mirror_refs)
    firsts, thirds, downs = [], [], []
    for mirror_ref in mirror_refs:
        first, third = part_halves(mirror_ref[0:units, :], head_size)
        firsts.append(first)
        thirds.append(third)
        downs.extend(part_halves(mirror_ref[units:, :], head_size))
    first, third, down = (jnp.concatenate(parts, axis=0) for parts in (firsts, thirds, downs))
    for index, other in enumerate((first, third, down)):
        before = weight_ref[index].astype(jnp.float32)
        axis = 1
        if index == 2:
            before = before.T
            axis = 0
        grad = grad_ref[index, :, 0:head_size] + other.astype(jnp.float32)
        updated = before - grad
        scale_old = jnp.sqrt(jnp.mean(before * before, axis=axis, keepdims=True) + epsilon)
        scale_new = jnp.sqrt(jnp.mean(updated * updated, axis=axis, keepdims=True) + epsilon)
        out_ref[index] = (updated * (scale_old / scale_new)).astype(jnp.bfloat16)


def apply_kernel(height, frames_here, shards, order_ref, *refs):
    near_refs, far_refs = refs[: shards // 2], refs[shards // 2 : shards]
    before_ref, grad_ref, *mirror_refs = refs[shards:-6]
    gain_ref, tap_ref, out_ref = refs[-6:-3]
    weight_ref, grid_ref, turned_ref = refs[-3:]
    half = far_refs[0].shape[0] // 2
    query_parts = [ref[ref.shape[0] - half :, :] for ref in near_refs]
    for index, ref in enumerate(far_refs):
        query_parts.append(ref[index % 2 * half : (index % 2 + 1) * half, :])
    renorm(before_ref, grad_ref, mirror_refs, weight_ref)
    width = 2 * half // height
    head_size = weight_ref.shape[-1]
    full = head_size // LANES
    tail = head_size - full * LANES
    top = 8
    edge = jnp.zeros((top, LANES), jnp.float32)
    whole = jnp.zeros(grid_ref.shape[3:], jnp.float32)
    for shard in range(shards):
        for tile in range(full + 1):
            grid_ref[shard, tile, 0] = whole
            grid_ref[shard, tile, width + 1] = whole
            for column in range(1, width + 1):
                grid_ref[shard, tile, column, 0:top] = edge
                grid_ref[shard, tile, column, top + height :] = edge
    gain = gain_ref[...]
    for shard in range(shards):
        rows = jnp.concatenate(part_halves(query_parts[shard], head_size), axis=0)
        proj_first = contract(rows, weight_ref[0], NT)
        proj_third = contract(rows, weight_ref[1], NT)
        mixed = (proj_first * jax.nn.sigmoid(proj_first) * proj_third).astype(jnp.bfloat16)
        outputs = contract(mixed, weight_ref[2], NN)
        scale = lax.rsqrt(jnp.mean(outputs * outputs, axis=-1, keepdims=True) + epsilon)
        normed = (outputs * scale * gain).astype(jnp.bfloat16).astype(jnp.float32)
        frame = order_ref[shard]
        block = frame // frames_here
        slot = frame % frames_here
        for tile in range(full + 1):
            lanes = slice(tile * LANES, min((tile + 1) * LANES, head_size))
            for column in range(width):
                grid_ref[shard, tile, column + 1, top : top + height, 0 : lanes.stop - lanes.start] = (
                    normed[column * height : (column + 1) * height, lanes]
                )
            taps = [
                tap_ref[index : index + 1, tile * LANES : (tile + 1) * LANES] for index in range(9)
            ]
            for column in range(width):
                total = None
                for row_tap in range(3):
                    first = top + row_tap - 1
                    for col_tap in range(3):
                        term = taps[row_tap * 3 + col_tap] * grid_ref[
                            shard, tile, column + col_tap, first : first + height, :
                        ]
                        total = term if total is None else total + term
                turned_ref[
                    block, column, tile, pl.ds(slot, height, stride=frames_here), :
                ] = total
    blocks = turned_ref.shape[0]
    side_rows = out_ref.shape[1]
    for block in range(blocks):
        for column in range(width):
            sides = [
                [
                    turned_ref[block, column, tile, side * side_rows : (side + 1) * side_rows, :]
                    for tile in range(full + 1)
                ]
                for side in range(2)
            ]
            for tile, part in enumerate(join_halves(sides[0], sides[1], tail)):
                out_ref[column * blocks + block, :, tile * LANES : (tile + 1) * LANES] = part.astype(
                    jnp.bfloat16
                )


def gate_kernel(blocks, conv_ref, gate_ref, out_ref):
    chunks, side_rows, _ = conv_ref.shape
    height, frames_here, channels = gate_ref.shape
    head_size = channels // chunks
    shards = chunks // blocks
    rows_here = height // 2
    for pair in range(chunks // 2):
        lanes = slice(pair * 2 * head_size, (pair + 1) * 2 * head_size)
        halves = []
        for head in (2 * pair, 2 * pair + 1):
            chunk = (head % shards) * blocks + head // shards
            halves.append(part_halves(conv_ref[chunk].astype(jnp.float32), head_size))
        for side in range(2):
            conv = jnp.concatenate([halves[0][side], halves[1][side]], axis=1)
            gate = gate_ref[side * rows_here : (side + 1) * rows_here, :, lanes].astype(jnp.float32)
            conv = conv.reshape(rows_here, frames_here, 2 * head_size)
            out_ref[side * rows_here : (side + 1) * rows_here, :, lanes] = (
                conv * (gate * sigmoid(gate))
            ).astype(jnp.bfloat16)


def in_vmem(count):
    return [pl.BlockSpec(memory_space=pltpu.VMEM)] * count


def call(kernel, out, operands, scratch=(), specs=None, leave=True):
    specs = specs or in_vmem(len(operands))
    operands = [
        pltpu.with_memory_space_constraint(item, pltpu.VMEM)
        if spec.memory_space == pltpu.VMEM
        else item
        for item, spec in zip(operands, specs)
    ]
    if leave:
        out = jax.tree.map(lambda item: pltpu.VMEM(item.shape, item.dtype), out)
    return pl.pallas_call(
        kernel,
        out_shape=out,
        in_specs=specs,
        out_specs=jax.tree.map(lambda _: pl.BlockSpec(memory_space=pltpu.VMEM), out),
        scratch_shapes=scratch,
        compiler_params=pltpu.CompilerParams(vmem_limit_bytes=VMEM_BYTES),
        cost_estimate=pl.CostEstimate(flops=0, bytes_accessed=0, transcendentals=0),
    )(*operands)


def after(part, *earlier):
    anywhere = pl.BlockSpec(memory_space=pl.ANY)
    return pl.pallas_call(
        lambda *refs: None,
        out_shape=jax.ShapeDtypeStruct(part.shape, part.dtype),
        in_specs=[anywhere] * (1 + len(earlier)),
        out_specs=anywhere,
        input_output_aliases={0: 0},
        compiler_params=pltpu.CompilerParams(vmem_limit_bytes=1024 * 1024),
        cost_estimate=pl.CostEstimate(flops=0, bytes_accessed=0, transcendentals=0),
    )(part, *earlier)


def by_heads(
    queries, keys, values, rates, fast_weights, norm_gain, frame_order, gate_input, conv_weights
):
    tok_rows = queries.shape[0]
    head_count = queries.shape[1] * queries.shape[2]
    head_size = queries.shape[3]
    height, frames_here = gate_input.shape[:2]
    shards = lax.axis_size("tok")
    blocks = lax.axis_size("head")
    half = tok_rows // 2
    wide = 2 * head_size
    tiles = head_size // LANES + 1
    own = lax.axis_index("tok")
    own_channel = lax.axis_index("head") * head_count + own

    def rows_of(array):
        return array.reshape(tok_rows, head_count, head_size)

    def own_of(array, place):
        return lax.dynamic_index_in_dim(array, place, 0, keepdims=False)

    line = shards // 2
    tile_scratch = pltpu.VMEM((tiles, tok_rows * head_count, LANES), jnp.float32)
    token_rates = rates.reshape(head_count, tok_rows)
    chips = line // 2

    one = jax.ShapeDtypeStruct((tok_rows, wide), jnp.bfloat16)
    mirrored = call(
        pack_mirror_kernel,
        [one] * line,
        (rows_of(keys), rows_of(values), token_rates),
        (tile_scratch, tile_scratch),
    )
    mirrored = [mirrored[0]] + [send(mirrored[k], k) for k in range(1, line)]
    across = call(
        functools.partial(pack_across_kernel, height),
        [one] * chips,
        (rows_of(queries),),
        (tile_scratch,),
    )
    across_landed = [send(part, line + 2 * index) for index, part in enumerate(across)]
    weights = fast_weights.reshape(head_count, 3, head_size, head_size)
    own_weights = own_of(weights, own)
    mirror_weights = own_of(weights, own ^ line)
    own_gain = own_of(norm_gain.reshape(head_count, 1, head_size), own)
    taps = conv_weights.reshape(9, blocks * head_count, head_size)
    own_taps = lax.dynamic_index_in_dim(taps, own_channel, 1, keepdims=False)
    own_taps = jnp.pad(own_taps, ((0, 0), (0, tiles * LANES - head_size)))
    frames = frame_order[own ^ jnp.arange(shards, dtype=jnp.int32)]
    grad_shape = (3, head_size, tiles * LANES)
    grad_struct = jax.ShapeDtypeStruct(grad_shape, jnp.float32)
    unread = pl.BlockSpec(memory_space=pl.ANY)
    mirror_sum = call(
        functools.partial(sum_kernel, 2, tok_rows, False),
        grad_struct,
        (*mirrored[:2], mirror_weights),
    )
    early = (across[0], own_weights, own_gain, own_taps, frames, mirror_sum)
    packed = call(
        functools.partial(pack_near_kernel, height, len(early)),
        [jax.ShapeDtypeStruct((tok_rows + half, wide), jnp.bfloat16)] * line,
        (rows_of(keys), rows_of(values), token_rates, rows_of(queries), *early),
        (tile_scratch, tile_scratch, tile_scratch),
        specs=in_vmem(4) + [unread] * len(early),
    )
    held = [after(part, *mirrored[1:], *across_landed) for part in packed[1:]]
    near = [packed[0]] + [send(held[k - 1], k) for k in range(1, line)]
    ahead = (*across_landed, *held)
    crossing = call(
        functools.partial(mirror_kernel, line - 2, tok_rows),
        jax.ShapeDtypeStruct((head_size + head_size // 2, wide), jnp.bfloat16),
        (*mirrored[2:], mirror_weights, mirror_sum, *ahead),
        (pltpu.VMEM(grad_shape, jnp.float32),),
        specs=in_vmem(line) + [unread] * len(ahead),
    )
    crossed = send(crossing, line)
    own_sum = call(
        functools.partial(sum_kernel, 2, tok_rows, False),
        grad_struct,
        (*near[:2], own_weights, crossing),
        specs=in_vmem(3) + [unread],
    )
    across = relay([after(part, own_sum) for part in across_landed])
    gradients = call(
        functools.partial(sum_kernel, line - 2, tok_rows, True),
        grad_struct,
        (*near[2:], own_weights, own_sum),
    )
    side_rows = frames_here * height // 2
    outgoing = call(
        functools.partial(apply_kernel, height, frames_here, shards),
        jax.ShapeDtypeStruct((shards * blocks, side_rows, wide), jnp.bfloat16),
        (frames, *near, *across, own_weights, gradients, crossed, own_gain, own_taps),
        (
            pltpu.VMEM((3, head_size, head_size), jnp.bfloat16),
            pltpu.VMEM((shards, tiles, shards + 2, height + 16, LANES), jnp.float32),
            pltpu.VMEM((blocks, shards, tiles, 2 * side_rows, LANES), jnp.float32),
        ),
        specs=[pl.BlockSpec(memory_space=pltpu.SMEM)] + in_vmem(shards + 5),
    )
    arrived = lax.all_to_all(outgoing, ("tok", "head"), split_axis=0, concat_axis=0, tiled=True)
    gate = gate_input.reshape(height, frames_here, gate_input.shape[3])
    gated = call(
        functools.partial(gate_kernel, blocks),
        jax.ShapeDtypeStruct(gate.shape, jnp.bfloat16),
        (arrived, gate),
        leave=False,
    )
    return gated.reshape(gate_input.shape)


def fits_by_heads(queries, gate_input, frame_order):
    tok_rows, head_size = queries.shape[0], queries.shape[3]
    head_count = queries.shape[1] * queries.shape[2]
    height, frames_here, col_width = gate_input.shape[:3]
    shards = lax.axis_size("tok")
    return (
        head_count == shards
        and frame_order.shape[0] == shards
        and lax.axis_size("tile") == 1
        and col_width == 1
        and shards >= 8
        and shards & (shards - 1) == 0
        and head_size % LANES == LANES // 2
        and height % 8 == 0
        and tok_rows == height * shards
        and tok_rows % 32 == 0
        and head_size % 64 == 0
        and frames_here * height % 32 == 0
        and frames_here * lax.axis_size("head") == shards
        and lax.axis_size("head") & (lax.axis_size("head") - 1) == 0
    )


def renormed(previous, gradient):
    before = previous.astype(jnp.float32)
    updated = before - gradient
    scale_old = jnp.sqrt(jnp.mean(before * before, axis=-1, keepdims=True) + epsilon)
    scale_new = jnp.sqrt(jnp.mean(updated * updated, axis=-1, keepdims=True) + epsilon)
    return (updated * (scale_old / scale_new)).astype(jnp.bfloat16)


def by_tokens(
    queries, keys, values, rates, fast_weights, norm_gain, frame_order, gate_input, conv_weights
):
    tok_rows = queries.shape[0]
    head_count = queries.shape[1] * queries.shape[2]
    head_size = queries.shape[3]
    query_rows = queries.reshape(tok_rows, head_count, head_size)
    key_rows = keys.reshape(tok_rows, head_count, head_size)
    value_rows = values.reshape(tok_rows, head_count, head_size)
    token_rates = rates.reshape(head_count, tok_rows)
    weights = fast_weights.reshape(head_count, 3, head_size, head_size)
    head_gains = norm_gain.reshape(head_count, head_size)
    first_pre = jnp.einsum(
        "thd,hfd->htf", key_rows, weights[:, 0], preferred_element_type=jnp.float32
    )
    third_pre = jnp.einsum(
        "thd,hfd->htf", key_rows, weights[:, 1], preferred_element_type=jnp.float32
    )
    sigmoid_first = jax.nn.sigmoid(first_pre)
    activated = first_pre * sigmoid_first
    hidden = (activated * third_pre).astype(jnp.bfloat16)
    target = (-token_rates.T[:, :, None] * value_rows.astype(jnp.float32)).astype(jnp.bfloat16)
    grad_down = jnp.einsum("thd,htf->hdf", target, hidden, preferred_element_type=jnp.float32)
    hidden_grad = jnp.einsum(
        "thd,hdf->htf", target, weights[:, 2], preferred_element_type=jnp.float32
    )
    grad_first_in = (
        hidden_grad * third_pre * sigmoid_first * (1.0 + first_pre * (1.0 - sigmoid_first))
    ).astype(jnp.bfloat16)
    grad_third_in = (hidden_grad * activated).astype(jnp.bfloat16)
    grad_first = jnp.einsum(
        "htf,thd->hfd", grad_first_in, key_rows, preferred_element_type=jnp.float32
    )
    grad_third = jnp.einsum(
        "htf,thd->hfd", grad_third_in, key_rows, preferred_element_type=jnp.float32
    )
    gradients = jnp.stack([grad_first, grad_third, grad_down], axis=1)
    row_share = lax.psum_scatter(gradients, "tok", scatter_dimension=2, tiled=True)
    row_count = row_share.shape[2]
    own_rows = lax.dynamic_slice_in_dim(weights, lax.axis_index("tok") * row_count, row_count, 2)
    updated = lax.all_gather(renormed(own_rows, row_share), "tok", axis=2, tiled=True)
    proj_first = jnp.einsum(
        "thd,hfd->thf", query_rows, updated[:, 0], preferred_element_type=jnp.float32
    )
    proj_third = jnp.einsum(
        "thd,hfd->thf", query_rows, updated[:, 1], preferred_element_type=jnp.float32
    )
    mixed_hidden = (jax.nn.silu(proj_first) * proj_third).astype(jnp.bfloat16)
    outputs = jnp.einsum(
        "thf,hdf->thd", mixed_hidden, updated[:, 2], preferred_element_type=jnp.float32
    )
    normed = (
        outputs
        * lax.rsqrt(jnp.mean(outputs * outputs, axis=-1, keepdims=True) + epsilon)
        * head_gains[None]
    )
    normed = normed.astype(jnp.bfloat16)
    height = gate_input.shape[0]
    col_width = gate_input.shape[2]
    shards = lax.axis_size("tok")
    full_width = col_width * shards
    channels_here = head_count * head_size
    frame_grid = normed.reshape(height, full_width, channels_here)
    own_taps = lax.dynamic_slice_in_dim(
        conv_weights, lax.axis_index("head") * channels_here, channels_here, 2
    )
    padded = jnp.pad(frame_grid, ((1, 1), (1, 1), (0, 0)))
    local_sum = jnp.zeros((height, full_width, channels_here), jnp.float32)
    for row_tap in range(3):
        for col_tap in range(3):
            local_sum = local_sum + own_taps[row_tap, col_tap] * padded[
                row_tap : row_tap + height, col_tap : col_tap + full_width
            ].astype(jnp.float32)
    outgoing = local_sum.astype(jnp.bfloat16).reshape(height, shards, col_width, channels_here)
    arrived = lax.all_to_all(outgoing, "tok", split_axis=1, concat_axis=1, tiled=True)
    frame_count = frame_order.shape[0]
    numbers = jnp.arange(frame_count, dtype=jnp.int32)
    inverse = jnp.sum(
        jnp.where(frame_order[None, :] == numbers[:, None], numbers[None, :], 0), axis=1
    )
    ordered = jnp.take(arrived, inverse, axis=1)
    tile_block = lax.all_to_all(ordered, "head", split_axis=1, concat_axis=3, tiled=True)
    return (tile_block.astype(jnp.float32) * jax.nn.silu(gate_input.astype(jnp.float32))).astype(
        jnp.bfloat16
    )


def local(queries, keys, values, rates, fast_weights, norm_gain, frame_order, gate_input, conv_weights):
    args = (
        queries, keys, values, rates, fast_weights, norm_gain, frame_order, gate_input, conv_weights
    )
    if fits_by_heads(queries, gate_input, frame_order):
        return by_heads(*args)
    return by_tokens(*args)


def solution(mesh):
    in_specs = (
        P(("groups", "tok"), "tile", "head", None),
        P(("groups", "tok"), "tile", "head", None),
        P(("groups", "tok"), "tile", "head", None),
        P("tile", "head", ("groups", "tok")),
        P("tile", "head", None, None, None),
        P("tile", "head", None),
        P("groups"),
        P(None, ("groups", "head"), "tok", "tile"),
        P(None, None, "tile"),
    )
    out_specs = P(None, ("groups", "head"), "tok", "tile")
    return jax.shard_map(local, mesh=mesh, in_specs=in_specs, out_specs=out_specs, check_vma=False)
```

```python
import functools

import jax
import jax.numpy as jnp
from jax import lax
from jax.experimental import pallas as pl
from jax.experimental.pallas import tpu as pltpu
from jax.sharding import PartitionSpec as P

epsilon = 1e-06
LANES = 128
VMEM_BYTES = 24 * 1024 * 1024


def split_lanes(source, scratch, rows, head_size):
    full = head_size // LANES
    tail = head_size - full * LANES
    wide = source.reshape(rows, head_size).astype(jnp.float32)
    for tile in range(full):
        scratch[tile] = wide[:, tile * LANES : (tile + 1) * LANES]
    scratch[full, :, 0:tail] = wide[:, full * LANES :]


def join_halves(first, second, tail):
    lane = lax.broadcasted_iota(jnp.int32, first[-1].shape, 1)
    middle = jnp.where(lane < tail, first[-1], pltpu.roll(second[-1], tail, 1))
    return first[:-1] + [middle] + second[:-1]


def part_halves(packed, head_size):
    full = head_size // LANES
    tail = head_size - full * LANES
    first = packed[:, :head_size]
    middle = packed[:, head_size : (full + 1) * LANES]
    second = jnp.concatenate([packed[:, (full + 1) * LANES :], middle], axis=1)
    return first, second


def partner_head(partner):
    return lax.axis_index("tok") ^ partner


def pack_pairs(head, rate_ref, key_tiles, value_tiles, out_ref, start, head_size):
    heads, tok_rows = rate_ref.shape
    half = tok_rows // 2
    full = head_size // LANES
    tail = head_size - full * LANES
    rate_row = -rate_ref[pl.ds(head, 1), :]
    rates = jnp.broadcast_to(rate_row, (LANES, tok_rows)).T
    for row, tiles in ((start, key_tiles), (start + half, value_tiles)):
        sides = []
        for side in range(2):
            parts = [
                tiles[tile, pl.ds(side * half * heads + head, half, stride=heads), :]
                for tile in range(full + 1)
            ]
            if tiles is value_tiles:
                rate = rates[side * half : (side + 1) * half]
                parts = [rate * part for part in parts]
            sides.append(parts)
        for tile, part in enumerate(join_halves(sides[0], sides[1], tail)):
            out_ref[row : row + half, tile * LANES : (tile + 1) * LANES] = part.astype(jnp.bfloat16)


def pack_query(head, heads, height, query_tiles, out_ref, start, head_size):
    tok_rows = query_tiles.shape[1] // heads
    half = tok_rows // 2
    width = tok_rows // height
    full = head_size // LANES
    tail = head_size - full * LANES
    sides = []
    for side in range(2):
        sides.append(
            [
                jnp.concatenate(
                    [
                        query_tiles[
                            tile, pl.ds(column * heads + head, height, stride=width * heads), :
                        ]
                        for column in range(side * width // 2, (side + 1) * width // 2)
                    ],
                    axis=0,
                )
                for tile in range(full + 1)
            ]
        )
    for tile, part in enumerate(join_halves(sides[0], sides[1], tail)):
        out_ref[start : start + half, tile * LANES : (tile + 1) * LANES] = part.astype(jnp.bfloat16)


def pack_mirror_kernel(key_ref, value_ref, rate_ref, *rest):
    outs, (key_tiles, value_tiles) = rest[:-2], rest[-2:]
    tok_rows, heads, head_size = key_ref.shape
    split_lanes(key_ref[...], key_tiles, tok_rows * heads, head_size)
    split_lanes(value_ref[...], value_tiles, tok_rows * heads, head_size)
    for partner, out_ref in enumerate(outs):
        head = partner_head(partner ^ (heads // 2))
        pack_pairs(head, rate_ref, key_tiles, value_tiles, out_ref, 0, head_size)


def pack_across_kernel(height, query_ref, *rest):
    outs, query_tiles = rest[:-1], rest[-1]
    tok_rows, heads, head_size = query_ref.shape
    half = tok_rows // 2
    split_lanes(query_ref[...], query_tiles, tok_rows * heads, head_size)
    for partner in range(heads // 2):
        head = partner_head(partner ^ (heads // 2))
        start = partner % 2 * half
        pack_query(head, heads, height, query_tiles, outs[partner // 2], start, head_size)


def pack_near_kernel(height, unread, key_ref, value_ref, rate_ref, query_ref, *rest):
    outs, (key_tiles, value_tiles, query_tiles) = rest[unread:-3], rest[-3:]
    tok_rows, heads, head_size = key_ref.shape
    split_lanes(key_ref[...], key_tiles, tok_rows * heads, head_size)
    split_lanes(value_ref[...], value_tiles, tok_rows * heads, head_size)
    split_lanes(query_ref[...], query_tiles, tok_rows * heads, head_size)
    for partner, out_ref in enumerate(outs):
        head = partner_head(partner)
        pack_pairs(head, rate_ref, key_tiles, value_tiles, out_ref, 0, head_size)
        pack_query(head, heads, height, query_tiles, out_ref, tok_rows, head_size)


def send_far(part, partner, other):
    blocks = lax.axis_size("head")
    count = lax.axis_size("tok") * blocks
    pairs = [(place, place ^ (partner * blocks + other)) for place in range(count)]
    return lax.ppermute(part, ("tok", "head"), pairs)


def relay(landed):
    return [part for one in landed for part in (one, send(one, 1))]


def send(part, partner):
    pairs = [(place, place ^ partner) for place in range(lax.axis_size("tok"))]
    return lax.ppermute(part, "tok", pairs)


def sigmoid(value):
    return 0.5 + 0.5 * jnp.tanh(0.5 * value)


def contract(first, second, dims):
    return lax.dot_general(first, second, (dims, ((), ())), preferred_element_type=jnp.float32)


NN = ((1,), (0,))
NT = ((1,), (1,))


def add_gradients(pair_refs, tok_rows, weight_ref, prior_ref, grad_ref):
    half = tok_rows // 2
    head_size = weight_ref.shape[-1]
    first_weight = weight_ref[0]
    third_weight = weight_ref[1]
    down_turned = weight_ref[2].astype(jnp.float32).T.astype(jnp.bfloat16)
    step = 2 if len(pair_refs) % 2 == 0 else 1
    for start in range(0, len(pair_refs), step):
        key_parts, target_parts = [], []
        for pair_ref in pair_refs[start : start + step]:
            key_parts.extend(part_halves(pair_ref[0:half, :], head_size))
            target_parts.extend(part_halves(pair_ref[half:tok_rows, :], head_size))
        key_rows = jnp.concatenate(key_parts, axis=0)
        target = jnp.concatenate(target_parts, axis=0)
        first_pre = contract(first_weight, key_rows, NT)
        third_pre = contract(third_weight, key_rows, NT)
        hidden_grad = contract(down_turned, target, NT)
        sigmoid_first = sigmoid(first_pre)
        activated = first_pre * sigmoid_first
        mixed = (activated * third_pre).astype(jnp.bfloat16)
        grad_first_in = (
            hidden_grad * third_pre * sigmoid_first * (1.0 + first_pre * (1.0 - sigmoid_first))
        ).astype(jnp.bfloat16)
        grad_third_in = (hidden_grad * activated).astype(jnp.bfloat16)
        grads = (
            contract(grad_first_in, key_rows, NN),
            contract(grad_third_in, key_rows, NN),
            contract(mixed, target, NN),
        )
        for index, grad in enumerate(grads):
            if start == 0 and prior_ref is None:
                grad_ref[index, :, 0:head_size] = grad
            elif start == 0:
                grad_ref[index, :, 0:head_size] = prior_ref[index, :, 0:head_size] + grad
            else:
                grad_ref[index, :, 0:head_size] += grad


def sum_kernel(count, tok_rows, prior, *refs):
    pair_refs, weight_ref, out_ref = refs[:count], refs[count], refs[-1]
    prior_ref = refs[count + 1] if prior else None
    add_gradients(pair_refs, tok_rows, weight_ref, prior_ref, out_ref)


def mirror_kernel(count, tok_rows, *refs):
    pair_refs, weight_ref, prior_ref = refs[:count], refs[count], refs[count + 1]
    out_ref, grad_ref = refs[-2:]
    head_size = weight_ref.shape[-1]
    full = head_size // LANES
    tail = head_size - full * LANES
    half = head_size // 2
    add_gradients(pair_refs, tok_rows, weight_ref, prior_ref, grad_ref)

    def tiles_of(index, rows):
        return [
            grad_ref[index, rows, tile * LANES : (tile + 1) * LANES] for tile in range(full + 1)
        ]

    both = join_halves(tiles_of(0, slice(0, head_size)), tiles_of(1, slice(0, head_size)), tail)
    down = join_halves(tiles_of(2, slice(0, half)), tiles_of(2, slice(half, head_size)), tail)
    for tile, (above, below) in enumerate(zip(both, down)):
        lanes = slice(tile * LANES, (tile + 1) * LANES)
        out_ref[0:head_size, lanes] = above.astype(jnp.bfloat16)
        out_ref[head_size : head_size + half, lanes] = below.astype(jnp.bfloat16)


def renorm(weight_ref, grad_ref, mirror_refs, out_ref):
    head_size = weight_ref.shape[-1]
    units = head_size // len(mirror_refs)
    firsts, thirds, downs = [], [], []
    for mirror_ref in mirror_refs:
        first, third = part_halves(mirror_ref[0:units, :], head_size)
        firsts.append(first)
        thirds.append(third)
        downs.extend(part_halves(mirror_ref[units:, :], head_size))
    first, third, down = (jnp.concatenate(parts, axis=0) for parts in (firsts, thirds, downs))
    for index, other in enumerate((first, third, down)):
        before = weight_ref[index].astype(jnp.float32)
        axis = 1
        if index == 2:
            before = before.T
            axis = 0
        grad = grad_ref[index, :, 0:head_size] + other.astype(jnp.float32)
        updated = before - grad
        scale_old = jnp.sqrt(jnp.mean(before * before, axis=axis, keepdims=True) + epsilon)
        scale_new = jnp.sqrt(jnp.mean(updated * updated, axis=axis, keepdims=True) + epsilon)
        out_ref[index] = (updated * (scale_old / scale_new)).astype(jnp.bfloat16)


def apply_kernel(height, frames_here, shards, order_ref, *refs):
    near_refs, far_refs = refs[: shards // 2], refs[shards // 2 : shards]
    before_ref, grad_ref, mirror_ref = refs[shards : shards + 3]
    gain_ref, tap_ref = refs[shards + 3 : shards + 5]
    out_refs = refs[shards + 5 : -3]
    weight_ref, grid_ref, turned_ref = refs[-3:]
    half = far_refs[0].shape[0] // 2
    query_parts = [ref[ref.shape[0] - half :, :] for ref in near_refs]
    for index, ref in enumerate(far_refs):
        query_parts.append(ref[index % 2 * half : (index % 2 + 1) * half, :])
    renorm(before_ref, grad_ref, [mirror_ref], weight_ref)
    width = 2 * half // height
    head_size = weight_ref.shape[-1]
    full = head_size // LANES
    tail = head_size - full * LANES
    top = 8
    edge = jnp.zeros((top, LANES), jnp.float32)
    whole = jnp.zeros(grid_ref.shape[3:], jnp.float32)
    for shard in range(shards):
        for tile in range(full + 1):
            grid_ref[shard, tile, 0] = whole
            grid_ref[shard, tile, width + 1] = whole
            for column in range(1, width + 1):
                grid_ref[shard, tile, column, 0:top] = edge
                grid_ref[shard, tile, column, top + height :] = edge
    gain = gain_ref[...]
    for shard in range(shards):
        rows = jnp.concatenate(part_halves(query_parts[shard], head_size), axis=0)
        proj_first = contract(rows, weight_ref[0], NT)
        proj_third = contract(rows, weight_ref[1], NT)
        mixed = (proj_first * jax.nn.sigmoid(proj_first) * proj_third).astype(jnp.bfloat16)
        outputs = contract(mixed, weight_ref[2], NN)
        scale = lax.rsqrt(jnp.mean(outputs * outputs, axis=-1, keepdims=True) + epsilon)
        normed = (outputs * scale * gain).astype(jnp.bfloat16).astype(jnp.float32)
        frame = order_ref[shard]
        block = frame // frames_here
        slot = frame % frames_here
        for tile in range(full + 1):
            lanes = slice(tile * LANES, min((tile + 1) * LANES, head_size))
            for column in range(width):
                grid_ref[shard, tile, column + 1, top : top + height, 0 : lanes.stop - lanes.start] = (
                    normed[column * height : (column + 1) * height, lanes]
                )
            taps = [
                tap_ref[index : index + 1, tile * LANES : (tile + 1) * LANES] for index in range(9)
            ]
            for column in range(width):
                total = None
                for row_tap in range(3):
                    first = top + row_tap - 1
                    for col_tap in range(3):
                        term = taps[row_tap * 3 + col_tap] * grid_ref[
                            shard, tile, column + col_tap, first : first + height, :
                        ]
                        total = term if total is None else total + term
                turned_ref[
                    block, column, tile, pl.ds(slot, height, stride=frames_here), :
                ] = total
    blocks = turned_ref.shape[0]
    side_rows = turned_ref.shape[3] // 2
    for partner in range(shards):
        column = partner_head(partner)
        for other in range(blocks):
            block = lax.axis_index("head") ^ other
            sides = [
                [
                    turned_ref[block, column, tile, side * side_rows : (side + 1) * side_rows, :]
                    for tile in range(full + 1)
                ]
                for side in range(2)
            ]
            start = partner % 2 * side_rows
            if partner < 2 and other == 0:
                target, start = out_refs[partner], 0
            else:
                target = out_refs[1 + partner // 2 * blocks + other]
            for tile, part in enumerate(join_halves(sides[0], sides[1], tail)):
                target[start : start + side_rows, tile * LANES : (tile + 1) * LANES] = (
                    part.astype(jnp.bfloat16)
                )


def gate_kernel(blocks, own_ref, mate_ref, *refs):
    chip_refs, (gate_ref, out_ref) = refs[:-2], refs[-2:]
    height, frames_here, channels = out_ref.shape
    head_size = own_ref.shape[1] // 2
    shards = channels // head_size // blocks
    side_rows = own_ref.shape[0]
    rows_here = height // 2
    own = lax.axis_index("tok")
    odd = own % 2
    for partner in range(0, shards, 2):
        for other in range(blocks):
            index = partner // 2 * blocks + other - 1
            if index < 0:
                one, two = own_ref[...], mate_ref[...]
            else:
                one = chip_refs[2 * index][0:side_rows, :]
                two = chip_refs[2 * index + 1][side_rows:, :]
            one, two = one.astype(jnp.float32), two.astype(jnp.float32)
            low = part_halves(jnp.where(odd == 1, two, one), head_size)
            high = part_halves(jnp.where(odd == 1, one, two), head_size)
            head = (lax.axis_index("head") ^ other) * shards + ((own - odd) ^ partner)
            lanes = pl.ds(pl.multiple_of(head * head_size, 2 * head_size), 2 * head_size)
            for side in range(2):
                rows = slice(side * rows_here, (side + 1) * rows_here)
                conv = jnp.concatenate([low[side], high[side]], axis=1)
                conv = conv.reshape(rows_here, frames_here, 2 * head_size)
                gate = gate_ref[rows, :, lanes].astype(jnp.float32)
                out_ref[rows, :, lanes] = (conv * (gate * sigmoid(gate))).astype(jnp.bfloat16)


def in_vmem(count):
    return [pl.BlockSpec(memory_space=pltpu.VMEM)] * count


def call(kernel, out, operands, scratch=(), specs=None, leave=True):
    specs = specs or in_vmem(len(operands))
    operands = [
        pltpu.with_memory_space_constraint(item, pltpu.VMEM)
        if spec.memory_space == pltpu.VMEM
        else item
        for item, spec in zip(operands, specs)
    ]
    if leave:
        out = jax.tree.map(lambda item: pltpu.VMEM(item.shape, item.dtype), out)
    return pl.pallas_call(
        kernel,
        out_shape=out,
        in_specs=specs,
        out_specs=jax.tree.map(lambda _: pl.BlockSpec(memory_space=pltpu.VMEM), out),
        scratch_shapes=scratch,
        compiler_params=pltpu.CompilerParams(vmem_limit_bytes=VMEM_BYTES),
        cost_estimate=pl.CostEstimate(flops=0, bytes_accessed=0, transcendentals=0),
    )(*operands)


def after(part, *earlier):
    anywhere = pl.BlockSpec(memory_space=pl.ANY)
    return pl.pallas_call(
        lambda *refs: None,
        out_shape=jax.ShapeDtypeStruct(part.shape, part.dtype),
        in_specs=[anywhere] * (1 + len(earlier)),
        out_specs=anywhere,
        input_output_aliases={0: 0},
        compiler_params=pltpu.CompilerParams(vmem_limit_bytes=1024 * 1024),
        cost_estimate=pl.CostEstimate(flops=0, bytes_accessed=0, transcendentals=0),
    )(part, *earlier)


def by_heads(
    queries, keys, values, rates, fast_weights, norm_gain, frame_order, gate_input, conv_weights
):
    tok_rows = queries.shape[0]
    head_count = queries.shape[1] * queries.shape[2]
    head_size = queries.shape[3]
    height, frames_here = gate_input.shape[:2]
    shards = lax.axis_size("tok")
    blocks = lax.axis_size("head")
    half = tok_rows // 2
    wide = 2 * head_size
    tiles = head_size // LANES + 1
    own = lax.axis_index("tok")
    own_channel = lax.axis_index("head") * head_count + own

    def rows_of(array):
        return array.reshape(tok_rows, head_count, head_size)

    def own_of(array, place):
        return lax.dynamic_index_in_dim(array, place, 0, keepdims=False)

    line = shards // 2
    tile_scratch = pltpu.VMEM((tiles, tok_rows * head_count, LANES), jnp.float32)
    token_rates = rates.reshape(head_count, tok_rows)
    chips = line // 2

    one = jax.ShapeDtypeStruct((tok_rows, wide), jnp.bfloat16)
    mirrored = call(
        pack_mirror_kernel,
        [one] * line,
        (rows_of(keys), rows_of(values), token_rates),
        (tile_scratch, tile_scratch),
    )
    mirrored = [mirrored[0]] + [send(mirrored[k], k) for k in range(1, line)]
    across = call(
        functools.partial(pack_across_kernel, height),
        [one] * chips,
        (rows_of(queries),),
        (tile_scratch,),
    )
    across_landed = [send(part, line + 2 * index) for index, part in enumerate(across)]
    weights = fast_weights.reshape(head_count, 3, head_size, head_size)
    own_weights = own_of(weights, own)
    mirror_weights = own_of(weights, own ^ line)
    own_gain = own_of(norm_gain.reshape(head_count, 1, head_size), own)
    taps = conv_weights.reshape(9, blocks * head_count, head_size)
    own_taps = lax.dynamic_index_in_dim(taps, own_channel, 1, keepdims=False)
    own_taps = jnp.pad(own_taps, ((0, 0), (0, tiles * LANES - head_size)))
    frames = frame_order[own ^ jnp.arange(shards, dtype=jnp.int32)]
    grad_shape = (3, head_size, tiles * LANES)
    grad_struct = jax.ShapeDtypeStruct(grad_shape, jnp.float32)
    unread = pl.BlockSpec(memory_space=pl.ANY)
    mirror_sum = call(
        functools.partial(sum_kernel, 2, tok_rows, False),
        grad_struct,
        (*mirrored[:2], mirror_weights),
    )
    early = (across[0], own_weights, own_gain, own_taps, frames, mirror_sum)
    packed = call(
        functools.partial(pack_near_kernel, height, len(early)),
        [jax.ShapeDtypeStruct((tok_rows + half, wide), jnp.bfloat16)] * line,
        (rows_of(keys), rows_of(values), token_rates, rows_of(queries), *early),
        (tile_scratch, tile_scratch, tile_scratch),
        specs=in_vmem(4) + [unread] * len(early),
    )
    held = [after(part, *mirrored[1:], *across_landed) for part in packed[1:]]
    near = [packed[0]] + [send(held[k - 1], k) for k in range(1, line)]
    ahead = (*across_landed, *held)
    crossing = call(
        functools.partial(mirror_kernel, line - 2, tok_rows),
        jax.ShapeDtypeStruct((head_size + head_size // 2, wide), jnp.bfloat16),
        (*mirrored[2:], mirror_weights, mirror_sum, *ahead),
        (pltpu.VMEM(grad_shape, jnp.float32),),
        specs=in_vmem(line) + [unread] * len(ahead),
    )
    crossed = send(crossing, line)
    own_sum = call(
        functools.partial(sum_kernel, 2, tok_rows, False),
        grad_struct,
        (*near[:2], own_weights, crossing),
        specs=in_vmem(3) + [unread],
    )
    across = relay([after(part, own_sum) for part in across_landed])
    gradients = call(
        functools.partial(sum_kernel, line - 2, tok_rows, True),
        grad_struct,
        (*near[2:], own_weights, own_sum),
    )
    side_rows = frames_here * height // 2
    outgoing = call(
        functools.partial(apply_kernel, height, frames_here, shards),
        [jax.ShapeDtypeStruct((side_rows, wide), jnp.bfloat16)] * 2
        + [jax.ShapeDtypeStruct((2 * side_rows, wide), jnp.bfloat16)] * (shards // 2 * blocks - 1),
        (frames, *near, *across, own_weights, gradients, crossed, own_gain, own_taps),
        (
            pltpu.VMEM((3, head_size, head_size), jnp.bfloat16),
            pltpu.VMEM((shards, tiles, shards + 2, height + 16, LANES), jnp.float32),
            pltpu.VMEM((blocks, shards, tiles, 2 * side_rows, LANES), jnp.float32),
        ),
        specs=[pl.BlockSpec(memory_space=pltpu.SMEM)] + in_vmem(shards + 5),
    )
    places = [(k, x) for k in range(0, shards, 2) for x in range(blocks)][1:]
    landed = [send_far(part, k, x) for part, (k, x) in zip(outgoing[2:], places)]
    arrived = [outgoing[0], send(outgoing[1], 1), *relay(landed)]
    gate = gate_input.reshape(height, frames_here, gate_input.shape[3])
    gated = call(
        functools.partial(gate_kernel, blocks),
        jax.ShapeDtypeStruct(gate.shape, jnp.bfloat16),
        (*arrived, gate),
        leave=False,
    )
    return gated.reshape(gate_input.shape)


def fits_by_heads(queries, gate_input, frame_order):
    tok_rows, head_size = queries.shape[0], queries.shape[3]
    head_count = queries.shape[1] * queries.shape[2]
    height, frames_here, col_width = gate_input.shape[:3]
    shards = lax.axis_size("tok")
    return (
        head_count == shards
        and frame_order.shape[0] == shards
        and lax.axis_size("tile") == 1
        and col_width == 1
        and shards >= 8
        and shards & (shards - 1) == 0
        and head_size % LANES == LANES // 2
        and height % 8 == 0
        and tok_rows == height * shards
        and tok_rows % 32 == 0
        and head_size % 64 == 0
        and frames_here * height % 32 == 0
        and frames_here * lax.axis_size("head") == shards
        and lax.axis_size("head") & (lax.axis_size("head") - 1) == 0
    )


def renormed(previous, gradient):
    before = previous.astype(jnp.float32)
    updated = before - gradient
    scale_old = jnp.sqrt(jnp.mean(before * before, axis=-1, keepdims=True) + epsilon)
    scale_new = jnp.sqrt(jnp.mean(updated * updated, axis=-1, keepdims=True) + epsilon)
    return (updated * (scale_old / scale_new)).astype(jnp.bfloat16)


def by_tokens(
    queries, keys, values, rates, fast_weights, norm_gain, frame_order, gate_input, conv_weights
):
    tok_rows = queries.shape[0]
    head_count = queries.shape[1] * queries.shape[2]
    head_size = queries.shape[3]
    query_rows = queries.reshape(tok_rows, head_count, head_size)
    key_rows = keys.reshape(tok_rows, head_count, head_size)
    value_rows = values.reshape(tok_rows, head_count, head_size)
    token_rates = rates.reshape(head_count, tok_rows)
    weights = fast_weights.reshape(head_count, 3, head_size, head_size)
    head_gains = norm_gain.reshape(head_count, head_size)
    first_pre = jnp.einsum(
        "thd,hfd->htf", key_rows, weights[:, 0], preferred_element_type=jnp.float32
    )
    third_pre = jnp.einsum(
        "thd,hfd->htf", key_rows, weights[:, 1], preferred_element_type=jnp.float32
    )
    sigmoid_first = jax.nn.sigmoid(first_pre)
    activated = first_pre * sigmoid_first
    hidden = (activated * third_pre).astype(jnp.bfloat16)
    target = (-token_rates.T[:, :, None] * value_rows.astype(jnp.float32)).astype(jnp.bfloat16)
    grad_down = jnp.einsum("thd,htf->hdf", target, hidden, preferred_element_type=jnp.float32)
    hidden_grad = jnp.einsum(
        "thd,hdf->htf", target, weights[:, 2], preferred_element_type=jnp.float32
    )
    grad_first_in = (
        hidden_grad * third_pre * sigmoid_first * (1.0 + first_pre * (1.0 - sigmoid_first))
    ).astype(jnp.bfloat16)
    grad_third_in = (hidden_grad * activated).astype(jnp.bfloat16)
    grad_first = jnp.einsum(
        "htf,thd->hfd", grad_first_in, key_rows, preferred_element_type=jnp.float32
    )
    grad_third = jnp.einsum(
        "htf,thd->hfd", grad_third_in, key_rows, preferred_element_type=jnp.float32
    )
    gradients = jnp.stack([grad_first, grad_third, grad_down], axis=1)
    row_share = lax.psum_scatter(gradients, "tok", scatter_dimension=2, tiled=True)
    row_count = row_share.shape[2]
    own_rows = lax.dynamic_slice_in_dim(weights, lax.axis_index("tok") * row_count, row_count, 2)
    updated = lax.all_gather(renormed(own_rows, row_share), "tok", axis=2, tiled=True)
    proj_first = jnp.einsum(
        "thd,hfd->thf", query_rows, updated[:, 0], preferred_element_type=jnp.float32
    )
    proj_third = jnp.einsum(
        "thd,hfd->thf", query_rows, updated[:, 1], preferred_element_type=jnp.float32
    )
    mixed_hidden = (jax.nn.silu(proj_first) * proj_third).astype(jnp.bfloat16)
    outputs = jnp.einsum(
        "thf,hdf->thd", mixed_hidden, updated[:, 2], preferred_element_type=jnp.float32
    )
    normed = (
        outputs
        * lax.rsqrt(jnp.mean(outputs * outputs, axis=-1, keepdims=True) + epsilon)
        * head_gains[None]
    )
    normed = normed.astype(jnp.bfloat16)
    height = gate_input.shape[0]
    col_width = gate_input.shape[2]
    shards = lax.axis_size("tok")
    full_width = col_width * shards
    channels_here = head_count * head_size
    frame_grid = normed.reshape(height, full_width, channels_here)
    own_taps = lax.dynamic_slice_in_dim(
        conv_weights, lax.axis_index("head") * channels_here, channels_here, 2
    )
    padded = jnp.pad(frame_grid, ((1, 1), (1, 1), (0, 0)))
    local_sum = jnp.zeros((height, full_width, channels_here), jnp.float32)
    for row_tap in range(3):
        for col_tap in range(3):
            local_sum = local_sum + own_taps[row_tap, col_tap] * padded[
                row_tap : row_tap + height, col_tap : col_tap + full_width
            ].astype(jnp.float32)
    outgoing = local_sum.astype(jnp.bfloat16).reshape(height, shards, col_width, channels_here)
    arrived = lax.all_to_all(outgoing, "tok", split_axis=1, concat_axis=1, tiled=True)
    frame_count = frame_order.shape[0]
    numbers = jnp.arange(frame_count, dtype=jnp.int32)
    inverse = jnp.sum(
        jnp.where(frame_order[None, :] == numbers[:, None], numbers[None, :], 0), axis=1
    )
    ordered = jnp.take(arrived, inverse, axis=1)
    tile_block = lax.all_to_all(ordered, "head", split_axis=1, concat_axis=3, tiled=True)
    return (tile_block.astype(jnp.float32) * jax.nn.silu(gate_input.astype(jnp.float32))).astype(
        jnp.bfloat16
    )


def local(queries, keys, values, rates, fast_weights, norm_gain, frame_order, gate_input, conv_weights):
    args = (
        queries, keys, values, rates, fast_weights, norm_gain, frame_order, gate_input, conv_weights
    )
    if fits_by_heads(queries, gate_input, frame_order):
        return by_heads(*args)
    return by_tokens(*args)


def solution(mesh):
    in_specs = (
        P(("groups", "tok"), "tile", "head", None),
        P(("groups", "tok"), "tile", "head", None),
        P(("groups", "tok"), "tile", "head", None),
        P("tile", "head", ("groups", "tok")),
        P("tile", "head", None, None, None),
        P("tile", "head", None),
        P("groups"),
        P(None, ("groups", "head"), "tok", "tile"),
        P(None, None, "tile"),
    )
    out_specs = P(None, ("groups", "head"), "tok", "tile")
    return jax.shard_map(local, mesh=mesh, in_specs=in_specs, out_specs=out_specs, check_vma=False)
```

```python
import functools

import jax
import jax.numpy as jnp
from jax import lax
from jax.experimental import pallas as pl
from jax.experimental.pallas import tpu as pltpu
from jax.sharding import PartitionSpec as P

epsilon = 1e-06
LANES = 128
VMEM_BYTES = 24 * 1024 * 1024


def split_lanes(source, scratch, rows, head_size):
    full = head_size // LANES
    tail = head_size - full * LANES
    wide = source.reshape(rows, head_size).astype(jnp.float32)
    for tile in range(full):
        scratch[tile] = wide[:, tile * LANES : (tile + 1) * LANES]
    scratch[full, :, 0:tail] = wide[:, full * LANES :]


def join_halves(first, second, tail):
    lane = lax.broadcasted_iota(jnp.int32, first[-1].shape, 1)
    middle = jnp.where(lane < tail, first[-1], pltpu.roll(second[-1], tail, 1))
    return first[:-1] + [middle] + second[:-1]


def part_halves(packed, head_size):
    full = head_size // LANES
    tail = head_size - full * LANES
    first = packed[:, :head_size]
    middle = packed[:, head_size : (full + 1) * LANES]
    second = jnp.concatenate([packed[:, (full + 1) * LANES :], middle], axis=1)
    return first, second


def partner_head(partner):
    return lax.axis_index("tok") ^ partner


def pack_pairs(head, rate_ref, key_tiles, value_tiles, out_ref, start, head_size):
    heads, tok_rows = rate_ref.shape
    half = tok_rows // 2
    full = head_size // LANES
    tail = head_size - full * LANES
    rate_row = -rate_ref[pl.ds(head, 1), :]
    rates = jnp.broadcast_to(rate_row, (LANES, tok_rows)).T
    for row, tiles in ((start, key_tiles), (start + half, value_tiles)):
        sides = []
        for side in range(2):
            parts = [
                tiles[tile, pl.ds(side * half * heads + head, half, stride=heads), :]
                for tile in range(full + 1)
            ]
            if tiles is value_tiles:
                rate = rates[side * half : (side + 1) * half]
                parts = [rate * part for part in parts]
            sides.append(parts)
        for tile, part in enumerate(join_halves(sides[0], sides[1], tail)):
            out_ref[row : row + half, tile * LANES : (tile + 1) * LANES] = part.astype(jnp.bfloat16)


def pack_query(head, heads, height, query_tiles, out_ref, start, head_size):
    tok_rows = query_tiles.shape[1] // heads
    half = tok_rows // 2
    width = tok_rows // height
    full = head_size // LANES
    tail = head_size - full * LANES
    sides = []
    for side in range(2):
        sides.append(
            [
                jnp.concatenate(
                    [
                        query_tiles[
                            tile, pl.ds(column * heads + head, height, stride=width * heads), :
                        ]
                        for column in range(side * width // 2, (side + 1) * width // 2)
                    ],
                    axis=0,
                )
                for tile in range(full + 1)
            ]
        )
    for tile, part in enumerate(join_halves(sides[0], sides[1], tail)):
        out_ref[start : start + half, tile * LANES : (tile + 1) * LANES] = part.astype(jnp.bfloat16)


def pack_mirror_kernel(key_ref, value_ref, rate_ref, *rest):
    outs, (key_tiles, value_tiles) = rest[:-2], rest[-2:]
    tok_rows, heads, head_size = key_ref.shape
    split_lanes(key_ref[...], key_tiles, tok_rows * heads, head_size)
    split_lanes(value_ref[...], value_tiles, tok_rows * heads, head_size)
    for partner, out_ref in enumerate(outs):
        head = partner_head(partner ^ (heads // 2))
        pack_pairs(head, rate_ref, key_tiles, value_tiles, out_ref, 0, head_size)


def pack_across_kernel(height, query_ref, *rest):
    outs, query_tiles = rest[:-1], rest[-1]
    tok_rows, heads, head_size = query_ref.shape
    half = tok_rows // 2
    split_lanes(query_ref[...], query_tiles, tok_rows * heads, head_size)
    for partner in range(heads // 2):
        head = partner_head(partner ^ (heads // 2))
        start = partner % 2 * half
        pack_query(head, heads, height, query_tiles, outs[partner // 2], start, head_size)


def pack_near_kernel(height, unread, key_ref, value_ref, rate_ref, query_ref, *rest):
    outs, (key_tiles, value_tiles, query_tiles) = rest[unread:-3], rest[-3:]
    tok_rows, heads, head_size = key_ref.shape
    split_lanes(key_ref[...], key_tiles, tok_rows * heads, head_size)
    split_lanes(value_ref[...], value_tiles, tok_rows * heads, head_size)
    split_lanes(query_ref[...], query_tiles, tok_rows * heads, head_size)
    line = heads // 2
    for partner in range(line):
        head = partner_head(partner)
        pack_pairs(head, rate_ref, key_tiles, value_tiles, outs[partner], 0, head_size)
        pack_query(head, heads, height, query_tiles, outs[line + partner], 0, head_size)


def send_far(part, partner, other):
    blocks = lax.axis_size("head")
    count = lax.axis_size("tok") * blocks
    pairs = [(place, place ^ (partner * blocks + other)) for place in range(count)]
    return lax.ppermute(part, ("tok", "head"), pairs)


def relay(landed):
    return [part for one in landed for part in (one, send(one, 1))]


def send(part, partner):
    pairs = [(place, place ^ partner) for place in range(lax.axis_size("tok"))]
    return lax.ppermute(part, "tok", pairs)


def sigmoid(value):
    return 0.5 + 0.5 * jnp.tanh(0.5 * value)


def contract(first, second, dims):
    return lax.dot_general(first, second, (dims, ((), ())), preferred_element_type=jnp.float32)


NN = ((1,), (0,))
NT = ((1,), (1,))


def add_gradients(pair_refs, tok_rows, weight_ref, prior_ref, grad_ref):
    half = tok_rows // 2
    head_size = weight_ref.shape[-1]
    first_weight = weight_ref[0]
    third_weight = weight_ref[1]
    down_turned = weight_ref[2].astype(jnp.float32).T.astype(jnp.bfloat16)
    step = 2 if len(pair_refs) % 2 == 0 else 1
    for start in range(0, len(pair_refs), step):
        key_parts, target_parts = [], []
        for pair_ref in pair_refs[start : start + step]:
            key_parts.extend(part_halves(pair_ref[0:half, :], head_size))
            target_parts.extend(part_halves(pair_ref[half:tok_rows, :], head_size))
        key_rows = jnp.concatenate(key_parts, axis=0)
        target = jnp.concatenate(target_parts, axis=0)
        first_pre = contract(first_weight, key_rows, NT)
        third_pre = contract(third_weight, key_rows, NT)
        hidden_grad = contract(down_turned, target, NT)
        sigmoid_first = sigmoid(first_pre)
        activated = first_pre * sigmoid_first
        mixed = (activated * third_pre).astype(jnp.bfloat16)
        grad_first_in = (
            hidden_grad * third_pre * sigmoid_first * (1.0 + first_pre * (1.0 - sigmoid_first))
        ).astype(jnp.bfloat16)
        grad_third_in = (hidden_grad * activated).astype(jnp.bfloat16)
        grads = (
            contract(grad_first_in, key_rows, NN),
            contract(grad_third_in, key_rows, NN),
            contract(mixed, target, NN),
        )
        for index, grad in enumerate(grads):
            if start == 0 and prior_ref is None:
                grad_ref[index, :, 0:head_size] = grad
            elif start == 0:
                grad_ref[index, :, 0:head_size] = prior_ref[index, :, 0:head_size] + grad
            else:
                grad_ref[index, :, 0:head_size] += grad


def sum_kernel(count, tok_rows, prior, *refs):
    pair_refs, weight_ref, out_ref = refs[:count], refs[count], refs[-1]
    prior_ref = refs[count + 1] if prior else None
    add_gradients(pair_refs, tok_rows, weight_ref, prior_ref, out_ref)


def mirror_kernel(count, tok_rows, *refs):
    pair_refs, weight_ref, prior_ref = refs[:count], refs[count], refs[count + 1]
    out_ref, grad_ref = refs[-2:]
    head_size = weight_ref.shape[-1]
    full = head_size // LANES
    tail = head_size - full * LANES
    half = head_size // 2
    add_gradients(pair_refs, tok_rows, weight_ref, prior_ref, grad_ref)

    def tiles_of(index, rows):
        return [
            grad_ref[index, rows, tile * LANES : (tile + 1) * LANES] for tile in range(full + 1)
        ]

    both = join_halves(tiles_of(0, slice(0, head_size)), tiles_of(1, slice(0, head_size)), tail)
    down = join_halves(tiles_of(2, slice(0, half)), tiles_of(2, slice(half, head_size)), tail)
    for tile, (above, below) in enumerate(zip(both, down)):
        lanes = slice(tile * LANES, (tile + 1) * LANES)
        out_ref[0:head_size, lanes] = above.astype(jnp.bfloat16)
        out_ref[head_size : head_size + half, lanes] = below.astype(jnp.bfloat16)


def renorm(weight_ref, grad_ref, mirror_refs, out_ref):
    head_size = weight_ref.shape[-1]
    units = head_size // len(mirror_refs)
    firsts, thirds, downs = [], [], []
    for mirror_ref in mirror_refs:
        first, third = part_halves(mirror_ref[0:units, :], head_size)
        firsts.append(first)
        thirds.append(third)
        downs.extend(part_halves(mirror_ref[units:, :], head_size))
    first, third, down = (jnp.concatenate(parts, axis=0) for parts in (firsts, thirds, downs))
    for index, other in enumerate((first, third, down)):
        before = weight_ref[index].astype(jnp.float32)
        axis = 1
        if index == 2:
            before = before.T
            axis = 0
        grad = grad_ref[index, :, 0:head_size] + other.astype(jnp.float32)
        updated = before - grad
        scale_old = jnp.sqrt(jnp.mean(before * before, axis=axis, keepdims=True) + epsilon)
        scale_new = jnp.sqrt(jnp.mean(updated * updated, axis=axis, keepdims=True) + epsilon)
        out_ref[index] = (updated * (scale_old / scale_new)).astype(jnp.bfloat16)


def apply_shards(
    height, frames_here, parts, order_ref, weight_ref, gain_ref, tap_ref, grid_ref, turned_ref
):
    head_size = weight_ref.shape[-1]
    full = head_size // LANES
    width = grid_ref.shape[2] - 2
    top = 8
    edge = jnp.zeros((top, LANES), jnp.float32)
    whole = jnp.zeros(grid_ref.shape[3:], jnp.float32)
    for place in range(len(parts)):
        for tile in range(full + 1):
            grid_ref[place, tile, 0] = whole
            grid_ref[place, tile, width + 1] = whole
            for column in range(1, width + 1):
                grid_ref[place, tile, column, 0:top] = edge
                grid_ref[place, tile, column, top + height :] = edge
    gain = gain_ref[...]
    for place, (shard, queries) in enumerate(parts):
        rows = jnp.concatenate(part_halves(queries, head_size), axis=0)
        proj_first = contract(rows, weight_ref[0], NT)
        proj_third = contract(rows, weight_ref[1], NT)
        mixed = (proj_first * jax.nn.sigmoid(proj_first) * proj_third).astype(jnp.bfloat16)
        outputs = contract(mixed, weight_ref[2], NN)
        scale = lax.rsqrt(jnp.mean(outputs * outputs, axis=-1, keepdims=True) + epsilon)
        normed = (outputs * scale * gain).astype(jnp.bfloat16).astype(jnp.float32)
        frame = order_ref[shard]
        block = frame // frames_here
        slot = frame % frames_here
        for tile in range(full + 1):
            lanes = slice(tile * LANES, min((tile + 1) * LANES, head_size))
            for column in range(width):
                grid_ref[place, tile, column + 1, top : top + height, 0 : lanes.stop - lanes.start] = (
                    normed[column * height : (column + 1) * height, lanes]
                )
            taps = [
                tap_ref[index : index + 1, tile * LANES : (tile + 1) * LANES] for index in range(9)
            ]
            for column in range(width):
                total = None
                for row_tap in range(3):
                    first = top + row_tap - 1
                    for col_tap in range(3):
                        term = taps[row_tap * 3 + col_tap] * grid_ref[
                            place, tile, column + col_tap, first : first + height, :
                        ]
                        total = term if total is None else total + term
                turned_ref[
                    block, column, tile, pl.ds(slot, height, stride=frames_here), :
                ] = total


def apply_first_kernel(height, frames_here, near, far, order_ref, *refs):
    near_refs, far_refs = refs[: len(near)], refs[len(near) : len(near) + len(far)]
    before_ref, grad_ref, mirror_ref, gain_ref, tap_ref, weight_ref, turned_ref, grid_ref = refs[-8:]
    half = near_refs[0].shape[0]
    parts = [(shard, ref[...]) for shard, ref in zip(near, near_refs)]
    for shard, ref in zip(far, far_refs):
        parts.append((shard, ref[shard % 2 * half : (shard % 2 + 1) * half, :]))
    renorm(before_ref, grad_ref, [mirror_ref], weight_ref)
    apply_shards(
        height, frames_here, parts, order_ref, weight_ref, gain_ref, tap_ref, grid_ref, turned_ref
    )


def apply_last_kernel(height, frames_here, late, order_ref, *refs):
    query_refs = refs[: len(late)]
    weight_ref, done_ref, gain_ref, tap_ref = refs[len(late) : len(late) + 4]
    out_refs, (grid_ref, turned_ref) = refs[len(late) + 4 : -2], refs[-2:]
    turned_ref[...] = done_ref[...]
    parts = [(shard, ref[...]) for shard, ref in zip(late, query_refs)]
    apply_shards(
        height, frames_here, parts, order_ref, weight_ref, gain_ref, tap_ref, grid_ref, turned_ref
    )
    shards = turned_ref.shape[1]
    full = turned_ref.shape[2] - 1
    tail = weight_ref.shape[-1] - full * LANES
    blocks = turned_ref.shape[0]
    side_rows = turned_ref.shape[3] // 2
    for partner in range(shards):
        column = partner_head(partner)
        for other in range(blocks):
            block = lax.axis_index("head") ^ other
            sides = [
                [
                    turned_ref[block, column, tile, side * side_rows : (side + 1) * side_rows, :]
                    for tile in range(full + 1)
                ]
                for side in range(2)
            ]
            start = partner % 2 * side_rows
            if partner < 2 and other == 0:
                target, start = out_refs[partner], 0
            else:
                target = out_refs[1 + partner // 2 * blocks + other]
            for tile, part in enumerate(join_halves(sides[0], sides[1], tail)):
                target[start : start + side_rows, tile * LANES : (tile + 1) * LANES] = (
                    part.astype(jnp.bfloat16)
                )


def gate_kernel(blocks, own_ref, mate_ref, *refs):
    chip_refs, (gate_ref, out_ref) = refs[:-2], refs[-2:]
    height, frames_here, channels = out_ref.shape
    head_size = own_ref.shape[1] // 2
    shards = channels // head_size // blocks
    side_rows = own_ref.shape[0]
    rows_here = height // 2
    own = lax.axis_index("tok")
    odd = own % 2
    for partner in range(0, shards, 2):
        for other in range(blocks):
            index = partner // 2 * blocks + other - 1
            if index < 0:
                one, two = own_ref[...], mate_ref[...]
            else:
                one = chip_refs[2 * index][0:side_rows, :]
                two = chip_refs[2 * index + 1][side_rows:, :]
            one, two = one.astype(jnp.float32), two.astype(jnp.float32)
            low = part_halves(jnp.where(odd == 1, two, one), head_size)
            high = part_halves(jnp.where(odd == 1, one, two), head_size)
            head = (lax.axis_index("head") ^ other) * shards + ((own - odd) ^ partner)
            lanes = pl.ds(pl.multiple_of(head * head_size, 2 * head_size), 2 * head_size)
            for side in range(2):
                rows = slice(side * rows_here, (side + 1) * rows_here)
                conv = jnp.concatenate([low[side], high[side]], axis=1)
                conv = conv.reshape(rows_here, frames_here, 2 * head_size)
                gate = gate_ref[rows, :, lanes].astype(jnp.float32)
                out_ref[rows, :, lanes] = (conv * (gate * sigmoid(gate))).astype(jnp.bfloat16)


def in_vmem(count):
    return [pl.BlockSpec(memory_space=pltpu.VMEM)] * count


def call(kernel, out, operands, scratch=(), specs=None, leave=True):
    specs = specs or in_vmem(len(operands))
    operands = [
        pltpu.with_memory_space_constraint(item, pltpu.VMEM)
        if spec.memory_space == pltpu.VMEM
        else item
        for item, spec in zip(operands, specs)
    ]
    if leave:
        out = jax.tree.map(lambda item: pltpu.VMEM(item.shape, item.dtype), out)
    return pl.pallas_call(
        kernel,
        out_shape=out,
        in_specs=specs,
        out_specs=jax.tree.map(lambda _: pl.BlockSpec(memory_space=pltpu.VMEM), out),
        scratch_shapes=scratch,
        compiler_params=pltpu.CompilerParams(vmem_limit_bytes=VMEM_BYTES),
        cost_estimate=pl.CostEstimate(flops=0, bytes_accessed=0, transcendentals=0),
    )(*operands)


def after(part, *earlier):
    anywhere = pl.BlockSpec(memory_space=pl.ANY)
    return pl.pallas_call(
        lambda *refs: None,
        out_shape=jax.ShapeDtypeStruct(part.shape, part.dtype),
        in_specs=[anywhere] * (1 + len(earlier)),
        out_specs=anywhere,
        input_output_aliases={0: 0},
        compiler_params=pltpu.CompilerParams(vmem_limit_bytes=1024 * 1024),
        cost_estimate=pl.CostEstimate(flops=0, bytes_accessed=0, transcendentals=0),
    )(part, *earlier)


def by_heads(
    queries, keys, values, rates, fast_weights, norm_gain, frame_order, gate_input, conv_weights
):
    tok_rows = queries.shape[0]
    head_count = queries.shape[1] * queries.shape[2]
    head_size = queries.shape[3]
    height, frames_here = gate_input.shape[:2]
    shards = lax.axis_size("tok")
    blocks = lax.axis_size("head")
    half = tok_rows // 2
    wide = 2 * head_size
    tiles = head_size // LANES + 1
    own = lax.axis_index("tok")
    own_channel = lax.axis_index("head") * head_count + own

    def rows_of(array):
        return array.reshape(tok_rows, head_count, head_size)

    def own_of(array, place):
        return lax.dynamic_index_in_dim(array, place, 0, keepdims=False)

    line = shards // 2
    tile_scratch = pltpu.VMEM((tiles, tok_rows * head_count, LANES), jnp.float32)
    token_rates = rates.reshape(head_count, tok_rows)
    chips = line // 2

    one = jax.ShapeDtypeStruct((tok_rows, wide), jnp.bfloat16)
    mirrored = call(
        pack_mirror_kernel,
        [one] * line,
        (rows_of(keys), rows_of(values), token_rates),
        (tile_scratch, tile_scratch),
    )
    mirrored = [mirrored[0]] + [send(mirrored[k], k) for k in range(1, line)]
    across = call(
        functools.partial(pack_across_kernel, height),
        [one] * chips,
        (rows_of(queries),),
        (tile_scratch,),
    )
    across_landed = [send(part, line + 2 * index) for index, part in enumerate(across)]
    weights = fast_weights.reshape(head_count, 3, head_size, head_size)
    own_weights = own_of(weights, own)
    mirror_weights = own_of(weights, own ^ line)
    own_gain = own_of(norm_gain.reshape(head_count, 1, head_size), own)
    taps = conv_weights.reshape(9, blocks * head_count, head_size)
    own_taps = lax.dynamic_index_in_dim(taps, own_channel, 1, keepdims=False)
    own_taps = jnp.pad(own_taps, ((0, 0), (0, tiles * LANES - head_size)))
    frames = frame_order[own ^ jnp.arange(shards, dtype=jnp.int32)]
    grad_shape = (3, head_size, tiles * LANES)
    grad_struct = jax.ShapeDtypeStruct(grad_shape, jnp.float32)
    unread = pl.BlockSpec(memory_space=pl.ANY)
    mirror_sum = call(
        functools.partial(sum_kernel, 2, tok_rows, False),
        grad_struct,
        (*mirrored[:2], mirror_weights),
    )
    early = (across[0], own_weights, own_gain, own_taps, frames, mirror_sum)
    query_struct = jax.ShapeDtypeStruct((half, wide), jnp.bfloat16)
    packed = call(
        functools.partial(pack_near_kernel, height, len(early)),
        [one] * line + [query_struct] * line,
        (rows_of(keys), rows_of(values), token_rates, rows_of(queries), *early),
        (tile_scratch, tile_scratch, tile_scratch),
        specs=in_vmem(4) + [unread] * len(early),
    )
    near_queries = packed[line:]
    held = [after(part, *mirrored[1:], *across_landed) for part in packed[1:line]]
    near = [packed[0]] + [send(held[k - 1], k) for k in range(1, line)]
    ahead = (*across_landed, *held)
    crossing = call(
        functools.partial(mirror_kernel, line - 2, tok_rows),
        jax.ShapeDtypeStruct((head_size + head_size // 2, wide), jnp.bfloat16),
        (*mirrored[2:], mirror_weights, mirror_sum, *ahead),
        (pltpu.VMEM(grad_shape, jnp.float32),),
        specs=in_vmem(line) + [unread] * len(ahead),
    )
    crossed = send(crossing, line)
    own_sum = call(
        functools.partial(sum_kernel, 2, tok_rows, False),
        grad_struct,
        (*near[:2], own_weights, crossing),
        specs=in_vmem(3) + [unread],
    )
    across = relay([after(part, own_sum) for part in across_landed])
    gradients = call(
        functools.partial(sum_kernel, line - 2, tok_rows, True),
        grad_struct,
        (*near[2:], own_weights, own_sum),
    )
    mate_queries = send(after(near_queries[1], own_sum), 1)
    late_queries = [
        send(after(near_queries[k], *near[2:]), k) for k in range(2, line)
    ]
    side_rows = frames_here * height // 2
    first_shards, far_shards, late_shards = (0, 1), range(line, shards), range(2, line)
    grid_shape = (tiles, shards + 2, height + 16, LANES)
    turned_shape = (blocks, shards, tiles, 2 * side_rows, LANES)
    numbers = [pl.BlockSpec(memory_space=pltpu.SMEM)]
    updated, turned = call(
        functools.partial(apply_first_kernel, height, frames_here, first_shards, far_shards),
        [
            jax.ShapeDtypeStruct((3, head_size, head_size), jnp.bfloat16),
            jax.ShapeDtypeStruct(turned_shape, jnp.float32),
        ],
        (
            frames, near_queries[0], mate_queries, *across,
            own_weights, gradients, crossed, own_gain, own_taps,
        ),
        (pltpu.VMEM((2 + line, *grid_shape), jnp.float32),),
        specs=numbers + in_vmem(line + 7),
    )
    outgoing = call(
        functools.partial(apply_last_kernel, height, frames_here, late_shards),
        [jax.ShapeDtypeStruct((side_rows, wide), jnp.bfloat16)] * 2
        + [jax.ShapeDtypeStruct((2 * side_rows, wide), jnp.bfloat16)] * (shards // 2 * blocks - 1),
        (frames, *late_queries, updated, turned, own_gain, own_taps),
        (
            pltpu.VMEM((line - 2, *grid_shape), jnp.float32),
            pltpu.VMEM(turned_shape, jnp.float32),
        ),
        specs=numbers + in_vmem(line + 2),
    )
    places = [(k, x) for k in range(0, shards, 2) for x in range(blocks)][1:]
    landed = [send_far(part, k, x) for part, (k, x) in zip(outgoing[2:], places)]
    arrived = [outgoing[0], send(outgoing[1], 1), *relay(landed)]
    gate = gate_input.reshape(height, frames_here, gate_input.shape[3])
    gated = call(
        functools.partial(gate_kernel, blocks),
        jax.ShapeDtypeStruct(gate.shape, jnp.bfloat16),
        (*arrived, gate),
        leave=False,
    )
    return gated.reshape(gate_input.shape)


def fits_by_heads(queries, gate_input, frame_order):
    tok_rows, head_size = queries.shape[0], queries.shape[3]
    head_count = queries.shape[1] * queries.shape[2]
    height, frames_here, col_width = gate_input.shape[:3]
    shards = lax.axis_size("tok")
    return (
        head_count == shards
        and frame_order.shape[0] == shards
        and lax.axis_size("tile") == 1
        and col_width == 1
        and shards >= 8
        and shards & (shards - 1) == 0
        and head_size % LANES == LANES // 2
        and height % 8 == 0
        and tok_rows == height * shards
        and tok_rows % 32 == 0
        and head_size % 64 == 0
        and frames_here * height % 32 == 0
        and frames_here * lax.axis_size("head") == shards
        and lax.axis_size("head") & (lax.axis_size("head") - 1) == 0
    )


def renormed(previous, gradient):
    before = previous.astype(jnp.float32)
    updated = before - gradient
    scale_old = jnp.sqrt(jnp.mean(before * before, axis=-1, keepdims=True) + epsilon)
    scale_new = jnp.sqrt(jnp.mean(updated * updated, axis=-1, keepdims=True) + epsilon)
    return (updated * (scale_old / scale_new)).astype(jnp.bfloat16)


def by_tokens(
    queries, keys, values, rates, fast_weights, norm_gain, frame_order, gate_input, conv_weights
):
    tok_rows = queries.shape[0]
    head_count = queries.shape[1] * queries.shape[2]
    head_size = queries.shape[3]
    query_rows = queries.reshape(tok_rows, head_count, head_size)
    key_rows = keys.reshape(tok_rows, head_count, head_size)
    value_rows = values.reshape(tok_rows, head_count, head_size)
    token_rates = rates.reshape(head_count, tok_rows)
    weights = fast_weights.reshape(head_count, 3, head_size, head_size)
    head_gains = norm_gain.reshape(head_count, head_size)
    first_pre = jnp.einsum(
        "thd,hfd->htf", key_rows, weights[:, 0], preferred_element_type=jnp.float32
    )
    third_pre = jnp.einsum(
        "thd,hfd->htf", key_rows, weights[:, 1], preferred_element_type=jnp.float32
    )
    sigmoid_first = jax.nn.sigmoid(first_pre)
    activated = first_pre * sigmoid_first
    hidden = (activated * third_pre).astype(jnp.bfloat16)
    target = (-token_rates.T[:, :, None] * value_rows.astype(jnp.float32)).astype(jnp.bfloat16)
    grad_down = jnp.einsum("thd,htf->hdf", target, hidden, preferred_element_type=jnp.float32)
    hidden_grad = jnp.einsum(
        "thd,hdf->htf", target, weights[:, 2], preferred_element_type=jnp.float32
    )
    grad_first_in = (
        hidden_grad * third_pre * sigmoid_first * (1.0 + first_pre * (1.0 - sigmoid_first))
    ).astype(jnp.bfloat16)
    grad_third_in = (hidden_grad * activated).astype(jnp.bfloat16)
    grad_first = jnp.einsum(
        "htf,thd->hfd", grad_first_in, key_rows, preferred_element_type=jnp.float32
    )
    grad_third = jnp.einsum(
        "htf,thd->hfd", grad_third_in, key_rows, preferred_element_type=jnp.float32
    )
    gradients = jnp.stack([grad_first, grad_third, grad_down], axis=1)
    row_share = lax.psum_scatter(gradients, "tok", scatter_dimension=2, tiled=True)
    row_count = row_share.shape[2]
    own_rows = lax.dynamic_slice_in_dim(weights, lax.axis_index("tok") * row_count, row_count, 2)
    updated = lax.all_gather(renormed(own_rows, row_share), "tok", axis=2, tiled=True)
    proj_first = jnp.einsum(
        "thd,hfd->thf", query_rows, updated[:, 0], preferred_element_type=jnp.float32
    )
    proj_third = jnp.einsum(
        "thd,hfd->thf", query_rows, updated[:, 1], preferred_element_type=jnp.float32
    )
    mixed_hidden = (jax.nn.silu(proj_first) * proj_third).astype(jnp.bfloat16)
    outputs = jnp.einsum(
        "thf,hdf->thd", mixed_hidden, updated[:, 2], preferred_element_type=jnp.float32
    )
    normed = (
        outputs
        * lax.rsqrt(jnp.mean(outputs * outputs, axis=-1, keepdims=True) + epsilon)
        * head_gains[None]
    )
    normed = normed.astype(jnp.bfloat16)
    height = gate_input.shape[0]
    col_width = gate_input.shape[2]
    shards = lax.axis_size("tok")
    full_width = col_width * shards
    channels_here = head_count * head_size
    frame_grid = normed.reshape(height, full_width, channels_here)
    own_taps = lax.dynamic_slice_in_dim(
        conv_weights, lax.axis_index("head") * channels_here, channels_here, 2
    )
    padded = jnp.pad(frame_grid, ((1, 1), (1, 1), (0, 0)))
    local_sum = jnp.zeros((height, full_width, channels_here), jnp.float32)
    for row_tap in range(3):
        for col_tap in range(3):
            local_sum = local_sum + own_taps[row_tap, col_tap] * padded[
                row_tap : row_tap + height, col_tap : col_tap + full_width
            ].astype(jnp.float32)
    outgoing = local_sum.astype(jnp.bfloat16).reshape(height, shards, col_width, channels_here)
    arrived = lax.all_to_all(outgoing, "tok", split_axis=1, concat_axis=1, tiled=True)
    frame_count = frame_order.shape[0]
    numbers = jnp.arange(frame_count, dtype=jnp.int32)
    inverse = jnp.sum(
        jnp.where(frame_order[None, :] == numbers[:, None], numbers[None, :], 0), axis=1
    )
    ordered = jnp.take(arrived, inverse, axis=1)
    tile_block = lax.all_to_all(ordered, "head", split_axis=1, concat_axis=3, tiled=True)
    return (tile_block.astype(jnp.float32) * jax.nn.silu(gate_input.astype(jnp.float32))).astype(
        jnp.bfloat16
    )


def local(queries, keys, values, rates, fast_weights, norm_gain, frame_order, gate_input, conv_weights):
    args = (
        queries, keys, values, rates, fast_weights, norm_gain, frame_order, gate_input, conv_weights
    )
    if fits_by_heads(queries, gate_input, frame_order):
        return by_heads(*args)
    return by_tokens(*args)


def solution(mesh):
    in_specs = (
        P(("groups", "tok"), "tile", "head", None),
        P(("groups", "tok"), "tile", "head", None),
        P(("groups", "tok"), "tile", "head", None),
        P("tile", "head", ("groups", "tok")),
        P("tile", "head", None, None, None),
        P("tile", "head", None),
        P("groups"),
        P(None, ("groups", "head"), "tok", "tile"),
        P(None, None, "tile"),
    )
    out_specs = P(None, ("groups", "head"), "tok", "tile")
    return jax.shard_map(local, mesh=mesh, in_specs=in_specs, out_specs=out_specs, check_vma=False)
```

```python
import functools

import jax
import jax.numpy as jnp
from jax import lax
from jax.experimental import pallas as pl
from jax.experimental.pallas import tpu as pltpu
from jax.sharding import PartitionSpec as P

epsilon = 1e-06
LANES = 128
VMEM_BYTES = 24 * 1024 * 1024


def split_lanes(source, scratch, rows, head_size):
    full = head_size // LANES
    tail = head_size - full * LANES
    wide = source.reshape(rows, head_size).astype(jnp.float32)
    for tile in range(full):
        scratch[tile] = wide[:, tile * LANES : (tile + 1) * LANES]
    scratch[full, :, 0:tail] = wide[:, full * LANES :]


def join_halves(first, second, tail):
    lane = lax.broadcasted_iota(jnp.int32, first[-1].shape, 1)
    middle = jnp.where(lane < tail, first[-1], pltpu.roll(second[-1], tail, 1))
    return first[:-1] + [middle] + second[:-1]


def part_halves(packed, head_size):
    full = head_size // LANES
    tail = head_size - full * LANES
    first = packed[:, :head_size]
    middle = packed[:, head_size : (full + 1) * LANES]
    second = jnp.concatenate([packed[:, (full + 1) * LANES :], middle], axis=1)
    return first, second


def partner_head(partner):
    return lax.axis_index("tok") ^ partner


def pack_pairs(head, rate_ref, key_tiles, value_tiles, out_ref, start, head_size):
    heads, tok_rows = rate_ref.shape
    half = tok_rows // 2
    full = head_size // LANES
    tail = head_size - full * LANES
    rate_row = -rate_ref[pl.ds(head, 1), :]
    rates = jnp.broadcast_to(rate_row, (LANES, tok_rows)).T
    for row, tiles in ((start, key_tiles), (start + half, value_tiles)):
        sides = []
        for side in range(2):
            parts = [
                tiles[tile, pl.ds(side * half * heads + head, half, stride=heads), :]
                for tile in range(full + 1)
            ]
            if tiles is value_tiles:
                rate = rates[side * half : (side + 1) * half]
                parts = [rate * part for part in parts]
            sides.append(parts)
        for tile, part in enumerate(join_halves(sides[0], sides[1], tail)):
            out_ref[row : row + half, tile * LANES : (tile + 1) * LANES] = part.astype(jnp.bfloat16)


def pack_query(head, heads, height, query_tiles, out_ref, start, head_size):
    tok_rows = query_tiles.shape[1] // heads
    half = tok_rows // 2
    width = tok_rows // height
    full = head_size // LANES
    tail = head_size - full * LANES
    sides = []
    for side in range(2):
        sides.append(
            [
                jnp.concatenate(
                    [
                        query_tiles[
                            tile, pl.ds(column * heads + head, height, stride=width * heads), :
                        ]
                        for column in range(side * width // 2, (side + 1) * width // 2)
                    ],
                    axis=0,
                )
                for tile in range(full + 1)
            ]
        )
    for tile, part in enumerate(join_halves(sides[0], sides[1], tail)):
        out_ref[start : start + half, tile * LANES : (tile + 1) * LANES] = part.astype(jnp.bfloat16)


def pack_mirror_kernel(key_ref, value_ref, rate_ref, *rest):
    outs, (key_tiles, value_tiles) = rest[:-2], rest[-2:]
    tok_rows, heads, head_size = key_ref.shape
    split_lanes(key_ref[...], key_tiles, tok_rows * heads, head_size)
    split_lanes(value_ref[...], value_tiles, tok_rows * heads, head_size)
    for partner, out_ref in enumerate(outs):
        head = partner_head(partner ^ (heads // 2))
        pack_pairs(head, rate_ref, key_tiles, value_tiles, out_ref, 0, head_size)


def pack_across_kernel(height, query_ref, *rest):
    outs, query_tiles = rest[:-1], rest[-1]
    tok_rows, heads, head_size = query_ref.shape
    half = tok_rows // 2
    split_lanes(query_ref[...], query_tiles, tok_rows * heads, head_size)
    for partner in range(heads // 2):
        head = partner_head(partner ^ (heads // 2))
        start = partner % 2 * half
        pack_query(head, heads, height, query_tiles, outs[partner // 2], start, head_size)


def pack_near_kernel(height, unread, key_ref, value_ref, rate_ref, query_ref, *rest):
    outs, (key_tiles, value_tiles, query_tiles) = rest[unread:-3], rest[-3:]
    tok_rows, heads, head_size = key_ref.shape
    split_lanes(key_ref[...], key_tiles, tok_rows * heads, head_size)
    split_lanes(value_ref[...], value_tiles, tok_rows * heads, head_size)
    split_lanes(query_ref[...], query_tiles, tok_rows * heads, head_size)
    line = heads // 2
    for partner in range(line):
        head = partner_head(partner)
        pack_pairs(head, rate_ref, key_tiles, value_tiles, outs[partner], 0, head_size)
        pack_query(head, heads, height, query_tiles, outs[line + partner], 0, head_size)


def send_far(part, partner, other):
    blocks = lax.axis_size("head")
    count = lax.axis_size("tok") * blocks
    pairs = [(place, place ^ (partner * blocks + other)) for place in range(count)]
    return lax.ppermute(part, ("tok", "head"), pairs)


def relay(landed):
    return [part for one in landed for part in (one, send(one, 1))]


def send(part, partner):
    pairs = [(place, place ^ partner) for place in range(lax.axis_size("tok"))]
    return lax.ppermute(part, "tok", pairs)


def sigmoid(value):
    return 0.5 + 0.5 * jnp.tanh(0.5 * value)


def contract(first, second, dims):
    return lax.dot_general(first, second, (dims, ((), ())), preferred_element_type=jnp.float32)


NN = ((1,), (0,))
NT = ((1,), (1,))


def add_gradients(pair_refs, tok_rows, weight_ref, prior_ref, grad_ref):
    half = tok_rows // 2
    head_size = weight_ref.shape[-1]
    first_weight = weight_ref[0]
    third_weight = weight_ref[1]
    down_turned = weight_ref[2].astype(jnp.float32).T.astype(jnp.bfloat16)
    step = 2 if len(pair_refs) % 2 == 0 else 1
    for start in range(0, len(pair_refs), step):
        key_parts, target_parts = [], []
        for pair_ref in pair_refs[start : start + step]:
            key_parts.extend(part_halves(pair_ref[0:half, :], head_size))
            target_parts.extend(part_halves(pair_ref[half:tok_rows, :], head_size))
        key_rows = jnp.concatenate(key_parts, axis=0)
        target = jnp.concatenate(target_parts, axis=0)
        first_pre = contract(first_weight, key_rows, NT)
        third_pre = contract(third_weight, key_rows, NT)
        hidden_grad = contract(down_turned, target, NT)
        sigmoid_first = sigmoid(first_pre)
        activated = first_pre * sigmoid_first
        mixed = (activated * third_pre).astype(jnp.bfloat16)
        grad_first_in = (
            hidden_grad * third_pre * sigmoid_first * (1.0 + first_pre * (1.0 - sigmoid_first))
        ).astype(jnp.bfloat16)
        grad_third_in = (hidden_grad * activated).astype(jnp.bfloat16)
        grads = (
            contract(grad_first_in, key_rows, NN),
            contract(grad_third_in, key_rows, NN),
            contract(mixed, target, NN),
        )
        for index, grad in enumerate(grads):
            if start == 0 and prior_ref is None:
                grad_ref[index, :, 0:head_size] = grad
            elif start == 0:
                grad_ref[index, :, 0:head_size] = prior_ref[index, :, 0:head_size] + grad
            else:
                grad_ref[index, :, 0:head_size] += grad


def sum_kernel(count, tok_rows, prior, *refs):
    pair_refs, weight_ref, out_ref = refs[:count], refs[count], refs[-1]
    prior_ref = refs[count + 1] if prior else None
    add_gradients(pair_refs, tok_rows, weight_ref, prior_ref, out_ref)


def mirror_kernel(count, tok_rows, *refs):
    pair_refs, weight_ref, prior_ref = refs[:count], refs[count], refs[count + 1]
    out_ref, grad_ref = refs[-2:]
    head_size = weight_ref.shape[-1]
    full = head_size // LANES
    tail = head_size - full * LANES
    half = head_size // 2
    add_gradients(pair_refs, tok_rows, weight_ref, prior_ref, grad_ref)

    def tiles_of(index, rows):
        return [
            grad_ref[index, rows, tile * LANES : (tile + 1) * LANES] for tile in range(full + 1)
        ]

    both = join_halves(tiles_of(0, slice(0, head_size)), tiles_of(1, slice(0, head_size)), tail)
    down = join_halves(tiles_of(2, slice(0, half)), tiles_of(2, slice(half, head_size)), tail)
    for tile, (above, below) in enumerate(zip(both, down)):
        lanes = slice(tile * LANES, (tile + 1) * LANES)
        out_ref[0:head_size, lanes] = above.astype(jnp.bfloat16)
        out_ref[head_size : head_size + half, lanes] = below.astype(jnp.bfloat16)


def renorm(weight_ref, grad_ref, mirror_refs, out_ref):
    head_size = weight_ref.shape[-1]
    units = head_size // len(mirror_refs)
    firsts, thirds, downs = [], [], []
    for mirror_ref in mirror_refs:
        first, third = part_halves(mirror_ref[0:units, :], head_size)
        firsts.append(first)
        thirds.append(third)
        downs.extend(part_halves(mirror_ref[units:, :], head_size))
    first, third, down = (jnp.concatenate(parts, axis=0) for parts in (firsts, thirds, downs))
    for index, other in enumerate((first, third, down)):
        before = weight_ref[index].astype(jnp.float32)
        axis = 1
        if index == 2:
            before = before.T
            axis = 0
        grad = grad_ref[index, :, 0:head_size] + other.astype(jnp.float32)
        updated = before - grad
        scale_old = jnp.sqrt(jnp.mean(before * before, axis=axis, keepdims=True) + epsilon)
        scale_new = jnp.sqrt(jnp.mean(updated * updated, axis=axis, keepdims=True) + epsilon)
        out_ref[index] = (updated * (scale_old / scale_new)).astype(jnp.bfloat16)


def apply_shards(
    height, frames_here, parts, order_ref, weight_ref, gain_ref, tap_ref, grid_ref, turned_ref
):
    head_size = weight_ref.shape[-1]
    full = head_size // LANES
    width = grid_ref.shape[2] - 2
    top = 8
    edge = jnp.zeros((top, LANES), jnp.float32)
    whole = jnp.zeros(grid_ref.shape[3:], jnp.float32)
    for place in range(len(parts)):
        for tile in range(full + 1):
            grid_ref[place, tile, 0] = whole
            grid_ref[place, tile, width + 1] = whole
            for column in range(1, width + 1):
                grid_ref[place, tile, column, 0:top] = edge
                grid_ref[place, tile, column, top + height :] = edge
    gain = gain_ref[...]
    for place, (shard, queries) in enumerate(parts):
        rows = jnp.concatenate(part_halves(queries, head_size), axis=0)
        proj_first = contract(rows, weight_ref[0], NT)
        proj_third = contract(rows, weight_ref[1], NT)
        mixed = (proj_first * jax.nn.sigmoid(proj_first) * proj_third).astype(jnp.bfloat16)
        outputs = contract(mixed, weight_ref[2], NN)
        scale = lax.rsqrt(jnp.mean(outputs * outputs, axis=-1, keepdims=True) + epsilon)
        normed = (outputs * scale * gain).astype(jnp.bfloat16).astype(jnp.float32)
        frame = order_ref[shard]
        block = frame // frames_here
        slot = frame % frames_here
        for tile in range(full + 1):
            lanes = slice(tile * LANES, min((tile + 1) * LANES, head_size))
            for column in range(width):
                grid_ref[place, tile, column + 1, top : top + height, 0 : lanes.stop - lanes.start] = (
                    normed[column * height : (column + 1) * height, lanes]
                )
            taps = [
                tap_ref[index : index + 1, tile * LANES : (tile + 1) * LANES] for index in range(9)
            ]
            for column in range(width):
                total = None
                for row_tap in range(3):
                    first = top + row_tap - 1
                    for col_tap in range(3):
                        term = taps[row_tap * 3 + col_tap] * grid_ref[
                            place, tile, column + col_tap, first : first + height, :
                        ]
                        total = term if total is None else total + term
                turned_ref[
                    block, column, tile, pl.ds(slot, height, stride=frames_here), :
                ] = total


def apply_first_kernel(height, frames_here, near, far, order_ref, *refs):
    near_refs, far_refs = refs[: len(near)], refs[len(near) : len(near) + len(far)]
    before_ref, grad_ref, mirror_ref, gain_ref, tap_ref, weight_ref, turned_ref, grid_ref = refs[-8:]
    half = near_refs[0].shape[0]
    parts = [(shard, ref[...]) for shard, ref in zip(near, near_refs)]
    for shard, ref in zip(far, far_refs):
        parts.append((shard, ref[shard % 2 * half : (shard % 2 + 1) * half, :]))
    renorm(before_ref, grad_ref, [mirror_ref], weight_ref)
    apply_shards(
        height, frames_here, parts, order_ref, weight_ref, gain_ref, tap_ref, grid_ref, turned_ref
    )


def apply_last_kernel(height, frames_here, late, order, order_ref, *refs):
    query_refs = refs[: len(late)]
    weight_ref, done_ref, gain_ref, tap_ref = refs[len(late) : len(late) + 4]
    out_refs, (grid_ref, turned_ref) = refs[len(late) + 4 : -2], refs[-2:]
    turned_ref[...] = done_ref[...]
    parts = [(shard, ref[...]) for shard, ref in zip(late, query_refs)]
    apply_shards(
        height, frames_here, parts, order_ref, weight_ref, gain_ref, tap_ref, grid_ref, turned_ref
    )
    shards = turned_ref.shape[1]
    full = turned_ref.shape[2] - 1
    tail = weight_ref.shape[-1] - full * LANES
    blocks = turned_ref.shape[0]
    side_rows = turned_ref.shape[3] // 2
    for partner in range(shards):
        column = partner_head(partner)
        for other in range(blocks):
            block = lax.axis_index("head") ^ other
            sides = [
                [
                    turned_ref[block, column, tile, side * side_rows : (side + 1) * side_rows, :]
                    for tile in range(full + 1)
                ]
                for side in range(2)
            ]
            start = partner % 2 * side_rows
            if partner < 2 and other == 0:
                target, start = out_refs[partner], 0
            else:
                target = out_refs[2 + order.index((partner // 2 * 2, other))]
            for tile, part in enumerate(join_halves(sides[0], sides[1], tail)):
                target[start : start + side_rows, tile * LANES : (tile + 1) * LANES] = (
                    part.astype(jnp.bfloat16)
                )


def gate_kernel(blocks, order, own_ref, mate_ref, *refs):
    chip_refs, (gate_ref, out_ref) = refs[:-2], refs[-2:]
    height, frames_here, channels = out_ref.shape
    head_size = own_ref.shape[1] // 2
    shards = channels // head_size // blocks
    side_rows = own_ref.shape[0]
    rows_here = height // 2
    own = lax.axis_index("tok")
    odd = own % 2
    for partner in range(0, shards, 2):
        for other in range(blocks):
            if partner == 0 and other == 0:
                one, two = own_ref[...], mate_ref[...]
            else:
                index = order.index((partner, other))
                one = chip_refs[2 * index][0:side_rows, :]
                two = chip_refs[2 * index + 1][side_rows:, :]
            one, two = one.astype(jnp.float32), two.astype(jnp.float32)
            low = part_halves(jnp.where(odd == 1, two, one), head_size)
            high = part_halves(jnp.where(odd == 1, one, two), head_size)
            head = (lax.axis_index("head") ^ other) * shards + ((own - odd) ^ partner)
            lanes = pl.ds(pl.multiple_of(head * head_size, 2 * head_size), 2 * head_size)
            for side in range(2):
                rows = slice(side * rows_here, (side + 1) * rows_here)
                conv = jnp.concatenate([low[side], high[side]], axis=1)
                conv = conv.reshape(rows_here, frames_here, 2 * head_size)
                gate = gate_ref[rows, :, lanes].astype(jnp.float32)
                out_ref[rows, :, lanes] = (conv * (gate * sigmoid(gate))).astype(jnp.bfloat16)


def in_vmem(count):
    return [pl.BlockSpec(memory_space=pltpu.VMEM)] * count


def call(kernel, out, operands, scratch=(), specs=None, leave=True):
    specs = specs or in_vmem(len(operands))
    operands = [
        pltpu.with_memory_space_constraint(item, pltpu.VMEM)
        if spec.memory_space == pltpu.VMEM
        else item
        for item, spec in zip(operands, specs)
    ]
    if leave:
        out = jax.tree.map(lambda item: pltpu.VMEM(item.shape, item.dtype), out)
    return pl.pallas_call(
        kernel,
        out_shape=out,
        in_specs=specs,
        out_specs=jax.tree.map(lambda _: pl.BlockSpec(memory_space=pltpu.VMEM), out),
        scratch_shapes=scratch,
        compiler_params=pltpu.CompilerParams(vmem_limit_bytes=VMEM_BYTES),
        cost_estimate=pl.CostEstimate(flops=0, bytes_accessed=0, transcendentals=0),
    )(*operands)


def after(part, *earlier):
    anywhere = pl.BlockSpec(memory_space=pl.ANY)
    return pl.pallas_call(
        lambda *refs: None,
        out_shape=jax.ShapeDtypeStruct(part.shape, part.dtype),
        in_specs=[anywhere] * (1 + len(earlier)),
        out_specs=anywhere,
        input_output_aliases={0: 0},
        compiler_params=pltpu.CompilerParams(vmem_limit_bytes=1024 * 1024),
        cost_estimate=pl.CostEstimate(flops=0, bytes_accessed=0, transcendentals=0),
    )(part, *earlier)


def by_heads(
    queries, keys, values, rates, fast_weights, norm_gain, frame_order, gate_input, conv_weights
):
    tok_rows = queries.shape[0]
    head_count = queries.shape[1] * queries.shape[2]
    head_size = queries.shape[3]
    height, frames_here = gate_input.shape[:2]
    shards = lax.axis_size("tok")
    blocks = lax.axis_size("head")
    half = tok_rows // 2
    wide = 2 * head_size
    tiles = head_size // LANES + 1
    own = lax.axis_index("tok")
    own_channel = lax.axis_index("head") * head_count + own

    def rows_of(array):
        return array.reshape(tok_rows, head_count, head_size)

    def own_of(array, place):
        return lax.dynamic_index_in_dim(array, place, 0, keepdims=False)

    line = shards // 2
    tile_scratch = pltpu.VMEM((tiles, tok_rows * head_count, LANES), jnp.float32)
    token_rates = rates.reshape(head_count, tok_rows)
    chips = line // 2

    one = jax.ShapeDtypeStruct((tok_rows, wide), jnp.bfloat16)
    mirrored = call(
        pack_mirror_kernel,
        [one] * line,
        (rows_of(keys), rows_of(values), token_rates),
        (tile_scratch, tile_scratch),
    )
    mirrored = [mirrored[0]] + [send(mirrored[k], k) for k in range(1, line)]
    across = call(
        functools.partial(pack_across_kernel, height),
        [one] * chips,
        (rows_of(queries),),
        (tile_scratch,),
    )
    across_landed = [send(part, line + 2 * index) for index, part in enumerate(across)]
    weights = fast_weights.reshape(head_count, 3, head_size, head_size)
    own_weights = own_of(weights, own)
    mirror_weights = own_of(weights, own ^ line)
    own_gain = own_of(norm_gain.reshape(head_count, 1, head_size), own)
    taps = conv_weights.reshape(9, blocks * head_count, head_size)
    own_taps = lax.dynamic_index_in_dim(taps, own_channel, 1, keepdims=False)
    own_taps = jnp.pad(own_taps, ((0, 0), (0, tiles * LANES - head_size)))
    frames = frame_order[own ^ jnp.arange(shards, dtype=jnp.int32)]
    grad_shape = (3, head_size, tiles * LANES)
    grad_struct = jax.ShapeDtypeStruct(grad_shape, jnp.float32)
    unread = pl.BlockSpec(memory_space=pl.ANY)
    mirror_sum = call(
        functools.partial(sum_kernel, 2, tok_rows, False),
        grad_struct,
        (*mirrored[:2], mirror_weights),
    )
    early = (across[0], own_weights, own_gain, own_taps, frames, mirror_sum)
    query_struct = jax.ShapeDtypeStruct((half, wide), jnp.bfloat16)
    packed = call(
        functools.partial(pack_near_kernel, height, len(early)),
        [one] * line + [query_struct] * line,
        (rows_of(keys), rows_of(values), token_rates, rows_of(queries), *early),
        (tile_scratch, tile_scratch, tile_scratch),
        specs=in_vmem(4) + [unread] * len(early),
    )
    near_queries = packed[line:]
    held = [after(part, *mirrored[1:], *across_landed) for part in packed[1:line]]
    near = [packed[0]] + [send(held[k - 1], k) for k in range(1, line)]
    ahead = (*across_landed, *held)
    crossing = call(
        functools.partial(mirror_kernel, line - 2, tok_rows),
        jax.ShapeDtypeStruct((head_size + head_size // 2, wide), jnp.bfloat16),
        (*mirrored[2:], mirror_weights, mirror_sum, *ahead),
        (pltpu.VMEM(grad_shape, jnp.float32),),
        specs=in_vmem(line) + [unread] * len(ahead),
    )
    crossed = send(crossing, line)
    own_sum = call(
        functools.partial(sum_kernel, 2, tok_rows, False),
        grad_struct,
        (*near[:2], own_weights, crossing),
        specs=in_vmem(3) + [unread],
    )
    across = relay([after(part, own_sum) for part in across_landed])
    gradients = call(
        functools.partial(sum_kernel, line - 2, tok_rows, True),
        grad_struct,
        (*near[2:], own_weights, own_sum),
    )
    mate_queries = send(after(near_queries[1], own_sum), 1)
    late_queries = [
        send(after(near_queries[k], *near[2:]), k) for k in range(2, line)
    ]
    side_rows = frames_here * height // 2
    first_shards, far_shards, late_shards = (0, 1), range(line, shards), range(2, line)
    grid_shape = (tiles, shards + 2, height + 16, LANES)
    turned_shape = (blocks, shards, tiles, 2 * side_rows, LANES)
    numbers = [pl.BlockSpec(memory_space=pltpu.SMEM)]
    updated, turned = call(
        functools.partial(apply_first_kernel, height, frames_here, first_shards, far_shards),
        [
            jax.ShapeDtypeStruct((3, head_size, head_size), jnp.bfloat16),
            jax.ShapeDtypeStruct(turned_shape, jnp.float32),
        ],
        (
            frames, near_queries[0], mate_queries, *across,
            own_weights, gradients, crossed, own_gain, own_taps,
        ),
        (pltpu.VMEM((2 + line, *grid_shape), jnp.float32),),
        specs=numbers + in_vmem(line + 7),
    )
    order = [(k, x) for k in range(0, shards, 2) for x in range(blocks)][1:]
    order = sorted(order, key=lambda place: (place != (line, 0), place))
    outgoing = call(
        functools.partial(apply_last_kernel, height, frames_here, late_shards, order),
        [jax.ShapeDtypeStruct((side_rows, wide), jnp.bfloat16)] * 2
        + [jax.ShapeDtypeStruct((2 * side_rows, wide), jnp.bfloat16)] * (shards // 2 * blocks - 1),
        (frames, *late_queries, updated, turned, own_gain, own_taps),
        (
            pltpu.VMEM((line - 2, *grid_shape), jnp.float32),
            pltpu.VMEM(turned_shape, jnp.float32),
        ),
        specs=numbers + in_vmem(line + 2),
    )
    landed = [send_far(part, k, x) for part, (k, x) in zip(outgoing[2:], order)]
    arrived = [outgoing[0], send(outgoing[1], 1), *relay(landed)]
    gate = gate_input.reshape(height, frames_here, gate_input.shape[3])
    gated = call(
        functools.partial(gate_kernel, blocks, order),
        jax.ShapeDtypeStruct(gate.shape, jnp.bfloat16),
        (*arrived, gate),
        leave=False,
    )
    return gated.reshape(gate_input.shape)


def fits_by_heads(queries, gate_input, frame_order):
    tok_rows, head_size = queries.shape[0], queries.shape[3]
    head_count = queries.shape[1] * queries.shape[2]
    height, frames_here, col_width = gate_input.shape[:3]
    shards = lax.axis_size("tok")
    return (
        head_count == shards
        and frame_order.shape[0] == shards
        and lax.axis_size("tile") == 1
        and col_width == 1
        and shards >= 8
        and shards & (shards - 1) == 0
        and head_size % LANES == LANES // 2
        and height % 8 == 0
        and tok_rows == height * shards
        and tok_rows % 32 == 0
        and head_size % 64 == 0
        and frames_here * height % 32 == 0
        and frames_here * lax.axis_size("head") == shards
        and lax.axis_size("head") & (lax.axis_size("head") - 1) == 0
    )


def renormed(previous, gradient):
    before = previous.astype(jnp.float32)
    updated = before - gradient
    scale_old = jnp.sqrt(jnp.mean(before * before, axis=-1, keepdims=True) + epsilon)
    scale_new = jnp.sqrt(jnp.mean(updated * updated, axis=-1, keepdims=True) + epsilon)
    return (updated * (scale_old / scale_new)).astype(jnp.bfloat16)


def by_tokens(
    queries, keys, values, rates, fast_weights, norm_gain, frame_order, gate_input, conv_weights
):
    tok_rows = queries.shape[0]
    head_count = queries.shape[1] * queries.shape[2]
    head_size = queries.shape[3]
    query_rows = queries.reshape(tok_rows, head_count, head_size)
    key_rows = keys.reshape(tok_rows, head_count, head_size)
    value_rows = values.reshape(tok_rows, head_count, head_size)
    token_rates = rates.reshape(head_count, tok_rows)
    weights = fast_weights.reshape(head_count, 3, head_size, head_size)
    head_gains = norm_gain.reshape(head_count, head_size)
    first_pre = jnp.einsum(
        "thd,hfd->htf", key_rows, weights[:, 0], preferred_element_type=jnp.float32
    )
    third_pre = jnp.einsum(
        "thd,hfd->htf", key_rows, weights[:, 1], preferred_element_type=jnp.float32
    )
    sigmoid_first = jax.nn.sigmoid(first_pre)
    activated = first_pre * sigmoid_first
    hidden = (activated * third_pre).astype(jnp.bfloat16)
    target = (-token_rates.T[:, :, None] * value_rows.astype(jnp.float32)).astype(jnp.bfloat16)
    grad_down = jnp.einsum("thd,htf->hdf", target, hidden, preferred_element_type=jnp.float32)
    hidden_grad = jnp.einsum(
        "thd,hdf->htf", target, weights[:, 2], preferred_element_type=jnp.float32
    )
    grad_first_in = (
        hidden_grad * third_pre * sigmoid_first * (1.0 + first_pre * (1.0 - sigmoid_first))
    ).astype(jnp.bfloat16)
    grad_third_in = (hidden_grad * activated).astype(jnp.bfloat16)
    grad_first = jnp.einsum(
        "htf,thd->hfd", grad_first_in, key_rows, preferred_element_type=jnp.float32
    )
    grad_third = jnp.einsum(
        "htf,thd->hfd", grad_third_in, key_rows, preferred_element_type=jnp.float32
    )
    gradients = jnp.stack([grad_first, grad_third, grad_down], axis=1)
    row_share = lax.psum_scatter(gradients, "tok", scatter_dimension=2, tiled=True)
    row_count = row_share.shape[2]
    own_rows = lax.dynamic_slice_in_dim(weights, lax.axis_index("tok") * row_count, row_count, 2)
    updated = lax.all_gather(renormed(own_rows, row_share), "tok", axis=2, tiled=True)
    proj_first = jnp.einsum(
        "thd,hfd->thf", query_rows, updated[:, 0], preferred_element_type=jnp.float32
    )
    proj_third = jnp.einsum(
        "thd,hfd->thf", query_rows, updated[:, 1], preferred_element_type=jnp.float32
    )
    mixed_hidden = (jax.nn.silu(proj_first) * proj_third).astype(jnp.bfloat16)
    outputs = jnp.einsum(
        "thf,hdf->thd", mixed_hidden, updated[:, 2], preferred_element_type=jnp.float32
    )
    normed = (
        outputs
        * lax.rsqrt(jnp.mean(outputs * outputs, axis=-1, keepdims=True) + epsilon)
        * head_gains[None]
    )
    normed = normed.astype(jnp.bfloat16)
    height = gate_input.shape[0]
    col_width = gate_input.shape[2]
    shards = lax.axis_size("tok")
    full_width = col_width * shards
    channels_here = head_count * head_size
    frame_grid = normed.reshape(height, full_width, channels_here)
    own_taps = lax.dynamic_slice_in_dim(
        conv_weights, lax.axis_index("head") * channels_here, channels_here, 2
    )
    padded = jnp.pad(frame_grid, ((1, 1), (1, 1), (0, 0)))
    local_sum = jnp.zeros((height, full_width, channels_here), jnp.float32)
    for row_tap in range(3):
        for col_tap in range(3):
            local_sum = local_sum + own_taps[row_tap, col_tap] * padded[
                row_tap : row_tap + height, col_tap : col_tap + full_width
            ].astype(jnp.float32)
    outgoing = local_sum.astype(jnp.bfloat16).reshape(height, shards, col_width, channels_here)
    arrived = lax.all_to_all(outgoing, "tok", split_axis=1, concat_axis=1, tiled=True)
    frame_count = frame_order.shape[0]
    numbers = jnp.arange(frame_count, dtype=jnp.int32)
    inverse = jnp.sum(
        jnp.where(frame_order[None, :] == numbers[:, None], numbers[None, :], 0), axis=1
    )
    ordered = jnp.take(arrived, inverse, axis=1)
    tile_block = lax.all_to_all(ordered, "head", split_axis=1, concat_axis=3, tiled=True)
    return (tile_block.astype(jnp.float32) * jax.nn.silu(gate_input.astype(jnp.float32))).astype(
        jnp.bfloat16
    )


def local(queries, keys, values, rates, fast_weights, norm_gain, frame_order, gate_input, conv_weights):
    args = (
        queries, keys, values, rates, fast_weights, norm_gain, frame_order, gate_input, conv_weights
    )
    if fits_by_heads(queries, gate_input, frame_order):
        return by_heads(*args)
    return by_tokens(*args)


def solution(mesh):
    in_specs = (
        P(("groups", "tok"), "tile", "head", None),
        P(("groups", "tok"), "tile", "head", None),
        P(("groups", "tok"), "tile", "head", None),
        P("tile", "head", ("groups", "tok")),
        P("tile", "head", None, None, None),
        P("tile", "head", None),
        P("groups"),
        P(None, ("groups", "head"), "tok", "tile"),
        P(None, None, "tile"),
    )
    out_specs = P(None, ("groups", "head"), "tok", "tile")
    return jax.shard_map(local, mesh=mesh, in_specs=in_specs, out_specs=out_specs, check_vma=False)
```

```python
import functools

import jax
import jax.numpy as jnp
from jax import lax
from jax.experimental import pallas as pl
from jax.experimental.pallas import tpu as pltpu
from jax.sharding import PartitionSpec as P

epsilon = 1e-06
LANES = 128
VMEM_BYTES = 24 * 1024 * 1024


def split_lanes(source, scratch, rows, head_size):
    full = head_size // LANES
    tail = head_size - full * LANES
    wide = source.reshape(rows, head_size).astype(jnp.float32)
    for tile in range(full):
        scratch[tile] = wide[:, tile * LANES : (tile + 1) * LANES]
    scratch[full, :, 0:tail] = wide[:, full * LANES :]


def join_halves(first, second, tail):
    lane = lax.broadcasted_iota(jnp.int32, first[-1].shape, 1)
    middle = jnp.where(lane < tail, first[-1], pltpu.roll(second[-1], tail, 1))
    return first[:-1] + [middle] + second[:-1]


def part_halves(packed, head_size):
    full = head_size // LANES
    tail = head_size - full * LANES
    first = packed[:, :head_size]
    middle = packed[:, head_size : (full + 1) * LANES]
    second = jnp.concatenate([packed[:, (full + 1) * LANES :], middle], axis=1)
    return first, second


def partner_head(partner):
    return lax.axis_index("tok") ^ partner


def pack_pairs(head, rate_ref, key_tiles, value_tiles, out_ref, start, head_size):
    heads, tok_rows = rate_ref.shape
    half = tok_rows // 2
    full = head_size // LANES
    tail = head_size - full * LANES
    rate_row = -rate_ref[pl.ds(head, 1), :]
    rates = jnp.broadcast_to(rate_row, (LANES, tok_rows)).T
    for row, tiles in ((start, key_tiles), (start + half, value_tiles)):
        sides = []
        for side in range(2):
            parts = [
                tiles[tile, pl.ds(side * half * heads + head, half, stride=heads), :]
                for tile in range(full + 1)
            ]
            if tiles is value_tiles:
                rate = rates[side * half : (side + 1) * half]
                parts = [rate * part for part in parts]
            sides.append(parts)
        for tile, part in enumerate(join_halves(sides[0], sides[1], tail)):
            out_ref[row : row + half, tile * LANES : (tile + 1) * LANES] = part.astype(jnp.bfloat16)


def pack_query(head, heads, height, query_tiles, out_ref, start, head_size):
    tok_rows = query_tiles.shape[1] // heads
    half = tok_rows // 2
    width = tok_rows // height
    full = head_size // LANES
    tail = head_size - full * LANES
    sides = []
    for side in range(2):
        sides.append(
            [
                jnp.concatenate(
                    [
                        query_tiles[
                            tile, pl.ds(column * heads + head, height, stride=width * heads), :
                        ]
                        for column in range(side * width // 2, (side + 1) * width // 2)
                    ],
                    axis=0,
                )
                for tile in range(full + 1)
            ]
        )
    for tile, part in enumerate(join_halves(sides[0], sides[1], tail)):
        out_ref[start : start + half, tile * LANES : (tile + 1) * LANES] = part.astype(jnp.bfloat16)


def pack_mirror_kernel(key_ref, value_ref, rate_ref, *rest):
    outs, (key_tiles, value_tiles) = rest[:-2], rest[-2:]
    tok_rows, heads, head_size = key_ref.shape
    split_lanes(key_ref[...], key_tiles, tok_rows * heads, head_size)
    split_lanes(value_ref[...], value_tiles, tok_rows * heads, head_size)
    for partner, out_ref in enumerate(outs):
        head = partner_head(partner ^ (heads // 2))
        pack_pairs(head, rate_ref, key_tiles, value_tiles, out_ref, 0, head_size)


def pack_across_kernel(height, query_any, *rest):
    outs, (query_ref, query_tiles, sems) = rest[:-3], rest[-3:]
    tok_rows, heads, head_size = query_any.shape
    half = tok_rows // 2
    full = head_size // LANES
    pieces = sems.shape[0]
    rows = tok_rows // pieces
    copies = [
        pltpu.make_async_copy(
            query_any.at[pl.ds(piece * rows, rows)],
            query_ref.at[pl.ds(piece * rows, rows)],
            sems.at[piece],
        )
        for piece in range(pieces)
    ]
    for copy in copies:
        copy.start()
    for piece, copy in enumerate(copies):
        copy.wait()
        wide = query_ref[piece * rows : (piece + 1) * rows].reshape(rows * heads, head_size)
        wide = wide.astype(jnp.float32)
        place = slice(piece * rows * heads, (piece + 1) * rows * heads)
        for tile in range(full):
            query_tiles[tile, place] = wide[:, tile * LANES : (tile + 1) * LANES]
        query_tiles[full, place, 0 : head_size - full * LANES] = wide[:, full * LANES :]
    for partner in range(heads // 2):
        head = partner_head(partner ^ (heads // 2))
        start = partner % 2 * half
        pack_query(head, heads, height, query_tiles, outs[partner // 2], start, head_size)


def pack_near_kernel(height, unread, key_ref, value_ref, rate_ref, query_ref, *rest):
    outs, (key_tiles, value_tiles, query_tiles) = rest[unread:-3], rest[-3:]
    tok_rows, heads, head_size = key_ref.shape
    split_lanes(key_ref[...], key_tiles, tok_rows * heads, head_size)
    split_lanes(value_ref[...], value_tiles, tok_rows * heads, head_size)
    split_lanes(query_ref[...], query_tiles, tok_rows * heads, head_size)
    line = heads // 2
    for partner in range(line):
        head = partner_head(partner)
        pack_pairs(head, rate_ref, key_tiles, value_tiles, outs[partner], 0, head_size)
        pack_query(head, heads, height, query_tiles, outs[line + partner], 0, head_size)


def send_far(part, partner, other):
    blocks = lax.axis_size("head")
    count = lax.axis_size("tok") * blocks
    pairs = [(place, place ^ (partner * blocks + other)) for place in range(count)]
    return lax.ppermute(part, ("tok", "head"), pairs)


def relay(landed):
    return [part for one in landed for part in (one, send(one, 1))]


def send(part, partner):
    pairs = [(place, place ^ partner) for place in range(lax.axis_size("tok"))]
    return lax.ppermute(part, "tok", pairs)


def sigmoid(value):
    return 0.5 + 0.5 * jnp.tanh(0.5 * value)


def contract(first, second, dims):
    return lax.dot_general(first, second, (dims, ((), ())), preferred_element_type=jnp.float32)


NN = ((1,), (0,))
NT = ((1,), (1,))


def add_gradients(pair_refs, tok_rows, weight_ref, prior_ref, grad_ref):
    half = tok_rows // 2
    head_size = weight_ref.shape[-1]
    first_weight = weight_ref[0]
    third_weight = weight_ref[1]
    down_turned = weight_ref[2].astype(jnp.float32).T.astype(jnp.bfloat16)
    step = 2 if len(pair_refs) % 2 == 0 else 1
    for start in range(0, len(pair_refs), step):
        key_parts, target_parts = [], []
        for pair_ref in pair_refs[start : start + step]:
            key_parts.extend(part_halves(pair_ref[0:half, :], head_size))
            target_parts.extend(part_halves(pair_ref[half:tok_rows, :], head_size))
        key_rows = jnp.concatenate(key_parts, axis=0)
        target = jnp.concatenate(target_parts, axis=0)
        first_pre = contract(first_weight, key_rows, NT)
        third_pre = contract(third_weight, key_rows, NT)
        hidden_grad = contract(down_turned, target, NT)
        sigmoid_first = sigmoid(first_pre)
        activated = first_pre * sigmoid_first
        mixed = (activated * third_pre).astype(jnp.bfloat16)
        grad_first_in = (
            hidden_grad * third_pre * sigmoid_first * (1.0 + first_pre * (1.0 - sigmoid_first))
        ).astype(jnp.bfloat16)
        grad_third_in = (hidden_grad * activated).astype(jnp.bfloat16)
        grads = (
            contract(grad_first_in, key_rows, NN),
            contract(grad_third_in, key_rows, NN),
            contract(mixed, target, NN),
        )
        for index, grad in enumerate(grads):
            if start == 0 and prior_ref is None:
                grad_ref[index, :, 0:head_size] = grad
            elif start == 0:
                grad_ref[index, :, 0:head_size] = prior_ref[index, :, 0:head_size] + grad
            else:
                grad_ref[index, :, 0:head_size] += grad


def sum_kernel(count, tok_rows, prior, *refs):
    pair_refs, weight_ref, out_ref = refs[:count], refs[count], refs[-1]
    prior_ref = refs[count + 1] if prior else None
    add_gradients(pair_refs, tok_rows, weight_ref, prior_ref, out_ref)


def mirror_kernel(count, tok_rows, *refs):
    pair_refs, weight_ref, prior_ref = refs[:count], refs[count], refs[count + 1]
    out_ref, grad_ref = refs[-2:]
    head_size = weight_ref.shape[-1]
    full = head_size // LANES
    tail = head_size - full * LANES
    half = head_size // 2
    add_gradients(pair_refs, tok_rows, weight_ref, prior_ref, grad_ref)

    def tiles_of(index, rows):
        return [
            grad_ref[index, rows, tile * LANES : (tile + 1) * LANES] for tile in range(full + 1)
        ]

    both = join_halves(tiles_of(0, slice(0, head_size)), tiles_of(1, slice(0, head_size)), tail)
    down = join_halves(tiles_of(2, slice(0, half)), tiles_of(2, slice(half, head_size)), tail)
    for tile, (above, below) in enumerate(zip(both, down)):
        lanes = slice(tile * LANES, (tile + 1) * LANES)
        out_ref[0:head_size, lanes] = above.astype(jnp.bfloat16)
        out_ref[head_size : head_size + half, lanes] = below.astype(jnp.bfloat16)


def renorm(weight_ref, grad_ref, mirror_refs, out_ref):
    head_size = weight_ref.shape[-1]
    units = head_size // len(mirror_refs)
    firsts, thirds, downs = [], [], []
    for mirror_ref in mirror_refs:
        first, third = part_halves(mirror_ref[0:units, :], head_size)
        firsts.append(first)
        thirds.append(third)
        downs.extend(part_halves(mirror_ref[units:, :], head_size))
    first, third, down = (jnp.concatenate(parts, axis=0) for parts in (firsts, thirds, downs))
    for index, other in enumerate((first, third, down)):
        before = weight_ref[index].astype(jnp.float32)
        axis = 1
        if index == 2:
            before = before.T
            axis = 0
        grad = grad_ref[index, :, 0:head_size] + other.astype(jnp.float32)
        updated = before - grad
        scale_old = jnp.sqrt(jnp.mean(before * before, axis=axis, keepdims=True) + epsilon)
        scale_new = jnp.sqrt(jnp.mean(updated * updated, axis=axis, keepdims=True) + epsilon)
        out_ref[index] = (updated * (scale_old / scale_new)).astype(jnp.bfloat16)


def apply_shards(
    height, frames_here, parts, order_ref, weight_ref, gain_ref, tap_ref, grid_ref, turned_ref
):
    head_size = weight_ref.shape[-1]
    full = head_size // LANES
    width = grid_ref.shape[2] - 2
    top = 8
    edge = jnp.zeros((top, LANES), jnp.float32)
    whole = jnp.zeros(grid_ref.shape[3:], jnp.float32)
    for place in range(len(parts)):
        for tile in range(full + 1):
            grid_ref[place, tile, 0] = whole
            grid_ref[place, tile, width + 1] = whole
            for column in range(1, width + 1):
                grid_ref[place, tile, column, 0:top] = edge
                grid_ref[place, tile, column, top + height :] = edge
    gain = gain_ref[...]
    for place, (shard, queries) in enumerate(parts):
        rows = jnp.concatenate(part_halves(queries, head_size), axis=0)
        proj_first = contract(rows, weight_ref[0], NT)
        proj_third = contract(rows, weight_ref[1], NT)
        mixed = (proj_first * jax.nn.sigmoid(proj_first) * proj_third).astype(jnp.bfloat16)
        outputs = contract(mixed, weight_ref[2], NN)
        scale = lax.rsqrt(jnp.mean(outputs * outputs, axis=-1, keepdims=True) + epsilon)
        normed = (outputs * scale * gain).astype(jnp.bfloat16).astype(jnp.float32)
        frame = order_ref[shard]
        block = frame // frames_here
        slot = frame % frames_here
        for tile in range(full + 1):
            lanes = slice(tile * LANES, min((tile + 1) * LANES, head_size))
            for column in range(width):
                grid_ref[place, tile, column + 1, top : top + height, 0 : lanes.stop - lanes.start] = (
                    normed[column * height : (column + 1) * height, lanes]
                )
            taps = [
                tap_ref[index : index + 1, tile * LANES : (tile + 1) * LANES] for index in range(9)
            ]
            for column in range(width):
                total = None
                for row_tap in range(3):
                    first = top + row_tap - 1
                    for col_tap in range(3):
                        term = taps[row_tap * 3 + col_tap] * grid_ref[
                            place, tile, column + col_tap, first : first + height, :
                        ]
                        total = term if total is None else total + term
                turned_ref[
                    block, column, tile, pl.ds(slot, height, stride=frames_here), :
                ] = total


def apply_first_kernel(height, frames_here, near, far, order_ref, *refs):
    near_refs, far_refs = refs[: len(near)], refs[len(near) : len(near) + len(far)]
    before_ref, grad_ref, mirror_ref, gain_ref, tap_ref, weight_ref, turned_ref, grid_ref = refs[-8:]
    half = near_refs[0].shape[0]
    parts = [(shard, ref[...]) for shard, ref in zip(near, near_refs)]
    for shard, ref in zip(far, far_refs):
        parts.append((shard, ref[shard % 2 * half : (shard % 2 + 1) * half, :]))
    renorm(before_ref, grad_ref, [mirror_ref], weight_ref)
    apply_shards(
        height, frames_here, parts, order_ref, weight_ref, gain_ref, tap_ref, grid_ref, turned_ref
    )


def apply_last_kernel(height, frames_here, late, order, order_ref, *refs):
    query_refs = refs[: len(late)]
    weight_ref, done_ref, gain_ref, tap_ref = refs[len(late) : len(late) + 4]
    out_refs, (grid_ref, turned_ref) = refs[len(late) + 4 : -2], refs[-2:]
    turned_ref[...] = done_ref[...]
    parts = [(shard, ref[...]) for shard, ref in zip(late, query_refs)]
    apply_shards(
        height, frames_here, parts, order_ref, weight_ref, gain_ref, tap_ref, grid_ref, turned_ref
    )
    shards = turned_ref.shape[1]
    full = turned_ref.shape[2] - 1
    tail = weight_ref.shape[-1] - full * LANES
    blocks = turned_ref.shape[0]
    side_rows = turned_ref.shape[3] // 2
    for partner in range(shards):
        column = partner_head(partner)
        for other in range(blocks):
            block = lax.axis_index("head") ^ other
            sides = [
                [
                    turned_ref[block, column, tile, side * side_rows : (side + 1) * side_rows, :]
                    for tile in range(full + 1)
                ]
                for side in range(2)
            ]
            start = partner % 2 * side_rows
            if partner < 2 and other == 0:
                target, start = out_refs[partner], 0
            else:
                target = out_refs[2 + order.index((partner // 2 * 2, other))]
            for tile, part in enumerate(join_halves(sides[0], sides[1], tail)):
                target[start : start + side_rows, tile * LANES : (tile + 1) * LANES] = (
                    part.astype(jnp.bfloat16)
                )


def gate_kernel(blocks, shards, places, *refs):
    conv_refs = refs[: 2 * len(places)]
    gate_ref, out_any, product_ref, sems = refs[2 * len(places)], *refs[-3:]
    height = gate_ref.shape[0]
    frames_here = gate_ref.shape[1]
    head_size = gate_ref.shape[2] // blocks // shards
    side_rows = height * frames_here // 2
    rows_here = height // 2
    own = lax.axis_index("tok")
    odd = own % 2
    copies = []
    for index, (partner, other) in enumerate(places):
        one_ref, two_ref = conv_refs[2 * index : 2 * index + 2]
        one = one_ref[0:side_rows, :].astype(jnp.float32)
        two = two_ref[two_ref.shape[0] - side_rows :, :].astype(jnp.float32)
        low = part_halves(jnp.where(odd == 1, two, one), head_size)
        high = part_halves(jnp.where(odd == 1, one, two), head_size)
        head = (lax.axis_index("head") ^ other) * shards + ((own - odd) ^ partner)
        lanes = pl.ds(pl.multiple_of(head * head_size, 2 * head_size), 2 * head_size)
        for side in range(2):
            rows = slice(side * rows_here, (side + 1) * rows_here)
            conv = jnp.concatenate([low[side], high[side]], axis=1)
            conv = conv.reshape(rows_here, frames_here, 2 * head_size)
            gate = gate_ref[rows, :, lanes].astype(jnp.float32)
            product_ref[index, rows] = (conv * (gate * sigmoid(gate))).astype(jnp.bfloat16)
        copy = pltpu.make_async_copy(
            product_ref.at[index], out_any.at[:, :, lanes], sems.at[index]
        )
        copy.start()
        copies.append(copy)
    for copy in copies:
        copy.wait()


def in_vmem(count):
    return [pl.BlockSpec(memory_space=pltpu.VMEM)] * count


def call(kernel, out, operands, scratch=(), specs=None, leave=True):
    specs = specs or in_vmem(len(operands))
    operands = [
        pltpu.with_memory_space_constraint(item, pltpu.VMEM)
        if spec.memory_space == pltpu.VMEM
        else item
        for item, spec in zip(operands, specs)
    ]
    place = pltpu.VMEM if leave else pl.ANY
    if leave:
        out = jax.tree.map(lambda item: pltpu.VMEM(item.shape, item.dtype), out)
    return pl.pallas_call(
        kernel,
        out_shape=out,
        in_specs=specs,
        out_specs=jax.tree.map(lambda _: pl.BlockSpec(memory_space=place), out),
        scratch_shapes=scratch,
        compiler_params=pltpu.CompilerParams(vmem_limit_bytes=VMEM_BYTES),
        cost_estimate=pl.CostEstimate(flops=0, bytes_accessed=0, transcendentals=0),
    )(*operands)


def after(part, *earlier):
    anywhere = pl.BlockSpec(memory_space=pl.ANY)
    return pl.pallas_call(
        lambda *refs: None,
        out_shape=jax.ShapeDtypeStruct(part.shape, part.dtype),
        in_specs=[anywhere] * (1 + len(earlier)),
        out_specs=anywhere,
        input_output_aliases={0: 0},
        compiler_params=pltpu.CompilerParams(vmem_limit_bytes=1024 * 1024),
        cost_estimate=pl.CostEstimate(flops=0, bytes_accessed=0, transcendentals=0),
    )(part, *earlier)


def by_heads(
    queries, keys, values, rates, fast_weights, norm_gain, frame_order, gate_input, conv_weights
):
    tok_rows = queries.shape[0]
    head_count = queries.shape[1] * queries.shape[2]
    head_size = queries.shape[3]
    height, frames_here = gate_input.shape[:2]
    shards = lax.axis_size("tok")
    blocks = lax.axis_size("head")
    half = tok_rows // 2
    wide = 2 * head_size
    tiles = head_size // LANES + 1
    own = lax.axis_index("tok")
    own_channel = lax.axis_index("head") * head_count + own

    def rows_of(array):
        return array.reshape(tok_rows, head_count, head_size)

    def own_of(array, place):
        return lax.dynamic_index_in_dim(array, place, 0, keepdims=False)

    line = shards // 2
    tile_scratch = pltpu.VMEM((tiles, tok_rows * head_count, LANES), jnp.float32)
    token_rates = rates.reshape(head_count, tok_rows)
    chips = line // 2

    one = jax.ShapeDtypeStruct((tok_rows, wide), jnp.bfloat16)
    mirrored = call(
        pack_mirror_kernel,
        [one] * line,
        (rows_of(keys), rows_of(values), token_rates),
        (tile_scratch, tile_scratch),
    )
    mirrored = [mirrored[0]] + [send(mirrored[k], k) for k in range(1, line)]
    across = call(
        functools.partial(pack_across_kernel, height),
        [one] * chips,
        (rows_of(queries),),
        (
            pltpu.VMEM((tok_rows, head_count, head_size), jnp.bfloat16),
            tile_scratch,
            pltpu.SemaphoreType.DMA((4,)),
        ),
        specs=[pl.BlockSpec(memory_space=pl.ANY)],
    )
    across_landed = [send(part, line + 2 * index) for index, part in enumerate(across)]
    weights = fast_weights.reshape(head_count, 3, head_size, head_size)
    own_weights = own_of(weights, own)
    mirror_weights = own_of(weights, own ^ line)
    own_gain = own_of(norm_gain.reshape(head_count, 1, head_size), own)
    taps = conv_weights.reshape(9, blocks * head_count, head_size)
    own_taps = lax.dynamic_index_in_dim(taps, own_channel, 1, keepdims=False)
    own_taps = jnp.pad(own_taps, ((0, 0), (0, tiles * LANES - head_size)))
    frames = frame_order[own ^ jnp.arange(shards, dtype=jnp.int32)]
    grad_shape = (3, head_size, tiles * LANES)
    grad_struct = jax.ShapeDtypeStruct(grad_shape, jnp.float32)
    unread = pl.BlockSpec(memory_space=pl.ANY)
    mirror_sum = call(
        functools.partial(sum_kernel, 2, tok_rows, False),
        grad_struct,
        (*mirrored[:2], mirror_weights),
    )
    early = (across[0], own_weights, own_gain, own_taps, frames, mirror_sum)
    query_struct = jax.ShapeDtypeStruct((half, wide), jnp.bfloat16)
    packed = call(
        functools.partial(pack_near_kernel, height, len(early)),
        [one] * line + [query_struct] * line,
        (rows_of(keys), rows_of(values), token_rates, rows_of(queries), *early),
        (tile_scratch, tile_scratch, tile_scratch),
        specs=in_vmem(4) + [unread] * len(early),
    )
    near_queries = packed[line:]
    held = [after(part, *mirrored[1:], *across_landed) for part in packed[1:line]]
    near = [packed[0]] + [send(held[k - 1], k) for k in range(1, line)]
    ahead = (*across_landed, *held)
    crossing = call(
        functools.partial(mirror_kernel, line - 2, tok_rows),
        jax.ShapeDtypeStruct((head_size + head_size // 2, wide), jnp.bfloat16),
        (*mirrored[2:], mirror_weights, mirror_sum, *ahead),
        (pltpu.VMEM(grad_shape, jnp.float32),),
        specs=in_vmem(line) + [unread] * len(ahead),
    )
    crossed = send(crossing, line)
    own_sum = call(
        functools.partial(sum_kernel, 2, tok_rows, False),
        grad_struct,
        (*near[:2], own_weights, crossing),
        specs=in_vmem(3) + [unread],
    )
    across = relay([after(part, own_sum) for part in across_landed])
    gradients = call(
        functools.partial(sum_kernel, line - 2, tok_rows, True),
        grad_struct,
        (*near[2:], own_weights, own_sum),
    )
    mate_queries = send(after(near_queries[1], own_sum), 1)
    late_queries = [
        send(after(near_queries[k], *near[2:]), k) for k in range(2, line)
    ]
    side_rows = frames_here * height // 2
    first_shards, far_shards, late_shards = (0, 1), range(line, shards), range(2, line)
    grid_shape = (tiles, shards + 2, height + 16, LANES)
    turned_shape = (blocks, shards, tiles, 2 * side_rows, LANES)
    numbers = [pl.BlockSpec(memory_space=pltpu.SMEM)]
    updated, turned = call(
        functools.partial(apply_first_kernel, height, frames_here, first_shards, far_shards),
        [
            jax.ShapeDtypeStruct((3, head_size, head_size), jnp.bfloat16),
            jax.ShapeDtypeStruct(turned_shape, jnp.float32),
        ],
        (
            frames, near_queries[0], mate_queries, *across,
            own_weights, gradients, crossed, own_gain, own_taps,
        ),
        (pltpu.VMEM((2 + line, *grid_shape), jnp.float32),),
        specs=numbers + in_vmem(line + 7),
    )
    order = [(k, x) for k in range(0, shards, 2) for x in range(blocks)][1:]
    order = sorted(order, key=lambda place: (place != (line, 0), place))
    outgoing = call(
        functools.partial(apply_last_kernel, height, frames_here, late_shards, order),
        [jax.ShapeDtypeStruct((side_rows, wide), jnp.bfloat16)] * 2
        + [jax.ShapeDtypeStruct((2 * side_rows, wide), jnp.bfloat16)] * (shards // 2 * blocks - 1),
        (frames, *late_queries, updated, turned, own_gain, own_taps),
        (
            pltpu.VMEM((line - 2, *grid_shape), jnp.float32),
            pltpu.VMEM(turned_shape, jnp.float32),
        ),
        specs=numbers + in_vmem(line + 2),
    )
    landed = [send_far(part, k, x) for part, (k, x) in zip(outgoing[2:], order)]
    arrived = [outgoing[0], send(outgoing[1], 1), *relay(landed)]
    gate = gate_input.reshape(height, frames_here, gate_input.shape[3])
    places = [(0, 0), *order]
    gated = call(
        functools.partial(gate_kernel, blocks, shards, places),
        jax.ShapeDtypeStruct(gate.shape, jnp.bfloat16),
        (*arrived, gate),
        (
            pltpu.VMEM((len(places), *gate.shape[:2], wide), jnp.bfloat16),
            pltpu.SemaphoreType.DMA((len(places),)),
        ),
        leave=False,
    )
    return gated.reshape(gate_input.shape)


def fits_by_heads(queries, gate_input, frame_order):
    tok_rows, head_size = queries.shape[0], queries.shape[3]
    head_count = queries.shape[1] * queries.shape[2]
    height, frames_here, col_width = gate_input.shape[:3]
    shards = lax.axis_size("tok")
    return (
        head_count == shards
        and frame_order.shape[0] == shards
        and lax.axis_size("tile") == 1
        and col_width == 1
        and shards >= 8
        and shards & (shards - 1) == 0
        and head_size % LANES == LANES // 2
        and height % 8 == 0
        and tok_rows == height * shards
        and tok_rows % 64 == 0
        and head_size % 64 == 0
        and frames_here * height % 32 == 0
        and frames_here * lax.axis_size("head") == shards
        and lax.axis_size("head") & (lax.axis_size("head") - 1) == 0
    )


def renormed(previous, gradient):
    before = previous.astype(jnp.float32)
    updated = before - gradient
    scale_old = jnp.sqrt(jnp.mean(before * before, axis=-1, keepdims=True) + epsilon)
    scale_new = jnp.sqrt(jnp.mean(updated * updated, axis=-1, keepdims=True) + epsilon)
    return (updated * (scale_old / scale_new)).astype(jnp.bfloat16)


def by_tokens(
    queries, keys, values, rates, fast_weights, norm_gain, frame_order, gate_input, conv_weights
):
    tok_rows = queries.shape[0]
    head_count = queries.shape[1] * queries.shape[2]
    head_size = queries.shape[3]
    query_rows = queries.reshape(tok_rows, head_count, head_size)
    key_rows = keys.reshape(tok_rows, head_count, head_size)
    value_rows = values.reshape(tok_rows, head_count, head_size)
    token_rates = rates.reshape(head_count, tok_rows)
    weights = fast_weights.reshape(head_count, 3, head_size, head_size)
    head_gains = norm_gain.reshape(head_count, head_size)
    first_pre = jnp.einsum(
        "thd,hfd->htf", key_rows, weights[:, 0], preferred_element_type=jnp.float32
    )
    third_pre = jnp.einsum(
        "thd,hfd->htf", key_rows, weights[:, 1], preferred_element_type=jnp.float32
    )
    sigmoid_first = jax.nn.sigmoid(first_pre)
    activated = first_pre * sigmoid_first
    hidden = (activated * third_pre).astype(jnp.bfloat16)
    target = (-token_rates.T[:, :, None] * value_rows.astype(jnp.float32)).astype(jnp.bfloat16)
    grad_down = jnp.einsum("thd,htf->hdf", target, hidden, preferred_element_type=jnp.float32)
    hidden_grad = jnp.einsum(
        "thd,hdf->htf", target, weights[:, 2], preferred_element_type=jnp.float32
    )
    grad_first_in = (
        hidden_grad * third_pre * sigmoid_first * (1.0 + first_pre * (1.0 - sigmoid_first))
    ).astype(jnp.bfloat16)
    grad_third_in = (hidden_grad * activated).astype(jnp.bfloat16)
    grad_first = jnp.einsum(
        "htf,thd->hfd", grad_first_in, key_rows, preferred_element_type=jnp.float32
    )
    grad_third = jnp.einsum(
        "htf,thd->hfd", grad_third_in, key_rows, preferred_element_type=jnp.float32
    )
    gradients = jnp.stack([grad_first, grad_third, grad_down], axis=1)
    row_share = lax.psum_scatter(gradients, "tok", scatter_dimension=2, tiled=True)
    row_count = row_share.shape[2]
    own_rows = lax.dynamic_slice_in_dim(weights, lax.axis_index("tok") * row_count, row_count, 2)
    updated = lax.all_gather(renormed(own_rows, row_share), "tok", axis=2, tiled=True)
    proj_first = jnp.einsum(
        "thd,hfd->thf", query_rows, updated[:, 0], preferred_element_type=jnp.float32
    )
    proj_third = jnp.einsum(
        "thd,hfd->thf", query_rows, updated[:, 1], preferred_element_type=jnp.float32
    )
    mixed_hidden = (jax.nn.silu(proj_first) * proj_third).astype(jnp.bfloat16)
    outputs = jnp.einsum(
        "thf,hdf->thd", mixed_hidden, updated[:, 2], preferred_element_type=jnp.float32
    )
    normed = (
        outputs
        * lax.rsqrt(jnp.mean(outputs * outputs, axis=-1, keepdims=True) + epsilon)
        * head_gains[None]
    )
    normed = normed.astype(jnp.bfloat16)
    height = gate_input.shape[0]
    col_width = gate_input.shape[2]
    shards = lax.axis_size("tok")
    full_width = col_width * shards
    channels_here = head_count * head_size
    frame_grid = normed.reshape(height, full_width, channels_here)
    own_taps = lax.dynamic_slice_in_dim(
        conv_weights, lax.axis_index("head") * channels_here, channels_here, 2
    )
    padded = jnp.pad(frame_grid, ((1, 1), (1, 1), (0, 0)))
    local_sum = jnp.zeros((height, full_width, channels_here), jnp.float32)
    for row_tap in range(3):
        for col_tap in range(3):
            local_sum = local_sum + own_taps[row_tap, col_tap] * padded[
                row_tap : row_tap + height, col_tap : col_tap + full_width
            ].astype(jnp.float32)
    outgoing = local_sum.astype(jnp.bfloat16).reshape(height, shards, col_width, channels_here)
    arrived = lax.all_to_all(outgoing, "tok", split_axis=1, concat_axis=1, tiled=True)
    frame_count = frame_order.shape[0]
    numbers = jnp.arange(frame_count, dtype=jnp.int32)
    inverse = jnp.sum(
        jnp.where(frame_order[None, :] == numbers[:, None], numbers[None, :], 0), axis=1
    )
    ordered = jnp.take(arrived, inverse, axis=1)
    tile_block = lax.all_to_all(ordered, "head", split_axis=1, concat_axis=3, tiled=True)
    return (tile_block.astype(jnp.float32) * jax.nn.silu(gate_input.astype(jnp.float32))).astype(
        jnp.bfloat16
    )


def local(queries, keys, values, rates, fast_weights, norm_gain, frame_order, gate_input, conv_weights):
    args = (
        queries, keys, values, rates, fast_weights, norm_gain, frame_order, gate_input, conv_weights
    )
    if fits_by_heads(queries, gate_input, frame_order):
        return by_heads(*args)
    return by_tokens(*args)


def solution(mesh):
    in_specs = (
        P(("groups", "tok"), "tile", "head", None),
        P(("groups", "tok"), "tile", "head", None),
        P(("groups", "tok"), "tile", "head", None),
        P("tile", "head", ("groups", "tok")),
        P("tile", "head", None, None, None),
        P("tile", "head", None),
        P("groups"),
        P(None, ("groups", "head"), "tok", "tile"),
        P(None, None, "tile"),
    )
    out_specs = P(None, ("groups", "head"), "tok", "tile")
    return jax.shard_map(local, mesh=mesh, in_specs=in_specs, out_specs=out_specs, check_vma=False)
```

```python
import functools

import jax
import jax.numpy as jnp
from jax import lax
from jax.experimental import pallas as pl
from jax.experimental.pallas import tpu as pltpu
from jax.sharding import PartitionSpec as P

epsilon = 1e-06
LANES = 128
VMEM_BYTES = 24 * 1024 * 1024


def split_lanes(source, scratch, rows, head_size):
    full = head_size // LANES
    tail = head_size - full * LANES
    wide = source.reshape(rows, head_size).astype(jnp.float32)
    for tile in range(full):
        scratch[tile] = wide[:, tile * LANES : (tile + 1) * LANES]
    scratch[full, :, 0:tail] = wide[:, full * LANES :]


def join_halves(first, second, tail):
    lane = lax.broadcasted_iota(jnp.int32, first[-1].shape, 1)
    middle = jnp.where(lane < tail, first[-1], pltpu.roll(second[-1], tail, 1))
    return first[:-1] + [middle] + second[:-1]


def part_halves(packed, head_size):
    full = head_size // LANES
    tail = head_size - full * LANES
    first = packed[:, :head_size]
    middle = packed[:, head_size : (full + 1) * LANES]
    second = jnp.concatenate([packed[:, (full + 1) * LANES :], middle], axis=1)
    return first, second


def partner_head(partner):
    return lax.axis_index("tok") ^ partner


def pack_pairs(head, rate_ref, key_tiles, value_tiles, out_ref, start, head_size):
    heads, tok_rows = rate_ref.shape
    half = tok_rows // 2
    full = head_size // LANES
    tail = head_size - full * LANES
    rate_row = -rate_ref[pl.ds(head, 1), :]
    rates = jnp.broadcast_to(rate_row, (LANES, tok_rows)).T
    for row, tiles in ((start, key_tiles), (start + half, value_tiles)):
        sides = []
        for side in range(2):
            parts = [
                tiles[tile, pl.ds(side * half * heads + head, half, stride=heads), :]
                for tile in range(full + 1)
            ]
            if tiles is value_tiles:
                rate = rates[side * half : (side + 1) * half]
                parts = [rate * part for part in parts]
            sides.append(parts)
        for tile, part in enumerate(join_halves(sides[0], sides[1], tail)):
            out_ref[row : row + half, tile * LANES : (tile + 1) * LANES] = part.astype(jnp.bfloat16)


def pack_query(head, heads, height, query_tiles, out_ref, start, head_size):
    tok_rows = query_tiles.shape[1] // heads
    half = tok_rows // 2
    width = tok_rows // height
    full = head_size // LANES
    tail = head_size - full * LANES
    sides = []
    for side in range(2):
        sides.append(
            [
                jnp.concatenate(
                    [
                        query_tiles[
                            tile, pl.ds(column * heads + head, height, stride=width * heads), :
                        ]
                        for column in range(side * width // 2, (side + 1) * width // 2)
                    ],
                    axis=0,
                )
                for tile in range(full + 1)
            ]
        )
    for tile, part in enumerate(join_halves(sides[0], sides[1], tail)):
        out_ref[start : start + half, tile * LANES : (tile + 1) * LANES] = part.astype(jnp.bfloat16)


def pack_mirror_kernel(key_ref, value_ref, rate_ref, *rest):
    outs, (key_tiles, value_tiles) = rest[:-2], rest[-2:]
    tok_rows, heads, head_size = key_ref.shape
    split_lanes(key_ref[...], key_tiles, tok_rows * heads, head_size)
    split_lanes(value_ref[...], value_tiles, tok_rows * heads, head_size)
    for partner, out_ref in enumerate(outs):
        head = partner_head(partner ^ (heads // 2))
        pack_pairs(head, rate_ref, key_tiles, value_tiles, out_ref, 0, head_size)


def pack_across_kernel(height, query_any, *rest):
    outs, (query_ref, query_tiles, sems) = rest[:-3], rest[-3:]
    tok_rows, heads, head_size = query_any.shape
    half = tok_rows // 2
    full = head_size // LANES
    pieces = sems.shape[0]
    rows = tok_rows // pieces
    copies = [
        pltpu.make_async_copy(
            query_any.at[pl.ds(piece * rows, rows)],
            query_ref.at[pl.ds(piece * rows, rows)],
            sems.at[piece],
        )
        for piece in range(pieces)
    ]
    for copy in copies:
        copy.start()
    for piece, copy in enumerate(copies):
        copy.wait()
        wide = query_ref[piece * rows : (piece + 1) * rows].reshape(rows * heads, head_size)
        wide = wide.astype(jnp.float32)
        place = slice(piece * rows * heads, (piece + 1) * rows * heads)
        for tile in range(full):
            query_tiles[tile, place] = wide[:, tile * LANES : (tile + 1) * LANES]
        query_tiles[full, place, 0 : head_size - full * LANES] = wide[:, full * LANES :]
    for partner in range(heads // 2):
        head = partner_head(partner ^ (heads // 2))
        start = partner % 2 * half
        pack_query(head, heads, height, query_tiles, outs[partner // 2], start, head_size)


def pack_near_kernel(height, unread, key_ref, value_ref, rate_ref, query_ref, *rest):
    outs, (key_tiles, value_tiles, query_tiles) = rest[unread:-3], rest[-3:]
    tok_rows, heads, head_size = key_ref.shape
    split_lanes(key_ref[...], key_tiles, tok_rows * heads, head_size)
    split_lanes(value_ref[...], value_tiles, tok_rows * heads, head_size)
    split_lanes(query_ref[...], query_tiles, tok_rows * heads, head_size)
    line = heads // 2
    for partner in range(line):
        head = partner_head(partner)
        pack_pairs(head, rate_ref, key_tiles, value_tiles, outs[partner], 0, head_size)
        pack_query(head, heads, height, query_tiles, outs[line + partner], 0, head_size)


def send_far(part, partner, other):
    blocks = lax.axis_size("head")
    count = lax.axis_size("tok") * blocks
    pairs = [(place, place ^ (partner * blocks + other)) for place in range(count)]
    return lax.ppermute(part, ("tok", "head"), pairs)


def relay(landed):
    return [part for one in landed for part in (one, send(one, 1))]


def send(part, partner):
    pairs = [(place, place ^ partner) for place in range(lax.axis_size("tok"))]
    return lax.ppermute(part, "tok", pairs)


def sigmoid(value):
    return 0.5 + 0.5 * jnp.tanh(0.5 * value)


def contract(first, second, dims):
    return lax.dot_general(first, second, (dims, ((), ())), preferred_element_type=jnp.float32)


NN = ((1,), (0,))
NT = ((1,), (1,))


def add_gradients(pair_refs, tok_rows, weight_ref, prior_ref, grad_ref):
    half = tok_rows // 2
    head_size = weight_ref.shape[-1]
    first_weight = weight_ref[0]
    third_weight = weight_ref[1]
    down_turned = weight_ref[2].astype(jnp.float32).T.astype(jnp.bfloat16)
    step = 2 if len(pair_refs) % 2 == 0 else 1
    for start in range(0, len(pair_refs), step):
        key_parts, target_parts = [], []
        for pair_ref in pair_refs[start : start + step]:
            key_parts.extend(part_halves(pair_ref[0:half, :], head_size))
            target_parts.extend(part_halves(pair_ref[half:tok_rows, :], head_size))
        key_rows = jnp.concatenate(key_parts, axis=0)
        target = jnp.concatenate(target_parts, axis=0)
        first_pre = contract(first_weight, key_rows, NT)
        third_pre = contract(third_weight, key_rows, NT)
        hidden_grad = contract(down_turned, target, NT)
        sigmoid_first = sigmoid(first_pre)
        activated = first_pre * sigmoid_first
        mixed = (activated * third_pre).astype(jnp.bfloat16)
        grad_first_in = (
            hidden_grad * third_pre * sigmoid_first * (1.0 + first_pre * (1.0 - sigmoid_first))
        ).astype(jnp.bfloat16)
        grad_third_in = (hidden_grad * activated).astype(jnp.bfloat16)
        grads = (
            contract(grad_first_in, key_rows, NN),
            contract(grad_third_in, key_rows, NN),
            contract(mixed, target, NN),
        )
        for index, grad in enumerate(grads):
            if start == 0 and prior_ref is None:
                grad_ref[index, :, 0:head_size] = grad
            elif start == 0:
                grad_ref[index, :, 0:head_size] = prior_ref[index, :, 0:head_size] + grad
            else:
                grad_ref[index, :, 0:head_size] += grad


def sum_kernel(count, tok_rows, prior, *refs):
    pair_refs, weight_ref, out_ref = refs[:count], refs[count], refs[-1]
    prior_ref = refs[count + 1] if prior else None
    add_gradients(pair_refs, tok_rows, weight_ref, prior_ref, out_ref)


def mirror_kernel(count, tok_rows, *refs):
    pair_refs, weight_ref, prior_ref = refs[:count], refs[count], refs[count + 1]
    out_ref, grad_ref = refs[-2:]
    head_size = weight_ref.shape[-1]
    full = head_size // LANES
    tail = head_size - full * LANES
    half = head_size // 2
    add_gradients(pair_refs, tok_rows, weight_ref, prior_ref, grad_ref)

    def tiles_of(index, rows):
        return [
            grad_ref[index, rows, tile * LANES : (tile + 1) * LANES] for tile in range(full + 1)
        ]

    both = join_halves(tiles_of(0, slice(0, head_size)), tiles_of(1, slice(0, head_size)), tail)
    down = join_halves(tiles_of(2, slice(0, half)), tiles_of(2, slice(half, head_size)), tail)
    for tile, (above, below) in enumerate(zip(both, down)):
        lanes = slice(tile * LANES, (tile + 1) * LANES)
        out_ref[0:head_size, lanes] = above.astype(jnp.bfloat16)
        out_ref[head_size : head_size + half, lanes] = below.astype(jnp.bfloat16)


def renorm(weight_ref, grad_ref, mirror_refs, out_ref):
    head_size = weight_ref.shape[-1]
    units = head_size // len(mirror_refs)
    firsts, thirds, downs = [], [], []
    for mirror_ref in mirror_refs:
        first, third = part_halves(mirror_ref[0:units, :], head_size)
        firsts.append(first)
        thirds.append(third)
        downs.extend(part_halves(mirror_ref[units:, :], head_size))
    first, third, down = (jnp.concatenate(parts, axis=0) for parts in (firsts, thirds, downs))
    whole = head_size // LANES * LANES
    tail = head_size - whole
    for index, other in enumerate((first, third, down)):
        before = weight_ref[index].astype(jnp.float32)
        axis = 1
        if index == 2:
            before = before.T
            axis = 0
        grad = grad_ref[index, :, 0:head_size] + other.astype(jnp.float32)
        updated = before - grad
        scale_old = jnp.sqrt(jnp.mean(before * before, axis=axis, keepdims=True) + epsilon)
        scale_new = jnp.sqrt(jnp.mean(updated * updated, axis=axis, keepdims=True) + epsilon)
        result = (updated * (scale_old / scale_new)).astype(jnp.bfloat16)
        if index == 2:
            out_ref[2 * head_size :, :] = result
        else:
            out_ref[index * whole : (index + 1) * whole, :] = result[0:whole]
            start = 2 * whole + index * tail
            out_ref[start : start + tail, :] = result[whole:]


def apply_shards(
    height, frames_here, parts, order_ref, weight_ref, gain_ref, tap_ref, grid_ref, turned_ref
):
    head_size = weight_ref.shape[-1]
    full = head_size // LANES
    width = grid_ref.shape[2] - 2
    top = 8
    edge = jnp.zeros((top, LANES), jnp.float32)
    whole = jnp.zeros(grid_ref.shape[3:], jnp.float32)
    for place in range(len(parts)):
        for tile in range(full + 1):
            grid_ref[place, tile, 0] = whole
            grid_ref[place, tile, width + 1] = whole
            for column in range(1, width + 1):
                grid_ref[place, tile, column, 0:top] = edge
                grid_ref[place, tile, column, top + height :] = edge
    gain = gain_ref[...]
    even = full * LANES
    for place, (shard, queries) in enumerate(parts):
        rows = jnp.concatenate(part_halves(queries, head_size), axis=0)
        both = contract(rows, weight_ref[0 : 2 * head_size, :], NT)
        first, third, last = both[:, 0:even], both[:, even : 2 * even], both[:, 2 * even :]
        mixed = first * jax.nn.sigmoid(first) * third
        mixed_last = last * jax.nn.sigmoid(last) * pltpu.roll(last, head_size - even, 1)
        mixed = jnp.concatenate([mixed, mixed_last[:, 0 : head_size - even]], axis=1)
        outputs = contract(mixed.astype(jnp.bfloat16), weight_ref[2 * head_size :, :], NN)
        scale = lax.rsqrt(jnp.mean(outputs * outputs, axis=-1, keepdims=True) + epsilon)
        normed = (outputs * scale * gain).astype(jnp.bfloat16).astype(jnp.float32)
        frame = order_ref[shard]
        block = frame // frames_here
        slot = frame % frames_here
        for tile in range(full + 1):
            lanes = slice(tile * LANES, min((tile + 1) * LANES, head_size))
            for column in range(width):
                grid_ref[place, tile, column + 1, top : top + height, 0 : lanes.stop - lanes.start] = (
                    normed[column * height : (column + 1) * height, lanes]
                )
            taps = [
                tap_ref[index : index + 1, tile * LANES : (tile + 1) * LANES] for index in range(9)
            ]
            for column in range(width):
                total = None
                for row_tap in range(3):
                    first = top + row_tap - 1
                    for col_tap in range(3):
                        term = taps[row_tap * 3 + col_tap] * grid_ref[
                            place, tile, column + col_tap, first : first + height, :
                        ]
                        total = term if total is None else total + term
                turned_ref[
                    block, column, tile, pl.ds(slot, height, stride=frames_here), :
                ] = total


def apply_first_kernel(height, frames_here, near, far, order_ref, *refs):
    near_refs, far_refs = refs[: len(near)], refs[len(near) : len(near) + len(far)]
    before_ref, grad_ref, mirror_ref, gain_ref, tap_ref, weight_ref, turned_ref, grid_ref = refs[-8:]
    half = near_refs[0].shape[0]
    parts = [(shard, ref[...]) for shard, ref in zip(near, near_refs)]
    for shard, ref in zip(far, far_refs):
        parts.append((shard, ref[shard % 2 * half : (shard % 2 + 1) * half, :]))
    renorm(before_ref, grad_ref, [mirror_ref], weight_ref)
    apply_shards(
        height, frames_here, parts, order_ref, weight_ref, gain_ref, tap_ref, grid_ref, turned_ref
    )


def apply_last_kernel(height, frames_here, late, order, order_ref, *refs):
    query_refs = refs[: len(late)]
    weight_ref, done_ref, gain_ref, tap_ref = refs[len(late) : len(late) + 4]
    out_refs, (grid_ref, turned_ref) = refs[len(late) + 4 : -2], refs[-2:]
    turned_ref[...] = done_ref[...]
    parts = [(shard, ref[...]) for shard, ref in zip(late, query_refs)]
    apply_shards(
        height, frames_here, parts, order_ref, weight_ref, gain_ref, tap_ref, grid_ref, turned_ref
    )
    shards = turned_ref.shape[1]
    full = turned_ref.shape[2] - 1
    tail = weight_ref.shape[-1] - full * LANES
    blocks = turned_ref.shape[0]
    side_rows = turned_ref.shape[3] // 2
    for partner in range(shards):
        column = partner_head(partner)
        for other in range(blocks):
            block = lax.axis_index("head") ^ other
            sides = [
                [
                    turned_ref[block, column, tile, side * side_rows : (side + 1) * side_rows, :]
                    for tile in range(full + 1)
                ]
                for side in range(2)
            ]
            start = partner % 2 * side_rows
            if partner < 2 and other == 0:
                target, start = out_refs[partner], 0
            else:
                target = out_refs[2 + order.index((partner // 2 * 2, other))]
            for tile, part in enumerate(join_halves(sides[0], sides[1], tail)):
                target[start : start + side_rows, tile * LANES : (tile + 1) * LANES] = (
                    part.astype(jnp.bfloat16)
                )


def gate_kernel(blocks, shards, places, *refs):
    conv_refs = refs[: 2 * len(places)]
    gate_ref, out_any, product_ref, sems = refs[2 * len(places)], *refs[-3:]
    height = gate_ref.shape[0]
    frames_here = gate_ref.shape[1]
    head_size = gate_ref.shape[2] // blocks // shards
    side_rows = height * frames_here // 2
    rows_here = height // 2
    own = lax.axis_index("tok")
    odd = own % 2
    copies = []
    for index, (partner, other) in enumerate(places):
        one_ref, two_ref = conv_refs[2 * index : 2 * index + 2]
        one = one_ref[0:side_rows, :].astype(jnp.float32)
        two = two_ref[two_ref.shape[0] - side_rows :, :].astype(jnp.float32)
        low = part_halves(jnp.where(odd == 1, two, one), head_size)
        high = part_halves(jnp.where(odd == 1, one, two), head_size)
        head = (lax.axis_index("head") ^ other) * shards + ((own - odd) ^ partner)
        lanes = pl.ds(pl.multiple_of(head * head_size, 2 * head_size), 2 * head_size)
        for side in range(2):
            rows = slice(side * rows_here, (side + 1) * rows_here)
            conv = jnp.concatenate([low[side], high[side]], axis=1)
            conv = conv.reshape(rows_here, frames_here, 2 * head_size)
            gate = gate_ref[rows, :, lanes].astype(jnp.float32)
            product_ref[index, rows] = (conv * (gate * sigmoid(gate))).astype(jnp.bfloat16)
        copy = pltpu.make_async_copy(
            product_ref.at[index], out_any.at[:, :, lanes], sems.at[index]
        )
        copy.start()
        copies.append(copy)
    for copy in copies:
        copy.wait()


def in_vmem(count):
    return [pl.BlockSpec(memory_space=pltpu.VMEM)] * count


def call(kernel, out, operands, scratch=(), specs=None, leave=True):
    specs = specs or in_vmem(len(operands))
    operands = [
        pltpu.with_memory_space_constraint(item, pltpu.VMEM)
        if spec.memory_space == pltpu.VMEM
        else item
        for item, spec in zip(operands, specs)
    ]
    place = pltpu.VMEM if leave else pl.ANY
    if leave:
        out = jax.tree.map(lambda item: pltpu.VMEM(item.shape, item.dtype), out)
    return pl.pallas_call(
        kernel,
        out_shape=out,
        in_specs=specs,
        out_specs=jax.tree.map(lambda _: pl.BlockSpec(memory_space=place), out),
        scratch_shapes=scratch,
        compiler_params=pltpu.CompilerParams(vmem_limit_bytes=VMEM_BYTES),
        cost_estimate=pl.CostEstimate(flops=0, bytes_accessed=0, transcendentals=0),
    )(*operands)


def after(part, *earlier):
    anywhere = pl.BlockSpec(memory_space=pl.ANY)
    return pl.pallas_call(
        lambda *refs: None,
        out_shape=jax.ShapeDtypeStruct(part.shape, part.dtype),
        in_specs=[anywhere] * (1 + len(earlier)),
        out_specs=anywhere,
        input_output_aliases={0: 0},
        compiler_params=pltpu.CompilerParams(vmem_limit_bytes=1024 * 1024),
        cost_estimate=pl.CostEstimate(flops=0, bytes_accessed=0, transcendentals=0),
    )(part, *earlier)


def by_heads(
    queries, keys, values, rates, fast_weights, norm_gain, frame_order, gate_input, conv_weights
):
    tok_rows = queries.shape[0]
    head_count = queries.shape[1] * queries.shape[2]
    head_size = queries.shape[3]
    height, frames_here = gate_input.shape[:2]
    shards = lax.axis_size("tok")
    blocks = lax.axis_size("head")
    half = tok_rows // 2
    wide = 2 * head_size
    tiles = head_size // LANES + 1
    own = lax.axis_index("tok")
    own_channel = lax.axis_index("head") * head_count + own

    def rows_of(array):
        return array.reshape(tok_rows, head_count, head_size)

    def own_of(array, place):
        return lax.dynamic_index_in_dim(array, place, 0, keepdims=False)

    line = shards // 2
    tile_scratch = pltpu.VMEM((tiles, tok_rows * head_count, LANES), jnp.float32)
    token_rates = rates.reshape(head_count, tok_rows)
    chips = line // 2

    one = jax.ShapeDtypeStruct((tok_rows, wide), jnp.bfloat16)
    mirrored = call(
        pack_mirror_kernel,
        [one] * line,
        (rows_of(keys), rows_of(values), token_rates),
        (tile_scratch, tile_scratch),
    )
    mirrored = [mirrored[0]] + [send(mirrored[k], k) for k in range(1, line)]
    across = call(
        functools.partial(pack_across_kernel, height),
        [one] * chips,
        (pltpu.with_memory_space_constraint(rows_of(queries), pltpu.HBM),),
        (
            pltpu.VMEM((tok_rows, head_count, head_size), jnp.bfloat16),
            tile_scratch,
            pltpu.SemaphoreType.DMA((4,)),
        ),
        specs=[pl.BlockSpec(memory_space=pltpu.HBM)],
    )
    across_landed = [send(part, line + 2 * index) for index, part in enumerate(across)]
    weights = fast_weights.reshape(head_count, 3, head_size, head_size)
    own_weights = own_of(weights, own)
    mirror_weights = own_of(weights, own ^ line)
    own_gain = own_of(norm_gain.reshape(head_count, 1, head_size), own)
    taps = conv_weights.reshape(9, blocks * head_count, head_size)
    own_taps = lax.dynamic_index_in_dim(taps, own_channel, 1, keepdims=False)
    own_taps = jnp.pad(own_taps, ((0, 0), (0, tiles * LANES - head_size)))
    frames = frame_order[own ^ jnp.arange(shards, dtype=jnp.int32)]
    grad_shape = (3, head_size, tiles * LANES)
    grad_struct = jax.ShapeDtypeStruct(grad_shape, jnp.float32)
    unread = pl.BlockSpec(memory_space=pl.ANY)
    mirror_sum = call(
        functools.partial(sum_kernel, 2, tok_rows, False),
        grad_struct,
        (*mirrored[:2], mirror_weights),
    )
    early = (across[0], own_weights, own_gain, own_taps, frames, mirror_sum)
    query_struct = jax.ShapeDtypeStruct((half, wide), jnp.bfloat16)
    packed = call(
        functools.partial(pack_near_kernel, height, len(early)),
        [one] * line + [query_struct] * line,
        (rows_of(keys), rows_of(values), token_rates, rows_of(queries), *early),
        (tile_scratch, tile_scratch, tile_scratch),
        specs=in_vmem(4) + [unread] * len(early),
    )
    near_queries = packed[line:]
    held = [after(part, *mirrored[1:], *across_landed) for part in packed[1:line]]
    near = [packed[0]] + [send(held[k - 1], k) for k in range(1, line)]
    ahead = (*across_landed, *held)
    crossing = call(
        functools.partial(mirror_kernel, line - 2, tok_rows),
        jax.ShapeDtypeStruct((head_size + head_size // 2, wide), jnp.bfloat16),
        (*mirrored[2:], mirror_weights, mirror_sum, *ahead),
        (pltpu.VMEM(grad_shape, jnp.float32),),
        specs=in_vmem(line) + [unread] * len(ahead),
    )
    crossed = send(crossing, line)
    own_sum = call(
        functools.partial(sum_kernel, 2, tok_rows, False),
        grad_struct,
        (*near[:2], own_weights, crossing),
        specs=in_vmem(3) + [unread],
    )
    across = relay([after(part, own_sum) for part in across_landed])
    gradients = call(
        functools.partial(sum_kernel, line - 2, tok_rows, True),
        grad_struct,
        (*near[2:], own_weights, own_sum),
    )
    mate_queries = send(after(near_queries[1], own_sum), 1)
    late_queries = [
        send(after(near_queries[k], *near[2:]), k) for k in range(2, line)
    ]
    side_rows = frames_here * height // 2
    first_shards, far_shards, late_shards = (0, 1), range(line, shards), range(2, line)
    grid_shape = (tiles, shards + 2, height + 16, LANES)
    turned_shape = (blocks, shards, tiles, 2 * side_rows, LANES)
    numbers = [pl.BlockSpec(memory_space=pltpu.SMEM)]
    updated, turned = call(
        functools.partial(apply_first_kernel, height, frames_here, first_shards, far_shards),
        [
            jax.ShapeDtypeStruct((3 * head_size, head_size), jnp.bfloat16),
            jax.ShapeDtypeStruct(turned_shape, jnp.float32),
        ],
        (
            frames, near_queries[0], mate_queries, *across,
            own_weights, gradients, crossed, own_gain, own_taps,
        ),
        (pltpu.VMEM((2 + line, *grid_shape), jnp.float32),),
        specs=numbers + in_vmem(line + 7),
    )
    order = [(k, x) for k in range(0, shards, 2) for x in range(blocks)][1:]
    order = sorted(order, key=lambda place: (place != (line, 0), place))
    outgoing = call(
        functools.partial(apply_last_kernel, height, frames_here, late_shards, order),
        [jax.ShapeDtypeStruct((side_rows, wide), jnp.bfloat16)] * 2
        + [jax.ShapeDtypeStruct((2 * side_rows, wide), jnp.bfloat16)] * (shards // 2 * blocks - 1),
        (frames, *late_queries, updated, turned, own_gain, own_taps),
        (
            pltpu.VMEM((line - 2, *grid_shape), jnp.float32),
            pltpu.VMEM(turned_shape, jnp.float32),
        ),
        specs=numbers + in_vmem(line + 2),
    )
    landed = [send_far(part, k, x) for part, (k, x) in zip(outgoing[2:], order)]
    arrived = [outgoing[0], send(outgoing[1], 1), *relay(landed)]
    gate = gate_input.reshape(height, frames_here, gate_input.shape[3])
    places = [(0, 0), *order]
    gated = call(
        functools.partial(gate_kernel, blocks, shards, places),
        jax.ShapeDtypeStruct(gate.shape, jnp.bfloat16),
        (*arrived, gate),
        (
            pltpu.VMEM((len(places), *gate.shape[:2], wide), jnp.bfloat16),
            pltpu.SemaphoreType.DMA((len(places),)),
        ),
        leave=False,
    )
    return gated.reshape(gate_input.shape)


def fits_by_heads(queries, gate_input, frame_order):
    tok_rows, head_size = queries.shape[0], queries.shape[3]
    head_count = queries.shape[1] * queries.shape[2]
    height, frames_here, col_width = gate_input.shape[:3]
    shards = lax.axis_size("tok")
    return (
        head_count == shards
        and frame_order.shape[0] == shards
        and lax.axis_size("tile") == 1
        and col_width == 1
        and shards >= 8
        and shards & (shards - 1) == 0
        and head_size % LANES == LANES // 2
        and height % 8 == 0
        and tok_rows == height * shards
        and tok_rows % 64 == 0
        and head_size % 64 == 0
        and frames_here * height % 32 == 0
        and frames_here * lax.axis_size("head") == shards
        and lax.axis_size("head") & (lax.axis_size("head") - 1) == 0
    )


def renormed(previous, gradient):
    before = previous.astype(jnp.float32)
    updated = before - gradient
    scale_old = jnp.sqrt(jnp.mean(before * before, axis=-1, keepdims=True) + epsilon)
    scale_new = jnp.sqrt(jnp.mean(updated * updated, axis=-1, keepdims=True) + epsilon)
    return (updated * (scale_old / scale_new)).astype(jnp.bfloat16)


def by_tokens(
    queries, keys, values, rates, fast_weights, norm_gain, frame_order, gate_input, conv_weights
):
    tok_rows = queries.shape[0]
    head_count = queries.shape[1] * queries.shape[2]
    head_size = queries.shape[3]
    query_rows = queries.reshape(tok_rows, head_count, head_size)
    key_rows = keys.reshape(tok_rows, head_count, head_size)
    value_rows = values.reshape(tok_rows, head_count, head_size)
    token_rates = rates.reshape(head_count, tok_rows)
    weights = fast_weights.reshape(head_count, 3, head_size, head_size)
    head_gains = norm_gain.reshape(head_count, head_size)
    first_pre = jnp.einsum(
        "thd,hfd->htf", key_rows, weights[:, 0], preferred_element_type=jnp.float32
    )
    third_pre = jnp.einsum(
        "thd,hfd->htf", key_rows, weights[:, 1], preferred_element_type=jnp.float32
    )
    sigmoid_first = jax.nn.sigmoid(first_pre)
    activated = first_pre * sigmoid_first
    hidden = (activated * third_pre).astype(jnp.bfloat16)
    target = (-token_rates.T[:, :, None] * value_rows.astype(jnp.float32)).astype(jnp.bfloat16)
    grad_down = jnp.einsum("thd,htf->hdf", target, hidden, preferred_element_type=jnp.float32)
    hidden_grad = jnp.einsum(
        "thd,hdf->htf", target, weights[:, 2], preferred_element_type=jnp.float32
    )
    grad_first_in = (
        hidden_grad * third_pre * sigmoid_first * (1.0 + first_pre * (1.0 - sigmoid_first))
    ).astype(jnp.bfloat16)
    grad_third_in = (hidden_grad * activated).astype(jnp.bfloat16)
    grad_first = jnp.einsum(
        "htf,thd->hfd", grad_first_in, key_rows, preferred_element_type=jnp.float32
    )
    grad_third = jnp.einsum(
        "htf,thd->hfd", grad_third_in, key_rows, preferred_element_type=jnp.float32
    )
    gradients = jnp.stack([grad_first, grad_third, grad_down], axis=1)
    row_share = lax.psum_scatter(gradients, "tok", scatter_dimension=2, tiled=True)
    row_count = row_share.shape[2]
    own_rows = lax.dynamic_slice_in_dim(weights, lax.axis_index("tok") * row_count, row_count, 2)
    updated = lax.all_gather(renormed(own_rows, row_share), "tok", axis=2, tiled=True)
    proj_first = jnp.einsum(
        "thd,hfd->thf", query_rows, updated[:, 0], preferred_element_type=jnp.float32
    )
    proj_third = jnp.einsum(
        "thd,hfd->thf", query_rows, updated[:, 1], preferred_element_type=jnp.float32
    )
    mixed_hidden = (jax.nn.silu(proj_first) * proj_third).astype(jnp.bfloat16)
    outputs = jnp.einsum(
        "thf,hdf->thd", mixed_hidden, updated[:, 2], preferred_element_type=jnp.float32
    )
    normed = (
        outputs
        * lax.rsqrt(jnp.mean(outputs * outputs, axis=-1, keepdims=True) + epsilon)
        * head_gains[None]
    )
    normed = normed.astype(jnp.bfloat16)
    height = gate_input.shape[0]
    col_width = gate_input.shape[2]
    shards = lax.axis_size("tok")
    full_width = col_width * shards
    channels_here = head_count * head_size
    frame_grid = normed.reshape(height, full_width, channels_here)
    own_taps = lax.dynamic_slice_in_dim(
        conv_weights, lax.axis_index("head") * channels_here, channels_here, 2
    )
    padded = jnp.pad(frame_grid, ((1, 1), (1, 1), (0, 0)))
    local_sum = jnp.zeros((height, full_width, channels_here), jnp.float32)
    for row_tap in range(3):
        for col_tap in range(3):
            local_sum = local_sum + own_taps[row_tap, col_tap] * padded[
                row_tap : row_tap + height, col_tap : col_tap + full_width
            ].astype(jnp.float32)
    outgoing = local_sum.astype(jnp.bfloat16).reshape(height, shards, col_width, channels_here)
    arrived = lax.all_to_all(outgoing, "tok", split_axis=1, concat_axis=1, tiled=True)
    frame_count = frame_order.shape[0]
    numbers = jnp.arange(frame_count, dtype=jnp.int32)
    inverse = jnp.sum(
        jnp.where(frame_order[None, :] == numbers[:, None], numbers[None, :], 0), axis=1
    )
    ordered = jnp.take(arrived, inverse, axis=1)
    tile_block = lax.all_to_all(ordered, "head", split_axis=1, concat_axis=3, tiled=True)
    return (tile_block.astype(jnp.float32) * jax.nn.silu(gate_input.astype(jnp.float32))).astype(
        jnp.bfloat16
    )


def local(queries, keys, values, rates, fast_weights, norm_gain, frame_order, gate_input, conv_weights):
    args = (
        queries, keys, values, rates, fast_weights, norm_gain, frame_order, gate_input, conv_weights
    )
    if fits_by_heads(queries, gate_input, frame_order):
        return by_heads(*args)
    return by_tokens(*args)


def solution(mesh):
    in_specs = (
        P(("groups", "tok"), "tile", "head", None),
        P(("groups", "tok"), "tile", "head", None),
        P(("groups", "tok"), "tile", "head", None),
        P("tile", "head", ("groups", "tok")),
        P("tile", "head", None, None, None),
        P("tile", "head", None),
        P("groups"),
        P(None, ("groups", "head"), "tok", "tile"),
        P(None, None, "tile"),
    )
    out_specs = P(None, ("groups", "head"), "tok", "tile")
    return jax.shard_map(local, mesh=mesh, in_specs=in_specs, out_specs=out_specs, check_vma=False)
```

```python
import functools

import jax
import jax.numpy as jnp
from jax import lax
from jax.experimental import pallas as pl
from jax.experimental.pallas import tpu as pltpu
from jax.sharding import PartitionSpec as P

epsilon = 1e-06
LANES = 128
VMEM_BYTES = 24 * 1024 * 1024


def split_lanes(source, scratch, rows, head_size):
    full = head_size // LANES
    tail = head_size - full * LANES
    wide = source.reshape(rows, head_size).astype(jnp.float32)
    for tile in range(full):
        scratch[tile] = wide[:, tile * LANES : (tile + 1) * LANES]
    scratch[full, :, 0:tail] = wide[:, full * LANES :]


def join_halves(first, second, tail):
    lane = lax.broadcasted_iota(jnp.int32, first[-1].shape, 1)
    middle = jnp.where(lane < tail, first[-1], pltpu.roll(second[-1], tail, 1))
    return first[:-1] + [middle] + second[:-1]


def part_halves(packed, head_size):
    full = head_size // LANES
    tail = head_size - full * LANES
    first = packed[:, :head_size]
    middle = packed[:, head_size : (full + 1) * LANES]
    second = jnp.concatenate([packed[:, (full + 1) * LANES :], middle], axis=1)
    return first, second


def partner_head(partner):
    return lax.axis_index("tok") ^ partner


def pack_pairs(head, rate_ref, key_tiles, value_tiles, out_ref, start, head_size):
    heads, tok_rows = rate_ref.shape
    half = tok_rows // 2
    full = head_size // LANES
    tail = head_size - full * LANES
    rate_row = -rate_ref[pl.ds(head, 1), :]
    rates = jnp.broadcast_to(rate_row, (LANES, tok_rows)).T
    for row, tiles in ((start, key_tiles), (start + half, value_tiles)):
        sides = []
        for side in range(2):
            parts = [
                tiles[tile, pl.ds(side * half * heads + head, half, stride=heads), :]
                for tile in range(full + 1)
            ]
            if tiles is value_tiles:
                rate = rates[side * half : (side + 1) * half]
                parts = [rate * part for part in parts]
            sides.append(parts)
        for tile, part in enumerate(join_halves(sides[0], sides[1], tail)):
            out_ref[row : row + half, tile * LANES : (tile + 1) * LANES] = part.astype(jnp.bfloat16)


def pack_query(head, heads, height, query_tiles, out_ref, start, head_size):
    tok_rows = query_tiles.shape[1] // heads
    half = tok_rows // 2
    width = tok_rows // height
    full = head_size // LANES
    tail = head_size - full * LANES
    sides = []
    for side in range(2):
        sides.append(
            [
                jnp.concatenate(
                    [
                        query_tiles[
                            tile, pl.ds(column * heads + head, height, stride=width * heads), :
                        ]
                        for column in range(side * width // 2, (side + 1) * width // 2)
                    ],
                    axis=0,
                )
                for tile in range(full + 1)
            ]
        )
    for tile, part in enumerate(join_halves(sides[0], sides[1], tail)):
        out_ref[start : start + half, tile * LANES : (tile + 1) * LANES] = part.astype(jnp.bfloat16)


def pack_mirror_kernel(key_ref, value_ref, rate_ref, *rest):
    outs, (key_tiles, value_tiles) = rest[:-2], rest[-2:]
    tok_rows, heads, head_size = key_ref.shape
    split_lanes(key_ref[...], key_tiles, tok_rows * heads, head_size)
    split_lanes(value_ref[...], value_tiles, tok_rows * heads, head_size)
    for partner, out_ref in enumerate(outs):
        head = partner_head(partner ^ (heads // 2))
        pack_pairs(head, rate_ref, key_tiles, value_tiles, out_ref, 0, head_size)


def pack_across_kernel(height, query_any, *rest):
    outs, (query_ref, query_tiles, sems) = rest[:-3], rest[-3:]
    tok_rows, heads, head_size = query_any.shape
    half = tok_rows // 2
    full = head_size // LANES
    pieces = sems.shape[0]
    rows = tok_rows // pieces
    copies = [
        pltpu.make_async_copy(
            query_any.at[pl.ds(piece * rows, rows)],
            query_ref.at[pl.ds(piece * rows, rows)],
            sems.at[piece],
        )
        for piece in range(pieces)
    ]
    for copy in copies:
        copy.start()
    for piece, copy in enumerate(copies):
        copy.wait()
        wide = query_ref[piece * rows : (piece + 1) * rows].reshape(rows * heads, head_size)
        wide = wide.astype(jnp.float32)
        place = slice(piece * rows * heads, (piece + 1) * rows * heads)
        for tile in range(full):
            query_tiles[tile, place] = wide[:, tile * LANES : (tile + 1) * LANES]
        query_tiles[full, place, 0 : head_size - full * LANES] = wide[:, full * LANES :]
    for partner in range(heads // 2):
        head = partner_head(partner ^ (heads // 2))
        start = partner % 2 * half
        pack_query(head, heads, height, query_tiles, outs[partner // 2], start, head_size)


def pack_near_kernel(height, unread, key_ref, value_ref, rate_ref, query_ref, *rest):
    outs, (key_tiles, value_tiles, query_tiles) = rest[unread:-3], rest[-3:]
    tok_rows, heads, head_size = key_ref.shape
    split_lanes(key_ref[...], key_tiles, tok_rows * heads, head_size)
    split_lanes(value_ref[...], value_tiles, tok_rows * heads, head_size)
    split_lanes(query_ref[...], query_tiles, tok_rows * heads, head_size)
    line = heads // 2
    for partner in range(line):
        head = partner_head(partner)
        pack_pairs(head, rate_ref, key_tiles, value_tiles, outs[partner], 0, head_size)
        pack_query(head, heads, height, query_tiles, outs[line + partner], 0, head_size)


def send_far(part, partner, other):
    blocks = lax.axis_size("head")
    count = lax.axis_size("tok") * blocks
    pairs = [(place, place ^ (partner * blocks + other)) for place in range(count)]
    return lax.ppermute(part, ("tok", "head"), pairs)


def relay(landed):
    return [part for one in landed for part in (one, send(one, 1))]


def send(part, partner):
    pairs = [(place, place ^ partner) for place in range(lax.axis_size("tok"))]
    return lax.ppermute(part, "tok", pairs)


def sigmoid(value):
    return 0.5 + 0.5 * jnp.tanh(0.5 * value)


def contract(first, second, dims):
    return lax.dot_general(first, second, (dims, ((), ())), preferred_element_type=jnp.float32)


NN = ((1,), (0,))
NT = ((1,), (1,))


def add_gradients(pair_refs, tok_rows, weight_ref, prior_ref, grad_ref):
    half = tok_rows // 2
    head_size = weight_ref.shape[-1]
    first_weight = weight_ref[0]
    third_weight = weight_ref[1]
    down_turned = weight_ref[2].astype(jnp.float32).T.astype(jnp.bfloat16)
    step = 2 if len(pair_refs) % 2 == 0 else 1
    for start in range(0, len(pair_refs), step):
        key_parts, target_parts = [], []
        for pair_ref in pair_refs[start : start + step]:
            key_parts.extend(part_halves(pair_ref[0:half, :], head_size))
            target_parts.extend(part_halves(pair_ref[half:tok_rows, :], head_size))
        key_rows = jnp.concatenate(key_parts, axis=0)
        target = jnp.concatenate(target_parts, axis=0)
        first_pre = contract(first_weight, key_rows, NT)
        third_pre = contract(third_weight, key_rows, NT)
        hidden_grad = contract(down_turned, target, NT)
        sigmoid_first = sigmoid(first_pre)
        activated = first_pre * sigmoid_first
        mixed = (activated * third_pre).astype(jnp.bfloat16)
        grad_first_in = (
            hidden_grad * third_pre * sigmoid_first * (1.0 + first_pre * (1.0 - sigmoid_first))
        ).astype(jnp.bfloat16)
        grad_third_in = (hidden_grad * activated).astype(jnp.bfloat16)
        grads = (
            contract(grad_first_in, key_rows, NN),
            contract(grad_third_in, key_rows, NN),
            contract(mixed, target, NN),
        )
        for index, grad in enumerate(grads):
            if start == 0 and prior_ref is None:
                grad_ref[index, :, 0:head_size] = grad
            elif start == 0:
                grad_ref[index, :, 0:head_size] = prior_ref[index, :, 0:head_size] + grad
            else:
                grad_ref[index, :, 0:head_size] += grad


def sum_kernel(count, tok_rows, prior, *refs):
    pair_refs, weight_ref, out_ref = refs[:count], refs[count], refs[-1]
    prior_ref = refs[count + 1] if prior else None
    add_gradients(pair_refs, tok_rows, weight_ref, prior_ref, out_ref)


def mirror_kernel(count, tok_rows, *refs):
    pair_refs, weight_ref, prior_ref = refs[:count], refs[count], refs[count + 1]
    out_ref, grad_ref = refs[-2:]
    head_size = weight_ref.shape[-1]
    full = head_size // LANES
    tail = head_size - full * LANES
    half = head_size // 2
    add_gradients(pair_refs, tok_rows, weight_ref, prior_ref, grad_ref)

    def tiles_of(index, rows):
        return [
            grad_ref[index, rows, tile * LANES : (tile + 1) * LANES] for tile in range(full + 1)
        ]

    both = join_halves(tiles_of(0, slice(0, head_size)), tiles_of(1, slice(0, head_size)), tail)
    down = join_halves(tiles_of(2, slice(0, half)), tiles_of(2, slice(half, head_size)), tail)
    for tile, (above, below) in enumerate(zip(both, down)):
        lanes = slice(tile * LANES, (tile + 1) * LANES)
        out_ref[0:head_size, lanes] = above.astype(jnp.bfloat16)
        out_ref[head_size : head_size + half, lanes] = below.astype(jnp.bfloat16)


def renorm(weight_ref, grad_ref, mirror_refs, out_ref):
    head_size = weight_ref.shape[-1]
    units = head_size // len(mirror_refs)
    firsts, thirds, downs = [], [], []
    for mirror_ref in mirror_refs:
        first, third = part_halves(mirror_ref[0:units, :], head_size)
        firsts.append(first)
        thirds.append(third)
        downs.extend(part_halves(mirror_ref[units:, :], head_size))
    first, third, down = (jnp.concatenate(parts, axis=0) for parts in (firsts, thirds, downs))
    for index, other in enumerate((first, third, down)):
        before = weight_ref[index].astype(jnp.float32)
        axis = 1
        if index == 2:
            before = before.T
            axis = 0
        grad = grad_ref[index, :, 0:head_size] + other.astype(jnp.float32)
        updated = before - grad
        scale_old = jnp.sqrt(jnp.mean(before * before, axis=axis, keepdims=True) + epsilon)
        scale_new = jnp.sqrt(jnp.mean(updated * updated, axis=axis, keepdims=True) + epsilon)
        out_ref[index] = (updated * (scale_old / scale_new)).astype(jnp.bfloat16)


def apply_shards(
    height, frames_here, parts, order_ref, weight_ref, gain_ref, tap_ref, grid_ref, turned_ref
):
    head_size = weight_ref.shape[-1]
    full = head_size // LANES
    width = grid_ref.shape[2]
    top = 8
    edge = jnp.zeros((top, LANES), jnp.float32)
    for place in range(len(parts)):
        for tile in range(full + 1):
            for column in range(width):
                grid_ref[place, tile, column, 0:top] = edge
                grid_ref[place, tile, column, top + height :] = edge
    gain = gain_ref[...]
    for place, (shard, queries) in enumerate(parts):
        rows = jnp.concatenate(part_halves(queries, head_size), axis=0)
        proj_first = contract(rows, weight_ref[0], NT)
        proj_third = contract(rows, weight_ref[1], NT)
        mixed = (proj_first * jax.nn.sigmoid(proj_first) * proj_third).astype(jnp.bfloat16)
        outputs = contract(mixed, weight_ref[2], NN)
        scale = lax.rsqrt(jnp.mean(outputs * outputs, axis=-1, keepdims=True) + epsilon)
        normed = (outputs * scale * gain).astype(jnp.bfloat16).astype(jnp.float32)
        frame = order_ref[shard]
        block = frame // frames_here
        slot = frame % frames_here
        for tile in range(full + 1):
            lanes = slice(tile * LANES, min((tile + 1) * LANES, head_size))
            for column in range(width):
                grid_ref[place, tile, column, top : top + height, 0 : lanes.stop - lanes.start] = (
                    normed[column * height : (column + 1) * height, lanes]
                )
            taps = [
                tap_ref[index : index + 1, tile * LANES : (tile + 1) * LANES] for index in range(9)
            ]
            loaded = {}
            for column in range(width):
                total = None
                for col_tap in range(3):
                    source = column + col_tap - 1
                    if not 0 <= source < width:
                        continue
                    if source not in loaded:
                        loaded[source] = [
                            grid_ref[place, tile, source, first : first + height, :]
                            for first in range(top - 1, top + 2)
                        ]
                    for row_tap in range(3):
                        term = taps[row_tap * 3 + col_tap] * loaded[source][row_tap]
                        total = term if total is None else total + term
                turned_ref[
                    block, column, tile, pl.ds(slot, height, stride=frames_here), :
                ] = total


def apply_first_kernel(height, frames_here, near, far, order_ref, *refs):
    near_refs, far_refs = refs[: len(near)], refs[len(near) : len(near) + len(far)]
    before_ref, grad_ref, mirror_ref, gain_ref, tap_ref, weight_ref, turned_ref, grid_ref = refs[-8:]
    half = near_refs[0].shape[0]
    parts = [(shard, ref[...]) for shard, ref in zip(near, near_refs)]
    for shard, ref in zip(far, far_refs):
        parts.append((shard, ref[shard % 2 * half : (shard % 2 + 1) * half, :]))
    renorm(before_ref, grad_ref, [mirror_ref], weight_ref)
    apply_shards(
        height, frames_here, parts, order_ref, weight_ref, gain_ref, tap_ref, grid_ref, turned_ref
    )


def apply_last_kernel(height, frames_here, late, order, order_ref, *refs):
    query_refs = refs[: len(late)]
    weight_ref, done_ref, gain_ref, tap_ref = refs[len(late) : len(late) + 4]
    out_refs, (grid_ref, turned_ref) = refs[len(late) + 4 : -2], refs[-2:]
    turned_ref[...] = done_ref[...]
    parts = [(shard, ref[...]) for shard, ref in zip(late, query_refs)]
    apply_shards(
        height, frames_here, parts, order_ref, weight_ref, gain_ref, tap_ref, grid_ref, turned_ref
    )
    shards = turned_ref.shape[1]
    full = turned_ref.shape[2] - 1
    tail = weight_ref.shape[-1] - full * LANES
    blocks = turned_ref.shape[0]
    side_rows = turned_ref.shape[3] // 2
    for partner in range(shards):
        column = partner_head(partner)
        for other in range(blocks):
            block = lax.axis_index("head") ^ other
            sides = [
                [
                    turned_ref[block, column, tile, side * side_rows : (side + 1) * side_rows, :]
                    for tile in range(full + 1)
                ]
                for side in range(2)
            ]
            start = partner % 2 * side_rows
            if partner < 2 and other == 0:
                target, start = out_refs[partner], 0
            else:
                target = out_refs[2 + order.index((partner // 2 * 2, other))]
            for tile, part in enumerate(join_halves(sides[0], sides[1], tail)):
                target[start : start + side_rows, tile * LANES : (tile + 1) * LANES] = (
                    part.astype(jnp.bfloat16)
                )


def gate_kernel(blocks, shards, places, *refs):
    conv_refs = refs[: 2 * len(places)]
    gate_ref, out_any, product_ref, sems = refs[2 * len(places)], *refs[-3:]
    height = gate_ref.shape[0]
    frames_here = gate_ref.shape[1]
    head_size = gate_ref.shape[2] // blocks // shards
    side_rows = height * frames_here // 2
    rows_here = height // 2
    own = lax.axis_index("tok")
    odd = own % 2
    copies = []
    for index, (partner, other) in enumerate(places):
        one_ref, two_ref = conv_refs[2 * index : 2 * index + 2]
        one = one_ref[0:side_rows, :].astype(jnp.float32)
        two = two_ref[two_ref.shape[0] - side_rows :, :].astype(jnp.float32)
        low = part_halves(jnp.where(odd == 1, two, one), head_size)
        high = part_halves(jnp.where(odd == 1, one, two), head_size)
        head = (lax.axis_index("head") ^ other) * shards + ((own - odd) ^ partner)
        lanes = pl.ds(pl.multiple_of(head * head_size, 2 * head_size), 2 * head_size)
        for side in range(2):
            rows = slice(side * rows_here, (side + 1) * rows_here)
            conv = jnp.concatenate([low[side], high[side]], axis=1)
            conv = conv.reshape(rows_here, frames_here, 2 * head_size)
            gate = gate_ref[rows, :, lanes].astype(jnp.float32)
            product_ref[index, rows] = (conv * (gate * sigmoid(gate))).astype(jnp.bfloat16)
        copy = pltpu.make_async_copy(
            product_ref.at[index], out_any.at[:, :, lanes], sems.at[index]
        )
        copy.start()
        copies.append(copy)
    for copy in copies:
        copy.wait()


def in_vmem(count):
    return [pl.BlockSpec(memory_space=pltpu.VMEM)] * count


def call(kernel, out, operands, scratch=(), specs=None, leave=True):
    specs = specs or in_vmem(len(operands))
    operands = [
        pltpu.with_memory_space_constraint(item, pltpu.VMEM)
        if spec.memory_space == pltpu.VMEM
        else item
        for item, spec in zip(operands, specs)
    ]
    place = pltpu.VMEM if leave else pl.ANY
    if leave:
        out = jax.tree.map(lambda item: pltpu.VMEM(item.shape, item.dtype), out)
    return pl.pallas_call(
        kernel,
        out_shape=out,
        in_specs=specs,
        out_specs=jax.tree.map(lambda _: pl.BlockSpec(memory_space=place), out),
        scratch_shapes=scratch,
        compiler_params=pltpu.CompilerParams(vmem_limit_bytes=VMEM_BYTES),
        cost_estimate=pl.CostEstimate(flops=0, bytes_accessed=0, transcendentals=0),
    )(*operands)


def after(part, *earlier):
    anywhere = pl.BlockSpec(memory_space=pl.ANY)
    return pl.pallas_call(
        lambda *refs: None,
        out_shape=jax.ShapeDtypeStruct(part.shape, part.dtype),
        in_specs=[anywhere] * (1 + len(earlier)),
        out_specs=anywhere,
        input_output_aliases={0: 0},
        compiler_params=pltpu.CompilerParams(vmem_limit_bytes=1024 * 1024),
        cost_estimate=pl.CostEstimate(flops=0, bytes_accessed=0, transcendentals=0),
    )(part, *earlier)


def by_heads(
    queries, keys, values, rates, fast_weights, norm_gain, frame_order, gate_input, conv_weights
):
    tok_rows = queries.shape[0]
    head_count = queries.shape[1] * queries.shape[2]
    head_size = queries.shape[3]
    height, frames_here = gate_input.shape[:2]
    shards = lax.axis_size("tok")
    blocks = lax.axis_size("head")
    half = tok_rows // 2
    wide = 2 * head_size
    tiles = head_size // LANES + 1
    own = lax.axis_index("tok")
    own_channel = lax.axis_index("head") * head_count + own

    def rows_of(array):
        return array.reshape(tok_rows, head_count, head_size)

    def own_of(array, place):
        return lax.dynamic_index_in_dim(array, place, 0, keepdims=False)

    line = shards // 2
    tile_scratch = pltpu.VMEM((tiles, tok_rows * head_count, LANES), jnp.float32)
    token_rates = rates.reshape(head_count, tok_rows)
    chips = line // 2

    one = jax.ShapeDtypeStruct((tok_rows, wide), jnp.bfloat16)
    mirrored = call(
        pack_mirror_kernel,
        [one] * line,
        (rows_of(keys), rows_of(values), token_rates),
        (tile_scratch, tile_scratch),
    )
    mirrored = [mirrored[0]] + [send(mirrored[k], k) for k in range(1, line)]
    across = call(
        functools.partial(pack_across_kernel, height),
        [one] * chips,
        (pltpu.with_memory_space_constraint(rows_of(queries), pltpu.HBM),),
        (
            pltpu.VMEM((tok_rows, head_count, head_size), jnp.bfloat16),
            tile_scratch,
            pltpu.SemaphoreType.DMA((4,)),
        ),
        specs=[pl.BlockSpec(memory_space=pltpu.HBM)],
    )
    across_landed = [send(part, line + 2 * index) for index, part in enumerate(across)]
    weights = fast_weights.reshape(head_count, 3, head_size, head_size)
    own_weights = own_of(weights, own)
    mirror_weights = own_of(weights, own ^ line)
    own_gain = own_of(norm_gain.reshape(head_count, 1, head_size), own)
    taps = conv_weights.reshape(9, blocks * head_count, head_size)
    own_taps = lax.dynamic_index_in_dim(taps, own_channel, 1, keepdims=False)
    own_taps = jnp.pad(own_taps, ((0, 0), (0, tiles * LANES - head_size)))
    frames = frame_order[own ^ jnp.arange(shards, dtype=jnp.int32)]
    grad_shape = (3, head_size, tiles * LANES)
    grad_struct = jax.ShapeDtypeStruct(grad_shape, jnp.float32)
    unread = pl.BlockSpec(memory_space=pl.ANY)
    mirror_sum = call(
        functools.partial(sum_kernel, 2, tok_rows, False),
        grad_struct,
        (*mirrored[:2], mirror_weights),
    )
    early = (across[0], own_weights, own_gain, own_taps, frames, mirror_sum)
    query_struct = jax.ShapeDtypeStruct((half, wide), jnp.bfloat16)
    packed = call(
        functools.partial(pack_near_kernel, height, len(early)),
        [one] * line + [query_struct] * line,
        (rows_of(keys), rows_of(values), token_rates, rows_of(queries), *early),
        (tile_scratch, tile_scratch, tile_scratch),
        specs=in_vmem(4) + [unread] * len(early),
    )
    near_queries = packed[line:]
    held = [after(part, *mirrored[1:], *across_landed) for part in packed[1:line]]
    near = [packed[0]] + [send(held[k - 1], k) for k in range(1, line)]
    ahead = (*across_landed, *held)
    crossing = call(
        functools.partial(mirror_kernel, line - 2, tok_rows),
        jax.ShapeDtypeStruct((head_size + head_size // 2, wide), jnp.bfloat16),
        (*mirrored[2:], mirror_weights, mirror_sum, *ahead),
        (pltpu.VMEM(grad_shape, jnp.float32),),
        specs=in_vmem(line) + [unread] * len(ahead),
    )
    crossed = send(crossing, line)
    own_sum = call(
        functools.partial(sum_kernel, 2, tok_rows, False),
        grad_struct,
        (*near[:2], own_weights, crossing),
        specs=in_vmem(3) + [unread],
    )
    across = relay([after(part, own_sum) for part in across_landed])
    gradients = call(
        functools.partial(sum_kernel, line - 2, tok_rows, True),
        grad_struct,
        (*near[2:], own_weights, own_sum),
    )
    mate_queries = send(after(near_queries[1], own_sum), 1)
    late_queries = [
        send(after(near_queries[k], *near[2:]), k) for k in range(2, line)
    ]
    side_rows = frames_here * height // 2
    first_shards, far_shards, late_shards = (0, 1), range(line, shards), range(2, line)
    grid_shape = (tiles, shards, height + 16, LANES)
    turned_shape = (blocks, shards, tiles, 2 * side_rows, LANES)
    numbers = [pl.BlockSpec(memory_space=pltpu.SMEM)]
    updated, turned = call(
        functools.partial(apply_first_kernel, height, frames_here, first_shards, far_shards),
        [
            jax.ShapeDtypeStruct((3, head_size, head_size), jnp.bfloat16),
            jax.ShapeDtypeStruct(turned_shape, jnp.float32),
        ],
        (
            frames, near_queries[0], mate_queries, *across,
            own_weights, gradients, crossed, own_gain, own_taps,
        ),
        (pltpu.VMEM((2 + line, *grid_shape), jnp.float32),),
        specs=numbers + in_vmem(line + 7),
    )
    order = [(k, x) for k in range(0, shards, 2) for x in range(blocks)][1:]
    order = sorted(order, key=lambda place: (place != (line, 0), place))
    outgoing = call(
        functools.partial(apply_last_kernel, height, frames_here, late_shards, order),
        [jax.ShapeDtypeStruct((side_rows, wide), jnp.bfloat16)] * 2
        + [jax.ShapeDtypeStruct((2 * side_rows, wide), jnp.bfloat16)] * (shards // 2 * blocks - 1),
        (frames, *late_queries, updated, turned, own_gain, own_taps),
        (
            pltpu.VMEM((line - 2, *grid_shape), jnp.float32),
            pltpu.VMEM(turned_shape, jnp.float32),
        ),
        specs=numbers + in_vmem(line + 2),
    )
    landed = [send_far(part, k, x) for part, (k, x) in zip(outgoing[2:], order)]
    arrived = [outgoing[0], send(outgoing[1], 1), *relay(landed)]
    gate = gate_input.reshape(height, frames_here, gate_input.shape[3])
    places = [(0, 0), *order]
    gated = call(
        functools.partial(gate_kernel, blocks, shards, places),
        jax.ShapeDtypeStruct(gate.shape, jnp.bfloat16),
        (*arrived, gate),
        (
            pltpu.VMEM((len(places), *gate.shape[:2], wide), jnp.bfloat16),
            pltpu.SemaphoreType.DMA((len(places),)),
        ),
        leave=False,
    )
    return gated.reshape(gate_input.shape)


def fits_by_heads(queries, gate_input, frame_order):
    tok_rows, head_size = queries.shape[0], queries.shape[3]
    head_count = queries.shape[1] * queries.shape[2]
    height, frames_here, col_width = gate_input.shape[:3]
    shards = lax.axis_size("tok")
    return (
        head_count == shards
        and frame_order.shape[0] == shards
        and lax.axis_size("tile") == 1
        and col_width == 1
        and shards >= 8
        and shards & (shards - 1) == 0
        and head_size % LANES == LANES // 2
        and height % 8 == 0
        and tok_rows == height * shards
        and tok_rows % 64 == 0
        and head_size % 64 == 0
        and frames_here * height % 32 == 0
        and frames_here * lax.axis_size("head") == shards
        and lax.axis_size("head") & (lax.axis_size("head") - 1) == 0
    )


def renormed(previous, gradient):
    before = previous.astype(jnp.float32)
    updated = before - gradient
    scale_old = jnp.sqrt(jnp.mean(before * before, axis=-1, keepdims=True) + epsilon)
    scale_new = jnp.sqrt(jnp.mean(updated * updated, axis=-1, keepdims=True) + epsilon)
    return (updated * (scale_old / scale_new)).astype(jnp.bfloat16)


def by_tokens(
    queries, keys, values, rates, fast_weights, norm_gain, frame_order, gate_input, conv_weights
):
    tok_rows = queries.shape[0]
    head_count = queries.shape[1] * queries.shape[2]
    head_size = queries.shape[3]
    query_rows = queries.reshape(tok_rows, head_count, head_size)
    key_rows = keys.reshape(tok_rows, head_count, head_size)
    value_rows = values.reshape(tok_rows, head_count, head_size)
    token_rates = rates.reshape(head_count, tok_rows)
    weights = fast_weights.reshape(head_count, 3, head_size, head_size)
    head_gains = norm_gain.reshape(head_count, head_size)
    first_pre = jnp.einsum(
        "thd,hfd->htf", key_rows, weights[:, 0], preferred_element_type=jnp.float32
    )
    third_pre = jnp.einsum(
        "thd,hfd->htf", key_rows, weights[:, 1], preferred_element_type=jnp.float32
    )
    sigmoid_first = jax.nn.sigmoid(first_pre)
    activated = first_pre * sigmoid_first
    hidden = (activated * third_pre).astype(jnp.bfloat16)
    target = (-token_rates.T[:, :, None] * value_rows.astype(jnp.float32)).astype(jnp.bfloat16)
    grad_down = jnp.einsum("thd,htf->hdf", target, hidden, preferred_element_type=jnp.float32)
    hidden_grad = jnp.einsum(
        "thd,hdf->htf", target, weights[:, 2], preferred_element_type=jnp.float32
    )
    grad_first_in = (
        hidden_grad * third_pre * sigmoid_first * (1.0 + first_pre * (1.0 - sigmoid_first))
    ).astype(jnp.bfloat16)
    grad_third_in = (hidden_grad * activated).astype(jnp.bfloat16)
    grad_first = jnp.einsum(
        "htf,thd->hfd", grad_first_in, key_rows, preferred_element_type=jnp.float32
    )
    grad_third = jnp.einsum(
        "htf,thd->hfd", grad_third_in, key_rows, preferred_element_type=jnp.float32
    )
    gradients = jnp.stack([grad_first, grad_third, grad_down], axis=1)
    row_share = lax.psum_scatter(gradients, "tok", scatter_dimension=2, tiled=True)
    row_count = row_share.shape[2]
    own_rows = lax.dynamic_slice_in_dim(weights, lax.axis_index("tok") * row_count, row_count, 2)
    updated = lax.all_gather(renormed(own_rows, row_share), "tok", axis=2, tiled=True)
    proj_first = jnp.einsum(
        "thd,hfd->thf", query_rows, updated[:, 0], preferred_element_type=jnp.float32
    )
    proj_third = jnp.einsum(
        "thd,hfd->thf", query_rows, updated[:, 1], preferred_element_type=jnp.float32
    )
    mixed_hidden = (jax.nn.silu(proj_first) * proj_third).astype(jnp.bfloat16)
    outputs = jnp.einsum(
        "thf,hdf->thd", mixed_hidden, updated[:, 2], preferred_element_type=jnp.float32
    )
    normed = (
        outputs
        * lax.rsqrt(jnp.mean(outputs * outputs, axis=-1, keepdims=True) + epsilon)
        * head_gains[None]
    )
    normed = normed.astype(jnp.bfloat16)
    height = gate_input.shape[0]
    col_width = gate_input.shape[2]
    shards = lax.axis_size("tok")
    full_width = col_width * shards
    channels_here = head_count * head_size
    frame_grid = normed.reshape(height, full_width, channels_here)
    own_taps = lax.dynamic_slice_in_dim(
        conv_weights, lax.axis_index("head") * channels_here, channels_here, 2
    )
    padded = jnp.pad(frame_grid, ((1, 1), (1, 1), (0, 0)))
    local_sum = jnp.zeros((height, full_width, channels_here), jnp.float32)
    for row_tap in range(3):
        for col_tap in range(3):
            local_sum = local_sum + own_taps[row_tap, col_tap] * padded[
                row_tap : row_tap + height, col_tap : col_tap + full_width
            ].astype(jnp.float32)
    outgoing = local_sum.astype(jnp.bfloat16).reshape(height, shards, col_width, channels_here)
    arrived = lax.all_to_all(outgoing, "tok", split_axis=1, concat_axis=1, tiled=True)
    frame_count = frame_order.shape[0]
    numbers = jnp.arange(frame_count, dtype=jnp.int32)
    inverse = jnp.sum(
        jnp.where(frame_order[None, :] == numbers[:, None], numbers[None, :], 0), axis=1
    )
    ordered = jnp.take(arrived, inverse, axis=1)
    tile_block = lax.all_to_all(ordered, "head", split_axis=1, concat_axis=3, tiled=True)
    return (tile_block.astype(jnp.float32) * jax.nn.silu(gate_input.astype(jnp.float32))).astype(
        jnp.bfloat16
    )


def local(queries, keys, values, rates, fast_weights, norm_gain, frame_order, gate_input, conv_weights):
    args = (
        queries, keys, values, rates, fast_weights, norm_gain, frame_order, gate_input, conv_weights
    )
    if fits_by_heads(queries, gate_input, frame_order):
        return by_heads(*args)
    return by_tokens(*args)


def solution(mesh):
    in_specs = (
        P(("groups", "tok"), "tile", "head", None),
        P(("groups", "tok"), "tile", "head", None),
        P(("groups", "tok"), "tile", "head", None),
        P("tile", "head", ("groups", "tok")),
        P("tile", "head", None, None, None),
        P("tile", "head", None),
        P("groups"),
        P(None, ("groups", "head"), "tok", "tile"),
        P(None, None, "tile"),
    )
    out_specs = P(None, ("groups", "head"), "tok", "tile")
    return jax.shard_map(local, mesh=mesh, in_specs=in_specs, out_specs=out_specs, check_vma=False)
```

```python
import functools

import jax
import jax.numpy as jnp
from jax import lax
from jax.experimental import pallas as pl
from jax.experimental.pallas import tpu as pltpu
from jax.sharding import PartitionSpec as P

epsilon = 1e-06
LANES = 128
VMEM_BYTES = 24 * 1024 * 1024


def split_lanes(source, scratch, rows, head_size):
    full = head_size // LANES
    tail = head_size - full * LANES
    wide = source.reshape(rows, head_size).astype(jnp.float32)
    for tile in range(full):
        scratch[tile] = wide[:, tile * LANES : (tile + 1) * LANES]
    scratch[full, :, 0:tail] = wide[:, full * LANES :]


def join_halves(first, second, tail):
    lane = lax.broadcasted_iota(jnp.int32, first[-1].shape, 1)
    middle = jnp.where(lane < tail, first[-1], pltpu.roll(second[-1], tail, 1))
    return first[:-1] + [middle] + second[:-1]


def part_halves(packed, head_size):
    full = head_size // LANES
    tail = head_size - full * LANES
    first = packed[:, :head_size]
    middle = packed[:, head_size : (full + 1) * LANES]
    second = jnp.concatenate([packed[:, (full + 1) * LANES :], middle], axis=1)
    return first, second


def partner_head(partner):
    return lax.axis_index("tok") ^ partner


def pack_pairs(head, rate_ref, key_tiles, value_tiles, out_ref, start, head_size):
    heads, tok_rows = rate_ref.shape
    half = tok_rows // 2
    full = head_size // LANES
    tail = head_size - full * LANES
    rate_row = -rate_ref[pl.ds(head, 1), :]
    rates = jnp.broadcast_to(rate_row, (LANES, tok_rows)).T
    for row, tiles in ((start, key_tiles), (start + half, value_tiles)):
        sides = []
        for side in range(2):
            parts = [
                tiles[tile, pl.ds(side * half * heads + head, half, stride=heads), :]
                for tile in range(full + 1)
            ]
            if tiles is value_tiles:
                rate = rates[side * half : (side + 1) * half]
                parts = [rate * part for part in parts]
            sides.append(parts)
        for tile, part in enumerate(join_halves(sides[0], sides[1], tail)):
            out_ref[row : row + half, tile * LANES : (tile + 1) * LANES] = part.astype(jnp.bfloat16)


def pack_query(head, heads, height, query_tiles, out_ref, start, head_size):
    tok_rows = query_tiles.shape[1] // heads
    half = tok_rows // 2
    width = tok_rows // height
    full = head_size // LANES
    tail = head_size - full * LANES
    sides = []
    for side in range(2):
        sides.append(
            [
                jnp.concatenate(
                    [
                        query_tiles[
                            tile, pl.ds(column * heads + head, height, stride=width * heads), :
                        ]
                        for column in range(side * width // 2, (side + 1) * width // 2)
                    ],
                    axis=0,
                )
                for tile in range(full + 1)
            ]
        )
    for tile, part in enumerate(join_halves(sides[0], sides[1], tail)):
        out_ref[start : start + half, tile * LANES : (tile + 1) * LANES] = part.astype(jnp.bfloat16)


def pack_mirror_kernel(key_ref, value_ref, rate_ref, *rest):
    outs, (key_tiles, value_tiles) = rest[:-2], rest[-2:]
    tok_rows, heads, head_size = key_ref.shape
    split_lanes(key_ref[...], key_tiles, tok_rows * heads, head_size)
    split_lanes(value_ref[...], value_tiles, tok_rows * heads, head_size)
    for partner, out_ref in enumerate(outs):
        head = partner_head(partner ^ (heads // 2))
        pack_pairs(head, rate_ref, key_tiles, value_tiles, out_ref, 0, head_size)


def pack_across_kernel(height, query_any, *rest):
    outs, (query_ref, query_tiles, sems) = rest[:-3], rest[-3:]
    tok_rows, heads, head_size = query_any.shape
    half = tok_rows // 2
    full = head_size // LANES
    pieces = sems.shape[0]
    rows = tok_rows // pieces
    copies = [
        pltpu.make_async_copy(
            query_any.at[pl.ds(piece * rows, rows)],
            query_ref.at[pl.ds(piece * rows, rows)],
            sems.at[piece],
        )
        for piece in range(pieces)
    ]
    for copy in copies:
        copy.start()
    for piece, copy in enumerate(copies):
        copy.wait()
        wide = query_ref[piece * rows : (piece + 1) * rows].reshape(rows * heads, head_size)
        wide = wide.astype(jnp.float32)
        place = slice(piece * rows * heads, (piece + 1) * rows * heads)
        for tile in range(full):
            query_tiles[tile, place] = wide[:, tile * LANES : (tile + 1) * LANES]
        query_tiles[full, place, 0 : head_size - full * LANES] = wide[:, full * LANES :]
    for partner in range(heads // 2):
        head = partner_head(partner ^ (heads // 2))
        start = partner % 2 * half
        pack_query(head, heads, height, query_tiles, outs[partner // 2], start, head_size)


def pack_near_kernel(height, unread, key_ref, value_ref, rate_ref, query_ref, *rest):
    outs, (key_tiles, value_tiles, query_tiles) = rest[unread:-3], rest[-3:]
    tok_rows, heads, head_size = key_ref.shape
    split_lanes(key_ref[...], key_tiles, tok_rows * heads, head_size)
    split_lanes(value_ref[...], value_tiles, tok_rows * heads, head_size)
    split_lanes(query_ref[...], query_tiles, tok_rows * heads, head_size)
    line = heads // 2
    for partner in range(line):
        head = partner_head(partner)
        pack_pairs(head, rate_ref, key_tiles, value_tiles, outs[partner], 0, head_size)
        pack_query(head, heads, height, query_tiles, outs[line + partner], 0, head_size)


def send_far(part, partner, other):
    blocks = lax.axis_size("head")
    count = lax.axis_size("tok") * blocks
    pairs = [(place, place ^ (partner * blocks + other)) for place in range(count)]
    return lax.ppermute(part, ("tok", "head"), pairs)


def relay(landed):
    return [part for one in landed for part in (one, send(one, 1))]


def send(part, partner):
    pairs = [(place, place ^ partner) for place in range(lax.axis_size("tok"))]
    return lax.ppermute(part, "tok", pairs)


def sigmoid(value):
    return 0.5 + 0.5 * jnp.tanh(0.5 * value)


def contract(first, second, dims):
    return lax.dot_general(first, second, (dims, ((), ())), preferred_element_type=jnp.float32)


NN = ((1,), (0,))
NT = ((1,), (1,))


def add_gradients(pair_refs, tok_rows, weight_ref, prior_ref, grad_ref):
    half = tok_rows // 2
    head_size = weight_ref.shape[-1]
    first_weight = weight_ref[0]
    third_weight = weight_ref[1]
    down_turned = weight_ref[2].astype(jnp.float32).T.astype(jnp.bfloat16)
    step = 2 if len(pair_refs) % 2 == 0 else 1
    for start in range(0, len(pair_refs), step):
        key_parts, target_parts = [], []
        for pair_ref in pair_refs[start : start + step]:
            key_parts.extend(part_halves(pair_ref[0:half, :], head_size))
            target_parts.extend(part_halves(pair_ref[half:tok_rows, :], head_size))
        key_rows = jnp.concatenate(key_parts, axis=0)
        target = jnp.concatenate(target_parts, axis=0)
        first_pre = contract(first_weight, key_rows, NT)
        third_pre = contract(third_weight, key_rows, NT)
        hidden_grad = contract(down_turned, target, NT)
        sigmoid_first = sigmoid(first_pre)
        activated = first_pre * sigmoid_first
        mixed = (activated * third_pre).astype(jnp.bfloat16)
        grad_first_in = (
            hidden_grad * third_pre * sigmoid_first * (1.0 + first_pre * (1.0 - sigmoid_first))
        ).astype(jnp.bfloat16)
        grad_third_in = (hidden_grad * activated).astype(jnp.bfloat16)
        grads = (
            contract(grad_first_in, key_rows, NN),
            contract(grad_third_in, key_rows, NN),
            contract(mixed, target, NN),
        )
        for index, grad in enumerate(grads):
            if start == 0 and prior_ref is None:
                grad_ref[index, :, 0:head_size] = grad
            elif start == 0:
                grad_ref[index, :, 0:head_size] = prior_ref[index, :, 0:head_size] + grad
            else:
                grad_ref[index, :, 0:head_size] += grad


def sum_kernel(count, tok_rows, prior, *refs):
    pair_refs, weight_ref, out_ref = refs[:count], refs[count], refs[-1]
    prior_ref = refs[count + 1] if prior else None
    add_gradients(pair_refs, tok_rows, weight_ref, prior_ref, out_ref)


def mirror_kernel(count, tok_rows, *refs):
    pair_refs, weight_ref, prior_ref = refs[:count], refs[count], refs[count + 1]
    out_ref, grad_ref = refs[-2:]
    head_size = weight_ref.shape[-1]
    full = head_size // LANES
    tail = head_size - full * LANES
    half = head_size // 2
    add_gradients(pair_refs, tok_rows, weight_ref, prior_ref, grad_ref)

    def tiles_of(index, rows):
        return [
            grad_ref[index, rows, tile * LANES : (tile + 1) * LANES] for tile in range(full + 1)
        ]

    both = join_halves(tiles_of(0, slice(0, head_size)), tiles_of(1, slice(0, head_size)), tail)
    down = join_halves(tiles_of(2, slice(0, half)), tiles_of(2, slice(half, head_size)), tail)
    for tile, (above, below) in enumerate(zip(both, down)):
        lanes = slice(tile * LANES, (tile + 1) * LANES)
        out_ref[0:head_size, lanes] = above.astype(jnp.bfloat16)
        out_ref[head_size : head_size + half, lanes] = below.astype(jnp.bfloat16)


def renorm(weight_ref, grad_ref, mirror_refs, out_ref):
    head_size = weight_ref.shape[-1]
    units = head_size // len(mirror_refs)
    firsts, thirds, downs = [], [], []
    for mirror_ref in mirror_refs:
        first, third = part_halves(mirror_ref[0:units, :], head_size)
        firsts.append(first)
        thirds.append(third)
        downs.extend(part_halves(mirror_ref[units:, :], head_size))
    first, third, down = (jnp.concatenate(parts, axis=0) for parts in (firsts, thirds, downs))
    for index, other in enumerate((first, third, down)):
        before = weight_ref[index].astype(jnp.float32)
        axis = 1
        if index == 2:
            before = before.T
            axis = 0
        grad = grad_ref[index, :, 0:head_size] + other.astype(jnp.float32)
        updated = before - grad
        scale_old = jnp.sqrt(jnp.mean(before * before, axis=axis, keepdims=True) + epsilon)
        scale_new = jnp.sqrt(jnp.mean(updated * updated, axis=axis, keepdims=True) + epsilon)
        out_ref[index] = (updated * (scale_old / scale_new)).astype(jnp.bfloat16)


def apply_shards(
    height, frames_here, parts, order_ref, weight_ref, gain_ref, tap_ref, grid_ref, turned_ref
):
    head_size = weight_ref.shape[-1]
    full = head_size // LANES
    width = grid_ref.shape[2]
    top = 8
    edge = jnp.zeros((top, LANES), jnp.float32)
    for place in range(len(parts)):
        for tile in range(full + 1):
            for column in range(width):
                grid_ref[place, tile, column, 0:top] = edge
                grid_ref[place, tile, column, top + height :] = edge
    gain = gain_ref[...]
    for place, (shard, queries) in enumerate(parts):
        rows = jnp.concatenate(part_halves(queries, head_size), axis=0)
        proj_first = contract(rows, weight_ref[0], NT)
        proj_third = contract(rows, weight_ref[1], NT)
        mixed = (proj_first * jax.nn.sigmoid(proj_first) * proj_third).astype(jnp.bfloat16)
        outputs = contract(mixed, weight_ref[2], NN)
        scale = lax.rsqrt(jnp.mean(outputs * outputs, axis=-1, keepdims=True) + epsilon)
        normed = (outputs * scale * gain).astype(jnp.bfloat16).astype(jnp.float32)
        frame = order_ref[shard]
        block = frame // frames_here
        slot = frame % frames_here
        for tile in range(full + 1):
            lanes = slice(tile * LANES, min((tile + 1) * LANES, head_size))
            for column in range(width):
                grid_ref[place, tile, column, top : top + height, 0 : lanes.stop - lanes.start] = (
                    normed[column * height : (column + 1) * height, lanes]
                )
            taps = [
                tap_ref[index : index + 1, tile * LANES : (tile + 1) * LANES] for index in range(9)
            ]
            loaded = {}
            for column in range(width):
                total = None
                for col_tap in range(3):
                    source = column + col_tap - 1
                    if not 0 <= source < width:
                        continue
                    if source not in loaded:
                        loaded[source] = [
                            grid_ref[place, tile, source, first : first + height, :]
                            for first in range(top - 1, top + 2)
                        ]
                    for row_tap in range(3):
                        term = taps[row_tap * 3 + col_tap] * loaded[source][row_tap]
                        total = term if total is None else total + term
                turned_ref[
                    block, column, tile, pl.ds(slot, height, stride=frames_here), :
                ] = total


def apply_first_kernel(height, frames_here, near, far, order_ref, *refs):
    near_refs, far_refs = refs[: len(near)], refs[len(near) : len(near) + len(far)]
    before_ref, grad_ref, mirror_ref, gain_ref, tap_ref, weight_ref, turned_ref, grid_ref = refs[-8:]
    half = near_refs[0].shape[0]
    parts = [(shard, ref[...]) for shard, ref in zip(near, near_refs)]
    for shard, ref in zip(far, far_refs):
        parts.append((shard, ref[shard % 2 * half : (shard % 2 + 1) * half, :]))
    renorm(before_ref, grad_ref, [mirror_ref], weight_ref)
    apply_shards(
        height, frames_here, parts, order_ref, weight_ref, gain_ref, tap_ref, grid_ref, turned_ref
    )


def apply_last_kernel(height, frames_here, late, order, order_ref, *refs):
    query_refs = refs[: len(late)]
    weight_ref, done_ref, gain_ref, tap_ref = refs[len(late) : len(late) + 4]
    out_refs, (grid_ref, turned_ref) = refs[len(late) + 4 : -2], refs[-2:]
    turned_ref[...] = done_ref[...]
    parts = [(shard, ref[...]) for shard, ref in zip(late, query_refs)]
    apply_shards(
        height, frames_here, parts, order_ref, weight_ref, gain_ref, tap_ref, grid_ref, turned_ref
    )
    shards = turned_ref.shape[1]
    full = turned_ref.shape[2] - 1
    tail = weight_ref.shape[-1] - full * LANES
    blocks = turned_ref.shape[0]
    side_rows = turned_ref.shape[3] // 2
    for partner in range(shards):
        column = partner_head(partner)
        for other in range(blocks):
            block = lax.axis_index("head") ^ other
            sides = [
                [
                    turned_ref[block, column, tile, side * side_rows : (side + 1) * side_rows, :]
                    for tile in range(full + 1)
                ]
                for side in range(2)
            ]
            start = partner % 2 * side_rows
            if partner < 2 and other == 0:
                target, start = out_refs[partner], 0
            else:
                target = out_refs[2 + order.index((partner // 2 * 2, other))]
            for tile, part in enumerate(join_halves(sides[0], sides[1], tail)):
                target[start : start + side_rows, tile * LANES : (tile + 1) * LANES] = (
                    part.astype(jnp.bfloat16)
                )


def silu_kernel(gate_ref, out_ref):
    height, frames_here, channels = gate_ref.shape
    gate = gate_ref[...].astype(jnp.float32)
    out_ref[...] = (gate * jax.nn.sigmoid(gate)).reshape(height * frames_here, channels)


def gate_kernel(blocks, shards, places, *refs):
    conv_refs = refs[: 2 * len(places)]
    gate_ref, out_any, product_ref, sems = refs[2 * len(places)], *refs[-3:]
    height, frames_here, channels = out_any.shape
    head_size = channels // blocks // shards
    side_rows = height * frames_here // 2
    rows_here = height // 2
    own = lax.axis_index("tok")
    odd = own % 2
    copies = []
    for index, (partner, other) in enumerate(places):
        one_ref, two_ref = conv_refs[2 * index : 2 * index + 2]
        one = one_ref[0:side_rows, :].astype(jnp.float32)
        two = two_ref[two_ref.shape[0] - side_rows :, :].astype(jnp.float32)
        low = part_halves(jnp.where(odd == 1, two, one), head_size)
        high = part_halves(jnp.where(odd == 1, one, two), head_size)
        head = (lax.axis_index("head") ^ other) * shards + ((own - odd) ^ partner)
        lanes = pl.ds(pl.multiple_of(head * head_size, 2 * head_size), 2 * head_size)
        for side in range(2):
            rows = slice(side * rows_here, (side + 1) * rows_here)
            conv = jnp.concatenate([low[side], high[side]], axis=1)
            conv = conv * gate_ref[side * side_rows : (side + 1) * side_rows, lanes]
            conv = conv.reshape(rows_here, frames_here, 2 * head_size)
            product_ref[index, rows] = conv.astype(jnp.bfloat16)
        copy = pltpu.make_async_copy(
            product_ref.at[index], out_any.at[:, :, lanes], sems.at[index]
        )
        copy.start()
        copies.append(copy)
    for copy in copies:
        copy.wait()


def in_vmem(count):
    return [pl.BlockSpec(memory_space=pltpu.VMEM)] * count


def call(kernel, out, operands, scratch=(), specs=None, leave=True):
    specs = specs or in_vmem(len(operands))
    operands = [
        pltpu.with_memory_space_constraint(item, pltpu.VMEM)
        if spec.memory_space == pltpu.VMEM
        else item
        for item, spec in zip(operands, specs)
    ]
    place = pltpu.VMEM if leave else pl.ANY
    if leave:
        out = jax.tree.map(lambda item: pltpu.VMEM(item.shape, item.dtype), out)
    return pl.pallas_call(
        kernel,
        out_shape=out,
        in_specs=specs,
        out_specs=jax.tree.map(lambda _: pl.BlockSpec(memory_space=place), out),
        scratch_shapes=scratch,
        compiler_params=pltpu.CompilerParams(vmem_limit_bytes=VMEM_BYTES),
        cost_estimate=pl.CostEstimate(flops=0, bytes_accessed=0, transcendentals=0),
    )(*operands)


def after(part, *earlier):
    anywhere = pl.BlockSpec(memory_space=pl.ANY)
    return pl.pallas_call(
        lambda *refs: None,
        out_shape=jax.ShapeDtypeStruct(part.shape, part.dtype),
        in_specs=[anywhere] * (1 + len(earlier)),
        out_specs=anywhere,
        input_output_aliases={0: 0},
        compiler_params=pltpu.CompilerParams(vmem_limit_bytes=1024 * 1024),
        cost_estimate=pl.CostEstimate(flops=0, bytes_accessed=0, transcendentals=0),
    )(part, *earlier)


def by_heads(
    queries, keys, values, rates, fast_weights, norm_gain, frame_order, gate_input, conv_weights
):
    tok_rows = queries.shape[0]
    head_count = queries.shape[1] * queries.shape[2]
    head_size = queries.shape[3]
    height, frames_here = gate_input.shape[:2]
    shards = lax.axis_size("tok")
    blocks = lax.axis_size("head")
    half = tok_rows // 2
    wide = 2 * head_size
    tiles = head_size // LANES + 1
    own = lax.axis_index("tok")
    own_channel = lax.axis_index("head") * head_count + own

    def rows_of(array):
        return array.reshape(tok_rows, head_count, head_size)

    def own_of(array, place):
        return lax.dynamic_index_in_dim(array, place, 0, keepdims=False)

    line = shards // 2
    tile_scratch = pltpu.VMEM((tiles, tok_rows * head_count, LANES), jnp.float32)
    token_rates = rates.reshape(head_count, tok_rows)
    chips = line // 2

    one = jax.ShapeDtypeStruct((tok_rows, wide), jnp.bfloat16)
    mirrored = call(
        pack_mirror_kernel,
        [one] * line,
        (rows_of(keys), rows_of(values), token_rates),
        (tile_scratch, tile_scratch),
    )
    mirrored = [mirrored[0]] + [send(mirrored[k], k) for k in range(1, line)]
    across = call(
        functools.partial(pack_across_kernel, height),
        [one] * chips,
        (pltpu.with_memory_space_constraint(rows_of(queries), pltpu.HBM),),
        (
            pltpu.VMEM((tok_rows, head_count, head_size), jnp.bfloat16),
            tile_scratch,
            pltpu.SemaphoreType.DMA((4,)),
        ),
        specs=[pl.BlockSpec(memory_space=pltpu.HBM)],
    )
    across_landed = [send(part, line + 2 * index) for index, part in enumerate(across)]
    weights = fast_weights.reshape(head_count, 3, head_size, head_size)
    own_weights = own_of(weights, own)
    mirror_weights = own_of(weights, own ^ line)
    own_gain = own_of(norm_gain.reshape(head_count, 1, head_size), own)
    taps = conv_weights.reshape(9, blocks * head_count, head_size)
    own_taps = lax.dynamic_index_in_dim(taps, own_channel, 1, keepdims=False)
    own_taps = jnp.pad(own_taps, ((0, 0), (0, tiles * LANES - head_size)))
    frames = frame_order[own ^ jnp.arange(shards, dtype=jnp.int32)]
    grad_shape = (3, head_size, tiles * LANES)
    grad_struct = jax.ShapeDtypeStruct(grad_shape, jnp.float32)
    unread = pl.BlockSpec(memory_space=pl.ANY)
    mirror_sum = call(
        functools.partial(sum_kernel, 2, tok_rows, False),
        grad_struct,
        (*mirrored[:2], mirror_weights),
    )
    gate = gate_input.reshape(height, frames_here, gate_input.shape[3])
    opened = call(
        silu_kernel,
        jax.ShapeDtypeStruct((height * frames_here, gate_input.shape[3]), jnp.float32),
        (gate,),
    )
    early = (opened, across[0], own_weights, own_gain, own_taps, frames, mirror_sum)
    query_struct = jax.ShapeDtypeStruct((half, wide), jnp.bfloat16)
    packed = call(
        functools.partial(pack_near_kernel, height, len(early)),
        [one] * line + [query_struct] * line,
        (rows_of(keys), rows_of(values), token_rates, rows_of(queries), *early),
        (tile_scratch, tile_scratch, tile_scratch),
        specs=in_vmem(4) + [unread] * len(early),
    )
    near_queries = packed[line:]
    held = [after(part, *mirrored[1:], *across_landed) for part in packed[1:line]]
    near = [packed[0]] + [send(held[k - 1], k) for k in range(1, line)]
    ahead = (*across_landed, *held)
    crossing = call(
        functools.partial(mirror_kernel, line - 2, tok_rows),
        jax.ShapeDtypeStruct((head_size + head_size // 2, wide), jnp.bfloat16),
        (*mirrored[2:], mirror_weights, mirror_sum, *ahead),
        (pltpu.VMEM(grad_shape, jnp.float32),),
        specs=in_vmem(line) + [unread] * len(ahead),
    )
    crossed = send(crossing, line)
    own_sum = call(
        functools.partial(sum_kernel, 2, tok_rows, False),
        grad_struct,
        (*near[:2], own_weights, crossing),
        specs=in_vmem(3) + [unread],
    )
    across = relay([after(part, own_sum) for part in across_landed])
    gradients = call(
        functools.partial(sum_kernel, line - 2, tok_rows, True),
        grad_struct,
        (*near[2:], own_weights, own_sum),
    )
    mate_queries = send(after(near_queries[1], own_sum), 1)
    late_queries = [
        send(after(near_queries[k], *near[2:]), k) for k in range(2, line)
    ]
    side_rows = frames_here * height // 2
    first_shards, far_shards, late_shards = (0, 1), range(line, shards), range(2, line)
    grid_shape = (tiles, shards, height + 16, LANES)
    turned_shape = (blocks, shards, tiles, 2 * side_rows, LANES)
    numbers = [pl.BlockSpec(memory_space=pltpu.SMEM)]
    updated, turned = call(
        functools.partial(apply_first_kernel, height, frames_here, first_shards, far_shards),
        [
            jax.ShapeDtypeStruct((3, head_size, head_size), jnp.bfloat16),
            jax.ShapeDtypeStruct(turned_shape, jnp.float32),
        ],
        (
            frames, near_queries[0], mate_queries, *across,
            own_weights, gradients, crossed, own_gain, own_taps,
        ),
        (pltpu.VMEM((2 + line, *grid_shape), jnp.float32),),
        specs=numbers + in_vmem(line + 7),
    )
    order = [(k, x) for k in range(0, shards, 2) for x in range(blocks)][1:]
    order = sorted(order, key=lambda place: (place != (line, 0), place))
    outgoing = call(
        functools.partial(apply_last_kernel, height, frames_here, late_shards, order),
        [jax.ShapeDtypeStruct((side_rows, wide), jnp.bfloat16)] * 2
        + [jax.ShapeDtypeStruct((2 * side_rows, wide), jnp.bfloat16)] * (shards // 2 * blocks - 1),
        (frames, *late_queries, updated, turned, own_gain, own_taps),
        (
            pltpu.VMEM((line - 2, *grid_shape), jnp.float32),
            pltpu.VMEM(turned_shape, jnp.float32),
        ),
        specs=numbers + in_vmem(line + 2),
    )
    landed = [send_far(part, k, x) for part, (k, x) in zip(outgoing[2:], order)]
    arrived = [outgoing[0], send(outgoing[1], 1), *relay(landed)]
    places = [(0, 0), *order]
    gated = call(
        functools.partial(gate_kernel, blocks, shards, places),
        jax.ShapeDtypeStruct(gate.shape, jnp.bfloat16),
        (*arrived, opened),
        (
            pltpu.VMEM((len(places), *gate.shape[:2], wide), jnp.bfloat16),
            pltpu.SemaphoreType.DMA((len(places),)),
        ),
        leave=False,
    )
    return gated.reshape(gate_input.shape)


def fits_by_heads(queries, gate_input, frame_order):
    tok_rows, head_size = queries.shape[0], queries.shape[3]
    head_count = queries.shape[1] * queries.shape[2]
    height, frames_here, col_width = gate_input.shape[:3]
    shards = lax.axis_size("tok")
    return (
        head_count == shards
        and frame_order.shape[0] == shards
        and lax.axis_size("tile") == 1
        and col_width == 1
        and shards >= 8
        and shards & (shards - 1) == 0
        and head_size % LANES == LANES // 2
        and height % 8 == 0
        and tok_rows == height * shards
        and tok_rows % 64 == 0
        and head_size % 64 == 0
        and frames_here * height % 32 == 0
        and frames_here * lax.axis_size("head") == shards
        and lax.axis_size("head") & (lax.axis_size("head") - 1) == 0
    )


def renormed(previous, gradient):
    before = previous.astype(jnp.float32)
    updated = before - gradient
    scale_old = jnp.sqrt(jnp.mean(before * before, axis=-1, keepdims=True) + epsilon)
    scale_new = jnp.sqrt(jnp.mean(updated * updated, axis=-1, keepdims=True) + epsilon)
    return (updated * (scale_old / scale_new)).astype(jnp.bfloat16)


def by_tokens(
    queries, keys, values, rates, fast_weights, norm_gain, frame_order, gate_input, conv_weights
):
    tok_rows = queries.shape[0]
    head_count = queries.shape[1] * queries.shape[2]
    head_size = queries.shape[3]
    query_rows = queries.reshape(tok_rows, head_count, head_size)
    key_rows = keys.reshape(tok_rows, head_count, head_size)
    value_rows = values.reshape(tok_rows, head_count, head_size)
    token_rates = rates.reshape(head_count, tok_rows)
    weights = fast_weights.reshape(head_count, 3, head_size, head_size)
    head_gains = norm_gain.reshape(head_count, head_size)
    first_pre = jnp.einsum(
        "thd,hfd->htf", key_rows, weights[:, 0], preferred_element_type=jnp.float32
    )
    third_pre = jnp.einsum(
        "thd,hfd->htf", key_rows, weights[:, 1], preferred_element_type=jnp.float32
    )
    sigmoid_first = jax.nn.sigmoid(first_pre)
    activated = first_pre * sigmoid_first
    hidden = (activated * third_pre).astype(jnp.bfloat16)
    target = (-token_rates.T[:, :, None] * value_rows.astype(jnp.float32)).astype(jnp.bfloat16)
    grad_down = jnp.einsum("thd,htf->hdf", target, hidden, preferred_element_type=jnp.float32)
    hidden_grad = jnp.einsum(
        "thd,hdf->htf", target, weights[:, 2], preferred_element_type=jnp.float32
    )
    grad_first_in = (
        hidden_grad * third_pre * sigmoid_first * (1.0 + first_pre * (1.0 - sigmoid_first))
    ).astype(jnp.bfloat16)
    grad_third_in = (hidden_grad * activated).astype(jnp.bfloat16)
    grad_first = jnp.einsum(
        "htf,thd->hfd", grad_first_in, key_rows, preferred_element_type=jnp.float32
    )
    grad_third = jnp.einsum(
        "htf,thd->hfd", grad_third_in, key_rows, preferred_element_type=jnp.float32
    )
    gradients = jnp.stack([grad_first, grad_third, grad_down], axis=1)
    row_share = lax.psum_scatter(gradients, "tok", scatter_dimension=2, tiled=True)
    row_count = row_share.shape[2]
    own_rows = lax.dynamic_slice_in_dim(weights, lax.axis_index("tok") * row_count, row_count, 2)
    updated = lax.all_gather(renormed(own_rows, row_share), "tok", axis=2, tiled=True)
    proj_first = jnp.einsum(
        "thd,hfd->thf", query_rows, updated[:, 0], preferred_element_type=jnp.float32
    )
    proj_third = jnp.einsum(
        "thd,hfd->thf", query_rows, updated[:, 1], preferred_element_type=jnp.float32
    )
    mixed_hidden = (jax.nn.silu(proj_first) * proj_third).astype(jnp.bfloat16)
    outputs = jnp.einsum(
        "thf,hdf->thd", mixed_hidden, updated[:, 2], preferred_element_type=jnp.float32
    )
    normed = (
        outputs
        * lax.rsqrt(jnp.mean(outputs * outputs, axis=-1, keepdims=True) + epsilon)
        * head_gains[None]
    )
    normed = normed.astype(jnp.bfloat16)
    height = gate_input.shape[0]
    col_width = gate_input.shape[2]
    shards = lax.axis_size("tok")
    full_width = col_width * shards
    channels_here = head_count * head_size
    frame_grid = normed.reshape(height, full_width, channels_here)
    own_taps = lax.dynamic_slice_in_dim(
        conv_weights, lax.axis_index("head") * channels_here, channels_here, 2
    )
    padded = jnp.pad(frame_grid, ((1, 1), (1, 1), (0, 0)))
    local_sum = jnp.zeros((height, full_width, channels_here), jnp.float32)
    for row_tap in range(3):
        for col_tap in range(3):
            local_sum = local_sum + own_taps[row_tap, col_tap] * padded[
                row_tap : row_tap + height, col_tap : col_tap + full_width
            ].astype(jnp.float32)
    outgoing = local_sum.astype(jnp.bfloat16).reshape(height, shards, col_width, channels_here)
    arrived = lax.all_to_all(outgoing, "tok", split_axis=1, concat_axis=1, tiled=True)
    frame_count = frame_order.shape[0]
    numbers = jnp.arange(frame_count, dtype=jnp.int32)
    inverse = jnp.sum(
        jnp.where(frame_order[None, :] == numbers[:, None], numbers[None, :], 0), axis=1
    )
    ordered = jnp.take(arrived, inverse, axis=1)
    tile_block = lax.all_to_all(ordered, "head", split_axis=1, concat_axis=3, tiled=True)
    return (tile_block.astype(jnp.float32) * jax.nn.silu(gate_input.astype(jnp.float32))).astype(
        jnp.bfloat16
    )


def local(queries, keys, values, rates, fast_weights, norm_gain, frame_order, gate_input, conv_weights):
    args = (
        queries, keys, values, rates, fast_weights, norm_gain, frame_order, gate_input, conv_weights
    )
    if fits_by_heads(queries, gate_input, frame_order):
        return by_heads(*args)
    return by_tokens(*args)


def solution(mesh):
    in_specs = (
        P(("groups", "tok"), "tile", "head", None),
        P(("groups", "tok"), "tile", "head", None),
        P(("groups", "tok"), "tile", "head", None),
        P("tile", "head", ("groups", "tok")),
        P("tile", "head", None, None, None),
        P("tile", "head", None),
        P("groups"),
        P(None, ("groups", "head"), "tok", "tile"),
        P(None, None, "tile"),
    )
    out_specs = P(None, ("groups", "head"), "tok", "tile")
    return jax.shard_map(local, mesh=mesh, in_specs=in_specs, out_specs=out_specs, check_vma=False)
```

```python
import functools

import jax
import jax.numpy as jnp
from jax import lax
from jax.experimental import pallas as pl
from jax.experimental.pallas import tpu as pltpu
from jax.sharding import PartitionSpec as P

epsilon = 1e-06
LANES = 128
VMEM_BYTES = 24 * 1024 * 1024


def split_lanes(source, scratch, rows, head_size):
    full = head_size // LANES
    tail = head_size - full * LANES
    wide = source.reshape(rows, head_size).astype(jnp.float32)
    for tile in range(full):
        scratch[tile] = wide[:, tile * LANES : (tile + 1) * LANES]
    scratch[full, :, 0:tail] = wide[:, full * LANES :]


def join_halves(first, second, tail):
    lane = lax.broadcasted_iota(jnp.int32, first[-1].shape, 1)
    middle = jnp.where(lane < tail, first[-1], pltpu.roll(second[-1], tail, 1))
    return first[:-1] + [middle] + second[:-1]


def part_halves(packed, head_size):
    full = head_size // LANES
    tail = head_size - full * LANES
    first = packed[:, :head_size]
    middle = packed[:, head_size : (full + 1) * LANES]
    second = jnp.concatenate([packed[:, (full + 1) * LANES :], middle], axis=1)
    return first, second


def partner_head(partner):
    return lax.axis_index("tok") ^ partner


def pack_pairs(head, rate_ref, key_tiles, value_tiles, out_ref, start, head_size):
    heads, tok_rows = rate_ref.shape
    half = tok_rows // 2
    full = head_size // LANES
    tail = head_size - full * LANES
    rate_row = -rate_ref[pl.ds(head, 1), :]
    rates = jnp.broadcast_to(rate_row, (LANES, tok_rows)).T
    for row, tiles in ((start, key_tiles), (start + half, value_tiles)):
        sides = []
        for side in range(2):
            parts = [
                tiles[tile, pl.ds(side * half * heads + head, half, stride=heads), :]
                for tile in range(full + 1)
            ]
            if tiles is value_tiles:
                rate = rates[side * half : (side + 1) * half]
                parts = [rate * part for part in parts]
            sides.append(parts)
        for tile, part in enumerate(join_halves(sides[0], sides[1], tail)):
            out_ref[row : row + half, tile * LANES : (tile + 1) * LANES] = part.astype(jnp.bfloat16)


def pack_query(head, heads, height, query_tiles, out_ref, start, head_size):
    tok_rows = query_tiles.shape[1] // heads
    half = tok_rows // 2
    width = tok_rows // height
    full = head_size // LANES
    tail = head_size - full * LANES
    sides = []
    for side in range(2):
        sides.append(
            [
                jnp.concatenate(
                    [
                        query_tiles[
                            tile, pl.ds(column * heads + head, height, stride=width * heads), :
                        ]
                        for column in range(side * width // 2, (side + 1) * width // 2)
                    ],
                    axis=0,
                )
                for tile in range(full + 1)
            ]
        )
    for tile, part in enumerate(join_halves(sides[0], sides[1], tail)):
        out_ref[start : start + half, tile * LANES : (tile + 1) * LANES] = part.astype(jnp.bfloat16)


def pack_mirror_kernel(key_ref, value_ref, rate_ref, *rest):
    outs, (key_tiles, value_tiles) = rest[:-2], rest[-2:]
    tok_rows, heads, head_size = key_ref.shape
    split_lanes(key_ref[...], key_tiles, tok_rows * heads, head_size)
    split_lanes(value_ref[...], value_tiles, tok_rows * heads, head_size)
    for partner, out_ref in enumerate(outs):
        head = partner_head(partner ^ (heads // 2))
        pack_pairs(head, rate_ref, key_tiles, value_tiles, out_ref, 0, head_size)


def pack_across_kernel(height, query_any, *rest):
    outs, (query_ref, query_tiles, sems) = rest[:-3], rest[-3:]
    tok_rows, heads, head_size = query_any.shape
    half = tok_rows // 2
    full = head_size // LANES
    pieces = sems.shape[0]
    rows = tok_rows // pieces
    copies = [
        pltpu.make_async_copy(
            query_any.at[pl.ds(piece * rows, rows)],
            query_ref.at[pl.ds(piece * rows, rows)],
            sems.at[piece],
        )
        for piece in range(pieces)
    ]
    for copy in copies:
        copy.start()
    for piece, copy in enumerate(copies):
        copy.wait()
        wide = query_ref[piece * rows : (piece + 1) * rows].reshape(rows * heads, head_size)
        wide = wide.astype(jnp.float32)
        place = slice(piece * rows * heads, (piece + 1) * rows * heads)
        for tile in range(full):
            query_tiles[tile, place] = wide[:, tile * LANES : (tile + 1) * LANES]
        query_tiles[full, place, 0 : head_size - full * LANES] = wide[:, full * LANES :]
    for partner in range(heads // 2):
        head = partner_head(partner ^ (heads // 2))
        start = partner % 2 * half
        pack_query(head, heads, height, query_tiles, outs[partner // 2], start, head_size)


def pack_near_kernel(height, unread, key_ref, value_ref, rate_ref, query_ref, *rest):
    outs, (key_tiles, value_tiles, query_tiles) = rest[unread:-3], rest[-3:]
    tok_rows, heads, head_size = key_ref.shape
    split_lanes(key_ref[...], key_tiles, tok_rows * heads, head_size)
    split_lanes(value_ref[...], value_tiles, tok_rows * heads, head_size)
    split_lanes(query_ref[...], query_tiles, tok_rows * heads, head_size)
    line = heads // 2
    for partner in range(line):
        head = partner_head(partner)
        pack_pairs(head, rate_ref, key_tiles, value_tiles, outs[partner], 0, head_size)
        pack_query(head, heads, height, query_tiles, outs[line + partner], 0, head_size)


def send_far(part, partner, other):
    blocks = lax.axis_size("head")
    count = lax.axis_size("tok") * blocks
    pairs = [(place, place ^ (partner * blocks + other)) for place in range(count)]
    return lax.ppermute(part, ("tok", "head"), pairs)


def relay(landed):
    return [part for one in landed for part in (one, send(one, 1))]


def send(part, partner):
    pairs = [(place, place ^ partner) for place in range(lax.axis_size("tok"))]
    return lax.ppermute(part, "tok", pairs)


def sigmoid(value):
    return 0.5 + 0.5 * jnp.tanh(0.5 * value)


def contract(first, second, dims):
    return lax.dot_general(first, second, (dims, ((), ())), preferred_element_type=jnp.float32)


NN = ((1,), (0,))
NT = ((1,), (1,))


def add_gradients(pair_refs, tok_rows, weight_ref, prior_ref, grad_ref):
    half = tok_rows // 2
    head_size = weight_ref.shape[-1]
    first_weight = weight_ref[0]
    third_weight = weight_ref[1]
    down_turned = weight_ref[2].astype(jnp.float32).T.astype(jnp.bfloat16)
    step = 2 if len(pair_refs) % 2 == 0 else 1
    for start in range(0, len(pair_refs), step):
        key_parts, target_parts = [], []
        for pair_ref in pair_refs[start : start + step]:
            key_parts.extend(part_halves(pair_ref[0:half, :], head_size))
            target_parts.extend(part_halves(pair_ref[half:tok_rows, :], head_size))
        key_rows = jnp.concatenate(key_parts, axis=0)
        target = jnp.concatenate(target_parts, axis=0)
        first_pre = contract(first_weight, key_rows, NT)
        third_pre = contract(third_weight, key_rows, NT)
        hidden_grad = contract(down_turned, target, NT)
        sigmoid_first = sigmoid(first_pre)
        activated = first_pre * sigmoid_first
        mixed = (activated * third_pre).astype(jnp.bfloat16)
        grad_first_in = (
            hidden_grad * third_pre * sigmoid_first * (1.0 + first_pre * (1.0 - sigmoid_first))
        ).astype(jnp.bfloat16)
        grad_third_in = (hidden_grad * activated).astype(jnp.bfloat16)
        grads = (
            contract(grad_first_in, key_rows, NN),
            contract(grad_third_in, key_rows, NN),
            contract(mixed, target, NN),
        )
        for index, grad in enumerate(grads):
            if start == 0 and prior_ref is None:
                grad_ref[index, :, 0:head_size] = grad
            elif start == 0:
                grad_ref[index, :, 0:head_size] = prior_ref[index, :, 0:head_size] + grad
            else:
                grad_ref[index, :, 0:head_size] += grad


def sum_kernel(count, tok_rows, prior, *refs):
    pair_refs, weight_ref, out_ref = refs[:count], refs[count], refs[-1]
    prior_ref = refs[count + 1] if prior else None
    add_gradients(pair_refs, tok_rows, weight_ref, prior_ref, out_ref)


def mirror_kernel(count, tok_rows, *refs):
    pair_refs, weight_ref, prior_ref = refs[:count], refs[count], refs[count + 1]
    out_ref, grad_ref = refs[-2:]
    head_size = weight_ref.shape[-1]
    full = head_size // LANES
    tail = head_size - full * LANES
    half = head_size // 2
    add_gradients(pair_refs, tok_rows, weight_ref, prior_ref, grad_ref)

    def tiles_of(index, rows):
        return [
            grad_ref[index, rows, tile * LANES : (tile + 1) * LANES] for tile in range(full + 1)
        ]

    both = join_halves(tiles_of(0, slice(0, head_size)), tiles_of(1, slice(0, head_size)), tail)
    down = join_halves(tiles_of(2, slice(0, half)), tiles_of(2, slice(half, head_size)), tail)
    for tile, (above, below) in enumerate(zip(both, down)):
        lanes = slice(tile * LANES, (tile + 1) * LANES)
        out_ref[0:head_size, lanes] = above.astype(jnp.bfloat16)
        out_ref[head_size : head_size + half, lanes] = below.astype(jnp.bfloat16)


def renorm(weight_ref, grad_ref, mirror_refs, out_ref):
    head_size = weight_ref.shape[-1]
    units = head_size // len(mirror_refs)
    firsts, thirds, downs = [], [], []
    for mirror_ref in mirror_refs:
        first, third = part_halves(mirror_ref[0:units, :], head_size)
        firsts.append(first)
        thirds.append(third)
        downs.extend(part_halves(mirror_ref[units:, :], head_size))
    first, third, down = (jnp.concatenate(parts, axis=0) for parts in (firsts, thirds, downs))
    for index, other in enumerate((first, third, down)):
        before = weight_ref[index].astype(jnp.float32)
        axis = 1
        if index == 2:
            before = before.T
            axis = 0
        grad = grad_ref[index, :, 0:head_size] + other.astype(jnp.float32)
        updated = before - grad
        scale_old = jnp.sqrt(jnp.mean(before * before, axis=axis, keepdims=True) + epsilon)
        scale_new = jnp.sqrt(jnp.mean(updated * updated, axis=axis, keepdims=True) + epsilon)
        out_ref[index] = (updated * (scale_old / scale_new)).astype(jnp.bfloat16)


def apply_shards(
    height, frames_here, parts, order_ref, weight_ref, gain_ref, tap_ref, grid_ref, turned_ref
):
    head_size = weight_ref.shape[-1]
    full = head_size // LANES
    width = grid_ref.shape[2]
    top = 8
    edge = jnp.zeros((top, LANES), jnp.float32)
    for place in range(len(parts)):
        for tile in range(full + 1):
            for column in range(width):
                grid_ref[place, tile, column, 0:top] = edge
                grid_ref[place, tile, column, top + height :] = edge
    gain = gain_ref[...]
    for place, (shard, queries) in enumerate(parts):
        rows = jnp.concatenate(part_halves(queries, head_size), axis=0)
        proj_first = contract(rows, weight_ref[0], NT)
        proj_third = contract(rows, weight_ref[1], NT)
        mixed = (proj_first * jax.nn.sigmoid(proj_first) * proj_third).astype(jnp.bfloat16)
        outputs = contract(mixed, weight_ref[2], NN)
        scale = lax.rsqrt(jnp.mean(outputs * outputs, axis=-1, keepdims=True) + epsilon)
        normed = (outputs * scale * gain).astype(jnp.bfloat16).astype(jnp.float32)
        frame = order_ref[shard]
        block = frame // frames_here
        slot = frame % frames_here
        for tile in range(full + 1):
            lanes = slice(tile * LANES, min((tile + 1) * LANES, head_size))
            for column in range(width):
                grid_ref[place, tile, column, top : top + height, 0 : lanes.stop - lanes.start] = (
                    normed[column * height : (column + 1) * height, lanes]
                )
            taps = [
                tap_ref[index : index + 1, tile * LANES : (tile + 1) * LANES] for index in range(9)
            ]
            loaded = {}
            for column in range(width):
                total = None
                for col_tap in range(3):
                    source = column + col_tap - 1
                    if not 0 <= source < width:
                        continue
                    if source not in loaded:
                        loaded[source] = [
                            grid_ref[place, tile, source, first : first + height, :]
                            for first in range(top - 1, top + 2)
                        ]
                    for row_tap in range(3):
                        term = taps[row_tap * 3 + col_tap] * loaded[source][row_tap]
                        total = term if total is None else total + term
                turned_ref[
                    block, column, tile, pl.ds(slot, height, stride=frames_here), :
                ] = total


def apply_first_kernel(height, frames_here, near, far, order_ref, *refs):
    near_refs, far_refs = refs[: len(near)], refs[len(near) : len(near) + len(far)]
    before_ref, grad_ref, mirror_ref, gain_ref, tap_ref, weight_ref, turned_ref, grid_ref = refs[-8:]
    half = near_refs[0].shape[0]
    parts = [(shard, ref[...]) for shard, ref in zip(near, near_refs)]
    for shard, ref in zip(far, far_refs):
        parts.append((shard, ref[shard % 2 * half : (shard % 2 + 1) * half, :]))
    renorm(before_ref, grad_ref, [mirror_ref], weight_ref)
    apply_shards(
        height, frames_here, parts, order_ref, weight_ref, gain_ref, tap_ref, grid_ref, turned_ref
    )


def apply_last_kernel(height, frames_here, late, order, order_ref, *refs):
    query_refs = refs[: len(late)]
    weight_ref, done_ref, gain_ref, tap_ref = refs[len(late) : len(late) + 4]
    out_refs, (grid_ref, turned_ref) = refs[len(late) + 4 : -2], refs[-2:]
    turned_ref[...] = done_ref[...]
    parts = [(shard, ref[...]) for shard, ref in zip(late, query_refs)]
    apply_shards(
        height, frames_here, parts, order_ref, weight_ref, gain_ref, tap_ref, grid_ref, turned_ref
    )
    shards = turned_ref.shape[1]
    full = turned_ref.shape[2] - 1
    tail = weight_ref.shape[-1] - full * LANES
    blocks = turned_ref.shape[0]
    side_rows = turned_ref.shape[3] // 2
    for partner in range(shards):
        column = partner_head(partner)
        for other in range(blocks):
            block = lax.axis_index("head") ^ other
            sides = [
                [
                    turned_ref[block, column, tile, side * side_rows : (side + 1) * side_rows, :]
                    for tile in range(full + 1)
                ]
                for side in range(2)
            ]
            start = partner % 2 * side_rows
            if partner < 2 and other == 0:
                target, start = out_refs[partner], 0
            else:
                target = out_refs[2 + order.index((partner // 2 * 2, other))]
            for tile, part in enumerate(join_halves(sides[0], sides[1], tail)):
                target[start : start + side_rows, tile * LANES : (tile + 1) * LANES] = (
                    part.astype(jnp.bfloat16)
                )


def silu_kernel(gate_any, out_ref, gate_ref, sem):
    height, frames_here, channels = gate_ref.shape
    copy = pltpu.make_async_copy(gate_any, gate_ref, sem)
    copy.start()
    copy.wait()
    gate = gate_ref[...].astype(jnp.float32)
    out_ref[...] = (gate * jax.nn.sigmoid(gate)).reshape(height * frames_here, channels)


def gate_kernel(blocks, shards, places, *refs):
    conv_refs = refs[: 2 * len(places)]
    gate_ref, out_any, product_ref, sems = refs[2 * len(places)], *refs[-3:]
    height, frames_here, channels = out_any.shape
    head_size = channels // blocks // shards
    side_rows = height * frames_here // 2
    rows_here = height // 2
    own = lax.axis_index("tok")
    odd = own % 2
    copies = []
    for index, (partner, other) in enumerate(places):
        one_ref, two_ref = conv_refs[2 * index : 2 * index + 2]
        one = one_ref[0:side_rows, :].astype(jnp.float32)
        two = two_ref[two_ref.shape[0] - side_rows :, :].astype(jnp.float32)
        low = part_halves(jnp.where(odd == 1, two, one), head_size)
        high = part_halves(jnp.where(odd == 1, one, two), head_size)
        head = (lax.axis_index("head") ^ other) * shards + ((own - odd) ^ partner)
        lanes = pl.ds(pl.multiple_of(head * head_size, 2 * head_size), 2 * head_size)
        for side in range(2):
            rows = slice(side * rows_here, (side + 1) * rows_here)
            conv = jnp.concatenate([low[side], high[side]], axis=1)
            conv = conv * gate_ref[side * side_rows : (side + 1) * side_rows, lanes]
            conv = conv.reshape(rows_here, frames_here, 2 * head_size)
            product_ref[index, rows] = conv.astype(jnp.bfloat16)
        copy = pltpu.make_async_copy(
            product_ref.at[index], out_any.at[:, :, lanes], sems.at[index]
        )
        copy.start()
        copies.append(copy)
    for copy in copies:
        copy.wait()


def in_vmem(count):
    return [pl.BlockSpec(memory_space=pltpu.VMEM)] * count


def call(kernel, out, operands, scratch=(), specs=None, leave=True):
    specs = specs or in_vmem(len(operands))
    operands = [
        pltpu.with_memory_space_constraint(item, pltpu.VMEM)
        if spec.memory_space == pltpu.VMEM
        else item
        for item, spec in zip(operands, specs)
    ]
    place = pltpu.VMEM if leave else pl.ANY
    if leave:
        out = jax.tree.map(lambda item: pltpu.VMEM(item.shape, item.dtype), out)
    return pl.pallas_call(
        kernel,
        out_shape=out,
        in_specs=specs,
        out_specs=jax.tree.map(lambda _: pl.BlockSpec(memory_space=place), out),
        scratch_shapes=scratch,
        compiler_params=pltpu.CompilerParams(vmem_limit_bytes=VMEM_BYTES),
        cost_estimate=pl.CostEstimate(flops=0, bytes_accessed=0, transcendentals=0),
    )(*operands)


def after(part, *earlier):
    anywhere = pl.BlockSpec(memory_space=pl.ANY)
    return pl.pallas_call(
        lambda *refs: None,
        out_shape=jax.ShapeDtypeStruct(part.shape, part.dtype),
        in_specs=[anywhere] * (1 + len(earlier)),
        out_specs=anywhere,
        input_output_aliases={0: 0},
        compiler_params=pltpu.CompilerParams(vmem_limit_bytes=1024 * 1024),
        cost_estimate=pl.CostEstimate(flops=0, bytes_accessed=0, transcendentals=0),
    )(part, *earlier)


def by_heads(
    queries, keys, values, rates, fast_weights, norm_gain, frame_order, gate_input, conv_weights
):
    tok_rows = queries.shape[0]
    head_count = queries.shape[1] * queries.shape[2]
    head_size = queries.shape[3]
    height, frames_here = gate_input.shape[:2]
    shards = lax.axis_size("tok")
    blocks = lax.axis_size("head")
    half = tok_rows // 2
    wide = 2 * head_size
    tiles = head_size // LANES + 1
    own = lax.axis_index("tok")
    own_channel = lax.axis_index("head") * head_count + own

    def rows_of(array):
        return array.reshape(tok_rows, head_count, head_size)

    def own_of(array, place):
        return lax.dynamic_index_in_dim(array, place, 0, keepdims=False)

    line = shards // 2
    tile_scratch = pltpu.VMEM((tiles, tok_rows * head_count, LANES), jnp.float32)
    token_rates = rates.reshape(head_count, tok_rows)
    chips = line // 2

    one = jax.ShapeDtypeStruct((tok_rows, wide), jnp.bfloat16)
    mirrored = call(
        pack_mirror_kernel,
        [one] * line,
        (rows_of(keys), rows_of(values), token_rates),
        (tile_scratch, tile_scratch),
    )
    mirrored = [mirrored[0]] + [send(mirrored[k], k) for k in range(1, line)]
    across = call(
        functools.partial(pack_across_kernel, height),
        [one] * chips,
        (pltpu.with_memory_space_constraint(rows_of(queries), pltpu.HBM),),
        (
            pltpu.VMEM((tok_rows, head_count, head_size), jnp.bfloat16),
            tile_scratch,
            pltpu.SemaphoreType.DMA((4,)),
        ),
        specs=[pl.BlockSpec(memory_space=pltpu.HBM)],
    )
    across_landed = [send(part, line + 2 * index) for index, part in enumerate(across)]
    weights = fast_weights.reshape(head_count, 3, head_size, head_size)
    own_weights = own_of(weights, own)
    mirror_weights = own_of(weights, own ^ line)
    own_gain = own_of(norm_gain.reshape(head_count, 1, head_size), own)
    taps = conv_weights.reshape(9, blocks * head_count, head_size)
    own_taps = lax.dynamic_index_in_dim(taps, own_channel, 1, keepdims=False)
    own_taps = jnp.pad(own_taps, ((0, 0), (0, tiles * LANES - head_size)))
    frames = frame_order[own ^ jnp.arange(shards, dtype=jnp.int32)]
    grad_shape = (3, head_size, tiles * LANES)
    grad_struct = jax.ShapeDtypeStruct(grad_shape, jnp.float32)
    unread = pl.BlockSpec(memory_space=pl.ANY)
    mirror_sum = call(
        functools.partial(sum_kernel, 2, tok_rows, False),
        grad_struct,
        (*mirrored[:2], mirror_weights),
    )
    gate = gate_input.reshape(height, frames_here, gate_input.shape[3])
    opened = call(
        silu_kernel,
        jax.ShapeDtypeStruct((height * frames_here, gate_input.shape[3]), jnp.float32),
        (pltpu.with_memory_space_constraint(gate, pltpu.HBM),),
        (pltpu.VMEM(gate.shape, jnp.bfloat16), pltpu.SemaphoreType.DMA(())),
        specs=[pl.BlockSpec(memory_space=pltpu.HBM)],
    )
    early = (opened, across[0], own_weights, own_gain, own_taps, frames, mirror_sum)
    query_struct = jax.ShapeDtypeStruct((half, wide), jnp.bfloat16)
    packed = call(
        functools.partial(pack_near_kernel, height, len(early)),
        [one] * line + [query_struct] * line,
        (rows_of(keys), rows_of(values), token_rates, rows_of(queries), *early),
        (tile_scratch, tile_scratch, tile_scratch),
        specs=in_vmem(4) + [unread] * len(early),
    )
    near_queries = packed[line:]
    held = [after(part, *mirrored[1:], *across_landed) for part in packed[1:line]]
    near = [packed[0]] + [send(held[k - 1], k) for k in range(1, line)]
    ahead = (*across_landed, *held)
    crossing = call(
        functools.partial(mirror_kernel, line - 2, tok_rows),
        jax.ShapeDtypeStruct((head_size + head_size // 2, wide), jnp.bfloat16),
        (*mirrored[2:], mirror_weights, mirror_sum, *ahead),
        (pltpu.VMEM(grad_shape, jnp.float32),),
        specs=in_vmem(line) + [unread] * len(ahead),
    )
    crossed = send(crossing, line)
    own_sum = call(
        functools.partial(sum_kernel, 2, tok_rows, False),
        grad_struct,
        (*near[:2], own_weights, crossing),
        specs=in_vmem(3) + [unread],
    )
    across = relay([after(part, own_sum) for part in across_landed])
    gradients = call(
        functools.partial(sum_kernel, line - 2, tok_rows, True),
        grad_struct,
        (*near[2:], own_weights, own_sum),
    )
    mate_queries = send(after(near_queries[1], own_sum), 1)
    late_queries = [
        send(after(near_queries[k], *near[2:]), k) for k in range(2, line)
    ]
    side_rows = frames_here * height // 2
    first_shards, far_shards, late_shards = (0, 1), range(line, shards), range(2, line)
    grid_shape = (tiles, shards, height + 16, LANES)
    turned_shape = (blocks, shards, tiles, 2 * side_rows, LANES)
    numbers = [pl.BlockSpec(memory_space=pltpu.SMEM)]
    updated, turned = call(
        functools.partial(apply_first_kernel, height, frames_here, first_shards, far_shards),
        [
            jax.ShapeDtypeStruct((3, head_size, head_size), jnp.bfloat16),
            jax.ShapeDtypeStruct(turned_shape, jnp.float32),
        ],
        (
            frames, near_queries[0], mate_queries, *across,
            own_weights, gradients, crossed, own_gain, own_taps,
        ),
        (pltpu.VMEM((2 + line, *grid_shape), jnp.float32),),
        specs=numbers + in_vmem(line + 7),
    )
    order = [(k, x) for k in range(0, shards, 2) for x in range(blocks)][1:]
    order = sorted(order, key=lambda place: (place != (line, 0), place))
    outgoing = call(
        functools.partial(apply_last_kernel, height, frames_here, late_shards, order),
        [jax.ShapeDtypeStruct((side_rows, wide), jnp.bfloat16)] * 2
        + [jax.ShapeDtypeStruct((2 * side_rows, wide), jnp.bfloat16)] * (shards // 2 * blocks - 1),
        (frames, *late_queries, updated, turned, own_gain, own_taps),
        (
            pltpu.VMEM((line - 2, *grid_shape), jnp.float32),
            pltpu.VMEM(turned_shape, jnp.float32),
        ),
        specs=numbers + in_vmem(line + 2),
    )
    landed = [send_far(part, k, x) for part, (k, x) in zip(outgoing[2:], order)]
    arrived = [outgoing[0], send(outgoing[1], 1), *relay(landed)]
    places = [(0, 0), *order]
    gated = call(
        functools.partial(gate_kernel, blocks, shards, places),
        jax.ShapeDtypeStruct(gate.shape, jnp.bfloat16),
        (*arrived, opened),
        (
            pltpu.VMEM((len(places), *gate.shape[:2], wide), jnp.bfloat16),
            pltpu.SemaphoreType.DMA((len(places),)),
        ),
        leave=False,
    )
    return gated.reshape(gate_input.shape)


def fits_by_heads(queries, gate_input, frame_order):
    tok_rows, head_size = queries.shape[0], queries.shape[3]
    head_count = queries.shape[1] * queries.shape[2]
    height, frames_here, col_width = gate_input.shape[:3]
    shards = lax.axis_size("tok")
    return (
        head_count == shards
        and frame_order.shape[0] == shards
        and lax.axis_size("tile") == 1
        and col_width == 1
        and shards >= 8
        and shards & (shards - 1) == 0
        and head_size % LANES == LANES // 2
        and height % 8 == 0
        and tok_rows == height * shards
        and tok_rows % 64 == 0
        and head_size % 64 == 0
        and frames_here * height % 32 == 0
        and frames_here * lax.axis_size("head") == shards
        and lax.axis_size("head") & (lax.axis_size("head") - 1) == 0
    )


def renormed(previous, gradient):
    before = previous.astype(jnp.float32)
    updated = before - gradient
    scale_old = jnp.sqrt(jnp.mean(before * before, axis=-1, keepdims=True) + epsilon)
    scale_new = jnp.sqrt(jnp.mean(updated * updated, axis=-1, keepdims=True) + epsilon)
    return (updated * (scale_old / scale_new)).astype(jnp.bfloat16)


def by_tokens(
    queries, keys, values, rates, fast_weights, norm_gain, frame_order, gate_input, conv_weights
):
    tok_rows = queries.shape[0]
    head_count = queries.shape[1] * queries.shape[2]
    head_size = queries.shape[3]
    query_rows = queries.reshape(tok_rows, head_count, head_size)
    key_rows = keys.reshape(tok_rows, head_count, head_size)
    value_rows = values.reshape(tok_rows, head_count, head_size)
    token_rates = rates.reshape(head_count, tok_rows)
    weights = fast_weights.reshape(head_count, 3, head_size, head_size)
    head_gains = norm_gain.reshape(head_count, head_size)
    first_pre = jnp.einsum(
        "thd,hfd->htf", key_rows, weights[:, 0], preferred_element_type=jnp.float32
    )
    third_pre = jnp.einsum(
        "thd,hfd->htf", key_rows, weights[:, 1], preferred_element_type=jnp.float32
    )
    sigmoid_first = jax.nn.sigmoid(first_pre)
    activated = first_pre * sigmoid_first
    hidden = (activated * third_pre).astype(jnp.bfloat16)
    target = (-token_rates.T[:, :, None] * value_rows.astype(jnp.float32)).astype(jnp.bfloat16)
    grad_down = jnp.einsum("thd,htf->hdf", target, hidden, preferred_element_type=jnp.float32)
    hidden_grad = jnp.einsum(
        "thd,hdf->htf", target, weights[:, 2], preferred_element_type=jnp.float32
    )
    grad_first_in = (
        hidden_grad * third_pre * sigmoid_first * (1.0 + first_pre * (1.0 - sigmoid_first))
    ).astype(jnp.bfloat16)
    grad_third_in = (hidden_grad * activated).astype(jnp.bfloat16)
    grad_first = jnp.einsum(
        "htf,thd->hfd", grad_first_in, key_rows, preferred_element_type=jnp.float32
    )
    grad_third = jnp.einsum(
        "htf,thd->hfd", grad_third_in, key_rows, preferred_element_type=jnp.float32
    )
    gradients = jnp.stack([grad_first, grad_third, grad_down], axis=1)
    row_share = lax.psum_scatter(gradients, "tok", scatter_dimension=2, tiled=True)
    row_count = row_share.shape[2]
    own_rows = lax.dynamic_slice_in_dim(weights, lax.axis_index("tok") * row_count, row_count, 2)
    updated = lax.all_gather(renormed(own_rows, row_share), "tok", axis=2, tiled=True)
    proj_first = jnp.einsum(
        "thd,hfd->thf", query_rows, updated[:, 0], preferred_element_type=jnp.float32
    )
    proj_third = jnp.einsum(
        "thd,hfd->thf", query_rows, updated[:, 1], preferred_element_type=jnp.float32
    )
    mixed_hidden = (jax.nn.silu(proj_first) * proj_third).astype(jnp.bfloat16)
    outputs = jnp.einsum(
        "thf,hdf->thd", mixed_hidden, updated[:, 2], preferred_element_type=jnp.float32
    )
    normed = (
        outputs
        * lax.rsqrt(jnp.mean(outputs * outputs, axis=-1, keepdims=True) + epsilon)
        * head_gains[None]
    )
    normed = normed.astype(jnp.bfloat16)
    height = gate_input.shape[0]
    col_width = gate_input.shape[2]
    shards = lax.axis_size("tok")
    full_width = col_width * shards
    channels_here = head_count * head_size
    frame_grid = normed.reshape(height, full_width, channels_here)
    own_taps = lax.dynamic_slice_in_dim(
        conv_weights, lax.axis_index("head") * channels_here, channels_here, 2
    )
    padded = jnp.pad(frame_grid, ((1, 1), (1, 1), (0, 0)))
    local_sum = jnp.zeros((height, full_width, channels_here), jnp.float32)
    for row_tap in range(3):
        for col_tap in range(3):
            local_sum = local_sum + own_taps[row_tap, col_tap] * padded[
                row_tap : row_tap + height, col_tap : col_tap + full_width
            ].astype(jnp.float32)
    outgoing = local_sum.astype(jnp.bfloat16).reshape(height, shards, col_width, channels_here)
    arrived = lax.all_to_all(outgoing, "tok", split_axis=1, concat_axis=1, tiled=True)
    frame_count = frame_order.shape[0]
    numbers = jnp.arange(frame_count, dtype=jnp.int32)
    inverse = jnp.sum(
        jnp.where(frame_order[None, :] == numbers[:, None], numbers[None, :], 0), axis=1
    )
    ordered = jnp.take(arrived, inverse, axis=1)
    tile_block = lax.all_to_all(ordered, "head", split_axis=1, concat_axis=3, tiled=True)
    return (tile_block.astype(jnp.float32) * jax.nn.silu(gate_input.astype(jnp.float32))).astype(
        jnp.bfloat16
    )


def local(queries, keys, values, rates, fast_weights, norm_gain, frame_order, gate_input, conv_weights):
    args = (
        queries, keys, values, rates, fast_weights, norm_gain, frame_order, gate_input, conv_weights
    )
    if fits_by_heads(queries, gate_input, frame_order):
        return by_heads(*args)
    return by_tokens(*args)


def solution(mesh):
    in_specs = (
        P(("groups", "tok"), "tile", "head", None),
        P(("groups", "tok"), "tile", "head", None),
        P(("groups", "tok"), "tile", "head", None),
        P("tile", "head", ("groups", "tok")),
        P("tile", "head", None, None, None),
        P("tile", "head", None),
        P("groups"),
        P(None, ("groups", "head"), "tok", "tile"),
        P(None, None, "tile"),
    )
    out_specs = P(None, ("groups", "head"), "tok", "tile")
    return jax.shard_map(local, mesh=mesh, in_specs=in_specs, out_specs=out_specs, check_vma=False)
```

```python
import functools

import jax
import jax.numpy as jnp
from jax import lax
from jax.experimental import pallas as pl
from jax.experimental.pallas import tpu as pltpu
from jax.sharding import PartitionSpec as P

epsilon = 1e-06
LANES = 128
VMEM_BYTES = 24 * 1024 * 1024


def split_lanes(source, scratch, rows, head_size):
    full = head_size // LANES
    tail = head_size - full * LANES
    wide = source.reshape(rows, head_size).astype(jnp.float32)
    for tile in range(full):
        scratch[tile] = wide[:, tile * LANES : (tile + 1) * LANES]
    scratch[full, :, 0:tail] = wide[:, full * LANES :]


def join_halves(first, second, tail):
    lane = lax.broadcasted_iota(jnp.int32, first[-1].shape, 1)
    middle = jnp.where(lane < tail, first[-1], pltpu.roll(second[-1], tail, 1))
    return first[:-1] + [middle] + second[:-1]


def part_halves(packed, head_size):
    full = head_size // LANES
    tail = head_size - full * LANES
    first = packed[:, :head_size]
    middle = packed[:, head_size : (full + 1) * LANES]
    second = jnp.concatenate([packed[:, (full + 1) * LANES :], middle], axis=1)
    return first, second


def partner_head(partner):
    return lax.axis_index("tok") ^ partner


def pack_pairs(head, rate_ref, key_tiles, value_tiles, out_ref, start, head_size):
    heads, tok_rows = rate_ref.shape
    half = tok_rows // 2
    full = head_size // LANES
    tail = head_size - full * LANES
    rate_row = -rate_ref[pl.ds(head, 1), :]
    rates = jnp.broadcast_to(rate_row, (LANES, tok_rows)).T
    for row, tiles in ((start, key_tiles), (start + half, value_tiles)):
        sides = []
        for side in range(2):
            parts = [
                tiles[tile, pl.ds(side * half * heads + head, half, stride=heads), :]
                for tile in range(full + 1)
            ]
            if tiles is value_tiles:
                rate = rates[side * half : (side + 1) * half]
                parts = [rate * part for part in parts]
            sides.append(parts)
        for tile, part in enumerate(join_halves(sides[0], sides[1], tail)):
            out_ref[row : row + half, tile * LANES : (tile + 1) * LANES] = part.astype(jnp.bfloat16)


def pack_query(head, heads, height, query_tiles, out_ref, start, head_size):
    tok_rows = query_tiles.shape[1] // heads
    half = tok_rows // 2
    width = tok_rows // height
    full = head_size // LANES
    tail = head_size - full * LANES
    sides = []
    for side in range(2):
        sides.append(
            [
                jnp.concatenate(
                    [
                        query_tiles[
                            tile, pl.ds(column * heads + head, height, stride=width * heads), :
                        ]
                        for column in range(side * width // 2, (side + 1) * width // 2)
                    ],
                    axis=0,
                )
                for tile in range(full + 1)
            ]
        )
    for tile, part in enumerate(join_halves(sides[0], sides[1], tail)):
        out_ref[start : start + half, tile * LANES : (tile + 1) * LANES] = part.astype(jnp.bfloat16)


def pack_mirror_kernel(key_ref, value_ref, rate_ref, *rest):
    outs, (key_tiles, value_tiles) = rest[:-2], rest[-2:]
    tok_rows, heads, head_size = key_ref.shape
    split_lanes(key_ref[...], key_tiles, tok_rows * heads, head_size)
    split_lanes(value_ref[...], value_tiles, tok_rows * heads, head_size)
    for partner, out_ref in enumerate(outs):
        head = partner_head(partner ^ (heads // 2))
        pack_pairs(head, rate_ref, key_tiles, value_tiles, out_ref, 0, head_size)


def pack_across_kernel(height, query_any, *rest):
    outs, (query_ref, query_tiles, sems) = rest[:-3], rest[-3:]
    tok_rows, heads, head_size = query_any.shape
    half = tok_rows // 2
    full = head_size // LANES
    pieces = sems.shape[0]
    rows = tok_rows // pieces
    copies = [
        pltpu.make_async_copy(
            query_any.at[pl.ds(piece * rows, rows)],
            query_ref.at[pl.ds(piece * rows, rows)],
            sems.at[piece],
        )
        for piece in range(pieces)
    ]
    for copy in copies:
        copy.start()
    for piece, copy in enumerate(copies):
        copy.wait()
        wide = query_ref[piece * rows : (piece + 1) * rows].reshape(rows * heads, head_size)
        wide = wide.astype(jnp.float32)
        place = slice(piece * rows * heads, (piece + 1) * rows * heads)
        for tile in range(full):
            query_tiles[tile, place] = wide[:, tile * LANES : (tile + 1) * LANES]
        query_tiles[full, place, 0 : head_size - full * LANES] = wide[:, full * LANES :]
    for partner in range(heads // 2):
        head = partner_head(partner ^ (heads // 2))
        start = partner % 2 * half
        pack_query(head, heads, height, query_tiles, outs[partner // 2], start, head_size)


def pack_near_kernel(height, unread, key_ref, value_ref, rate_ref, query_ref, *rest):
    outs, (key_tiles, value_tiles, query_tiles) = rest[unread:-3], rest[-3:]
    tok_rows, heads, head_size = key_ref.shape
    split_lanes(key_ref[...], key_tiles, tok_rows * heads, head_size)
    split_lanes(value_ref[...], value_tiles, tok_rows * heads, head_size)
    split_lanes(query_ref[...], query_tiles, tok_rows * heads, head_size)
    line = heads // 2
    for partner in range(line):
        head = partner_head(partner)
        pack_pairs(head, rate_ref, key_tiles, value_tiles, outs[partner], 0, head_size)
        pack_query(head, heads, height, query_tiles, outs[line + partner], 0, head_size)


def send_far(part, partner, other):
    blocks = lax.axis_size("head")
    count = lax.axis_size("tok") * blocks
    pairs = [(place, place ^ (partner * blocks + other)) for place in range(count)]
    return lax.ppermute(part, ("tok", "head"), pairs)


def relay(landed):
    return [part for one in landed for part in (one, send(one, 1))]


def send(part, partner):
    pairs = [(place, place ^ partner) for place in range(lax.axis_size("tok"))]
    return lax.ppermute(part, "tok", pairs)


def sigmoid(value):
    return 0.5 + 0.5 * jnp.tanh(0.5 * value)


def contract(first, second, dims):
    return lax.dot_general(first, second, (dims, ((), ())), preferred_element_type=jnp.float32)


NN = ((1,), (0,))
NT = ((1,), (1,))


def add_gradients(pair_refs, tok_rows, weight_ref, prior_ref, grad_ref):
    half = tok_rows // 2
    head_size = weight_ref.shape[-1]
    first_weight = weight_ref[0]
    third_weight = weight_ref[1]
    down_turned = weight_ref[2].astype(jnp.float32).T.astype(jnp.bfloat16)
    step = 2 if len(pair_refs) % 2 == 0 else 1
    for start in range(0, len(pair_refs), step):
        key_parts, target_parts = [], []
        for pair_ref in pair_refs[start : start + step]:
            key_parts.extend(part_halves(pair_ref[0:half, :], head_size))
            target_parts.extend(part_halves(pair_ref[half:tok_rows, :], head_size))
        key_rows = jnp.concatenate(key_parts, axis=0)
        target = jnp.concatenate(target_parts, axis=0)
        first_pre = contract(first_weight, key_rows, NT)
        third_pre = contract(third_weight, key_rows, NT)
        hidden_grad = contract(down_turned, target, NT)
        sigmoid_first = sigmoid(first_pre)
        activated = first_pre * sigmoid_first
        mixed = (activated * third_pre).astype(jnp.bfloat16)
        grad_first_in = (
            hidden_grad * third_pre * sigmoid_first * (1.0 + first_pre * (1.0 - sigmoid_first))
        ).astype(jnp.bfloat16)
        grad_third_in = (hidden_grad * activated).astype(jnp.bfloat16)
        grads = (
            contract(grad_first_in, key_rows, NN),
            contract(grad_third_in, key_rows, NN),
            contract(mixed, target, NN),
        )
        for index, grad in enumerate(grads):
            if start == 0 and prior_ref is None:
                grad_ref[index, :, 0:head_size] = grad
            elif start == 0:
                grad_ref[index, :, 0:head_size] = prior_ref[index, :, 0:head_size] + grad
            else:
                grad_ref[index, :, 0:head_size] += grad


def sum_kernel(count, tok_rows, prior, *refs):
    pair_refs, weight_ref, out_ref = refs[:count], refs[count], refs[-1]
    prior_ref = refs[count + 1] if prior else None
    add_gradients(pair_refs, tok_rows, weight_ref, prior_ref, out_ref)


def mirror_kernel(count, tok_rows, *refs):
    pair_refs, weight_ref, prior_ref = refs[:count], refs[count], refs[count + 1]
    out_ref, grad_ref = refs[-2:]
    head_size = weight_ref.shape[-1]
    full = head_size // LANES
    tail = head_size - full * LANES
    half = head_size // 2
    add_gradients(pair_refs, tok_rows, weight_ref, prior_ref, grad_ref)

    def tiles_of(index, rows):
        return [
            grad_ref[index, rows, tile * LANES : (tile + 1) * LANES] for tile in range(full + 1)
        ]

    both = join_halves(tiles_of(0, slice(0, head_size)), tiles_of(1, slice(0, head_size)), tail)
    down = join_halves(tiles_of(2, slice(0, half)), tiles_of(2, slice(half, head_size)), tail)
    for tile, (above, below) in enumerate(zip(both, down)):
        lanes = slice(tile * LANES, (tile + 1) * LANES)
        out_ref[0:head_size, lanes] = above.astype(jnp.bfloat16)
        out_ref[head_size : head_size + half, lanes] = below.astype(jnp.bfloat16)


def renorm(weight_ref, grad_ref, mirror_refs, out_ref):
    head_size = weight_ref.shape[-1]
    units = head_size // len(mirror_refs)
    firsts, thirds, downs = [], [], []
    for mirror_ref in mirror_refs:
        first, third = part_halves(mirror_ref[0:units, :], head_size)
        firsts.append(first)
        thirds.append(third)
        downs.extend(part_halves(mirror_ref[units:, :], head_size))
    first, third, down = (jnp.concatenate(parts, axis=0) for parts in (firsts, thirds, downs))
    for index, other in enumerate((first, third, down)):
        before = weight_ref[index].astype(jnp.float32)
        axis = 1
        if index == 2:
            before = before.T
            axis = 0
        grad = grad_ref[index, :, 0:head_size] + other.astype(jnp.float32)
        updated = before - grad
        scale_old = jnp.sqrt(jnp.mean(before * before, axis=axis, keepdims=True) + epsilon)
        scale_new = jnp.sqrt(jnp.mean(updated * updated, axis=axis, keepdims=True) + epsilon)
        out_ref[index] = (updated * (scale_old / scale_new)).astype(jnp.bfloat16)


def apply_shards(
    height, frames_here, parts, order_ref, weight_ref, gain_ref, tap_ref, grid_ref, turned_ref
):
    head_size = weight_ref.shape[-1]
    full = head_size // LANES
    width = grid_ref.shape[2]
    top = 8
    edge = jnp.zeros((top, LANES), jnp.float32)
    for place in range(len(parts)):
        for tile in range(full + 1):
            for column in range(width):
                grid_ref[place, tile, column, 0:top] = edge
                grid_ref[place, tile, column, top + height :] = edge
    gain = gain_ref[...]
    for place, (shard, queries) in enumerate(parts):
        rows = jnp.concatenate(part_halves(queries, head_size), axis=0)
        proj_first = contract(rows, weight_ref[0], NT)
        proj_third = contract(rows, weight_ref[1], NT)
        mixed = (proj_first * jax.nn.sigmoid(proj_first) * proj_third).astype(jnp.bfloat16)
        outputs = contract(mixed, weight_ref[2], NN)
        scale = lax.rsqrt(jnp.mean(outputs * outputs, axis=-1, keepdims=True) + epsilon)
        normed = (outputs * scale * gain).astype(jnp.bfloat16).astype(jnp.float32)
        frame = order_ref[shard]
        block = frame // frames_here
        slot = frame % frames_here
        for tile in range(full + 1):
            lanes = slice(tile * LANES, min((tile + 1) * LANES, head_size))
            for column in range(width):
                grid_ref[place, tile, column, top : top + height, 0 : lanes.stop - lanes.start] = (
                    normed[column * height : (column + 1) * height, lanes]
                )
            taps = [
                tap_ref[index : index + 1, tile * LANES : (tile + 1) * LANES] for index in range(9)
            ]
            loaded = {}
            for column in range(width):
                total = None
                for col_tap in range(3):
                    source = column + col_tap - 1
                    if not 0 <= source < width:
                        continue
                    if source not in loaded:
                        loaded[source] = [
                            grid_ref[place, tile, source, first : first + height, :]
                            for first in range(top - 1, top + 2)
                        ]
                    for row_tap in range(3):
                        term = taps[row_tap * 3 + col_tap] * loaded[source][row_tap]
                        total = term if total is None else total + term
                turned_ref[
                    block, column, tile, pl.ds(slot, height, stride=frames_here), :
                ] = total


def apply_first_kernel(height, frames_here, near, far, order_ref, *refs):
    near_refs, far_refs = refs[: len(near)], refs[len(near) : len(near) + len(far)]
    before_ref, grad_ref, mirror_ref, gain_ref, tap_ref, weight_ref, turned_ref, grid_ref = refs[-8:]
    half = near_refs[0].shape[0]
    parts = [(shard, ref[...]) for shard, ref in zip(near, near_refs)]
    for shard, ref in zip(far, far_refs):
        parts.append((shard, ref[shard % 2 * half : (shard % 2 + 1) * half, :]))
    renorm(before_ref, grad_ref, [mirror_ref], weight_ref)
    apply_shards(
        height, frames_here, parts, order_ref, weight_ref, gain_ref, tap_ref, grid_ref, turned_ref
    )


def apply_last_kernel(height, frames_here, late, order, order_ref, *refs):
    query_refs = refs[: len(late)]
    weight_ref, done_ref, gain_ref, tap_ref = refs[len(late) : len(late) + 4]
    out_refs, (grid_ref, turned_ref) = refs[len(late) + 4 : -2], refs[-2:]
    turned_ref[...] = done_ref[...]
    parts = [(shard, ref[...]) for shard, ref in zip(late, query_refs)]
    apply_shards(
        height, frames_here, parts, order_ref, weight_ref, gain_ref, tap_ref, grid_ref, turned_ref
    )
    shards = turned_ref.shape[1]
    full = turned_ref.shape[2] - 1
    tail = weight_ref.shape[-1] - full * LANES
    blocks = turned_ref.shape[0]
    side_rows = turned_ref.shape[3] // 2
    for partner in range(shards):
        column = partner_head(partner)
        for other in range(blocks):
            block = lax.axis_index("head") ^ other
            sides = [
                [
                    turned_ref[block, column, tile, side * side_rows : (side + 1) * side_rows, :]
                    for tile in range(full + 1)
                ]
                for side in range(2)
            ]
            start = partner % 2 * side_rows
            if partner < 2 and other == 0:
                target, start = out_refs[partner], 0
            else:
                target = out_refs[2 + order.index((partner // 2 * 2, other))]
            for tile, part in enumerate(join_halves(sides[0], sides[1], tail)):
                target[start : start + side_rows, tile * LANES : (tile + 1) * LANES] = (
                    part.astype(jnp.bfloat16)
                )


def silu_kernel(gate_any, unread_any, out_ref, gate_ref, sem):
    height, frames_here, channels = gate_ref.shape
    copy = pltpu.make_async_copy(gate_any, gate_ref, sem)
    copy.start()
    copy.wait()
    gate = gate_ref[...].astype(jnp.float32)
    out_ref[...] = (gate * jax.nn.sigmoid(gate)).reshape(height * frames_here, channels)


def gate_kernel(blocks, shards, places, *refs):
    conv_refs = refs[: 2 * len(places)]
    gate_ref, out_any, product_ref, sems = refs[2 * len(places)], *refs[-3:]
    height, frames_here, channels = out_any.shape
    head_size = channels // blocks // shards
    side_rows = height * frames_here // 2
    rows_here = height // 2
    own = lax.axis_index("tok")
    odd = own % 2
    copies = []
    for index, (partner, other) in enumerate(places):
        one_ref, two_ref = conv_refs[2 * index : 2 * index + 2]
        one = one_ref[0:side_rows, :].astype(jnp.float32)
        two = two_ref[two_ref.shape[0] - side_rows :, :].astype(jnp.float32)
        low = part_halves(jnp.where(odd == 1, two, one), head_size)
        high = part_halves(jnp.where(odd == 1, one, two), head_size)
        head = (lax.axis_index("head") ^ other) * shards + ((own - odd) ^ partner)
        lanes = pl.ds(pl.multiple_of(head * head_size, 2 * head_size), 2 * head_size)
        for side in range(2):
            rows = slice(side * rows_here, (side + 1) * rows_here)
            conv = jnp.concatenate([low[side], high[side]], axis=1)
            conv = conv * gate_ref[side * side_rows : (side + 1) * side_rows, lanes]
            conv = conv.reshape(rows_here, frames_here, 2 * head_size)
            product_ref[index, rows] = conv.astype(jnp.bfloat16)
        copy = pltpu.make_async_copy(
            product_ref.at[index], out_any.at[:, :, lanes], sems.at[index]
        )
        copy.start()
        copies.append(copy)
    for copy in copies:
        copy.wait()


def in_vmem(count):
    return [pl.BlockSpec(memory_space=pltpu.VMEM)] * count


def call(kernel, out, operands, scratch=(), specs=None, leave=True):
    specs = specs or in_vmem(len(operands))
    operands = [
        pltpu.with_memory_space_constraint(item, pltpu.VMEM)
        if spec.memory_space == pltpu.VMEM
        else item
        for item, spec in zip(operands, specs)
    ]
    place = pltpu.VMEM if leave else pl.ANY
    if leave:
        out = jax.tree.map(lambda item: pltpu.VMEM(item.shape, item.dtype), out)
    return pl.pallas_call(
        kernel,
        out_shape=out,
        in_specs=specs,
        out_specs=jax.tree.map(lambda _: pl.BlockSpec(memory_space=place), out),
        scratch_shapes=scratch,
        compiler_params=pltpu.CompilerParams(vmem_limit_bytes=VMEM_BYTES),
        cost_estimate=pl.CostEstimate(flops=0, bytes_accessed=0, transcendentals=0),
    )(*operands)


def after(part, *earlier):
    anywhere = pl.BlockSpec(memory_space=pl.ANY)
    return pl.pallas_call(
        lambda *refs: None,
        out_shape=jax.ShapeDtypeStruct(part.shape, part.dtype),
        in_specs=[anywhere] * (1 + len(earlier)),
        out_specs=anywhere,
        input_output_aliases={0: 0},
        compiler_params=pltpu.CompilerParams(vmem_limit_bytes=1024 * 1024),
        cost_estimate=pl.CostEstimate(flops=0, bytes_accessed=0, transcendentals=0),
    )(part, *earlier)


def by_heads(
    queries, keys, values, rates, fast_weights, norm_gain, frame_order, gate_input, conv_weights
):
    tok_rows = queries.shape[0]
    head_count = queries.shape[1] * queries.shape[2]
    head_size = queries.shape[3]
    height, frames_here = gate_input.shape[:2]
    shards = lax.axis_size("tok")
    blocks = lax.axis_size("head")
    half = tok_rows // 2
    wide = 2 * head_size
    tiles = head_size // LANES + 1
    own = lax.axis_index("tok")
    own_channel = lax.axis_index("head") * head_count + own

    def rows_of(array):
        return array.reshape(tok_rows, head_count, head_size)

    def own_of(array, place):
        return lax.dynamic_index_in_dim(array, place, 0, keepdims=False)

    line = shards // 2
    tile_scratch = pltpu.VMEM((tiles, tok_rows * head_count, LANES), jnp.float32)
    token_rates = rates.reshape(head_count, tok_rows)
    chips = line // 2

    one = jax.ShapeDtypeStruct((tok_rows, wide), jnp.bfloat16)
    mirrored = call(
        pack_mirror_kernel,
        [one] * line,
        (rows_of(keys), rows_of(values), token_rates),
        (tile_scratch, tile_scratch),
    )
    mirrored = [mirrored[0]] + [send(mirrored[k], k) for k in range(1, line)]
    across = call(
        functools.partial(pack_across_kernel, height),
        [one] * chips,
        (pltpu.with_memory_space_constraint(rows_of(queries), pltpu.HBM),),
        (
            pltpu.VMEM((tok_rows, head_count, head_size), jnp.bfloat16),
            tile_scratch,
            pltpu.SemaphoreType.DMA((4,)),
        ),
        specs=[pl.BlockSpec(memory_space=pltpu.HBM)],
    )
    across_landed = [send(part, line + 2 * index) for index, part in enumerate(across)]
    weights = fast_weights.reshape(head_count, 3, head_size, head_size)
    own_weights = own_of(weights, own)
    mirror_weights = own_of(weights, own ^ line)
    own_gain = own_of(norm_gain.reshape(head_count, 1, head_size), own)
    taps = conv_weights.reshape(9, blocks * head_count, head_size)
    own_taps = lax.dynamic_index_in_dim(taps, own_channel, 1, keepdims=False)
    own_taps = jnp.pad(own_taps, ((0, 0), (0, tiles * LANES - head_size)))
    frames = frame_order[own ^ jnp.arange(shards, dtype=jnp.int32)]
    grad_shape = (3, head_size, tiles * LANES)
    grad_struct = jax.ShapeDtypeStruct(grad_shape, jnp.float32)
    unread = pl.BlockSpec(memory_space=pl.ANY)
    mirror_sum = call(
        functools.partial(sum_kernel, 2, tok_rows, False),
        grad_struct,
        (*mirrored[:2], mirror_weights),
    )
    early = (across[0], own_weights, own_gain, own_taps, frames, mirror_sum)
    query_struct = jax.ShapeDtypeStruct((half, wide), jnp.bfloat16)
    packed = call(
        functools.partial(pack_near_kernel, height, len(early)),
        [one] * line + [query_struct] * line,
        (rows_of(keys), rows_of(values), token_rates, rows_of(queries), *early),
        (tile_scratch, tile_scratch, tile_scratch),
        specs=in_vmem(4) + [unread] * len(early),
    )
    near_queries = packed[line:]
    held = [after(part, *mirrored[1:], *across_landed) for part in packed[1:line]]
    near = [packed[0]] + [send(held[k - 1], k) for k in range(1, line)]
    ahead = (*across_landed, *held)
    crossing = call(
        functools.partial(mirror_kernel, line - 2, tok_rows),
        jax.ShapeDtypeStruct((head_size + head_size // 2, wide), jnp.bfloat16),
        (*mirrored[2:], mirror_weights, mirror_sum, *ahead),
        (pltpu.VMEM(grad_shape, jnp.float32),),
        specs=in_vmem(line) + [unread] * len(ahead),
    )
    crossed = send(crossing, line)
    own_sum = call(
        functools.partial(sum_kernel, 2, tok_rows, False),
        grad_struct,
        (*near[:2], own_weights, crossing),
        specs=in_vmem(3) + [unread],
    )
    across = relay([after(part, own_sum) for part in across_landed])
    gate = gate_input.reshape(height, frames_here, gate_input.shape[3])
    opened = call(
        silu_kernel,
        jax.ShapeDtypeStruct((height * frames_here, gate_input.shape[3]), jnp.float32),
        (pltpu.with_memory_space_constraint(gate, pltpu.HBM), own_sum),
        (pltpu.VMEM(gate.shape, jnp.bfloat16), pltpu.SemaphoreType.DMA(())),
        specs=[pl.BlockSpec(memory_space=pltpu.HBM), unread],
    )
    gradients = call(
        functools.partial(sum_kernel, line - 2, tok_rows, True),
        grad_struct,
        (*near[2:], own_weights, own_sum, opened),
        specs=in_vmem(line) + [unread],
    )
    mate_queries = send(after(near_queries[1], own_sum), 1)
    late_queries = [
        send(after(near_queries[k], *near[2:]), k) for k in range(2, line)
    ]
    side_rows = frames_here * height // 2
    first_shards, far_shards, late_shards = (0, 1), range(line, shards), range(2, line)
    grid_shape = (tiles, shards, height + 16, LANES)
    turned_shape = (blocks, shards, tiles, 2 * side_rows, LANES)
    numbers = [pl.BlockSpec(memory_space=pltpu.SMEM)]
    updated, turned = call(
        functools.partial(apply_first_kernel, height, frames_here, first_shards, far_shards),
        [
            jax.ShapeDtypeStruct((3, head_size, head_size), jnp.bfloat16),
            jax.ShapeDtypeStruct(turned_shape, jnp.float32),
        ],
        (
            frames, near_queries[0], mate_queries, *across,
            own_weights, gradients, crossed, own_gain, own_taps,
        ),
        (pltpu.VMEM((2 + line, *grid_shape), jnp.float32),),
        specs=numbers + in_vmem(line + 7),
    )
    order = [(k, x) for k in range(0, shards, 2) for x in range(blocks)][1:]
    order = sorted(order, key=lambda place: (place != (line, 0), place))
    outgoing = call(
        functools.partial(apply_last_kernel, height, frames_here, late_shards, order),
        [jax.ShapeDtypeStruct((side_rows, wide), jnp.bfloat16)] * 2
        + [jax.ShapeDtypeStruct((2 * side_rows, wide), jnp.bfloat16)] * (shards // 2 * blocks - 1),
        (frames, *late_queries, updated, turned, own_gain, own_taps),
        (
            pltpu.VMEM((line - 2, *grid_shape), jnp.float32),
            pltpu.VMEM(turned_shape, jnp.float32),
        ),
        specs=numbers + in_vmem(line + 2),
    )
    landed = [send_far(part, k, x) for part, (k, x) in zip(outgoing[2:], order)]
    arrived = [outgoing[0], send(outgoing[1], 1), *relay(landed)]
    places = [(0, 0), *order]
    gated = call(
        functools.partial(gate_kernel, blocks, shards, places),
        jax.ShapeDtypeStruct(gate.shape, jnp.bfloat16),
        (*arrived, opened),
        (
            pltpu.VMEM((len(places), *gate.shape[:2], wide), jnp.bfloat16),
            pltpu.SemaphoreType.DMA((len(places),)),
        ),
        leave=False,
    )
    return gated.reshape(gate_input.shape)


def fits_by_heads(queries, gate_input, frame_order):
    tok_rows, head_size = queries.shape[0], queries.shape[3]
    head_count = queries.shape[1] * queries.shape[2]
    height, frames_here, col_width = gate_input.shape[:3]
    shards = lax.axis_size("tok")
    return (
        head_count == shards
        and frame_order.shape[0] == shards
        and lax.axis_size("tile") == 1
        and col_width == 1
        and shards >= 8
        and shards & (shards - 1) == 0
        and head_size % LANES == LANES // 2
        and height % 8 == 0
        and tok_rows == height * shards
        and tok_rows % 64 == 0
        and head_size % 64 == 0
        and frames_here * height % 32 == 0
        and frames_here * lax.axis_size("head") == shards
        and lax.axis_size("head") & (lax.axis_size("head") - 1) == 0
    )


def renormed(previous, gradient):
    before = previous.astype(jnp.float32)
    updated = before - gradient
    scale_old = jnp.sqrt(jnp.mean(before * before, axis=-1, keepdims=True) + epsilon)
    scale_new = jnp.sqrt(jnp.mean(updated * updated, axis=-1, keepdims=True) + epsilon)
    return (updated * (scale_old / scale_new)).astype(jnp.bfloat16)


def by_tokens(
    queries, keys, values, rates, fast_weights, norm_gain, frame_order, gate_input, conv_weights
):
    tok_rows = queries.shape[0]
    head_count = queries.shape[1] * queries.shape[2]
    head_size = queries.shape[3]
    query_rows = queries.reshape(tok_rows, head_count, head_size)
    key_rows = keys.reshape(tok_rows, head_count, head_size)
    value_rows = values.reshape(tok_rows, head_count, head_size)
    token_rates = rates.reshape(head_count, tok_rows)
    weights = fast_weights.reshape(head_count, 3, head_size, head_size)
    head_gains = norm_gain.reshape(head_count, head_size)
    first_pre = jnp.einsum(
        "thd,hfd->htf", key_rows, weights[:, 0], preferred_element_type=jnp.float32
    )
    third_pre = jnp.einsum(
        "thd,hfd->htf", key_rows, weights[:, 1], preferred_element_type=jnp.float32
    )
    sigmoid_first = jax.nn.sigmoid(first_pre)
    activated = first_pre * sigmoid_first
    hidden = (activated * third_pre).astype(jnp.bfloat16)
    target = (-token_rates.T[:, :, None] * value_rows.astype(jnp.float32)).astype(jnp.bfloat16)
    grad_down = jnp.einsum("thd,htf->hdf", target, hidden, preferred_element_type=jnp.float32)
    hidden_grad = jnp.einsum(
        "thd,hdf->htf", target, weights[:, 2], preferred_element_type=jnp.float32
    )
    grad_first_in = (
        hidden_grad * third_pre * sigmoid_first * (1.0 + first_pre * (1.0 - sigmoid_first))
    ).astype(jnp.bfloat16)
    grad_third_in = (hidden_grad * activated).astype(jnp.bfloat16)
    grad_first = jnp.einsum(
        "htf,thd->hfd", grad_first_in, key_rows, preferred_element_type=jnp.float32
    )
    grad_third = jnp.einsum(
        "htf,thd->hfd", grad_third_in, key_rows, preferred_element_type=jnp.float32
    )
    gradients = jnp.stack([grad_first, grad_third, grad_down], axis=1)
    row_share = lax.psum_scatter(gradients, "tok", scatter_dimension=2, tiled=True)
    row_count = row_share.shape[2]
    own_rows = lax.dynamic_slice_in_dim(weights, lax.axis_index("tok") * row_count, row_count, 2)
    updated = lax.all_gather(renormed(own_rows, row_share), "tok", axis=2, tiled=True)
    proj_first = jnp.einsum(
        "thd,hfd->thf", query_rows, updated[:, 0], preferred_element_type=jnp.float32
    )
    proj_third = jnp.einsum(
        "thd,hfd->thf", query_rows, updated[:, 1], preferred_element_type=jnp.float32
    )
    mixed_hidden = (jax.nn.silu(proj_first) * proj_third).astype(jnp.bfloat16)
    outputs = jnp.einsum(
        "thf,hdf->thd", mixed_hidden, updated[:, 2], preferred_element_type=jnp.float32
    )
    normed = (
        outputs
        * lax.rsqrt(jnp.mean(outputs * outputs, axis=-1, keepdims=True) + epsilon)
        * head_gains[None]
    )
    normed = normed.astype(jnp.bfloat16)
    height = gate_input.shape[0]
    col_width = gate_input.shape[2]
    shards = lax.axis_size("tok")
    full_width = col_width * shards
    channels_here = head_count * head_size
    frame_grid = normed.reshape(height, full_width, channels_here)
    own_taps = lax.dynamic_slice_in_dim(
        conv_weights, lax.axis_index("head") * channels_here, channels_here, 2
    )
    padded = jnp.pad(frame_grid, ((1, 1), (1, 1), (0, 0)))
    local_sum = jnp.zeros((height, full_width, channels_here), jnp.float32)
    for row_tap in range(3):
        for col_tap in range(3):
            local_sum = local_sum + own_taps[row_tap, col_tap] * padded[
                row_tap : row_tap + height, col_tap : col_tap + full_width
            ].astype(jnp.float32)
    outgoing = local_sum.astype(jnp.bfloat16).reshape(height, shards, col_width, channels_here)
    arrived = lax.all_to_all(outgoing, "tok", split_axis=1, concat_axis=1, tiled=True)
    frame_count = frame_order.shape[0]
    numbers = jnp.arange(frame_count, dtype=jnp.int32)
    inverse = jnp.sum(
        jnp.where(frame_order[None, :] == numbers[:, None], numbers[None, :], 0), axis=1
    )
    ordered = jnp.take(arrived, inverse, axis=1)
    tile_block = lax.all_to_all(ordered, "head", split_axis=1, concat_axis=3, tiled=True)
    return (tile_block.astype(jnp.float32) * jax.nn.silu(gate_input.astype(jnp.float32))).astype(
        jnp.bfloat16
    )


def local(queries, keys, values, rates, fast_weights, norm_gain, frame_order, gate_input, conv_weights):
    args = (
        queries, keys, values, rates, fast_weights, norm_gain, frame_order, gate_input, conv_weights
    )
    if fits_by_heads(queries, gate_input, frame_order):
        return by_heads(*args)
    return by_tokens(*args)


def solution(mesh):
    in_specs = (
        P(("groups", "tok"), "tile", "head", None),
        P(("groups", "tok"), "tile", "head", None),
        P(("groups", "tok"), "tile", "head", None),
        P("tile", "head", ("groups", "tok")),
        P("tile", "head", None, None, None),
        P("tile", "head", None),
        P("groups"),
        P(None, ("groups", "head"), "tok", "tile"),
        P(None, None, "tile"),
    )
    out_specs = P(None, ("groups", "head"), "tok", "tile")
    return jax.shard_map(local, mesh=mesh, in_specs=in_specs, out_specs=out_specs, check_vma=False)
```
